32 devices in a mesh: groups: 2 (over y), seq: 4 (over z), mp: 4 (over x, core).
Axes of the slice: x: 2, y: 2, z: 4, core: 2. Of those that a mesh axis runs over, the one named last changes fastest.
Arguments:
- queries: bfloat16 [2048, 4096], P(('groups', 'seq'), 'mp'), parts along dimension 0, may hold values from -170 to 170
- keys: bfloat16 [2048, 512], P(('groups', 'seq'), 'mp'), parts along dimension 0, may hold values from -4.5 to 4.5
- values: bfloat16 [2048, 512], P(('groups', 'seq'), 'mp'), parts along dimension 0, may hold values from -6 to 6
- lengths: int32 [6], P('groups'), parts along dimension 0, may hold values from 1 to 512, 1024 in all
- old_place: int32 [256], P('groups'), parts along dimension 0, may hold values from 0 to 127, as said below
Outputs:
- attended: bfloat16 [2048, 4096], P(('groups', 'seq'), 'mp'), parts along dimension 0
The draws below stay inside these ranges and needn't reach their ends.
There are 2 independent parts, one for each index of `groups`. The reference program is written for one: setup_inputs(seed, part) draws one part's arguments, and reference() takes and returns one part's arrays. A program takes and returns all parts, laid end to end along the dimension named above; each array names one. Nothing has to cross between parts.
Inputs may be any that keep to these rules, and one draw needn't show every extreme that they name: Each of the 3 lengths is at least 1, they sum to 1024, and the largest is exactly 512. `old_place`: A permutation of the 128 block places; places p * 32 to p * 32 + 31 belong to old owner p, blocks p * 32 to p * 32 + 31 to new owner p (index p of seq). Between any old owner and any new owner either no block or exactly 8 blocks move.
All inputs are finite; a program needn't handle non-finite values.
Results may differ from the reference program's by a relative error of at most 0.0029.
Values may be sent and summed in bfloat16 or wider, within the bound.
No kernel may reach another device: no remote copies, remote signals or barrier semaphores. Data moves between devices by JAX's collectives and lax.ppermute only.
A program may use at most 64 MiB of HBM per device.

```python
import math
import jax
import jax.numpy as jnp
import numpy as np
from jax import lax

QUERY_HEAD_TOTAL = 32
SHARED_KV_HEADS = 4
HEAD_WIDTH = 128
BLK = 8
TRAJ = 3
TOK_DEV = 256
REPLICA_TOKENS = 1024
LONGEST_LENGTH = 512
KB = 32
NB = 128
CAP = 8


def draw_keys(key, part):
    key = jax.random.fold_in(key, 5)
    return jnp.clip(jax.random.normal(key, (REPLICA_TOKENS, SHARED_KV_HEADS * HEAD_WIDTH), jnp.float32), -4.5, 4.5).astype(jnp.bfloat16)


def draw_queries(key, part):
    key = jax.random.fold_in(key, 7)
    return jnp.clip(2.5 * jax.random.normal(key, (REPLICA_TOKENS, QUERY_HEAD_TOTAL * HEAD_WIDTH), jnp.float32), -15.0, 15.0).astype(jnp.bfloat16)


def draw_old_place(key, part):
    key = jax.random.fold_in(key, 11)
    owners = REPLICA_TOKENS // TOK_DEV
    first_key, second_key, third_key = jax.random.split(key, 3)
    offsets_pool = jax.random.permutation(first_key, owners)[:KB // CAP]
    assign = jax.random.permutation(second_key, KB) // CAP
    offset = offsets_pool[assign]
    row_keys = jax.random.split(third_key, owners)
    slot_order = jax.vmap(lambda one_key: jax.random.permutation(one_key, KB))(row_keys)
    new_owner = jnp.arange(owners, dtype=jnp.int32)[:, None]
    old_owner = (new_owner + offset[None, :]) % owners
    old_slot = slot_order[old_owner, jnp.arange(KB, dtype=jnp.int32)[None, :]]
    return (old_owner * KB + old_slot).reshape(-1).astype(jnp.int32)


def block_scale(own_key, dims, cuts, low, largest):
    factor_of = 1.0
    for axis_at, parts in cuts:
        heights = jax.random.uniform(jax.random.fold_in(jax.random.fold_in(own_key, 6), axis_at), (parts,), jnp.float32, low / len(cuts), largest / len(cuts))
        factor_of = factor_of * jnp.repeat(jnp.exp(heights), dims[axis_at] // parts).reshape((-1,) + (1,) * (len(dims) - 1 - axis_at))
    return factor_of


def length_profile(amount, total, most, skew):
    loads = [(1 << 20) // math.isqrt(standing ** skew) + 1 for standing in range(2, amount + 1)]
    surplus, holding = total - most - (amount - 1), [1] * (amount - 1)
    while surplus > 0:
        free = [i for i in range(amount - 1) if holding[i] < most]
        whole, left = sum([loads[i] for i in free]), surplus
        for i in free:
            addition = min(most - holding[i], max(1, left * loads[i] // whole), surplus)
            holding[i] = holding[i] + addition
            surplus = surplus - addition
    return np.array([most] + holding)


def uneven(own_key, number_of, total, bound, slope):
    if number_of == 2:
        one = jax.random.randint(own_key, (), max(1, total - bound), min(bound, total - 1) + 1)
        return jnp.stack([one, total - one])
    tallies = jnp.asarray(length_profile(number_of, total, bound, slope), jnp.int32)
    twos = (number_of - 1) // 2
    giver, taker = tallies[1:1 + 2 * twos:2], tallies[2:2 + 2 * twos:2]
    room = jnp.minimum(giver - 1, bound - taker)
    shifted = jax.random.randint(jax.random.fold_in(own_key, 1), (twos,), 0, 1 << 20) % (room + 1)
    tallies = tallies.at[1:1 + 2 * twos:2].set(giver - shifted).at[2:2 + 2 * twos:2].set(taker + shifted)
    return tallies[jax.random.permutation(jax.random.fold_in(own_key, 2), number_of)]


def noise(stream_key, extent, scale, reach, cuts=(), kind=jnp.bfloat16):
    entries = jax.random.normal(stream_key, extent, jnp.float32) * scale
    if len(cuts) > 0:
        entries = block_scale(stream_key, extent, cuts, -0.22, 0.18) * entries
    return jnp.clip(entries, min=-reach, max=reach).astype(kind)


def setup_inputs(seed: int = 0, part: int = 0) -> dict:
    seeds = jax.random.split(jax.random.key(seed), 6)
    part_keys = jax.random.split(jax.random.fold_in(seeds[5], part), 6)
    queries = draw_queries(jax.random.fold_in(jax.random.fold_in(seeds[5], part), 71), part)
    keys = draw_keys(jax.random.fold_in(jax.random.fold_in(seeds[5], part), 71), part)
    values = noise(part_keys[2], (REPLICA_TOKENS, SHARED_KV_HEADS * HEAD_WIDTH), 1.0, 6.0, ((0, 4), (1, 4)))
    lengths = uneven(part_keys[3], TRAJ, REPLICA_TOKENS, LONGEST_LENGTH, 2).astype(jnp.int32)
    old_place = draw_old_place(jax.random.fold_in(jax.random.fold_in(seeds[5], part), 71), part)
    return dict(queries=queries, keys=keys, values=values, lengths=lengths, old_place=old_place)


NEG_FILL = -1e30


def trajectory_starts(lengths, positions):
    bounds = jnp.cumsum(lengths).astype(jnp.int32)
    passed = bounds[None, :] <= positions[:, None]
    return jnp.max(jnp.where(passed, bounds[None, :], 0), axis=1).astype(jnp.int32)


def reference(queries, keys, values, lengths, old_place):
    query_group_width = QUERY_HEAD_TOTAL // SHARED_KV_HEADS
    factor = HEAD_WIDTH ** -0.5

    def reorder(source):
        return source.reshape(NB, BLK, -1)[old_place].reshape(REPLICA_TOKENS, -1)

    new_queries = reorder(queries)
    fresh_keys = reorder(keys)
    new_values = reorder(values)
    positions = jnp.arange(REPLICA_TOKENS, dtype=jnp.int32)
    starts = trajectory_starts(lengths, positions)
    query_block = min(REPLICA_TOKENS, 512)
    window = LONGEST_LENGTH + query_block
    padding_rows = jnp.zeros((LONGEST_LENGTH, SHARED_KV_HEADS * HEAD_WIDTH), fresh_keys.dtype)
    padded_keys = jnp.concatenate([padding_rows, fresh_keys], axis=0)
    padded_values = jnp.concatenate([padding_rows, new_values], axis=0)

    def one_block(block_id):
        first_row = (block_id * query_block).astype(jnp.int32)
        query_rows = lax.dynamic_slice_in_dim(new_queries, first_row, query_block, 0)
        key_rows = lax.dynamic_slice_in_dim(padded_keys, first_row, window, 0)
        value_rows = lax.dynamic_slice_in_dim(padded_values, first_row, window, 0)
        query_pos = first_row + jnp.arange(query_block, dtype=jnp.int32)
        query_start = lax.dynamic_slice_in_dim(starts, first_row, query_block, 0)
        key_pos = first_row - LONGEST_LENGTH + jnp.arange(window, dtype=jnp.int32)
        visible = (key_pos[None, :] >= query_start[:, None]) & (key_pos[None, :] <= query_pos[:, None])
        visible = jnp.repeat(visible, query_group_width, axis=0)
        pieces = []
        for shared_value_head in range(SHARED_KV_HEADS):
            query_head = query_rows[:, shared_value_head * query_group_width * HEAD_WIDTH:(shared_value_head + 1) * query_group_width * HEAD_WIDTH]
            query_head = query_head.reshape(query_block * query_group_width, HEAD_WIDTH)
            key_head = key_rows[:, shared_value_head * HEAD_WIDTH:(shared_value_head + 1) * HEAD_WIDTH]
            value_head = value_rows[:, shared_value_head * HEAD_WIDTH:(shared_value_head + 1) * HEAD_WIDTH]
            scores = jnp.dot(query_head, key_head.T, preferred_element_type=jnp.float32) * factor
            row_max = jnp.max(jnp.where(visible, scores, NEG_FILL), axis=1)
            weights = jnp.where(visible, jnp.exp(scores - row_max[:, None]), 0.0)
            totals = jnp.sum(weights, axis=1)
            attended_head = jnp.dot(weights.astype(jnp.bfloat16), value_head, preferred_element_type=jnp.float32) / totals[:, None]
            pieces.append(attended_head.reshape(query_block, query_group_width * HEAD_WIDTH))
        return jnp.concatenate(pieces, axis=1).astype(jnp.bfloat16)

    blocks = lax.map(one_block, jnp.arange(REPLICA_TOKENS // query_block, dtype=jnp.int32))
    attended_new = blocks.reshape(NB, BLK, QUERY_HEAD_TOTAL * HEAD_WIDTH)
    returned = jnp.zeros_like(attended_new).at[old_place].set(attended_new)
    return returned.reshape(REPLICA_TOKENS, QUERY_HEAD_TOTAL * HEAD_WIDTH)
```

```python
import jax
import jax.numpy as jnp
from jax import lax
from jax.experimental import pallas as pl
from jax.experimental.pallas import tpu as pltpu
from jax.sharding import PartitionSpec as P

HEAD_WIDTH = 128
LOG2_E = 1.4426950408889634
NEG_FILL = -1e30


def block_places(lengths, old_place, own_index, row_count, key_count):
    block_total = old_place.shape[0]
    block_rows = key_count // block_total
    ids = jnp.arange(block_total, dtype=jnp.int32)
    hit = old_place[:, None] == ids[None, :]
    new_block = jnp.sum(jnp.where(hit, ids[:, None], 0), axis=0)
    key_pos = (new_block[:, None] * block_rows + jnp.arange(block_rows, dtype=jnp.int32)).reshape(-1)
    query_pos = lax.dynamic_slice_in_dim(key_pos, own_index * row_count, row_count)
    bounds = jnp.cumsum(lengths)
    starts = jnp.max(jnp.where(bounds[None, :] <= query_pos[:, None], bounds[None, :], 0), axis=1)
    return key_pos.reshape(1, -1), query_pos.reshape(-1, 1), starts.reshape(-1, 1)


def weights_kernel(heads, q_ref, k_ref, key_pos_ref, query_pos_ref, start_ref, p_ref):
    rows = q_ref.shape[0]
    key_pos = key_pos_ref[...]
    visible = (key_pos >= start_ref[...]) & (key_pos <= query_pos_ref[...])
    bias = jnp.where(visible, 0.0, NEG_FILL)
    keys = k_ref[...]
    for head in range(heads):
        q = q_ref[:, head * HEAD_WIDTH:(head + 1) * HEAD_WIDTH]
        scores = lax.dot_general(
            q, keys, (((1,), (1,)), ((), ())), preferred_element_type=jnp.float32
        )
        scaled = scores * (HEAD_WIDTH ** -0.5 * LOG2_E) + bias
        peak = jnp.max(scaled, axis=1, keepdims=True)
        p_ref[head] = jnp.exp2(scaled - peak).astype(jnp.bfloat16)


def mix_kernel(heads, p_ref, v_ref, out_ref):
    values = v_ref[...]
    ext = jnp.concatenate([values, jnp.ones_like(values)], axis=1)
    for head in range(heads):
        acc = jnp.dot(p_ref[head], ext, preferred_element_type=jnp.float32)
        out_ref[:, head * HEAD_WIDTH:(head + 1) * HEAD_WIDTH] = (
            acc[:, :HEAD_WIDTH] / acc[:, HEAD_WIDTH:]
        ).astype(jnp.bfloat16)


def tiled_attention(queries, keys, values, key_pos, query_pos, starts, tile):
    rows, cols = queries.shape
    heads = cols // HEAD_WIDTH
    key_count = keys.shape[0]
    weights = pl.pallas_call(
        lambda *refs: weights_kernel(heads, *refs),
        grid=(rows // tile,),
        in_specs=[
            pl.BlockSpec((tile, cols), lambda i: (i, 0)),
            pl.BlockSpec((key_count, HEAD_WIDTH), lambda i: (0, 0)),
            pl.BlockSpec((1, key_count), lambda i: (0, 0)),
            pl.BlockSpec((tile, 1), lambda i: (i, 0)),
            pl.BlockSpec((tile, 1), lambda i: (i, 0)),
        ],
        out_specs=pl.BlockSpec((heads, tile, key_count), lambda i: (0, i, 0)),
        out_shape=jax.ShapeDtypeStruct((heads, rows, key_count), jnp.bfloat16),
        compiler_params=pltpu.CompilerParams(vmem_limit_bytes=32 << 20),
        cost_estimate=pl.CostEstimate(
            flops=2 * heads * rows * key_count * HEAD_WIDTH,
            bytes_accessed=2 * heads * rows * key_count,
            transcendentals=heads * rows * key_count,
        ),
        name="weights",
    )(queries, keys, key_pos, query_pos, starts)
    return pl.pallas_call(
        lambda *refs: mix_kernel(heads, *refs),
        grid=(rows // tile,),
        in_specs=[
            pl.BlockSpec((heads, tile, key_count), lambda i: (0, i, 0)),
            pl.BlockSpec((key_count, HEAD_WIDTH), lambda i: (0, 0)),
        ],
        out_specs=pl.BlockSpec((tile, cols), lambda i: (i, 0)),
        out_shape=jax.ShapeDtypeStruct((rows, cols), jnp.bfloat16),
        compiler_params=pltpu.CompilerParams(vmem_limit_bytes=32 << 20),
        cost_estimate=pl.CostEstimate(
            flops=4 * heads * rows * key_count * HEAD_WIDTH,
            bytes_accessed=2 * heads * rows * key_count,
            transcendentals=0,
        ),
        name="mix",
    )(weights, values)


def online_kernel(heads, q_ref, k_ref, v_ref, key_pos_ref, query_pos_ref, start_ref, out_ref, peak_ref, acc_ref):
    step = pl.program_id(0)

    @pl.when(step == 0)
    def _():
        peak_ref[...] = jnp.full(peak_ref.shape, NEG_FILL, jnp.float32)
        acc_ref[...] = jnp.zeros(acc_ref.shape, jnp.float32)

    key_pos = key_pos_ref[...]
    visible = (key_pos >= start_ref[...]) & (key_pos <= query_pos_ref[...])
    values = v_ref[...]
    ext = jnp.concatenate([values, jnp.ones_like(values)], axis=1)
    for head in range(heads):
        q = q_ref[:, head * HEAD_WIDTH:(head + 1) * HEAD_WIDTH]
        scores = lax.dot_general(
            q, k_ref[...], (((1,), (1,)), ((), ())), preferred_element_type=jnp.float32
        )
        scaled = jnp.where(visible, scores * (HEAD_WIDTH ** -0.5 * LOG2_E), NEG_FILL)
        before = peak_ref[head]
        peak = jnp.maximum(before, jnp.max(scaled, axis=1, keepdims=True))
        weights = jnp.where(visible, jnp.exp2(scaled - peak), 0.0).astype(jnp.bfloat16)
        peak_ref[head] = peak
        acc_ref[head] = acc_ref[head] * jnp.exp2(before - peak) + jnp.dot(
            weights, ext, preferred_element_type=jnp.float32
        )

    @pl.when(step == pl.num_programs(0) - 1)
    def _():
        for head in range(heads):
            acc = acc_ref[head]
            out_ref[:, head * HEAD_WIDTH:(head + 1) * HEAD_WIDTH] = (
                acc[:, :HEAD_WIDTH] / acc[:, HEAD_WIDTH:]
            ).astype(jnp.bfloat16)


def online_attention(queries, keys, values, key_pos, query_pos, starts, chunk):
    rows, cols = queries.shape
    heads = cols // HEAD_WIDTH
    key_count = keys.shape[0]
    return pl.pallas_call(
        lambda *refs: online_kernel(heads, *refs),
        grid=(key_count // chunk,),
        in_specs=[
            pl.BlockSpec((rows, cols), lambda j: (0, 0)),
            pl.BlockSpec((chunk, HEAD_WIDTH), lambda j: (j, 0)),
            pl.BlockSpec((chunk, HEAD_WIDTH), lambda j: (j, 0)),
            pl.BlockSpec((1, chunk), lambda j: (0, j)),
            pl.BlockSpec((rows, 1), lambda j: (0, 0)),
            pl.BlockSpec((rows, 1), lambda j: (0, 0)),
        ],
        out_specs=pl.BlockSpec((rows, cols), lambda j: (0, 0)),
        out_shape=jax.ShapeDtypeStruct((rows, cols), jnp.bfloat16),
        scratch_shapes=[
            pltpu.VMEM((heads, rows, 1), jnp.float32),
            pltpu.VMEM((heads, rows, 2 * HEAD_WIDTH), jnp.float32),
        ],
        compiler_params=pltpu.CompilerParams(vmem_limit_bytes=32 << 20),
        name="online",
    )(queries, keys, values, key_pos, query_pos, starts)


def body(queries, keys, values, lengths, old_place):
    own_index = lax.axis_index("seq")
    row_count = queries.shape[0]
    key_count = row_count * lax.axis_size("seq")
    all_keys = lax.all_gather(keys, "seq", axis=0, tiled=True)
    all_values = lax.all_gather(values, "seq", axis=0, tiled=True)
    key_pos, query_pos, starts = block_places(lengths, old_place, own_index, row_count, key_count)
    if key_count <= 1024:
        return tiled_attention(queries, all_keys, all_values, key_pos, query_pos, starts, 64)
    return online_attention(queries, all_keys, all_values, key_pos, query_pos, starts, 512)


def solution(mesh):
    in_specs = (
        P(("groups", "seq"), "mp"),
        P(("groups", "seq"), "mp"),
        P(("groups", "seq"), "mp"),
        P("groups"),
        P("groups"),
    )
    out_specs = P(("groups", "seq"), "mp")
    return jax.shard_map(body, mesh=mesh, in_specs=in_specs, out_specs=out_specs, check_vma=False)
```

```python
import jax
import jax.numpy as jnp
from jax import lax
from jax.experimental import pallas as pl
from jax.experimental.pallas import tpu as pltpu
from jax.sharding import PartitionSpec as P

HEAD_WIDTH = 128
LOG2_E = 1.4426950408889634
NEG_FILL = -1e30


def block_places(lengths, old_place, own_index, row_count, key_count):
    block_total = old_place.shape[0]
    block_rows = key_count // block_total
    ids = jnp.arange(block_total, dtype=jnp.int32)
    hit = old_place[:, None] == ids[None, :]
    new_block = jnp.sum(jnp.where(hit, ids[:, None], 0), axis=0)
    key_pos = (new_block[:, None] * block_rows + jnp.arange(block_rows, dtype=jnp.int32)).reshape(-1)
    query_pos = lax.dynamic_slice_in_dim(key_pos, own_index * row_count, row_count)
    bounds = jnp.cumsum(lengths)
    starts = jnp.max(jnp.where(bounds[None, :] <= query_pos[:, None], bounds[None, :], 0), axis=1)
    return key_pos.reshape(1, -1), query_pos.reshape(-1, 1), starts.reshape(-1, 1)


def weights_kernel(heads, q_ref, key_pos_ref, query_pos_ref, start_ref, *refs):
    k_refs, p_ref = refs[:-1], refs[-1]
    key_pos = key_pos_ref[...]
    visible = (key_pos >= start_ref[...]) & (key_pos <= query_pos_ref[...])
    bias = jnp.where(visible, 0.0, NEG_FILL)
    keys = jnp.concatenate([k_ref[...] for k_ref in k_refs], axis=0)
    for head in range(heads):
        q = q_ref[:, head * HEAD_WIDTH:(head + 1) * HEAD_WIDTH]
        scores = lax.dot_general(
            q, keys, (((1,), (1,)), ((), ())), preferred_element_type=jnp.float32
        )
        scaled = scores * (HEAD_WIDTH ** -0.5 * LOG2_E) + bias
        peak = jnp.max(scaled, axis=1, keepdims=True)
        p_ref[head] = jnp.exp2(scaled - peak).astype(jnp.bfloat16)


def mix_kernel(heads, p_ref, *refs):
    v_refs, out_ref = refs[:-1], refs[-1]
    values = jnp.concatenate([v_ref[...] for v_ref in v_refs], axis=0)
    ext = jnp.concatenate([values, jnp.ones_like(values)], axis=1)
    for head in range(heads):
        acc = jnp.dot(p_ref[head], ext, preferred_element_type=jnp.float32)
        out_ref[:, head * HEAD_WIDTH:(head + 1) * HEAD_WIDTH] = (
            acc[:, :HEAD_WIDTH] / acc[:, HEAD_WIDTH:]
        ).astype(jnp.bfloat16)


def tiled_attention(queries, keys, values, key_pos, query_pos, starts, tile):
    rows, cols = queries.shape
    heads = cols // HEAD_WIDTH
    key_count = sum(shard.shape[0] for shard in keys)
    weights = pl.pallas_call(
        lambda *refs: weights_kernel(heads, *refs),
        grid=(rows // tile,),
        in_specs=[
            pl.BlockSpec((tile, cols), lambda i: (i, 0)),
            pl.BlockSpec((1, key_count), lambda i: (0, 0)),
            pl.BlockSpec((tile, 1), lambda i: (i, 0)),
            pl.BlockSpec((tile, 1), lambda i: (i, 0)),
        ] + [pl.BlockSpec(shard.shape, lambda i: (0, 0)) for shard in keys],
        out_specs=pl.BlockSpec((heads, tile, key_count), lambda i: (0, i, 0)),
        out_shape=jax.ShapeDtypeStruct((heads, rows, key_count), jnp.bfloat16),
        compiler_params=pltpu.CompilerParams(vmem_limit_bytes=32 << 20),
        cost_estimate=pl.CostEstimate(
            flops=2 * heads * rows * key_count * HEAD_WIDTH,
            bytes_accessed=2 * heads * rows * key_count,
            transcendentals=heads * rows * key_count,
        ),
        name="weights",
    )(queries, key_pos, query_pos, starts, *keys)
    return pl.pallas_call(
        lambda *refs: mix_kernel(heads, *refs),
        grid=(rows // tile,),
        in_specs=[
            pl.BlockSpec((heads, tile, key_count), lambda i: (0, i, 0)),
        ] + [pl.BlockSpec(shard.shape, lambda i: (0, 0)) for shard in values],
        out_specs=pl.BlockSpec((tile, cols), lambda i: (i, 0)),
        out_shape=jax.ShapeDtypeStruct((rows, cols), jnp.bfloat16),
        compiler_params=pltpu.CompilerParams(vmem_limit_bytes=32 << 20),
        cost_estimate=pl.CostEstimate(
            flops=4 * heads * rows * key_count * HEAD_WIDTH,
            bytes_accessed=2 * heads * rows * key_count,
            transcendentals=0,
        ),
        name="mix",
    )(weights, *values)


def online_kernel(heads, q_ref, k_ref, v_ref, key_pos_ref, query_pos_ref, start_ref, out_ref, peak_ref, acc_ref):
    step = pl.program_id(0)

    @pl.when(step == 0)
    def _():
        peak_ref[...] = jnp.full(peak_ref.shape, NEG_FILL, jnp.float32)
        acc_ref[...] = jnp.zeros(acc_ref.shape, jnp.float32)

    key_pos = key_pos_ref[...]
    visible = (key_pos >= start_ref[...]) & (key_pos <= query_pos_ref[...])
    values = v_ref[...]
    ext = jnp.concatenate([values, jnp.ones_like(values)], axis=1)
    for head in range(heads):
        q = q_ref[:, head * HEAD_WIDTH:(head + 1) * HEAD_WIDTH]
        scores = lax.dot_general(
            q, k_ref[...], (((1,), (1,)), ((), ())), preferred_element_type=jnp.float32
        )
        scaled = jnp.where(visible, scores * (HEAD_WIDTH ** -0.5 * LOG2_E), NEG_FILL)
        before = peak_ref[head]
        peak = jnp.maximum(before, jnp.max(scaled, axis=1, keepdims=True))
        weights = jnp.where(visible, jnp.exp2(scaled - peak), 0.0).astype(jnp.bfloat16)
        peak_ref[head] = peak
        acc_ref[head] = acc_ref[head] * jnp.exp2(before - peak) + jnp.dot(
            weights, ext, preferred_element_type=jnp.float32
        )

    @pl.when(step == pl.num_programs(0) - 1)
    def _():
        for head in range(heads):
            acc = acc_ref[head]
            out_ref[:, head * HEAD_WIDTH:(head + 1) * HEAD_WIDTH] = (
                acc[:, :HEAD_WIDTH] / acc[:, HEAD_WIDTH:]
            ).astype(jnp.bfloat16)


def online_attention(queries, keys, values, key_pos, query_pos, starts, chunk):
    rows, cols = queries.shape
    heads = cols // HEAD_WIDTH
    key_count = keys.shape[0]
    return pl.pallas_call(
        lambda *refs: online_kernel(heads, *refs),
        grid=(key_count // chunk,),
        in_specs=[
            pl.BlockSpec((rows, cols), lambda j: (0, 0)),
            pl.BlockSpec((chunk, HEAD_WIDTH), lambda j: (j, 0)),
            pl.BlockSpec((chunk, HEAD_WIDTH), lambda j: (j, 0)),
            pl.BlockSpec((1, chunk), lambda j: (0, j)),
            pl.BlockSpec((rows, 1), lambda j: (0, 0)),
            pl.BlockSpec((rows, 1), lambda j: (0, 0)),
        ],
        out_specs=pl.BlockSpec((rows, cols), lambda j: (0, 0)),
        out_shape=jax.ShapeDtypeStruct((rows, cols), jnp.bfloat16),
        scratch_shapes=[
            pltpu.VMEM((heads, rows, 1), jnp.float32),
            pltpu.VMEM((heads, rows, 2 * HEAD_WIDTH), jnp.float32),
        ],
        compiler_params=pltpu.CompilerParams(vmem_limit_bytes=32 << 20),
        name="online",
    )(queries, keys, values, key_pos, query_pos, starts)


def from_others(matrix):
    devices = lax.axis_size("seq")
    return [
        lax.ppermute(matrix, "seq", [(i, (i + by) % devices) for i in range(devices)])
        for by in range(1, devices)
    ]


def body(queries, keys, values, lengths, old_place):
    own_index = lax.axis_index("seq")
    row_count = queries.shape[0]
    devices = lax.axis_size("seq")
    key_count = row_count * devices
    key_pos, query_pos, starts = block_places(lengths, old_place, own_index, row_count, key_count)
    if key_count <= 1024:
        all_keys = [keys] + from_others(keys)
        all_values = [values] + from_others(values)
        by_device = key_pos.reshape(devices, row_count)
        key_pos = jnp.concatenate([by_device[(own_index - by) % devices] for by in range(devices)]).reshape(1, -1)
        return tiled_attention(queries, all_keys, all_values, key_pos, query_pos, starts, 64)
    all_keys = lax.all_gather(keys, "seq", axis=0, tiled=True)
    all_values = lax.all_gather(values, "seq", axis=0, tiled=True)
    return online_attention(queries, all_keys, all_values, key_pos, query_pos, starts, 512)


def solution(mesh):
    in_specs = (
        P(("groups", "seq"), "mp"),
        P(("groups", "seq"), "mp"),
        P(("groups", "seq"), "mp"),
        P("groups"),
        P("groups"),
    )
    out_specs = P(("groups", "seq"), "mp")
    return jax.shard_map(body, mesh=mesh, in_specs=in_specs, out_specs=out_specs, check_vma=False)
```

```python
import jax
import jax.numpy as jnp
from jax import lax
from jax.experimental import pallas as pl
from jax.experimental.pallas import tpu as pltpu
from jax.sharding import PartitionSpec as P

HEAD_WIDTH = 128
LOG2_E = 1.4426950408889634
NEG_FILL = -1e30


def block_places(lengths, old_place, own_index, row_count, key_count):
    block_total = old_place.shape[0]
    block_rows = key_count // block_total
    ids = jnp.arange(block_total, dtype=jnp.int32)
    hit = old_place[:, None] == ids[None, :]
    new_block = jnp.sum(jnp.where(hit, ids[:, None], 0), axis=0)
    key_pos = (new_block[:, None] * block_rows + jnp.arange(block_rows, dtype=jnp.int32)).reshape(-1)
    query_pos = lax.dynamic_slice_in_dim(key_pos, own_index * row_count, row_count)
    bounds = jnp.cumsum(lengths)
    starts = jnp.max(jnp.where(bounds[None, :] <= query_pos[:, None], bounds[None, :], 0), axis=1)
    return key_pos.reshape(1, -1), query_pos.reshape(-1, 1), starts.reshape(-1, 1)


def iota(shape, dim):
    return lax.broadcasted_iota(jnp.int32, shape, dim)


def visible_bias(own, owners, lengths_ref, places_ref, first_row, rows, shard_rows):
    block_total = places_ref.shape[1]
    block_rows = shard_rows * lax.axis_size("seq") // block_total
    blocks = shard_rows // block_rows
    places = places_ref[...]
    row = iota((rows, block_total), 0) + first_row
    hit = places == own * blocks + row // block_rows
    at = jnp.where(hit, iota((rows, block_total), 1) * block_rows, 0).astype(jnp.float32)
    query_pos = jnp.sum(at, axis=1, keepdims=True) + (
        (iota((rows, 1), 0) + first_row) % block_rows
    ).astype(jnp.float32)
    starts = jnp.zeros_like(query_pos)
    bound = jnp.int32(0)
    for t in range(lengths_ref.shape[0]):
        bound = bound + lengths_ref[t]
        edge = bound.astype(jnp.float32)
        starts = jnp.where(edge <= query_pos, edge, starts)
    square = (block_total, block_total)
    as_column = jnp.sum(
        jnp.where(iota(square, 0) == iota(square, 1), places, 0).astype(jnp.float32),
        axis=1, keepdims=True,
    ).astype(jnp.int32)
    parts = []
    for owner in owners:
        shape = (block_total, shard_rows)
        hit = as_column == owner * blocks + iota(shape, 1) // block_rows
        at = jnp.where(hit, iota(shape, 0) * block_rows, 0).astype(jnp.float32)
        parts.append(
            jnp.sum(at, axis=0, keepdims=True)
            + (iota((1, shard_rows), 1) % block_rows).astype(jnp.float32)
        )
    key_pos = jnp.concatenate(parts, axis=1)
    visible = (key_pos >= starts) & (key_pos <= query_pos)
    return jnp.where(visible, 0.0, NEG_FILL)


def scaled_scores(q_ref, rows, heads, keys, bias):
    q = jnp.concatenate(
        [q_ref[rows, head * HEAD_WIDTH:(head + 1) * HEAD_WIDTH] for head in range(heads)], axis=0
    )
    scores = lax.dot_general(
        q, keys, (((1,), (1,)), ((), ())), preferred_element_type=jnp.float32
    )
    scores = scores.reshape(heads, bias.shape[0], bias.shape[1])
    return scores * (HEAD_WIDTH ** -0.5 * LOG2_E) + bias[None]


def weigh(scaled, peak, values):
    heads, rows, key_count = scaled.shape
    weights = jnp.exp2(scaled - peak).astype(jnp.bfloat16).reshape(heads * rows, key_count)
    with_ones = jnp.concatenate([values, jnp.ones_like(values)], axis=1)
    summed = jnp.dot(weights, with_ones, preferred_element_type=jnp.float32)
    return summed.reshape(heads, rows, 2 * HEAD_WIDTH)


def first_kernel(tile, masks, own_ref, lengths_ref, places_ref, q_ref, k_ref, v_ref, *refs):
    pair_refs, (peak_ref, sum_ref, total_ref) = refs[:-3], refs[-3:]
    heads = q_ref.shape[1] // HEAD_WIDTH
    own = own_ref[0]
    owners = [own] + [own ^ mask for mask in masks]
    keys = jnp.concatenate([k_ref[...]] + [ref[:, :HEAD_WIDTH] for ref in pair_refs], axis=0)
    values = jnp.concatenate([v_ref[...]] + [ref[:, HEAD_WIDTH:] for ref in pair_refs], axis=0)
    for first_row in range(0, q_ref.shape[0], tile):
        rows = slice(first_row, first_row + tile)
        bias = visible_bias(own, owners, lengths_ref, places_ref, first_row, tile, k_ref.shape[0])
        scaled = scaled_scores(q_ref, rows, heads, keys, bias)
        peak = jnp.max(scaled, axis=2, keepdims=True)
        summed = weigh(scaled, peak, values)
        peak_ref[:, rows, :] = jnp.broadcast_to(peak, (heads, tile, HEAD_WIDTH))
        sum_ref[:, rows, :] = summed[:, :, :HEAD_WIDTH]
        total_ref[:, rows, :] = summed[:, :, HEAD_WIDTH:]


def last_kernel(
    tile, mask, own_ref, lengths_ref, places_ref, q_ref, peak_ref, sum_ref, total_ref, pair_ref,
    out_ref, block_ref, sems,
):
    heads = q_ref.shape[1] // HEAD_WIDTH
    own = own_ref[0]
    keys = pair_ref[:, :HEAD_WIDTH]
    values = pair_ref[:, HEAD_WIDTH:]
    copies = []
    for first_row in range(0, q_ref.shape[0], tile):
        rows = slice(first_row, first_row + tile)
        bias = visible_bias(own, [own ^ mask], lengths_ref, places_ref, first_row, tile, pair_ref.shape[0])
        scaled = scaled_scores(q_ref, rows, heads, keys, bias)
        before = peak_ref[:, rows, :]
        peak = jnp.maximum(before, jnp.max(scaled, axis=2, keepdims=True))
        summed = weigh(scaled, peak[:, :, :1], values)
        rescale = jnp.exp2(before - peak)
        out = (sum_ref[:, rows, :] * rescale + summed[:, :, :HEAD_WIDTH]) / (
            total_ref[:, rows, :] * rescale + summed[:, :, HEAD_WIDTH:]
        )
        for head in range(heads):
            block_ref[rows, head * HEAD_WIDTH:(head + 1) * HEAD_WIDTH] = out[head].astype(jnp.bfloat16)
        copy = pltpu.make_async_copy(
            block_ref.at[rows, :], out_ref.at[rows, :], sems.at[len(copies)]
        )
        copy.start()
        copies.append(copy)
    for copy in copies:
        copy.wait()


def estimate(rows, heads, key_count):
    return pl.CostEstimate(
        flops=6 * heads * rows * key_count * HEAD_WIDTH,
        bytes_accessed=8 * heads * rows * HEAD_WIDTH,
        transcendentals=heads * rows * key_count,
    )


def staged_attention(queries, keys, values, pairs, lengths, old_place, tile):
    rows, cols = queries.shape
    heads = cols // HEAD_WIDTH
    own = lax.axis_index("seq").astype(jnp.int32).reshape(1)
    scalars = (own, lengths, old_place.reshape(1, -1))
    scalar_specs = [
        pl.BlockSpec(memory_space=pltpu.SMEM),
        pl.BlockSpec(memory_space=pltpu.SMEM),
        pl.BlockSpec(memory_space=pltpu.VMEM),
    ]
    in_vmem = pl.BlockSpec(memory_space=pltpu.VMEM)
    *early, late = pairs
    state = pltpu.VMEM((heads, rows, HEAD_WIDTH), jnp.float32)
    carried = pl.pallas_call(
        lambda *refs: first_kernel(tile, early, *refs),
        in_specs=scalar_specs + [in_vmem] * (3 + len(early)),
        out_specs=[in_vmem] * 3,
        out_shape=[state] * 3,
        compiler_params=pltpu.CompilerParams(vmem_limit_bytes=32 << 20),
        cost_estimate=estimate(rows, heads, keys.shape[0] * (1 + len(early))),
        name="first_shards",
    )(*scalars, queries, keys, values, *[pairs[mask] for mask in early])
    carried = [pltpu.with_memory_space_constraint(part, pltpu.VMEM) for part in carried]
    return pl.pallas_call(
        lambda *refs: last_kernel(tile, late, *refs),
        in_specs=scalar_specs + [in_vmem] * 5,
        out_specs=pl.BlockSpec(memory_space=pl.ANY),
        out_shape=jax.ShapeDtypeStruct((rows, cols), jnp.bfloat16),
        scratch_shapes=[
            pltpu.VMEM((rows, cols), jnp.bfloat16),
            pltpu.SemaphoreType.DMA((rows // tile,)),
        ],
        compiler_params=pltpu.CompilerParams(vmem_limit_bytes=32 << 20),
        cost_estimate=estimate(rows, heads, keys.shape[0]),
        name="last_shard",
    )(*scalars, queries, *carried, pairs[late])


def online_kernel(heads, q_ref, k_ref, v_ref, key_pos_ref, query_pos_ref, start_ref, out_ref, peak_ref, acc_ref):
    step = pl.program_id(0)

    @pl.when(step == 0)
    def _():
        peak_ref[...] = jnp.full(peak_ref.shape, NEG_FILL, jnp.float32)
        acc_ref[...] = jnp.zeros(acc_ref.shape, jnp.float32)

    key_pos = key_pos_ref[...]
    visible = (key_pos >= start_ref[...]) & (key_pos <= query_pos_ref[...])
    values = v_ref[...]
    ext = jnp.concatenate([values, jnp.ones_like(values)], axis=1)
    for head in range(heads):
        q = q_ref[:, head * HEAD_WIDTH:(head + 1) * HEAD_WIDTH]
        scores = lax.dot_general(
            q, k_ref[...], (((1,), (1,)), ((), ())), preferred_element_type=jnp.float32
        )
        scaled = jnp.where(visible, scores * (HEAD_WIDTH ** -0.5 * LOG2_E), NEG_FILL)
        before = peak_ref[head]
        peak = jnp.maximum(before, jnp.max(scaled, axis=1, keepdims=True))
        weights = jnp.where(visible, jnp.exp2(scaled - peak), 0.0).astype(jnp.bfloat16)
        peak_ref[head] = peak
        acc_ref[head] = acc_ref[head] * jnp.exp2(before - peak) + jnp.dot(
            weights, ext, preferred_element_type=jnp.float32
        )

    @pl.when(step == pl.num_programs(0) - 1)
    def _():
        for head in range(heads):
            acc = acc_ref[head]
            out_ref[:, head * HEAD_WIDTH:(head + 1) * HEAD_WIDTH] = (
                acc[:, :HEAD_WIDTH] / acc[:, HEAD_WIDTH:]
            ).astype(jnp.bfloat16)


def online_attention(queries, keys, values, key_pos, query_pos, starts, chunk):
    rows, cols = queries.shape
    heads = cols // HEAD_WIDTH
    key_count = keys.shape[0]
    return pl.pallas_call(
        lambda *refs: online_kernel(heads, *refs),
        grid=(key_count // chunk,),
        in_specs=[
            pl.BlockSpec((rows, cols), lambda j: (0, 0)),
            pl.BlockSpec((chunk, HEAD_WIDTH), lambda j: (j, 0)),
            pl.BlockSpec((chunk, HEAD_WIDTH), lambda j: (j, 0)),
            pl.BlockSpec((1, chunk), lambda j: (0, j)),
            pl.BlockSpec((rows, 1), lambda j: (0, 0)),
            pl.BlockSpec((rows, 1), lambda j: (0, 0)),
        ],
        out_specs=pl.BlockSpec((rows, cols), lambda j: (0, 0)),
        out_shape=jax.ShapeDtypeStruct((rows, cols), jnp.bfloat16),
        scratch_shapes=[
            pltpu.VMEM((heads, rows, 1), jnp.float32),
            pltpu.VMEM((heads, rows, 2 * HEAD_WIDTH), jnp.float32),
        ],
        compiler_params=pltpu.CompilerParams(vmem_limit_bytes=32 << 20),
        name="online",
    )(queries, keys, values, key_pos, query_pos, starts)


def body(queries, keys, values, lengths, old_place):
    devices = lax.axis_size("seq")
    row_count = queries.shape[0]
    key_count = row_count * devices
    if devices == 4 and key_count <= 1024:
        own_pair = jnp.concatenate([keys, values], axis=1)
        pairs = {
            mask: lax.ppermute(own_pair, "seq", [(i, i ^ mask) for i in range(devices)])
            for mask in (2, 1, 3)
        }
        return staged_attention(queries, keys, values, pairs, lengths, old_place, 64)
    all_keys = lax.all_gather(keys, "seq", axis=0, tiled=True)
    all_values = lax.all_gather(values, "seq", axis=0, tiled=True)
    key_pos, query_pos, starts = block_places(
        lengths, old_place, lax.axis_index("seq"), row_count, key_count
    )
    return online_attention(queries, all_keys, all_values, key_pos, query_pos, starts, 512)


def solution(mesh):
    in_specs = (
        P(("groups", "seq"), "mp"),
        P(("groups", "seq"), "mp"),
        P(("groups", "seq"), "mp"),
        P("groups"),
        P("groups"),
    )
    out_specs = P(("groups", "seq"), "mp")
    return jax.shard_map(body, mesh=mesh, in_specs=in_specs, out_specs=out_specs, check_vma=False)
```

```python
import jax
import jax.numpy as jnp
from jax import lax
from jax.experimental import pallas as pl
from jax.experimental.pallas import tpu as pltpu
from jax.sharding import PartitionSpec as P

HEAD_WIDTH = 128
LOG2_E = 1.4426950408889634
NEG_FILL = -1e30
ONES = 16


def block_places(lengths, old_place, own_index, row_count, key_count):
    block_total = old_place.shape[0]
    block_rows = key_count // block_total
    ids = jnp.arange(block_total, dtype=jnp.int32)
    hit = old_place[:, None] == ids[None, :]
    new_block = jnp.sum(jnp.where(hit, ids[:, None], 0), axis=0)
    key_pos = (new_block[:, None] * block_rows + jnp.arange(block_rows, dtype=jnp.int32)).reshape(-1)
    query_pos = lax.dynamic_slice_in_dim(key_pos, own_index * row_count, row_count)
    bounds = jnp.cumsum(lengths)
    starts = jnp.max(jnp.where(bounds[None, :] <= query_pos[:, None], bounds[None, :], 0), axis=1)
    return key_pos.reshape(1, -1), query_pos.reshape(-1, 1), starts.reshape(-1, 1)


def iota(shape, dim):
    return lax.broadcasted_iota(jnp.int32, shape, dim)


def mask_tables(own, owners, lengths_ref, places_ref, rows, bias_ref):
    block_total = places_ref.shape[1]
    block_rows = rows * lax.axis_size("seq") // block_total
    blocks = rows // block_rows
    places = places_ref[...]
    square = (block_total, block_total)
    as_column = jnp.sum(
        jnp.where(iota(square, 0) == iota(square, 1), places, 0).astype(jnp.float32),
        axis=1, keepdims=True,
    ).astype(jnp.int32)
    across = (block_total, rows)
    hit = as_column == own * blocks + iota(across, 1) // block_rows
    at = jnp.where(hit, iota(across, 0) * block_rows, 0).astype(jnp.float32)
    query_pos = jnp.sum(at, axis=0, keepdims=True) + (
        iota((1, rows), 1) % block_rows
    ).astype(jnp.float32)
    starts = jnp.zeros_like(query_pos)
    bound = jnp.int32(0)
    for t in range(lengths_ref.shape[0]):
        bound = bound + lengths_ref[t]
        edge = bound.astype(jnp.float32)
        starts = jnp.where(edge <= query_pos, edge, starts)
    down = (rows, block_total)
    for n, owner in enumerate(owners):
        hit = places == owner * blocks + iota(down, 0) // block_rows
        at = jnp.where(hit, iota(down, 1) * block_rows, 0).astype(jnp.float32)
        key_pos = jnp.sum(at, axis=1, keepdims=True) + (
            iota((rows, 1), 0) % block_rows
        ).astype(jnp.float32)
        visible = (key_pos >= starts) & (key_pos <= query_pos)
        bias_ref[n] = jnp.where(visible, 0.0, NEG_FILL)


def scaled_scores(keys, q_across, bias):
    scores = jnp.dot(keys, q_across, preferred_element_type=jnp.float32)
    return scores * (HEAD_WIDTH ** -0.5 * LOG2_E) + bias


def values_down(values):
    turned = jnp.transpose(values.astype(jnp.float32)).astype(jnp.bfloat16)
    return jnp.concatenate([turned, jnp.ones((ONES, values.shape[0]), jnp.bfloat16)], axis=0)


def weigh(scaled, peak, turned):
    weights = jnp.exp2(scaled - peak).astype(jnp.bfloat16)
    return jnp.dot(turned, weights, preferred_element_type=jnp.float32)


def own_kernel(
    masks, own_ref, lengths_ref, places_ref, q_ref, k_ref, v_ref,
    across_ref, bias_ref, peak_ref, sum_ref,
):
    heads = q_ref.shape[1] // HEAD_WIDTH
    own = own_ref[0]
    owners = [own] + [own ^ mask for mask in masks]
    mask_tables(own, owners, lengths_ref, places_ref, q_ref.shape[0], bias_ref)
    turned = values_down(v_ref[...])
    for head in range(heads):
        q = q_ref[:, head * HEAD_WIDTH:(head + 1) * HEAD_WIDTH]
        across = jnp.transpose(q.astype(jnp.float32)).astype(jnp.bfloat16)
        across_ref[head] = across
        scaled = scaled_scores(k_ref[...], across, bias_ref[0])
        peak = jnp.max(scaled, axis=0, keepdims=True)
        peak_ref[head:head + 1, :] = peak
        sum_ref[head] = weigh(scaled, peak, turned)


def add_shard(head, bias, keys, turned, across_ref, peak_ref, sum_ref):
    scaled = scaled_scores(keys, across_ref[head], bias)
    before = peak_ref[head:head + 1, :]
    peak = jnp.maximum(before, jnp.max(scaled, axis=0, keepdims=True))
    return peak, sum_ref[head] * jnp.exp2(before - peak) + weigh(scaled, peak, turned)


def next_kernel(at, across_ref, bias_ref, peak_ref, sum_ref, pair_ref, new_peak_ref, new_sum_ref):
    keys = pair_ref[:, :HEAD_WIDTH]
    turned = values_down(pair_ref[:, HEAD_WIDTH:])
    for head in range(across_ref.shape[0]):
        peak, summed = add_shard(head, bias_ref[at], keys, turned, across_ref, peak_ref, sum_ref)
        new_peak_ref[head:head + 1, :] = peak
        new_sum_ref[head] = summed


def last_kernel(at, across_ref, bias_ref, peak_ref, sum_ref, pair_ref, out_ref, block_ref, sems):
    keys = pair_ref[:, :HEAD_WIDTH]
    turned = values_down(pair_ref[:, HEAD_WIDTH:])
    copies = []
    for head in range(across_ref.shape[0]):
        _, summed = add_shard(head, bias_ref[at], keys, turned, across_ref, peak_ref, sum_ref)
        out = summed[:HEAD_WIDTH] / summed[HEAD_WIDTH:HEAD_WIDTH + 1]
        cols = slice(head * HEAD_WIDTH, (head + 1) * HEAD_WIDTH)
        block_ref[:, cols] = jnp.transpose(out).astype(jnp.bfloat16)
        copy = pltpu.make_async_copy(block_ref.at[:, cols], out_ref.at[:, cols], sems.at[head])
        copy.start()
        copies.append(copy)
    for copy in copies:
        copy.wait()


def estimate(rows, heads, key_count):
    return pl.CostEstimate(
        flops=6 * heads * rows * key_count * HEAD_WIDTH,
        bytes_accessed=8 * heads * rows * HEAD_WIDTH,
        transcendentals=heads * rows * key_count,
    )


def in_vmem(*arrays):
    return [pltpu.with_memory_space_constraint(array, pltpu.VMEM) for array in arrays]


def staged_attention(queries, keys, values, pairs, lengths, old_place):
    rows, cols = queries.shape
    heads = cols // HEAD_WIDTH
    own = lax.axis_index("seq").astype(jnp.int32).reshape(1)
    whole = pl.BlockSpec(memory_space=pltpu.VMEM)
    params = pltpu.CompilerParams(vmem_limit_bytes=32 << 20)
    state = [
        pltpu.VMEM((heads, rows), jnp.float32),
        pltpu.VMEM((heads, HEAD_WIDTH + ONES, rows), jnp.float32),
    ]
    across, bias, *carried = pl.pallas_call(
        lambda *refs: own_kernel(list(pairs), *refs),
        in_specs=[pl.BlockSpec(memory_space=pltpu.SMEM)] * 2 + [whole] * 4,
        out_specs=[whole] * 4,
        out_shape=[
            pltpu.VMEM((heads, HEAD_WIDTH, rows), jnp.bfloat16),
            pltpu.VMEM((1 + len(pairs), rows, rows), jnp.float32),
        ] + state,
        compiler_params=params,
        cost_estimate=estimate(rows, heads, rows),
        name="own_shard",
    )(own, lengths, old_place.reshape(1, -1), queries, keys, values)
    *early, last = pairs
    for at, mask in enumerate(early):
        carried = pl.pallas_call(
            lambda *refs, at=at: next_kernel(1 + at, *refs),
            in_specs=[whole] * 5,
            out_specs=[whole] * 2,
            out_shape=state,
            compiler_params=params,
            cost_estimate=estimate(rows, heads, rows),
            name="next_shard",
        )(*in_vmem(across, bias, *carried), pairs[mask])
    return pl.pallas_call(
        lambda *refs: last_kernel(1 + len(early), *refs),
        in_specs=[whole] * 5,
        out_specs=pl.BlockSpec(memory_space=pl.ANY),
        out_shape=jax.ShapeDtypeStruct((rows, cols), jnp.bfloat16),
        scratch_shapes=[
            pltpu.VMEM((rows, cols), jnp.bfloat16),
            pltpu.SemaphoreType.DMA((heads,)),
        ],
        compiler_params=params,
        cost_estimate=estimate(rows, heads, rows),
        name="last_shard",
    )(*in_vmem(across, bias, *carried), pairs[last])


def online_kernel(heads, q_ref, k_ref, v_ref, key_pos_ref, query_pos_ref, start_ref, out_ref, peak_ref, acc_ref):
    step = pl.program_id(0)

    @pl.when(step == 0)
    def _():
        peak_ref[...] = jnp.full(peak_ref.shape, NEG_FILL, jnp.float32)
        acc_ref[...] = jnp.zeros(acc_ref.shape, jnp.float32)

    key_pos = key_pos_ref[...]
    visible = (key_pos >= start_ref[...]) & (key_pos <= query_pos_ref[...])
    values = v_ref[...]
    ext = jnp.concatenate([values, jnp.ones_like(values)], axis=1)
    for head in range(heads):
        q = q_ref[:, head * HEAD_WIDTH:(head + 1) * HEAD_WIDTH]
        scores = lax.dot_general(
            q, k_ref[...], (((1,), (1,)), ((), ())), preferred_element_type=jnp.float32
        )
        scaled = jnp.where(visible, scores * (HEAD_WIDTH ** -0.5 * LOG2_E), NEG_FILL)
        before = peak_ref[head]
        peak = jnp.maximum(before, jnp.max(scaled, axis=1, keepdims=True))
        weights = jnp.where(visible, jnp.exp2(scaled - peak), 0.0).astype(jnp.bfloat16)
        peak_ref[head] = peak
        acc_ref[head] = acc_ref[head] * jnp.exp2(before - peak) + jnp.dot(
            weights, ext, preferred_element_type=jnp.float32
        )

    @pl.when(step == pl.num_programs(0) - 1)
    def _():
        for head in range(heads):
            acc = acc_ref[head]
            out_ref[:, head * HEAD_WIDTH:(head + 1) * HEAD_WIDTH] = (
                acc[:, :HEAD_WIDTH] / acc[:, HEAD_WIDTH:]
            ).astype(jnp.bfloat16)


def online_attention(queries, keys, values, key_pos, query_pos, starts, chunk):
    rows, cols = queries.shape
    heads = cols // HEAD_WIDTH
    key_count = keys.shape[0]
    return pl.pallas_call(
        lambda *refs: online_kernel(heads, *refs),
        grid=(key_count // chunk,),
        in_specs=[
            pl.BlockSpec((rows, cols), lambda j: (0, 0)),
            pl.BlockSpec((chunk, HEAD_WIDTH), lambda j: (j, 0)),
            pl.BlockSpec((chunk, HEAD_WIDTH), lambda j: (j, 0)),
            pl.BlockSpec((1, chunk), lambda j: (0, j)),
            pl.BlockSpec((rows, 1), lambda j: (0, 0)),
            pl.BlockSpec((rows, 1), lambda j: (0, 0)),
        ],
        out_specs=pl.BlockSpec((rows, cols), lambda j: (0, 0)),
        out_shape=jax.ShapeDtypeStruct((rows, cols), jnp.bfloat16),
        scratch_shapes=[
            pltpu.VMEM((heads, rows, 1), jnp.float32),
            pltpu.VMEM((heads, rows, 2 * HEAD_WIDTH), jnp.float32),
        ],
        compiler_params=pltpu.CompilerParams(vmem_limit_bytes=32 << 20),
        name="online",
    )(queries, keys, values, key_pos, query_pos, starts)


def body(queries, keys, values, lengths, old_place):
    devices = lax.axis_size("seq")
    row_count = queries.shape[0]
    key_count = row_count * devices
    if devices == 4 and key_count <= 1024:
        own_pair = jnp.concatenate([keys, values], axis=1)
        pairs = {
            mask: lax.ppermute(own_pair, "seq", [(i, i ^ mask) for i in range(devices)])
            for mask in (2, 1, 3)
        }
        return staged_attention(queries, keys, values, pairs, lengths, old_place)
    all_keys = lax.all_gather(keys, "seq", axis=0, tiled=True)
    all_values = lax.all_gather(values, "seq", axis=0, tiled=True)
    key_pos, query_pos, starts = block_places(
        lengths, old_place, lax.axis_index("seq"), row_count, key_count
    )
    return online_attention(queries, all_keys, all_values, key_pos, query_pos, starts, 512)


def solution(mesh):
    in_specs = (
        P(("groups", "seq"), "mp"),
        P(("groups", "seq"), "mp"),
        P(("groups", "seq"), "mp"),
        P("groups"),
        P("groups"),
    )
    out_specs = P(("groups", "seq"), "mp")
    return jax.shard_map(body, mesh=mesh, in_specs=in_specs, out_specs=out_specs, check_vma=False)
```

```python
import jax
import jax.numpy as jnp
from jax import lax
from jax.experimental import pallas as pl
from jax.experimental.pallas import tpu as pltpu
from jax.sharding import PartitionSpec as P

HEAD_WIDTH = 128
LOG2_E = 1.4426950408889634
NEG_FILL = -1e30
ONES = 16


def block_places(lengths, old_place, own_index, row_count, key_count):
    block_total = old_place.shape[0]
    block_rows = key_count // block_total
    ids = jnp.arange(block_total, dtype=jnp.int32)
    hit = old_place[:, None] == ids[None, :]
    new_block = jnp.sum(jnp.where(hit, ids[:, None], 0), axis=0)
    key_pos = (new_block[:, None] * block_rows + jnp.arange(block_rows, dtype=jnp.int32)).reshape(-1)
    query_pos = lax.dynamic_slice_in_dim(key_pos, own_index * row_count, row_count)
    bounds = jnp.cumsum(lengths)
    starts = jnp.max(jnp.where(bounds[None, :] <= query_pos[:, None], bounds[None, :], 0), axis=1)
    return key_pos.reshape(1, -1), query_pos.reshape(-1, 1), starts.reshape(-1, 1)


def iota(shape, dim):
    return lax.broadcasted_iota(jnp.int32, shape, dim)


def mask_tables(own, owners, lengths_ref, places_ref, rows, bias_ref):
    block_total = places_ref.shape[1]
    block_rows = rows * lax.axis_size("seq") // block_total
    blocks = rows // block_rows
    places = places_ref[...]
    square = (block_total, block_total)
    as_column = jnp.sum(
        jnp.where(iota(square, 0) == iota(square, 1), places, 0).astype(jnp.float32),
        axis=1, keepdims=True,
    ).astype(jnp.int32)
    across = (block_total, rows)
    hit = as_column == own * blocks + iota(across, 1) // block_rows
    at = jnp.where(hit, iota(across, 0) * block_rows, 0).astype(jnp.float32)
    query_pos = jnp.sum(at, axis=0, keepdims=True) + (
        iota((1, rows), 1) % block_rows
    ).astype(jnp.float32)
    starts = jnp.zeros_like(query_pos)
    bound = jnp.int32(0)
    for t in range(lengths_ref.shape[0]):
        bound = bound + lengths_ref[t]
        edge = bound.astype(jnp.float32)
        starts = jnp.where(edge <= query_pos, edge, starts)
    down = (rows, block_total)
    for n, owner in enumerate(owners):
        hit = places == owner * blocks + iota(down, 0) // block_rows
        at = jnp.where(hit, iota(down, 1) * block_rows, 0).astype(jnp.float32)
        key_pos = jnp.sum(at, axis=1, keepdims=True) + (
            iota((rows, 1), 0) % block_rows
        ).astype(jnp.float32)
        visible = (key_pos >= starts) & (key_pos <= query_pos)
        bias_ref[n] = jnp.where(visible, 0.0, NEG_FILL)


def values_down(values):
    turned = jnp.transpose(values.astype(jnp.float32)).astype(jnp.bfloat16)
    return jnp.concatenate([turned, jnp.ones((ONES, values.shape[0]), jnp.bfloat16)], axis=0)


def in_stages(heads, stages):
    results = [{} for _ in stages]
    for step in range(heads + len(stages) - 1):
        for late, stage in enumerate(stages):
            head = step - late
            if 0 <= head < heads:
                before = results[late - 1].pop(head) if late else None
                results[late][head] = stage(head, before)


def score_stage(keys, across_ref, bias_ref, at, scaled_ref, old_peak):
    def stage(head, _):
        scores = jnp.dot(keys, across_ref[head], preferred_element_type=jnp.float32)
        scaled = scores * (HEAD_WIDTH ** -0.5 * LOG2_E) + bias_ref[at]
        scaled_ref[head] = scaled
        peak = jnp.max(scaled, axis=0, keepdims=True)
        return peak if old_peak is None else jnp.maximum(old_peak(head), peak)

    return stage


def weight_stage(scaled_ref, weight_ref):
    def stage(head, peak):
        weight_ref[head] = jnp.exp2(scaled_ref[head] - peak).astype(jnp.bfloat16)
        return peak

    return stage


def pack_kernel(k_ref, v_ref, pair_ref, sems):
    copies = [
        pltpu.make_async_copy(ref, pair_ref.at[:, at * HEAD_WIDTH:(at + 1) * HEAD_WIDTH], sems.at[at])
        for at, ref in enumerate((k_ref, v_ref))
    ]
    for copy in copies:
        copy.start()
    for copy in copies:
        copy.wait()


def own_kernel(
    masks, own_ref, lengths_hbm, places_hbm, q_hbm, pair_ref,
    across_ref, bias_ref, peak_ref, sum_ref,
    lengths_ref, places_ref, q_ref, scaled_ref, weight_ref, sems,
):
    moves = ((lengths_hbm, lengths_ref), (places_hbm, places_ref), (q_hbm, q_ref))
    copies = [pltpu.make_async_copy(*move, sems.at[n]) for n, move in enumerate(moves)]
    for copy in copies:
        copy.start()
    turned = values_down(pair_ref[:, HEAD_WIDTH:])
    keys = pair_ref[:, :HEAD_WIDTH]
    copies[0].wait()
    copies[1].wait()
    heads, _, rows = across_ref.shape
    own = own_ref[0]
    owners = [own] + [own ^ mask for mask in masks]
    mask_tables(own, owners, lengths_ref, places_ref, rows, bias_ref)
    copies[2].wait()

    def turn(head, _):
        q = q_ref[:, head * HEAD_WIDTH:(head + 1) * HEAD_WIDTH]
        across_ref[head] = jnp.transpose(q.astype(jnp.float32)).astype(jnp.bfloat16)

    def mix(head, peak):
        peak_ref[head:head + 1, :] = peak
        sum_ref[head] = jnp.dot(turned, weight_ref[head], preferred_element_type=jnp.float32)

    in_stages(heads, [
        turn,
        score_stage(keys, across_ref, bias_ref, 0, scaled_ref, None),
        weight_stage(scaled_ref, weight_ref),
        mix,
    ])


def joined(head, peak, turned, weight_ref, peak_ref, sum_ref):
    added = jnp.dot(turned, weight_ref[head], preferred_element_type=jnp.float32)
    return sum_ref[head] * jnp.exp2(peak_ref[head:head + 1, :] - peak) + added


def next_kernel(
    at, across_ref, bias_ref, peak_ref, sum_ref, pair_ref, new_peak_ref, new_sum_ref,
    scaled_ref, weight_ref,
):
    turned = values_down(pair_ref[:, HEAD_WIDTH:])

    def mix(head, peak):
        new_peak_ref[head:head + 1, :] = peak
        new_sum_ref[head] = joined(head, peak, turned, weight_ref, peak_ref, sum_ref)

    in_stages(across_ref.shape[0], [
        score_stage(
            pair_ref[:, :HEAD_WIDTH], across_ref, bias_ref, at, scaled_ref,
            lambda head: peak_ref[head:head + 1, :],
        ),
        weight_stage(scaled_ref, weight_ref),
        mix,
    ])


def last_kernel(
    at, across_ref, bias_ref, peak_ref, sum_ref, pair_ref, out_ref,
    scaled_ref, weight_ref, block_ref, sems,
):
    turned = values_down(pair_ref[:, HEAD_WIDTH:])
    copies = []

    def mix(head, peak):
        summed = joined(head, peak, turned, weight_ref, peak_ref, sum_ref)
        return summed[:HEAD_WIDTH] / summed[HEAD_WIDTH:HEAD_WIDTH + 1]

    def send(head, out):
        cols = slice(head * HEAD_WIDTH, (head + 1) * HEAD_WIDTH)
        block_ref[:, cols] = jnp.transpose(out).astype(jnp.bfloat16)
        copy = pltpu.make_async_copy(block_ref.at[:, cols], out_ref.at[:, cols], sems.at[head])
        copy.start()
        copies.append(copy)

    in_stages(across_ref.shape[0], [
        score_stage(
            pair_ref[:, :HEAD_WIDTH], across_ref, bias_ref, at, scaled_ref,
            lambda head: peak_ref[head:head + 1, :],
        ),
        weight_stage(scaled_ref, weight_ref),
        mix,
        send,
    ])
    for copy in copies:
        copy.wait()


def estimate(rows, heads, key_count):
    return pl.CostEstimate(
        flops=6 * heads * rows * key_count * HEAD_WIDTH,
        bytes_accessed=8 * heads * rows * HEAD_WIDTH,
        transcendentals=heads * rows * key_count,
    )


def in_vmem(*arrays):
    return [pltpu.with_memory_space_constraint(array, pltpu.VMEM) for array in arrays]


def in_hbm(*arrays):
    return [pltpu.with_memory_space_constraint(array, pltpu.HBM) for array in arrays]


VMEM_REF = pl.BlockSpec(memory_space=pltpu.VMEM)
HBM_REF = pl.BlockSpec(memory_space=pltpu.HBM)
PARAMS = pltpu.CompilerParams(vmem_limit_bytes=32 << 20)


def packed_pair(keys, values):
    return pl.pallas_call(
        pack_kernel,
        in_specs=[HBM_REF] * 2,
        out_specs=VMEM_REF,
        out_shape=pltpu.VMEM((keys.shape[0], 2 * HEAD_WIDTH), keys.dtype),
        scratch_shapes=[pltpu.SemaphoreType.DMA((2,))],
        compiler_params=PARAMS,
        name="pack",
    )(*in_hbm(keys, values))


def staged_attention(queries, own_pair, pairs, lengths, old_place):
    rows, cols = queries.shape
    heads = cols // HEAD_WIDTH
    own = lax.axis_index("seq").astype(jnp.int32).reshape(1)
    places = old_place.reshape(1, -1)
    state = [
        pltpu.VMEM((heads, rows), jnp.float32),
        pltpu.VMEM((heads, HEAD_WIDTH + ONES, rows), jnp.float32),
    ]
    work = [
        pltpu.VMEM((heads, rows, rows), jnp.float32),
        pltpu.VMEM((heads, rows, rows), jnp.bfloat16),
    ]
    cost = estimate(rows, heads, rows)
    across, bias, *carried = pl.pallas_call(
        lambda *refs: own_kernel(list(pairs), *refs),
        in_specs=[pl.BlockSpec(memory_space=pltpu.SMEM)] + [HBM_REF] * 3 + [VMEM_REF],
        out_specs=[VMEM_REF] * 4,
        out_shape=[
            pltpu.VMEM((heads, HEAD_WIDTH, rows), jnp.bfloat16),
            pltpu.VMEM((1 + len(pairs), rows, rows), jnp.float32),
        ] + state,
        scratch_shapes=[
            pltpu.SMEM(lengths.shape, jnp.int32),
            pltpu.VMEM(places.shape, jnp.int32),
            pltpu.VMEM(queries.shape, jnp.bfloat16),
        ] + work + [pltpu.SemaphoreType.DMA((3,))],
        compiler_params=PARAMS,
        cost_estimate=cost,
        name="own_shard",
    )(own, *in_hbm(lengths, places, queries), *in_vmem(own_pair))
    *early, last = pairs
    for at, mask in enumerate(early):
        carried = pl.pallas_call(
            lambda *refs, at=at: next_kernel(1 + at, *refs),
            in_specs=[VMEM_REF] * 5,
            out_specs=[VMEM_REF] * 2,
            out_shape=state,
            scratch_shapes=work,
            compiler_params=PARAMS,
            cost_estimate=cost,
            name="next_shard",
        )(*in_vmem(across, bias, *carried), pairs[mask])
    return pl.pallas_call(
        lambda *refs: last_kernel(1 + len(early), *refs),
        in_specs=[VMEM_REF] * 5,
        out_specs=pl.BlockSpec(memory_space=pl.ANY),
        out_shape=jax.ShapeDtypeStruct((rows, cols), jnp.bfloat16),
        scratch_shapes=work + [
            pltpu.VMEM((rows, cols), jnp.bfloat16),
            pltpu.SemaphoreType.DMA((heads,)),
        ],
        compiler_params=PARAMS,
        cost_estimate=cost,
        name="last_shard",
    )(*in_vmem(across, bias, *carried), pairs[last])


def online_kernel(heads, q_ref, k_ref, v_ref, key_pos_ref, query_pos_ref, start_ref, out_ref, peak_ref, acc_ref):
    step = pl.program_id(0)

    @pl.when(step == 0)
    def _():
        peak_ref[...] = jnp.full(peak_ref.shape, NEG_FILL, jnp.float32)
        acc_ref[...] = jnp.zeros(acc_ref.shape, jnp.float32)

    key_pos = key_pos_ref[...]
    visible = (key_pos >= start_ref[...]) & (key_pos <= query_pos_ref[...])
    values = v_ref[...]
    ext = jnp.concatenate([values, jnp.ones_like(values)], axis=1)
    for head in range(heads):
        q = q_ref[:, head * HEAD_WIDTH:(head + 1) * HEAD_WIDTH]
        scores = lax.dot_general(
            q, k_ref[...], (((1,), (1,)), ((), ())), preferred_element_type=jnp.float32
        )
        scaled = jnp.where(visible, scores * (HEAD_WIDTH ** -0.5 * LOG2_E), NEG_FILL)
        before = peak_ref[head]
        peak = jnp.maximum(before, jnp.max(scaled, axis=1, keepdims=True))
        weights = jnp.where(visible, jnp.exp2(scaled - peak), 0.0).astype(jnp.bfloat16)
        peak_ref[head] = peak
        acc_ref[head] = acc_ref[head] * jnp.exp2(before - peak) + jnp.dot(
            weights, ext, preferred_element_type=jnp.float32
        )

    @pl.when(step == pl.num_programs(0) - 1)
    def _():
        for head in range(heads):
            acc = acc_ref[head]
            out_ref[:, head * HEAD_WIDTH:(head + 1) * HEAD_WIDTH] = (
                acc[:, :HEAD_WIDTH] / acc[:, HEAD_WIDTH:]
            ).astype(jnp.bfloat16)


def online_attention(queries, keys, values, key_pos, query_pos, starts, chunk):
    rows, cols = queries.shape
    heads = cols // HEAD_WIDTH
    key_count = keys.shape[0]
    return pl.pallas_call(
        lambda *refs: online_kernel(heads, *refs),
        grid=(key_count // chunk,),
        in_specs=[
            pl.BlockSpec((rows, cols), lambda j: (0, 0)),
            pl.BlockSpec((chunk, HEAD_WIDTH), lambda j: (j, 0)),
            pl.BlockSpec((chunk, HEAD_WIDTH), lambda j: (j, 0)),
            pl.BlockSpec((1, chunk), lambda j: (0, j)),
            pl.BlockSpec((rows, 1), lambda j: (0, 0)),
            pl.BlockSpec((rows, 1), lambda j: (0, 0)),
        ],
        out_specs=pl.BlockSpec((rows, cols), lambda j: (0, 0)),
        out_shape=jax.ShapeDtypeStruct((rows, cols), jnp.bfloat16),
        scratch_shapes=[
            pltpu.VMEM((heads, rows, 1), jnp.float32),
            pltpu.VMEM((heads, rows, 2 * HEAD_WIDTH), jnp.float32),
        ],
        compiler_params=pltpu.CompilerParams(vmem_limit_bytes=32 << 20),
        name="online",
    )(queries, keys, values, key_pos, query_pos, starts)


def body(queries, keys, values, lengths, old_place):
    devices = lax.axis_size("seq")
    row_count = queries.shape[0]
    key_count = row_count * devices
    if devices == 4 and key_count <= 1024:
        own_pair = packed_pair(keys, values)
        pairs = {
            mask: lax.ppermute(own_pair, "seq", [(i, i ^ mask) for i in range(devices)])
            for mask in (2, 1, 3)
        }
        return staged_attention(queries, own_pair, pairs, lengths, old_place)
    all_keys = lax.all_gather(keys, "seq", axis=0, tiled=True)
    all_values = lax.all_gather(values, "seq", axis=0, tiled=True)
    key_pos, query_pos, starts = block_places(
        lengths, old_place, lax.axis_index("seq"), row_count, key_count
    )
    return online_attention(queries, all_keys, all_values, key_pos, query_pos, starts, 512)


def solution(mesh):
    in_specs = (
        P(("groups", "seq"), "mp"),
        P(("groups", "seq"), "mp"),
        P(("groups", "seq"), "mp"),
        P("groups"),
        P("groups"),
    )
    out_specs = P(("groups", "seq"), "mp")
    return jax.shard_map(body, mesh=mesh, in_specs=in_specs, out_specs=out_specs, check_vma=False)
```

```python
import jax
import jax.numpy as jnp
from jax import lax
from jax.experimental import pallas as pl
from jax.experimental.pallas import tpu as pltpu
from jax.sharding import PartitionSpec as P

HEAD_WIDTH = 128
LOG2_E = 1.4426950408889634
NEG_FILL = -1e30
ONES = 16


def block_places(lengths, old_place, own_index, row_count, key_count):
    block_total = old_place.shape[0]
    block_rows = key_count // block_total
    ids = jnp.arange(block_total, dtype=jnp.int32)
    hit = old_place[:, None] == ids[None, :]
    new_block = jnp.sum(jnp.where(hit, ids[:, None], 0), axis=0)
    key_pos = (new_block[:, None] * block_rows + jnp.arange(block_rows, dtype=jnp.int32)).reshape(-1)
    query_pos = lax.dynamic_slice_in_dim(key_pos, own_index * row_count, row_count)
    bounds = jnp.cumsum(lengths)
    starts = jnp.max(jnp.where(bounds[None, :] <= query_pos[:, None], bounds[None, :], 0), axis=1)
    return key_pos.reshape(1, -1), query_pos.reshape(-1, 1), starts.reshape(-1, 1)


def iota(shape, dim):
    return lax.broadcasted_iota(jnp.int32, shape, dim)


def mask_tables(own, owners, lengths_ref, places_ref, rows, bias_ref):
    block_total = places_ref.shape[1]
    block_rows = rows * lax.axis_size("seq") // block_total
    blocks = rows // block_rows
    places = places_ref[...]
    square = (block_total, block_total)
    as_column = jnp.sum(
        jnp.where(iota(square, 0) == iota(square, 1), places, 0).astype(jnp.float32),
        axis=1, keepdims=True,
    ).astype(jnp.int32)
    across = (block_total, rows)
    hit = as_column == own * blocks + iota(across, 1) // block_rows
    at = jnp.where(hit, iota(across, 0) * block_rows, 0).astype(jnp.float32)
    query_pos = jnp.sum(at, axis=0, keepdims=True) + (
        iota((1, rows), 1) % block_rows
    ).astype(jnp.float32)
    starts = jnp.zeros_like(query_pos)
    bound = jnp.int32(0)
    for t in range(lengths_ref.shape[0]):
        bound = bound + lengths_ref[t]
        edge = bound.astype(jnp.float32)
        starts = jnp.where(edge <= query_pos, edge, starts)
    down = (rows, block_total)
    for n, owner in enumerate(owners):
        hit = places == owner * blocks + iota(down, 0) // block_rows
        at = jnp.where(hit, iota(down, 1) * block_rows, 0).astype(jnp.float32)
        key_pos = jnp.sum(at, axis=1, keepdims=True) + (
            iota((rows, 1), 0) % block_rows
        ).astype(jnp.float32)
        visible = (key_pos >= starts) & (key_pos <= query_pos)
        bias_ref[n] = jnp.where(visible, 0.0, NEG_FILL)


def values_down(values):
    turned = jnp.transpose(values.astype(jnp.float32)).astype(jnp.bfloat16)
    return jnp.concatenate([turned, jnp.ones((ONES, values.shape[0]), jnp.bfloat16)], axis=0)


def in_stages(heads, stages):
    results = [{} for _ in stages]
    for step in range(heads + len(stages) - 1):
        for late, stage in enumerate(stages):
            head = step - late
            if 0 <= head < heads:
                before = results[late - 1].pop(head) if late else None
                results[late][head] = stage(head, before)


def score_stage(keys, across_ref, bias_ref, at, scaled_ref, old_peak):
    def stage(head, _):
        scores = jnp.dot(keys, across_ref[head], preferred_element_type=jnp.float32)
        scaled = scores * (HEAD_WIDTH ** -0.5 * LOG2_E) + bias_ref[at]
        scaled_ref[head] = scaled
        peak = jnp.max(scaled, axis=0, keepdims=True)
        return peak if old_peak is None else jnp.maximum(old_peak(head), peak)

    return stage


def weight_stage(scaled_ref, weight_ref):
    def stage(head, peak):
        weight_ref[head] = jnp.exp2(scaled_ref[head] - peak).astype(jnp.bfloat16)
        return peak

    return stage


def pack_kernel(k_ref, v_ref, pair_ref, sems):
    copies = [
        pltpu.make_async_copy(ref, pair_ref.at[:, at * HEAD_WIDTH:(at + 1) * HEAD_WIDTH], sems.at[at])
        for at, ref in enumerate((k_ref, v_ref))
    ]
    for copy in copies:
        copy.start()
    for copy in copies:
        copy.wait()


def own_kernel(
    masks, own_ref, lengths_hbm, places_hbm, q_hbm, pair_ref,
    across_ref, bias_ref, peak_ref, sum_ref,
    lengths_ref, places_ref, q_ref, scaled_ref, weight_ref, sems,
):
    moves = ((lengths_hbm, lengths_ref), (places_hbm, places_ref), (q_hbm, q_ref))
    copies = [pltpu.make_async_copy(*move, sems.at[n]) for n, move in enumerate(moves)]
    for copy in copies:
        copy.start()
    turned = values_down(pair_ref[:, HEAD_WIDTH:])
    keys = pair_ref[:, :HEAD_WIDTH]
    copies[0].wait()
    copies[1].wait()
    heads, _, rows = across_ref.shape
    own = own_ref[0]
    owners = [own] + [own ^ mask for mask in masks]
    mask_tables(own, owners, lengths_ref, places_ref, rows, bias_ref)
    copies[2].wait()

    def turn(head, _):
        q = q_ref[:, head * HEAD_WIDTH:(head + 1) * HEAD_WIDTH]
        across_ref[head] = jnp.transpose(q.astype(jnp.float32)).astype(jnp.bfloat16)

    def mix(head, peak):
        peak_ref[head:head + 1, :] = peak
        sum_ref[head] = jnp.dot(turned, weight_ref[head], preferred_element_type=jnp.float32)

    in_stages(heads, [
        turn,
        score_stage(keys, across_ref, bias_ref, 0, scaled_ref, None),
        weight_stage(scaled_ref, weight_ref),
        mix,
    ])


def joined(head, peak, turned, weight_ref, peak_ref, sum_ref):
    added = jnp.dot(turned, weight_ref[head], preferred_element_type=jnp.float32)
    return sum_ref[head] * jnp.exp2(peak_ref[head:head + 1, :] - peak) + added


def next_kernel(
    at, across_ref, bias_ref, peak_ref, sum_ref, pair_ref, new_peak_ref, new_sum_ref,
    scaled_ref, weight_ref,
):
    turned = values_down(pair_ref[:, HEAD_WIDTH:])

    def mix(head, peak):
        new_peak_ref[head:head + 1, :] = peak
        new_sum_ref[head] = joined(head, peak, turned, weight_ref, peak_ref, sum_ref)

    in_stages(across_ref.shape[0], [
        score_stage(
            pair_ref[:, :HEAD_WIDTH], across_ref, bias_ref, at, scaled_ref,
            lambda head: peak_ref[head:head + 1, :],
        ),
        weight_stage(scaled_ref, weight_ref),
        mix,
    ])


def last_kernel(
    at, across_ref, bias_ref, peak_ref, sum_ref, pair_ref, out_ref,
    scaled_ref, weight_ref, block_ref, sems,
):
    turned = values_down(pair_ref[:, HEAD_WIDTH:])
    copies = []

    def mix(head, peak):
        summed = joined(head, peak, turned, weight_ref, peak_ref, sum_ref)
        return summed[:HEAD_WIDTH] / summed[HEAD_WIDTH:HEAD_WIDTH + 1]

    def send(head, out):
        cols = slice(head * HEAD_WIDTH, (head + 1) * HEAD_WIDTH)
        block_ref[:, cols] = jnp.transpose(out).astype(jnp.bfloat16)
        copy = pltpu.make_async_copy(block_ref.at[:, cols], out_ref.at[:, cols], sems.at[head])
        copy.start()
        copies.append(copy)

    in_stages(across_ref.shape[0], [
        score_stage(
            pair_ref[:, :HEAD_WIDTH], across_ref, bias_ref, at, scaled_ref,
            lambda head: peak_ref[head:head + 1, :],
        ),
        weight_stage(scaled_ref, weight_ref),
        mix,
        send,
    ])
    for copy in copies:
        copy.wait()


def estimate(rows, heads, key_count):
    return pl.CostEstimate(
        flops=6 * heads * rows * key_count * HEAD_WIDTH,
        bytes_accessed=8 * heads * rows * HEAD_WIDTH,
        transcendentals=heads * rows * key_count,
    )


def in_vmem(*arrays):
    return [pltpu.with_memory_space_constraint(array, pltpu.VMEM) for array in arrays]


def in_hbm(*arrays):
    return [pltpu.with_memory_space_constraint(array, pltpu.HBM) for array in arrays]


VMEM_REF = pl.BlockSpec(memory_space=pltpu.VMEM)
HBM_REF = pl.BlockSpec(memory_space=pltpu.HBM)
PARAMS = pltpu.CompilerParams(vmem_limit_bytes=32 << 20)


def packed_pair(keys, values):
    return pl.pallas_call(
        pack_kernel,
        in_specs=[HBM_REF] * 2,
        out_specs=VMEM_REF,
        out_shape=pltpu.VMEM((keys.shape[0], 2 * HEAD_WIDTH), keys.dtype),
        scratch_shapes=[pltpu.SemaphoreType.DMA((2,))],
        compiler_params=PARAMS,
        name="pack",
    )(*in_hbm(keys, values))


def staged_attention(queries, own_pair, pairs, lengths, old_place):
    rows, cols = queries.shape
    heads = cols // HEAD_WIDTH
    own = lax.axis_index("seq").astype(jnp.int32).reshape(1)
    places = old_place.reshape(1, -1)
    state = [
        pltpu.VMEM((heads, rows), jnp.float32),
        pltpu.VMEM((heads, HEAD_WIDTH + ONES, rows), jnp.float32),
    ]
    work = [
        pltpu.VMEM((heads, rows, rows), jnp.float32),
        pltpu.VMEM((heads, rows, rows), jnp.bfloat16),
    ]
    cost = estimate(rows, heads, rows)
    across, bias, *carried = pl.pallas_call(
        lambda *refs: own_kernel(list(pairs), *refs),
        in_specs=[pl.BlockSpec(memory_space=pltpu.SMEM)] + [HBM_REF] * 3 + [VMEM_REF],
        out_specs=[VMEM_REF] * 4,
        out_shape=[
            pltpu.VMEM((heads, HEAD_WIDTH, rows), jnp.bfloat16),
            pltpu.VMEM((1 + len(pairs), rows, rows), jnp.float32),
        ] + state,
        scratch_shapes=[
            pltpu.SMEM(lengths.shape, jnp.int32),
            pltpu.VMEM(places.shape, jnp.int32),
            pltpu.VMEM(queries.shape, jnp.bfloat16),
        ] + work + [pltpu.SemaphoreType.DMA((3,))],
        compiler_params=PARAMS,
        cost_estimate=cost,
        name="own_shard",
    )(own, *in_hbm(lengths, places, queries), *in_vmem(own_pair))
    *early, last = pairs
    for at, mask in enumerate(early):
        carried = pl.pallas_call(
            lambda *refs, at=at: next_kernel(1 + at, *refs),
            in_specs=[VMEM_REF] * 5,
            out_specs=[VMEM_REF] * 2,
            out_shape=state,
            scratch_shapes=work,
            compiler_params=PARAMS,
            cost_estimate=cost,
            name="next_shard",
        )(*in_vmem(across, bias, *carried), pairs[mask])
    return pl.pallas_call(
        lambda *refs: last_kernel(1 + len(early), *refs),
        in_specs=[VMEM_REF] * 5,
        out_specs=pl.BlockSpec(memory_space=pl.ANY),
        out_shape=jax.ShapeDtypeStruct((rows, cols), jnp.bfloat16),
        scratch_shapes=work + [
            pltpu.VMEM((rows, cols), jnp.bfloat16),
            pltpu.SemaphoreType.DMA((heads,)),
        ],
        compiler_params=PARAMS,
        cost_estimate=cost,
        name="last_shard",
    )(*in_vmem(across, bias, *carried), pairs[last])


def online_kernel(heads, q_ref, k_ref, v_ref, key_pos_ref, query_pos_ref, start_ref, out_ref, peak_ref, acc_ref):
    step = pl.program_id(0)

    @pl.when(step == 0)
    def _():
        peak_ref[...] = jnp.full(peak_ref.shape, NEG_FILL, jnp.float32)
        acc_ref[...] = jnp.zeros(acc_ref.shape, jnp.float32)

    key_pos = key_pos_ref[...]
    visible = (key_pos >= start_ref[...]) & (key_pos <= query_pos_ref[...])
    values = v_ref[...]
    ext = jnp.concatenate([values, jnp.ones_like(values)], axis=1)
    for head in range(heads):
        q = q_ref[:, head * HEAD_WIDTH:(head + 1) * HEAD_WIDTH]
        scores = lax.dot_general(
            q, k_ref[...], (((1,), (1,)), ((), ())), preferred_element_type=jnp.float32
        )
        scaled = jnp.where(visible, scores * (HEAD_WIDTH ** -0.5 * LOG2_E), NEG_FILL)
        before = peak_ref[head]
        peak = jnp.maximum(before, jnp.max(scaled, axis=1, keepdims=True))
        weights = jnp.where(visible, jnp.exp2(scaled - peak), 0.0).astype(jnp.bfloat16)
        peak_ref[head] = peak
        acc_ref[head] = acc_ref[head] * jnp.exp2(before - peak) + jnp.dot(
            weights, ext, preferred_element_type=jnp.float32
        )

    @pl.when(step == pl.num_programs(0) - 1)
    def _():
        for head in range(heads):
            acc = acc_ref[head]
            out_ref[:, head * HEAD_WIDTH:(head + 1) * HEAD_WIDTH] = (
                acc[:, :HEAD_WIDTH] / acc[:, HEAD_WIDTH:]
            ).astype(jnp.bfloat16)


def online_attention(queries, keys, values, key_pos, query_pos, starts, chunk):
    rows, cols = queries.shape
    heads = cols // HEAD_WIDTH
    key_count = keys.shape[0]
    return pl.pallas_call(
        lambda *refs: online_kernel(heads, *refs),
        grid=(key_count // chunk,),
        in_specs=[
            pl.BlockSpec((rows, cols), lambda j: (0, 0)),
            pl.BlockSpec((chunk, HEAD_WIDTH), lambda j: (j, 0)),
            pl.BlockSpec((chunk, HEAD_WIDTH), lambda j: (j, 0)),
            pl.BlockSpec((1, chunk), lambda j: (0, j)),
            pl.BlockSpec((rows, 1), lambda j: (0, 0)),
            pl.BlockSpec((rows, 1), lambda j: (0, 0)),
        ],
        out_specs=pl.BlockSpec((rows, cols), lambda j: (0, 0)),
        out_shape=jax.ShapeDtypeStruct((rows, cols), jnp.bfloat16),
        scratch_shapes=[
            pltpu.VMEM((heads, rows, 1), jnp.float32),
            pltpu.VMEM((heads, rows, 2 * HEAD_WIDTH), jnp.float32),
        ],
        compiler_params=pltpu.CompilerParams(vmem_limit_bytes=32 << 20),
        name="online",
    )(queries, keys, values, key_pos, query_pos, starts)


def moved(value, mask, devices):
    return lax.ppermute(value, "seq", [(i, i ^ mask) for i in range(devices)])


def body(queries, keys, values, lengths, old_place):
    devices = lax.axis_size("seq")
    row_count = queries.shape[0]
    key_count = row_count * devices
    if devices == 4 and key_count <= 1024:
        own_pair = packed_pair(keys, values)
        pairs = {}
        pairs[2] = moved(own_pair, 2, devices)
        pairs[1] = moved(own_pair, 1, devices)
        pairs[3] = moved(pairs[2], 1, devices)
        return staged_attention(queries, own_pair, pairs, lengths, old_place)
    all_keys = lax.all_gather(keys, "seq", axis=0, tiled=True)
    all_values = lax.all_gather(values, "seq", axis=0, tiled=True)
    key_pos, query_pos, starts = block_places(
        lengths, old_place, lax.axis_index("seq"), row_count, key_count
    )
    return online_attention(queries, all_keys, all_values, key_pos, query_pos, starts, 512)


def solution(mesh):
    in_specs = (
        P(("groups", "seq"), "mp"),
        P(("groups", "seq"), "mp"),
        P(("groups", "seq"), "mp"),
        P("groups"),
        P("groups"),
    )
    out_specs = P(("groups", "seq"), "mp")
    return jax.shard_map(body, mesh=mesh, in_specs=in_specs, out_specs=out_specs, check_vma=False)
```

```python
import jax
import jax.numpy as jnp
from jax import lax
from jax.experimental import pallas as pl
from jax.experimental.pallas import tpu as pltpu
from jax.sharding import PartitionSpec as P

HEAD_WIDTH = 128
LOG2_E = 1.4426950408889634
NEG_FILL = -1e30
ONES = 16


def block_places(lengths, old_place, own_index, row_count, key_count):
    block_total = old_place.shape[0]
    block_rows = key_count // block_total
    ids = jnp.arange(block_total, dtype=jnp.int32)
    hit = old_place[:, None] == ids[None, :]
    new_block = jnp.sum(jnp.where(hit, ids[:, None], 0), axis=0)
    key_pos = (new_block[:, None] * block_rows + jnp.arange(block_rows, dtype=jnp.int32)).reshape(-1)
    query_pos = lax.dynamic_slice_in_dim(key_pos, own_index * row_count, row_count)
    bounds = jnp.cumsum(lengths)
    starts = jnp.max(jnp.where(bounds[None, :] <= query_pos[:, None], bounds[None, :], 0), axis=1)
    return key_pos.reshape(1, -1), query_pos.reshape(-1, 1), starts.reshape(-1, 1)


def iota(shape, dim):
    return lax.broadcasted_iota(jnp.int32, shape, dim)


def mask_tables(own, owners, lengths_ref, places_ref, rows, bias_ref):
    block_total = places_ref.shape[1]
    block_rows = rows * lax.axis_size("seq") // block_total
    blocks = rows // block_rows
    places = places_ref[...]
    square = (block_total, block_total)
    as_column = jnp.sum(
        jnp.where(iota(square, 0) == iota(square, 1), places, 0).astype(jnp.float32),
        axis=1, keepdims=True,
    ).astype(jnp.int32)
    across = (block_total, rows)
    hit = as_column == own * blocks + iota(across, 1) // block_rows
    at = jnp.where(hit, iota(across, 0) * block_rows, 0).astype(jnp.float32)
    query_pos = jnp.sum(at, axis=0, keepdims=True) + (
        iota((1, rows), 1) % block_rows
    ).astype(jnp.float32)
    starts = jnp.zeros_like(query_pos)
    bound = jnp.int32(0)
    for t in range(lengths_ref.shape[0]):
        bound = bound + lengths_ref[t]
        edge = bound.astype(jnp.float32)
        starts = jnp.where(edge <= query_pos, edge, starts)
    down = (rows, block_total)
    for n, owner in enumerate(owners):
        hit = places == owner * blocks + iota(down, 0) // block_rows
        at = jnp.where(hit, iota(down, 1) * block_rows, 0).astype(jnp.float32)
        key_pos = jnp.sum(at, axis=1, keepdims=True) + (
            iota((rows, 1), 0) % block_rows
        ).astype(jnp.float32)
        visible = (key_pos >= starts) & (key_pos <= query_pos)
        bias_ref[n] = jnp.where(visible, 0.0, NEG_FILL)


def values_down(values):
    turned = jnp.transpose(values.astype(jnp.float32)).astype(jnp.bfloat16)
    return jnp.concatenate([turned, jnp.ones((ONES, values.shape[0]), jnp.bfloat16)], axis=0)


def in_stages(heads, stages):
    results = [{} for _ in stages]
    for step in range(heads + len(stages) - 1):
        for late, stage in enumerate(stages):
            head = step - late
            if 0 <= head < heads:
                before = results[late - 1].pop(head) if late else None
                results[late][head] = stage(head, before)


def score_stage(keys, across_ref, bias_ref, at, scaled_ref, old_peak):
    def stage(head, _):
        scores = jnp.dot(keys, across_ref[head], preferred_element_type=jnp.float32)
        scaled = scores * (HEAD_WIDTH ** -0.5 * LOG2_E) + bias_ref[at]
        scaled_ref[head] = scaled
        peak = jnp.max(scaled, axis=0, keepdims=True)
        return peak if old_peak is None else jnp.maximum(old_peak(head), peak)

    return stage


def weight_stage(scaled_ref, weight_ref):
    def stage(head, peak):
        weight_ref[head] = jnp.exp2(scaled_ref[head] - peak).astype(jnp.bfloat16)
        return peak

    return stage


def pack_kernel(k_ref, v_ref, pair_ref, sems):
    copies = [
        pltpu.make_async_copy(ref, pair_ref.at[:, at * HEAD_WIDTH:(at + 1) * HEAD_WIDTH], sems.at[at])
        for at, ref in enumerate((k_ref, v_ref))
    ]
    for copy in copies:
        copy.start()
    for copy in copies:
        copy.wait()


def own_kernel(
    masks, own_ref, lengths_hbm, places_hbm, q_hbm, pair_ref,
    across_ref, bias_ref, peak_ref, sum_ref,
    lengths_ref, places_ref, q_ref, scaled_ref, weight_ref, sems,
):
    moves = ((lengths_hbm, lengths_ref), (places_hbm, places_ref), (q_hbm, q_ref))
    copies = [pltpu.make_async_copy(*move, sems.at[n]) for n, move in enumerate(moves)]
    for copy in copies:
        copy.start()
    turned = values_down(pair_ref[:, HEAD_WIDTH:])
    keys = pair_ref[:, :HEAD_WIDTH]
    copies[0].wait()
    copies[1].wait()
    heads, _, rows = across_ref.shape
    own = own_ref[0]
    owners = [own] + [own ^ mask for mask in masks]
    mask_tables(own, owners, lengths_ref, places_ref, rows, bias_ref)
    copies[2].wait()

    def turn(head, _):
        q = q_ref[:, head * HEAD_WIDTH:(head + 1) * HEAD_WIDTH]
        across_ref[head] = jnp.transpose(q.astype(jnp.float32)).astype(jnp.bfloat16)

    def mix(head, peak):
        peak_ref[head:head + 1, :] = peak
        sum_ref[head] = jnp.dot(turned, weight_ref[head], preferred_element_type=jnp.float32)

    in_stages(heads, [
        turn,
        score_stage(keys, across_ref, bias_ref, 0, scaled_ref, None),
        weight_stage(scaled_ref, weight_ref),
        mix,
    ])


def joined(head, peak, turned, weight_ref, peak_ref, sum_ref):
    added = jnp.dot(turned, weight_ref[head], preferred_element_type=jnp.float32)
    return sum_ref[head] * jnp.exp2(peak_ref[head:head + 1, :] - peak) + added


def next_kernel(
    at, across_ref, bias_ref, peak_ref, sum_ref, pair_ref, new_peak_ref, new_sum_ref,
    scaled_ref, weight_ref,
):
    turned = values_down(pair_ref[:, HEAD_WIDTH:])

    def mix(head, peak):
        new_peak_ref[head:head + 1, :] = peak
        new_sum_ref[head] = joined(head, peak, turned, weight_ref, peak_ref, sum_ref)

    in_stages(across_ref.shape[0], [
        score_stage(
            pair_ref[:, :HEAD_WIDTH], across_ref, bias_ref, at, scaled_ref,
            lambda head: peak_ref[head:head + 1, :],
        ),
        weight_stage(scaled_ref, weight_ref),
        mix,
    ])


def last_kernel(
    at, across_ref, bias_ref, peak_ref, sum_ref, pair_ref, out_ref,
    scaled_ref, weight_ref, block_ref, sems,
):
    turned = values_down(pair_ref[:, HEAD_WIDTH:])
    copies = []

    def mix(head, peak):
        summed = joined(head, peak, turned, weight_ref, peak_ref, sum_ref)
        return summed[:HEAD_WIDTH] / summed[HEAD_WIDTH:HEAD_WIDTH + 1]

    def send(head, out):
        cols = slice(head * HEAD_WIDTH, (head + 1) * HEAD_WIDTH)
        block_ref[:, cols] = jnp.transpose(out).astype(jnp.bfloat16)
        copy = pltpu.make_async_copy(block_ref.at[:, cols], out_ref.at[:, cols], sems.at[head])
        copy.start()
        copies.append(copy)

    in_stages(across_ref.shape[0], [
        score_stage(
            pair_ref[:, :HEAD_WIDTH], across_ref, bias_ref, at, scaled_ref,
            lambda head: peak_ref[head:head + 1, :],
        ),
        weight_stage(scaled_ref, weight_ref),
        mix,
        send,
    ])
    for copy in copies:
        copy.wait()


def estimate(rows, heads, key_count):
    return pl.CostEstimate(
        flops=6 * heads * rows * key_count * HEAD_WIDTH,
        bytes_accessed=8 * heads * rows * HEAD_WIDTH,
        transcendentals=heads * rows * key_count,
    )


def in_vmem(*arrays):
    return [pltpu.with_memory_space_constraint(array, pltpu.VMEM) for array in arrays]


def in_hbm(*arrays):
    return [pltpu.with_memory_space_constraint(array, pltpu.HBM) for array in arrays]


VMEM_REF = pl.BlockSpec(memory_space=pltpu.VMEM)
HBM_REF = pl.BlockSpec(memory_space=pltpu.HBM)
PARAMS = pltpu.CompilerParams(vmem_limit_bytes=32 << 20)


def packed_pair(keys, values):
    return pl.pallas_call(
        pack_kernel,
        in_specs=[HBM_REF] * 2,
        out_specs=VMEM_REF,
        out_shape=pltpu.VMEM((keys.shape[0], 2 * HEAD_WIDTH), keys.dtype),
        scratch_shapes=[pltpu.SemaphoreType.DMA((2,))],
        compiler_params=PARAMS,
        name="pack",
    )(*in_hbm(keys, values))


def staged_attention(queries, own_pair, pairs, lengths, old_place):
    rows, cols = queries.shape
    heads = cols // HEAD_WIDTH
    devices = lax.axis_size("seq")
    masks = (1, 2, 3)
    own = lax.axis_index("seq").astype(jnp.int32).reshape(1)
    places = old_place.reshape(1, -1)
    state = [
        pltpu.VMEM((heads, rows), jnp.float32),
        pltpu.VMEM((heads, HEAD_WIDTH + ONES, rows), jnp.float32),
    ]
    work = [
        pltpu.VMEM((heads, rows, rows), jnp.float32),
        pltpu.VMEM((heads, rows, rows), jnp.bfloat16),
    ]
    cost = estimate(rows, heads, rows)
    across, bias, *carried = pl.pallas_call(
        lambda *refs: own_kernel(masks, *refs),
        in_specs=[pl.BlockSpec(memory_space=pltpu.SMEM)] + [HBM_REF] * 3 + [VMEM_REF],
        out_specs=[VMEM_REF] * 4,
        out_shape=[
            pltpu.VMEM((heads, HEAD_WIDTH, rows), jnp.bfloat16),
            pltpu.VMEM((devices, rows, rows), jnp.float32),
        ] + state,
        scratch_shapes=[
            pltpu.SMEM(lengths.shape, jnp.int32),
            pltpu.VMEM(places.shape, jnp.int32),
            pltpu.VMEM(queries.shape, jnp.bfloat16),
        ] + work + [pltpu.SemaphoreType.DMA((3,))],
        compiler_params=PARAMS,
        cost_estimate=cost,
        name="own_shard",
    )(own, *in_hbm(lengths, places, queries), *in_vmem(own_pair))
    relayed, *carried = lax.optimization_barrier((pairs[2], *carried))
    pairs[3] = moved(relayed, 1, devices)
    for mask in (2, 1):
        carried = pl.pallas_call(
            lambda *refs, mask=mask: next_kernel(mask, *refs),
            in_specs=[VMEM_REF] * 5,
            out_specs=[VMEM_REF] * 2,
            out_shape=state,
            scratch_shapes=work,
            compiler_params=PARAMS,
            cost_estimate=cost,
            name="next_shard",
        )(*in_vmem(across, bias, *carried), pairs[mask])
    return pl.pallas_call(
        lambda *refs: last_kernel(3, *refs),
        in_specs=[VMEM_REF] * 5,
        out_specs=pl.BlockSpec(memory_space=pl.ANY),
        out_shape=jax.ShapeDtypeStruct((rows, cols), jnp.bfloat16),
        scratch_shapes=work + [
            pltpu.VMEM((rows, cols), jnp.bfloat16),
            pltpu.SemaphoreType.DMA((heads,)),
        ],
        compiler_params=PARAMS,
        cost_estimate=cost,
        name="last_shard",
    )(*in_vmem(across, bias, *carried), pairs[3])


def online_kernel(heads, q_ref, k_ref, v_ref, key_pos_ref, query_pos_ref, start_ref, out_ref, peak_ref, acc_ref):
    step = pl.program_id(0)

    @pl.when(step == 0)
    def _():
        peak_ref[...] = jnp.full(peak_ref.shape, NEG_FILL, jnp.float32)
        acc_ref[...] = jnp.zeros(acc_ref.shape, jnp.float32)

    key_pos = key_pos_ref[...]
    visible = (key_pos >= start_ref[...]) & (key_pos <= query_pos_ref[...])
    values = v_ref[...]
    ext = jnp.concatenate([values, jnp.ones_like(values)], axis=1)
    for head in range(heads):
        q = q_ref[:, head * HEAD_WIDTH:(head + 1) * HEAD_WIDTH]
        scores = lax.dot_general(
            q, k_ref[...], (((1,), (1,)), ((), ())), preferred_element_type=jnp.float32
        )
        scaled = jnp.where(visible, scores * (HEAD_WIDTH ** -0.5 * LOG2_E), NEG_FILL)
        before = peak_ref[head]
        peak = jnp.maximum(before, jnp.max(scaled, axis=1, keepdims=True))
        weights = jnp.where(visible, jnp.exp2(scaled - peak), 0.0).astype(jnp.bfloat16)
        peak_ref[head] = peak
        acc_ref[head] = acc_ref[head] * jnp.exp2(before - peak) + jnp.dot(
            weights, ext, preferred_element_type=jnp.float32
        )

    @pl.when(step == pl.num_programs(0) - 1)
    def _():
        for head in range(heads):
            acc = acc_ref[head]
            out_ref[:, head * HEAD_WIDTH:(head + 1) * HEAD_WIDTH] = (
                acc[:, :HEAD_WIDTH] / acc[:, HEAD_WIDTH:]
            ).astype(jnp.bfloat16)


def online_attention(queries, keys, values, key_pos, query_pos, starts, chunk):
    rows, cols = queries.shape
    heads = cols // HEAD_WIDTH
    key_count = keys.shape[0]
    return pl.pallas_call(
        lambda *refs: online_kernel(heads, *refs),
        grid=(key_count // chunk,),
        in_specs=[
            pl.BlockSpec((rows, cols), lambda j: (0, 0)),
            pl.BlockSpec((chunk, HEAD_WIDTH), lambda j: (j, 0)),
            pl.BlockSpec((chunk, HEAD_WIDTH), lambda j: (j, 0)),
            pl.BlockSpec((1, chunk), lambda j: (0, j)),
            pl.BlockSpec((rows, 1), lambda j: (0, 0)),
            pl.BlockSpec((rows, 1), lambda j: (0, 0)),
        ],
        out_specs=pl.BlockSpec((rows, cols), lambda j: (0, 0)),
        out_shape=jax.ShapeDtypeStruct((rows, cols), jnp.bfloat16),
        scratch_shapes=[
            pltpu.VMEM((heads, rows, 1), jnp.float32),
            pltpu.VMEM((heads, rows, 2 * HEAD_WIDTH), jnp.float32),
        ],
        compiler_params=pltpu.CompilerParams(vmem_limit_bytes=32 << 20),
        name="online",
    )(queries, keys, values, key_pos, query_pos, starts)


def moved(value, mask, devices):
    return lax.ppermute(value, "seq", [(i, i ^ mask) for i in range(devices)])


def body(queries, keys, values, lengths, old_place):
    devices = lax.axis_size("seq")
    row_count = queries.shape[0]
    key_count = row_count * devices
    if devices == 4 and key_count <= 1024:
        own_pair = packed_pair(keys, values)
        pairs = {}
        pairs[2] = moved(own_pair, 2, devices)
        pairs[1] = moved(own_pair, 1, devices)
        return staged_attention(queries, own_pair, pairs, lengths, old_place)
    all_keys = lax.all_gather(keys, "seq", axis=0, tiled=True)
    all_values = lax.all_gather(values, "seq", axis=0, tiled=True)
    key_pos, query_pos, starts = block_places(
        lengths, old_place, lax.axis_index("seq"), row_count, key_count
    )
    return online_attention(queries, all_keys, all_values, key_pos, query_pos, starts, 512)


def solution(mesh):
    in_specs = (
        P(("groups", "seq"), "mp"),
        P(("groups", "seq"), "mp"),
        P(("groups", "seq"), "mp"),
        P("groups"),
        P("groups"),
    )
    out_specs = P(("groups", "seq"), "mp")
    return jax.shard_map(body, mesh=mesh, in_specs=in_specs, out_specs=out_specs, check_vma=False)
```

```python
import jax
import jax.numpy as jnp
from jax import lax
from jax.experimental import pallas as pl
from jax.experimental.pallas import tpu as pltpu
from jax.sharding import PartitionSpec as P

HEAD_WIDTH = 128
LOG2_E = 1.4426950408889634
NEG_FILL = -1e30
ONES = 16


def block_places(lengths, old_place, own_index, row_count, key_count):
    block_total = old_place.shape[0]
    block_rows = key_count // block_total
    ids = jnp.arange(block_total, dtype=jnp.int32)
    hit = old_place[:, None] == ids[None, :]
    new_block = jnp.sum(jnp.where(hit, ids[:, None], 0), axis=0)
    key_pos = (new_block[:, None] * block_rows + jnp.arange(block_rows, dtype=jnp.int32)).reshape(-1)
    query_pos = lax.dynamic_slice_in_dim(key_pos, own_index * row_count, row_count)
    bounds = jnp.cumsum(lengths)
    starts = jnp.max(jnp.where(bounds[None, :] <= query_pos[:, None], bounds[None, :], 0), axis=1)
    return key_pos.reshape(1, -1), query_pos.reshape(-1, 1), starts.reshape(-1, 1)


def iota(shape, dim):
    return lax.broadcasted_iota(jnp.int32, shape, dim)


def mask_tables(own, owners, lengths_ref, places_ref, rows, bias_ref):
    block_total = places_ref.shape[1]
    block_rows = rows * lax.axis_size("seq") // block_total
    blocks = rows // block_rows
    places = places_ref[...]
    square = (block_total, block_total)
    as_column = jnp.sum(
        jnp.where(iota(square, 0) == iota(square, 1), places, 0).astype(jnp.float32),
        axis=1, keepdims=True,
    ).astype(jnp.int32)
    across = (block_total, rows)
    hit = as_column == own * blocks + iota(across, 1) // block_rows
    at = jnp.where(hit, iota(across, 0) * block_rows, 0).astype(jnp.float32)
    query_pos = jnp.sum(at, axis=0, keepdims=True) + (
        iota((1, rows), 1) % block_rows
    ).astype(jnp.float32)
    starts = jnp.zeros_like(query_pos)
    bound = jnp.int32(0)
    for t in range(lengths_ref.shape[0]):
        bound = bound + lengths_ref[t]
        edge = bound.astype(jnp.float32)
        starts = jnp.where(edge <= query_pos, edge, starts)
    down = (rows, block_total)
    for n, owner in enumerate(owners):
        hit = places == owner * blocks + iota(down, 0) // block_rows
        at = jnp.where(hit, iota(down, 1) * block_rows, 0).astype(jnp.float32)
        key_pos = jnp.sum(at, axis=1, keepdims=True) + (
            iota((rows, 1), 0) % block_rows
        ).astype(jnp.float32)
        visible = (key_pos >= starts) & (key_pos <= query_pos)
        bias_ref[n] = jnp.where(visible, 0.0, NEG_FILL)


def values_down(values):
    turned = jnp.transpose(values.astype(jnp.float32)).astype(jnp.bfloat16)
    return jnp.concatenate([turned, jnp.ones((ONES, values.shape[0]), jnp.bfloat16)], axis=0)


def in_stages(heads, stages):
    results = [{} for _ in stages]
    for step in range(heads + len(stages) - 1):
        for late, stage in enumerate(stages):
            head = step - late
            if 0 <= head < heads:
                before = results[late - 1].pop(head) if late else None
                results[late][head] = stage(head, before)


def score_stage(keys, across_ref, bias_ref, at, scaled_ref, old_peak):
    def stage(head, _):
        scores = jnp.dot(keys, across_ref[head], preferred_element_type=jnp.float32)
        scaled = scores * (HEAD_WIDTH ** -0.5 * LOG2_E) + bias_ref[at]
        scaled_ref[head] = scaled
        peak = jnp.max(scaled, axis=0, keepdims=True)
        return peak if old_peak is None else jnp.maximum(old_peak(head), peak)

    return stage


def weight_stage(scaled_ref, weight_ref):
    def stage(head, peak):
        weight_ref[head] = jnp.exp2(scaled_ref[head] - peak).astype(jnp.bfloat16)
        return peak

    return stage


def pack_kernel(k_ref, v_ref, pair_ref, sems):
    copies = [
        pltpu.make_async_copy(ref, pair_ref.at[:, at * HEAD_WIDTH:(at + 1) * HEAD_WIDTH], sems.at[at])
        for at, ref in enumerate((k_ref, v_ref))
    ]
    for copy in copies:
        copy.start()
    for copy in copies:
        copy.wait()


def own_kernel(
    masks, own_ref, lengths_hbm, places_hbm, q_hbm, pair_ref,
    across_ref, bias_ref, peak_ref, sum_ref,
    lengths_ref, places_ref, q_ref, scaled_ref, weight_ref, sems,
):
    moves = ((lengths_hbm, lengths_ref), (places_hbm, places_ref), (q_hbm, q_ref))
    copies = [pltpu.make_async_copy(*move, sems.at[n]) for n, move in enumerate(moves)]
    for copy in copies:
        copy.start()
    turned = values_down(pair_ref[:, HEAD_WIDTH:])
    keys = pair_ref[:, :HEAD_WIDTH]
    copies[0].wait()
    copies[1].wait()
    heads, _, rows = across_ref.shape
    own = own_ref[0]
    owners = [own] + [own ^ mask for mask in masks]
    mask_tables(own, owners, lengths_ref, places_ref, rows, bias_ref)
    copies[2].wait()

    def turn(head, _):
        q = q_ref[:, head * HEAD_WIDTH:(head + 1) * HEAD_WIDTH]
        across_ref[head] = jnp.transpose(q.astype(jnp.float32)).astype(jnp.bfloat16)

    def mix(head, peak):
        peak_ref[head:head + 1, :] = peak
        sum_ref[head] = jnp.dot(turned, weight_ref[head], preferred_element_type=jnp.float32)

    in_stages(heads, [
        turn,
        score_stage(keys, across_ref, bias_ref, 0, scaled_ref, None),
        weight_stage(scaled_ref, weight_ref),
        mix,
    ])


def join_shard(at, across_ref, bias_ref, pair_ref, peak_ref, sum_ref, scaled_ref, weight_ref):
    turned = values_down(pair_ref[:, HEAD_WIDTH:])

    def mix(head, peak):
        added = jnp.dot(turned, weight_ref[head], preferred_element_type=jnp.float32)
        sum_ref[head] = sum_ref[head] * jnp.exp2(peak_ref[head:head + 1, :] - peak) + added
        peak_ref[head:head + 1, :] = peak

    in_stages(across_ref.shape[0], [
        score_stage(
            pair_ref[:, :HEAD_WIDTH], across_ref, bias_ref, at, scaled_ref,
            lambda head: peak_ref[head:head + 1, :],
        ),
        weight_stage(scaled_ref, weight_ref),
        mix,
    ])


def is_one_of(own, members):
    found = own == members[0]
    for member in members[1:]:
        found = found | (own == member)
    return found


def next_kernel(
    at, members, own_ref, across_ref, bias_ref, pair_ref, old_peak_ref, old_sum_ref,
    peak_ref, sum_ref, scaled_ref, weight_ref,
):
    @pl.when(is_one_of(own_ref[0], members))
    def _():
        join_shard(at, across_ref, bias_ref, pair_ref, peak_ref, sum_ref, scaled_ref, weight_ref)


def last_kernel(
    at, members, own_ref, across_ref, bias_ref, pair_ref, old_peak_ref, old_sum_ref,
    peak_ref, sum_ref, out_ref, scaled_ref, weight_ref, block_ref, sems,
):
    heads = across_ref.shape[0]

    def copy_of(head):
        cols = slice(head * HEAD_WIDTH, (head + 1) * HEAD_WIDTH)
        return pltpu.make_async_copy(block_ref.at[:, cols], out_ref.at[:, cols], sems.at[head])

    def finish(head, summed):
        cols = slice(head * HEAD_WIDTH, (head + 1) * HEAD_WIDTH)
        out = summed[:HEAD_WIDTH] / summed[HEAD_WIDTH:HEAD_WIDTH + 1]
        block_ref[:, cols] = jnp.transpose(out).astype(jnp.bfloat16)
        copy_of(head).start()

    active = is_one_of(own_ref[0], members)

    @pl.when(active)
    def _():
        turned = values_down(pair_ref[:, HEAD_WIDTH:])

        def mix(head, peak):
            added = jnp.dot(turned, weight_ref[head], preferred_element_type=jnp.float32)
            return sum_ref[head] * jnp.exp2(peak_ref[head:head + 1, :] - peak) + added

        in_stages(heads, [
            score_stage(
                pair_ref[:, :HEAD_WIDTH], across_ref, bias_ref, at, scaled_ref,
                lambda head: peak_ref[head:head + 1, :],
            ),
            weight_stage(scaled_ref, weight_ref),
            mix,
            finish,
        ])

    @pl.when(jnp.logical_not(active))
    def _():
        for head in range(heads):
            finish(head, sum_ref[head])

    for head in range(heads):
        copy_of(head).wait()


def estimate(rows, heads, key_count):
    return pl.CostEstimate(
        flops=6 * heads * rows * key_count * HEAD_WIDTH,
        bytes_accessed=8 * heads * rows * HEAD_WIDTH,
        transcendentals=heads * rows * key_count,
    )


def in_vmem(*arrays):
    return [pltpu.with_memory_space_constraint(array, pltpu.VMEM) for array in arrays]


def in_hbm(*arrays):
    return [pltpu.with_memory_space_constraint(array, pltpu.HBM) for array in arrays]


VMEM_REF = pl.BlockSpec(memory_space=pltpu.VMEM)
HBM_REF = pl.BlockSpec(memory_space=pltpu.HBM)
PARAMS = pltpu.CompilerParams(vmem_limit_bytes=32 << 20)


def packed_pair(keys, values):
    return pl.pallas_call(
        pack_kernel,
        in_specs=[HBM_REF] * 2,
        out_specs=VMEM_REF,
        out_shape=pltpu.VMEM((keys.shape[0], 2 * HEAD_WIDTH), keys.dtype),
        scratch_shapes=[pltpu.SemaphoreType.DMA((2,))],
        compiler_params=PARAMS,
        name="pack",
    )(*in_hbm(keys, values))


def staged_attention(queries, own_pair, lengths, old_place):
    rows, cols = queries.shape
    heads = cols // HEAD_WIDTH
    own = lax.axis_index("seq").astype(jnp.int32).reshape(1)
    places = old_place.reshape(1, -1)
    state = [
        pltpu.VMEM((heads, rows), jnp.float32),
        pltpu.VMEM((heads, HEAD_WIDTH + ONES, rows), jnp.float32),
    ]
    work = [
        pltpu.VMEM((heads, rows, rows), jnp.float32),
        pltpu.VMEM((heads, rows, rows), jnp.bfloat16),
    ]
    cost = estimate(rows, heads, rows)
    scalar = pl.BlockSpec(memory_space=pltpu.SMEM)
    across, bias, *carried = pl.pallas_call(
        lambda *refs: own_kernel((1, 2, 3), *refs),
        in_specs=[scalar] + [HBM_REF] * 3 + [VMEM_REF],
        out_specs=[VMEM_REF] * 4,
        out_shape=[
            pltpu.VMEM((heads, HEAD_WIDTH, rows), jnp.bfloat16),
            pltpu.VMEM((4, rows, rows), jnp.float32),
        ] + state,
        scratch_shapes=[
            pltpu.SMEM(lengths.shape, jnp.int32),
            pltpu.VMEM(places.shape, jnp.int32),
            pltpu.VMEM(queries.shape, jnp.bfloat16),
        ] + work + [pltpu.SemaphoreType.DMA((3,))],
        compiler_params=PARAMS,
        cost_estimate=cost,
        name="own_shard",
    )(own, *in_hbm(lengths, places, queries), *in_vmem(own_pair))
    *early, last = EXCHANGES
    for mask, members in early:
        pair = exchanged(own_pair, mask, members)
        carried = pl.pallas_call(
            lambda *refs, mask=mask, members=members: next_kernel(mask, members, *refs),
            in_specs=[scalar] + [VMEM_REF] * 5,
            out_specs=[VMEM_REF] * 2,
            out_shape=state,
            input_output_aliases={4: 0, 5: 1},
            scratch_shapes=work,
            compiler_params=PARAMS,
            cost_estimate=cost,
            name="next_shard",
        )(own, *in_vmem(across, bias, pair, *carried))
    mask, members = last
    pair = exchanged(own_pair, mask, members)
    *_, out = pl.pallas_call(
        lambda *refs: last_kernel(mask, members, *refs),
        in_specs=[scalar] + [VMEM_REF] * 5,
        out_specs=[VMEM_REF] * 2 + [pl.BlockSpec(memory_space=pl.ANY)],
        out_shape=state + [jax.ShapeDtypeStruct((rows, cols), jnp.bfloat16)],
        input_output_aliases={4: 0, 5: 1},
        scratch_shapes=work + [
            pltpu.VMEM((rows, cols), jnp.bfloat16),
            pltpu.SemaphoreType.DMA((heads,)),
        ],
        compiler_params=PARAMS,
        cost_estimate=cost,
        name="last_shard",
    )(own, *in_vmem(across, bias, pair, *carried))
    return out


def online_kernel(heads, q_ref, k_ref, v_ref, key_pos_ref, query_pos_ref, start_ref, out_ref, peak_ref, acc_ref):
    step = pl.program_id(0)

    @pl.when(step == 0)
    def _():
        peak_ref[...] = jnp.full(peak_ref.shape, NEG_FILL, jnp.float32)
        acc_ref[...] = jnp.zeros(acc_ref.shape, jnp.float32)

    key_pos = key_pos_ref[...]
    visible = (key_pos >= start_ref[...]) & (key_pos <= query_pos_ref[...])
    values = v_ref[...]
    ext = jnp.concatenate([values, jnp.ones_like(values)], axis=1)
    for head in range(heads):
        q = q_ref[:, head * HEAD_WIDTH:(head + 1) * HEAD_WIDTH]
        scores = lax.dot_general(
            q, k_ref[...], (((1,), (1,)), ((), ())), preferred_element_type=jnp.float32
        )
        scaled = jnp.where(visible, scores * (HEAD_WIDTH ** -0.5 * LOG2_E), NEG_FILL)
        before = peak_ref[head]
        peak = jnp.maximum(before, jnp.max(scaled, axis=1, keepdims=True))
        weights = jnp.where(visible, jnp.exp2(scaled - peak), 0.0).astype(jnp.bfloat16)
        peak_ref[head] = peak
        acc_ref[head] = acc_ref[head] * jnp.exp2(before - peak) + jnp.dot(
            weights, ext, preferred_element_type=jnp.float32
        )

    @pl.when(step == pl.num_programs(0) - 1)
    def _():
        for head in range(heads):
            acc = acc_ref[head]
            out_ref[:, head * HEAD_WIDTH:(head + 1) * HEAD_WIDTH] = (
                acc[:, :HEAD_WIDTH] / acc[:, HEAD_WIDTH:]
            ).astype(jnp.bfloat16)


def online_attention(queries, keys, values, key_pos, query_pos, starts, chunk):
    rows, cols = queries.shape
    heads = cols // HEAD_WIDTH
    key_count = keys.shape[0]
    return pl.pallas_call(
        lambda *refs: online_kernel(heads, *refs),
        grid=(key_count // chunk,),
        in_specs=[
            pl.BlockSpec((rows, cols), lambda j: (0, 0)),
            pl.BlockSpec((chunk, HEAD_WIDTH), lambda j: (j, 0)),
            pl.BlockSpec((chunk, HEAD_WIDTH), lambda j: (j, 0)),
            pl.BlockSpec((1, chunk), lambda j: (0, j)),
            pl.BlockSpec((rows, 1), lambda j: (0, 0)),
            pl.BlockSpec((rows, 1), lambda j: (0, 0)),
        ],
        out_specs=pl.BlockSpec((rows, cols), lambda j: (0, 0)),
        out_shape=jax.ShapeDtypeStruct((rows, cols), jnp.bfloat16),
        scratch_shapes=[
            pltpu.VMEM((heads, rows, 1), jnp.float32),
            pltpu.VMEM((heads, rows, 2 * HEAD_WIDTH), jnp.float32),
        ],
        compiler_params=pltpu.CompilerParams(vmem_limit_bytes=32 << 20),
        name="online",
    )(queries, keys, values, key_pos, query_pos, starts)


EXCHANGES = ((1, (0, 1)), (3, (0, 3)), (2, (0, 1, 2, 3)), (1, (2, 3)), (3, (1, 2)))


def exchanged(value, mask, members):
    return lax.ppermute(value, "seq", [(i, i ^ mask) for i in members])


def body(queries, keys, values, lengths, old_place):
    devices = lax.axis_size("seq")
    row_count = queries.shape[0]
    key_count = row_count * devices
    if devices == 4 and key_count <= 1024:
        own_pair = packed_pair(keys, values)
        return staged_attention(queries, own_pair, lengths, old_place)
    all_keys = lax.all_gather(keys, "seq", axis=0, tiled=True)
    all_values = lax.all_gather(values, "seq", axis=0, tiled=True)
    key_pos, query_pos, starts = block_places(
        lengths, old_place, lax.axis_index("seq"), row_count, key_count
    )
    return online_attention(queries, all_keys, all_values, key_pos, query_pos, starts, 512)


def solution(mesh):
    in_specs = (
        P(("groups", "seq"), "mp"),
        P(("groups", "seq"), "mp"),
        P(("groups", "seq"), "mp"),
        P("groups"),
        P("groups"),
    )
    out_specs = P(("groups", "seq"), "mp")
    return jax.shard_map(body, mesh=mesh, in_specs=in_specs, out_specs=out_specs, check_vma=False)
```

```python
import jax
import jax.numpy as jnp
from jax import lax
from jax.experimental import pallas as pl
from jax.experimental.pallas import tpu as pltpu
from jax.sharding import PartitionSpec as P

HEAD_WIDTH = 128
LOG2_E = 1.4426950408889634
NEG_FILL = -1e30
ONES = 16


def block_places(lengths, old_place, own_index, row_count, key_count):
    block_total = old_place.shape[0]
    block_rows = key_count // block_total
    ids = jnp.arange(block_total, dtype=jnp.int32)
    hit = old_place[:, None] == ids[None, :]
    new_block = jnp.sum(jnp.where(hit, ids[:, None], 0), axis=0)
    key_pos = (new_block[:, None] * block_rows + jnp.arange(block_rows, dtype=jnp.int32)).reshape(-1)
    query_pos = lax.dynamic_slice_in_dim(key_pos, own_index * row_count, row_count)
    bounds = jnp.cumsum(lengths)
    starts = jnp.max(jnp.where(bounds[None, :] <= query_pos[:, None], bounds[None, :], 0), axis=1)
    return key_pos.reshape(1, -1), query_pos.reshape(-1, 1), starts.reshape(-1, 1)


def iota(shape, dim):
    return lax.broadcasted_iota(jnp.int32, shape, dim)


def mask_tables(own, owners, lengths_ref, places_ref, rows, bias_ref):
    block_total = places_ref.shape[1]
    block_rows = rows * lax.axis_size("seq") // block_total
    blocks = rows // block_rows
    places = places_ref[...]
    square = (block_total, block_total)
    as_column = jnp.sum(
        jnp.where(iota(square, 0) == iota(square, 1), places, 0).astype(jnp.float32),
        axis=1, keepdims=True,
    ).astype(jnp.int32)
    across = (block_total, rows)
    hit = as_column == own * blocks + iota(across, 1) // block_rows
    at = jnp.where(hit, iota(across, 0) * block_rows, 0).astype(jnp.float32)
    query_pos = jnp.sum(at, axis=0, keepdims=True) + (
        iota((1, rows), 1) % block_rows
    ).astype(jnp.float32)
    starts = jnp.zeros_like(query_pos)
    bound = jnp.int32(0)
    for t in range(lengths_ref.shape[0]):
        bound = bound + lengths_ref[t]
        edge = bound.astype(jnp.float32)
        starts = jnp.where(edge <= query_pos, edge, starts)
    down = (rows, block_total)
    for n, owner in enumerate(owners):
        hit = places == owner * blocks + iota(down, 0) // block_rows
        at = jnp.where(hit, iota(down, 1) * block_rows, 0).astype(jnp.float32)
        key_pos = jnp.sum(at, axis=1, keepdims=True) + (
            iota((rows, 1), 0) % block_rows
        ).astype(jnp.float32)
        visible = (key_pos >= starts) & (key_pos <= query_pos)
        bias_ref[n] = jnp.where(visible, 0.0, NEG_FILL)


def values_down(values):
    turned = jnp.transpose(values.astype(jnp.float32)).astype(jnp.bfloat16)
    return jnp.concatenate([turned, jnp.ones((ONES, values.shape[0]), jnp.bfloat16)], axis=0)


def in_stages(heads, stages):
    results = [{} for _ in stages]
    for step in range(heads + len(stages) - 1):
        for late, stage in enumerate(stages):
            head = step - late
            if 0 <= head < heads:
                before = results[late - 1].pop(head) if late else None
                results[late][head] = stage(head, before)


def score_stage(keys, across_ref, bias_ref, at, scaled_ref, old_peak):
    def stage(head, _):
        scores = jnp.dot(keys, across_ref[head], preferred_element_type=jnp.float32)
        scaled = scores * (HEAD_WIDTH ** -0.5 * LOG2_E) + bias_ref[at]
        scaled_ref[head] = scaled
        peak = jnp.max(scaled, axis=0, keepdims=True)
        return peak if old_peak is None else jnp.maximum(old_peak(head), peak)

    return stage


def weight_stage(scaled_ref, weight_ref):
    def stage(head, peak):
        weight_ref[head] = jnp.exp2(scaled_ref[head] - peak).astype(jnp.bfloat16)
        return peak

    return stage


def own_kernel(
    masks, own_ref, lengths_hbm, places_hbm, q_hbm, k_hbm, v_hbm,
    across_ref, bias_ref, peak_ref, sum_ref,
    lengths_ref, places_ref, q_ref, k_ref, v_ref, scaled_ref, weight_ref, sems,
):
    moves = (
        (lengths_hbm, lengths_ref), (places_hbm, places_ref),
        (k_hbm, k_ref), (v_hbm, v_ref), (q_hbm, q_ref),
    )
    copies = [pltpu.make_async_copy(*move, sems.at[n]) for n, move in enumerate(moves)]
    for copy in copies:
        copy.start()
    copies[0].wait()
    copies[1].wait()
    heads, _, rows = across_ref.shape
    own = own_ref[0]
    owners = [own] + [own ^ mask for mask in masks]
    mask_tables(own, owners, lengths_ref, places_ref, rows, bias_ref)
    for copy in copies[2:]:
        copy.wait()
    keys = k_ref[...]
    turned = values_down(v_ref[...])

    def turn(head, _):
        q = q_ref[:, head * HEAD_WIDTH:(head + 1) * HEAD_WIDTH]
        across_ref[head] = jnp.transpose(q.astype(jnp.float32)).astype(jnp.bfloat16)

    def mix(head, peak):
        peak_ref[head:head + 1, :] = peak
        sum_ref[head] = jnp.dot(turned, weight_ref[head], preferred_element_type=jnp.float32)

    in_stages(heads, [
        turn,
        score_stage(keys, across_ref, bias_ref, 0, scaled_ref, None),
        weight_stage(scaled_ref, weight_ref),
        mix,
    ])


def joined(head, peak, turned, weight_ref, peak_ref, sum_ref):
    added = jnp.dot(turned, weight_ref[head], preferred_element_type=jnp.float32)
    return sum_ref[head] * jnp.exp2(peak_ref[head:head + 1, :] - peak) + added


def next_kernel(
    at, across_ref, bias_ref, peak_ref, sum_ref, k_ref, v_ref, new_peak_ref, new_sum_ref,
    scaled_ref, weight_ref,
):
    turned = values_down(v_ref[...])

    def mix(head, peak):
        new_peak_ref[head:head + 1, :] = peak
        new_sum_ref[head] = joined(head, peak, turned, weight_ref, peak_ref, sum_ref)

    in_stages(across_ref.shape[0], [
        score_stage(
            k_ref[...], across_ref, bias_ref, at, scaled_ref,
            lambda head: peak_ref[head:head + 1, :],
        ),
        weight_stage(scaled_ref, weight_ref),
        mix,
    ])


def last_kernel(
    at, across_ref, bias_ref, peak_ref, sum_ref, k_ref, v_ref, out_ref,
    scaled_ref, weight_ref, block_ref, sems,
):
    turned = values_down(v_ref[...])
    copies = []

    def mix(head, peak):
        summed = joined(head, peak, turned, weight_ref, peak_ref, sum_ref)
        return summed[:HEAD_WIDTH] / summed[HEAD_WIDTH:HEAD_WIDTH + 1]

    def send(head, out):
        cols = slice(head * HEAD_WIDTH, (head + 1) * HEAD_WIDTH)
        block_ref[:, cols] = jnp.transpose(out).astype(jnp.bfloat16)
        copy = pltpu.make_async_copy(block_ref.at[:, cols], out_ref.at[:, cols], sems.at[head])
        copy.start()
        copies.append(copy)

    in_stages(across_ref.shape[0], [
        score_stage(
            k_ref[...], across_ref, bias_ref, at, scaled_ref,
            lambda head: peak_ref[head:head + 1, :],
        ),
        weight_stage(scaled_ref, weight_ref),
        mix,
        send,
    ])
    for copy in copies:
        copy.wait()


def estimate(rows, heads, key_count):
    return pl.CostEstimate(
        flops=6 * heads * rows * key_count * HEAD_WIDTH,
        bytes_accessed=8 * heads * rows * HEAD_WIDTH,
        transcendentals=heads * rows * key_count,
    )


def in_vmem(*arrays):
    return [pltpu.with_memory_space_constraint(array, pltpu.VMEM) for array in arrays]


def in_hbm(*arrays):
    return [pltpu.with_memory_space_constraint(array, pltpu.HBM) for array in arrays]


VMEM_REF = pl.BlockSpec(memory_space=pltpu.VMEM)
HBM_REF = pl.BlockSpec(memory_space=pltpu.HBM)
PARAMS = pltpu.CompilerParams(vmem_limit_bytes=32 << 20)


def moved(value, mask):
    return lax.ppermute(value, "seq", [(i, i ^ mask) for i in range(lax.axis_size("seq"))])


def staged_attention(queries, keys, values, lengths, old_place):
    pairs = {mask: [moved(part, mask) for part in (keys, values)] for mask in (2, 1)}
    relayed_keys = moved(pairs[2][0], 1)
    rows, cols = queries.shape
    heads = cols // HEAD_WIDTH
    devices = lax.axis_size("seq")
    masks = (1, 2, 3)
    own = lax.axis_index("seq").astype(jnp.int32).reshape(1)
    places = old_place.reshape(1, -1)
    state = [
        pltpu.VMEM((heads, rows), jnp.float32),
        pltpu.VMEM((heads, HEAD_WIDTH + ONES, rows), jnp.float32),
    ]
    work = [
        pltpu.VMEM((heads, rows, rows), jnp.float32),
        pltpu.VMEM((heads, rows, rows), jnp.bfloat16),
    ]
    cost = estimate(rows, heads, rows)
    across, bias, *carried = pl.pallas_call(
        lambda *refs: own_kernel(masks, *refs),
        in_specs=[pl.BlockSpec(memory_space=pltpu.SMEM)] + [HBM_REF] * 5,
        out_specs=[VMEM_REF] * 4,
        out_shape=[
            pltpu.VMEM((heads, HEAD_WIDTH, rows), jnp.bfloat16),
            pltpu.VMEM((devices, rows, rows), jnp.float32),
        ] + state,
        scratch_shapes=[
            pltpu.SMEM(lengths.shape, jnp.int32),
            pltpu.VMEM(places.shape, jnp.int32),
            pltpu.VMEM(queries.shape, jnp.bfloat16),
            pltpu.VMEM(keys.shape, jnp.bfloat16),
            pltpu.VMEM(values.shape, jnp.bfloat16),
        ] + work + [pltpu.SemaphoreType.DMA((5,))],
        compiler_params=PARAMS,
        cost_estimate=cost,
        name="own_shard",
    )(own, *in_hbm(lengths, places, queries, keys, values))
    relayed, *carried = lax.optimization_barrier((pairs[2][1], *carried))
    pairs[3] = [relayed_keys, moved(relayed, 1)]
    for mask in (2, 1):
        carried = pl.pallas_call(
            lambda *refs, mask=mask: next_kernel(mask, *refs),
            in_specs=[VMEM_REF] * 6,
            out_specs=[VMEM_REF] * 2,
            out_shape=state,
            scratch_shapes=work,
            compiler_params=PARAMS,
            cost_estimate=cost,
            name="next_shard",
        )(*in_vmem(across, bias, *carried), *pairs[mask])
    return pl.pallas_call(
        lambda *refs: last_kernel(3, *refs),
        in_specs=[VMEM_REF] * 6,
        out_specs=pl.BlockSpec(memory_space=pl.ANY),
        out_shape=jax.ShapeDtypeStruct((rows, cols), jnp.bfloat16),
        scratch_shapes=work + [
            pltpu.VMEM((rows, cols), jnp.bfloat16),
            pltpu.SemaphoreType.DMA((heads,)),
        ],
        compiler_params=PARAMS,
        cost_estimate=cost,
        name="last_shard",
    )(*in_vmem(across, bias, *carried), *pairs[3])


def online_kernel(heads, q_ref, k_ref, v_ref, key_pos_ref, query_pos_ref, start_ref, out_ref, peak_ref, acc_ref):
    step = pl.program_id(0)

    @pl.when(step == 0)
    def _():
        peak_ref[...] = jnp.full(peak_ref.shape, NEG_FILL, jnp.float32)
        acc_ref[...] = jnp.zeros(acc_ref.shape, jnp.float32)

    key_pos = key_pos_ref[...]
    visible = (key_pos >= start_ref[...]) & (key_pos <= query_pos_ref[...])
    values = v_ref[...]
    ext = jnp.concatenate([values, jnp.ones_like(values)], axis=1)
    for head in range(heads):
        q = q_ref[:, head * HEAD_WIDTH:(head + 1) * HEAD_WIDTH]
        scores = lax.dot_general(
            q, k_ref[...], (((1,), (1,)), ((), ())), preferred_element_type=jnp.float32
        )
        scaled = jnp.where(visible, scores * (HEAD_WIDTH ** -0.5 * LOG2_E), NEG_FILL)
        before = peak_ref[head]
        peak = jnp.maximum(before, jnp.max(scaled, axis=1, keepdims=True))
        weights = jnp.where(visible, jnp.exp2(scaled - peak), 0.0).astype(jnp.bfloat16)
        peak_ref[head] = peak
        acc_ref[head] = acc_ref[head] * jnp.exp2(before - peak) + jnp.dot(
            weights, ext, preferred_element_type=jnp.float32
        )

    @pl.when(step == pl.num_programs(0) - 1)
    def _():
        for head in range(heads):
            acc = acc_ref[head]
            out_ref[:, head * HEAD_WIDTH:(head + 1) * HEAD_WIDTH] = (
                acc[:, :HEAD_WIDTH] / acc[:, HEAD_WIDTH:]
            ).astype(jnp.bfloat16)


def online_attention(queries, keys, values, key_pos, query_pos, starts, chunk):
    rows, cols = queries.shape
    heads = cols // HEAD_WIDTH
    key_count = keys.shape[0]
    return pl.pallas_call(
        lambda *refs: online_kernel(heads, *refs),
        grid=(key_count // chunk,),
        in_specs=[
            pl.BlockSpec((rows, cols), lambda j: (0, 0)),
            pl.BlockSpec((chunk, HEAD_WIDTH), lambda j: (j, 0)),
            pl.BlockSpec((chunk, HEAD_WIDTH), lambda j: (j, 0)),
            pl.BlockSpec((1, chunk), lambda j: (0, j)),
            pl.BlockSpec((rows, 1), lambda j: (0, 0)),
            pl.BlockSpec((rows, 1), lambda j: (0, 0)),
        ],
        out_specs=pl.BlockSpec((rows, cols), lambda j: (0, 0)),
        out_shape=jax.ShapeDtypeStruct((rows, cols), jnp.bfloat16),
        scratch_shapes=[
            pltpu.VMEM((heads, rows, 1), jnp.float32),
            pltpu.VMEM((heads, rows, 2 * HEAD_WIDTH), jnp.float32),
        ],
        compiler_params=pltpu.CompilerParams(vmem_limit_bytes=32 << 20),
        name="online",
    )(queries, keys, values, key_pos, query_pos, starts)


def body(queries, keys, values, lengths, old_place):
    devices = lax.axis_size("seq")
    row_count = queries.shape[0]
    key_count = row_count * devices
    if devices == 4 and key_count <= 1024:
        return staged_attention(queries, keys, values, lengths, old_place)
    all_keys = lax.all_gather(keys, "seq", axis=0, tiled=True)
    all_values = lax.all_gather(values, "seq", axis=0, tiled=True)
    key_pos, query_pos, starts = block_places(
        lengths, old_place, lax.axis_index("seq"), row_count, key_count
    )
    return online_attention(queries, all_keys, all_values, key_pos, query_pos, starts, 512)


def solution(mesh):
    in_specs = (
        P(("groups", "seq"), "mp"),
        P(("groups", "seq"), "mp"),
        P(("groups", "seq"), "mp"),
        P("groups"),
        P("groups"),
    )
    out_specs = P(("groups", "seq"), "mp")
    return jax.shard_map(body, mesh=mesh, in_specs=in_specs, out_specs=out_specs, check_vma=False)
```

```python
import jax
import jax.numpy as jnp
from jax import lax
from jax.experimental import pallas as pl
from jax.experimental.pallas import tpu as pltpu
from jax.sharding import PartitionSpec as P

HEAD_WIDTH = 128
LOG2_E = 1.4426950408889634
NEG_FILL = -1e30
ONES = 16


def block_places(lengths, old_place, own_index, row_count, key_count):
    block_total = old_place.shape[0]
    block_rows = key_count // block_total
    ids = jnp.arange(block_total, dtype=jnp.int32)
    hit = old_place[:, None] == ids[None, :]
    new_block = jnp.sum(jnp.where(hit, ids[:, None], 0), axis=0)
    key_pos = (new_block[:, None] * block_rows + jnp.arange(block_rows, dtype=jnp.int32)).reshape(-1)
    query_pos = lax.dynamic_slice_in_dim(key_pos, own_index * row_count, row_count)
    bounds = jnp.cumsum(lengths)
    starts = jnp.max(jnp.where(bounds[None, :] <= query_pos[:, None], bounds[None, :], 0), axis=1)
    return key_pos.reshape(1, -1), query_pos.reshape(-1, 1), starts.reshape(-1, 1)


def iota(shape, dim):
    return lax.broadcasted_iota(jnp.int32, shape, dim)


def mask_tables(own, owners, lengths_ref, places_ref, rows, bias_ref):
    block_total = places_ref.shape[1]
    block_rows = rows * lax.axis_size("seq") // block_total
    blocks = rows // block_rows
    places = places_ref[...]
    square = (block_total, block_total)
    as_column = jnp.sum(
        jnp.where(iota(square, 0) == iota(square, 1), places, 0).astype(jnp.float32),
        axis=1, keepdims=True,
    ).astype(jnp.int32)
    across = (block_total, rows)
    hit = as_column == own * blocks + iota(across, 1) // block_rows
    at = jnp.where(hit, iota(across, 0) * block_rows, 0).astype(jnp.float32)
    query_pos = jnp.sum(at, axis=0, keepdims=True) + (
        iota((1, rows), 1) % block_rows
    ).astype(jnp.float32)
    starts = jnp.zeros_like(query_pos)
    bound = jnp.int32(0)
    for t in range(lengths_ref.shape[0]):
        bound = bound + lengths_ref[t]
        edge = bound.astype(jnp.float32)
        starts = jnp.where(edge <= query_pos, edge, starts)
    down = (rows, block_total)
    for n, owner in enumerate(owners):
        hit = places == owner * blocks + iota(down, 0) // block_rows
        at = jnp.where(hit, iota(down, 1) * block_rows, 0).astype(jnp.float32)
        key_pos = jnp.sum(at, axis=1, keepdims=True) + (
            iota((rows, 1), 0) % block_rows
        ).astype(jnp.float32)
        visible = (key_pos >= starts) & (key_pos <= query_pos)
        bias_ref[n] = jnp.where(visible, 0.0, NEG_FILL)


def values_down(values):
    turned = jnp.transpose(values.astype(jnp.float32)).astype(jnp.bfloat16)
    return jnp.concatenate([turned, jnp.ones((ONES, values.shape[0]), jnp.bfloat16)], axis=0)


def in_stages(heads, stages):
    results = [{} for _ in stages]
    for step in range(heads + len(stages) - 1):
        for late, stage in enumerate(stages):
            head = step - late
            if 0 <= head < heads:
                before = results[late - 1].pop(head) if late else None
                results[late][head] = stage(head, before)


def score_stage(keys, across_ref, bias_ref, at, scaled_ref, old_peak):
    def stage(head, _):
        scores = jnp.dot(keys, across_ref[head], preferred_element_type=jnp.float32)
        scaled = scores * (HEAD_WIDTH ** -0.5 * LOG2_E) + bias_ref[at]
        scaled_ref[head] = scaled
        peak = jnp.max(scaled, axis=0, keepdims=True)
        return peak if old_peak is None else jnp.maximum(old_peak(head), peak)

    return stage


def weight_stage(scaled_ref, weight_ref):
    def stage(head, peak):
        weight_ref[head] = jnp.exp2(scaled_ref[head] - peak).astype(jnp.bfloat16)
        return peak

    return stage


def own_kernel(
    masks, own_ref, lengths_hbm, places_hbm, q_hbm, k_hbm, v_hbm,
    across_ref, bias_ref, peak_ref, sum_ref,
    lengths_ref, places_ref, q_ref, k_ref, v_ref, scaled_ref, weight_ref, sems,
):
    moves = (
        (lengths_hbm, lengths_ref), (places_hbm, places_ref),
        (k_hbm, k_ref), (v_hbm, v_ref), (q_hbm, q_ref),
    )
    copies = [pltpu.make_async_copy(*move, sems.at[n]) for n, move in enumerate(moves)]
    for copy in copies:
        copy.start()
    copies[0].wait()
    copies[1].wait()
    heads, _, rows = across_ref.shape
    own = own_ref[0]
    owners = [own] + [own ^ mask for mask in masks]
    mask_tables(own, owners, lengths_ref, places_ref, rows, bias_ref)
    for copy in copies[2:]:
        copy.wait()
    keys = k_ref[...]
    turned = values_down(v_ref[...])

    def turn(head, _):
        q = q_ref[:, head * HEAD_WIDTH:(head + 1) * HEAD_WIDTH]
        across_ref[head] = jnp.transpose(q.astype(jnp.float32)).astype(jnp.bfloat16)

    def mix(head, peak):
        peak_ref[head:head + 1, :] = peak
        sum_ref[head] = jnp.dot(turned, weight_ref[head], preferred_element_type=jnp.float32)

    in_stages(heads, [
        turn,
        score_stage(keys, across_ref, bias_ref, 0, scaled_ref, None),
        weight_stage(scaled_ref, weight_ref),
        mix,
    ])


def joined(head, peak, turned, weight_ref, peak_ref, sum_ref):
    added = jnp.dot(turned, weight_ref[head], preferred_element_type=jnp.float32)
    return sum_ref[head] * jnp.exp2(peak_ref[head:head + 1, :] - peak) + added


def next_kernel(
    at, across_ref, bias_ref, peak_ref, sum_ref, k_ref, v_ref, new_peak_ref, new_sum_ref,
    scaled_ref, weight_ref,
):
    turned = values_down(v_ref[...])

    def mix(head, peak):
        new_peak_ref[head:head + 1, :] = peak
        new_sum_ref[head] = joined(head, peak, turned, weight_ref, peak_ref, sum_ref)

    in_stages(across_ref.shape[0], [
        score_stage(
            k_ref[...], across_ref, bias_ref, at, scaled_ref,
            lambda head: peak_ref[head:head + 1, :],
        ),
        weight_stage(scaled_ref, weight_ref),
        mix,
    ])


def weights_kernel(
    at, across_ref, bias_ref, peak_ref, sum_ref, k_ref,
    new_peak_ref, new_sum_ref, weight_ref, scaled_ref,
):
    def rescale(head, peak):
        new_peak_ref[head:head + 1, :] = peak
        new_sum_ref[head] = sum_ref[head] * jnp.exp2(peak_ref[head:head + 1, :] - peak)

    in_stages(across_ref.shape[0], [
        score_stage(
            k_ref[...], across_ref, bias_ref, at, scaled_ref,
            lambda head: peak_ref[head:head + 1, :],
        ),
        weight_stage(scaled_ref, weight_ref),
        rescale,
    ])


def values_kernel(sum_ref, weight_ref, v_ref, new_sum_ref):
    turned = values_down(v_ref[...])
    for head in range(sum_ref.shape[0]):
        added = jnp.dot(turned, weight_ref[head], preferred_element_type=jnp.float32)
        new_sum_ref[head] = sum_ref[head] + added


def last_kernel(sum_ref, weight_ref, v_ref, out_ref, block_ref, sems):
    turned = values_down(v_ref[...])
    copies = []

    def mix(head, _):
        added = jnp.dot(turned, weight_ref[head], preferred_element_type=jnp.float32)
        summed = sum_ref[head] + added
        return summed[:HEAD_WIDTH] / summed[HEAD_WIDTH:HEAD_WIDTH + 1]

    def send(head, out):
        cols = slice(head * HEAD_WIDTH, (head + 1) * HEAD_WIDTH)
        block_ref[:, cols] = jnp.transpose(out).astype(jnp.bfloat16)
        copy = pltpu.make_async_copy(block_ref.at[:, cols], out_ref.at[:, cols], sems.at[head])
        copy.start()
        copies.append(copy)

    in_stages(sum_ref.shape[0], [mix, send])
    for copy in copies:
        copy.wait()


def estimate(rows, heads, key_count):
    return pl.CostEstimate(
        flops=6 * heads * rows * key_count * HEAD_WIDTH,
        bytes_accessed=8 * heads * rows * HEAD_WIDTH,
        transcendentals=heads * rows * key_count,
    )


def in_vmem(*arrays):
    return [pltpu.with_memory_space_constraint(array, pltpu.VMEM) for array in arrays]


def in_hbm(*arrays):
    return [pltpu.with_memory_space_constraint(array, pltpu.HBM) for array in arrays]


VMEM_REF = pl.BlockSpec(memory_space=pltpu.VMEM)
HBM_REF = pl.BlockSpec(memory_space=pltpu.HBM)
PARAMS = pltpu.CompilerParams(vmem_limit_bytes=32 << 20)


def moved(value, mask):
    return lax.ppermute(value, "seq", [(i, i ^ mask) for i in range(lax.axis_size("seq"))])


def staged_attention(queries, keys, values, lengths, old_place):
    pairs = {mask: [moved(part, mask) for part in (keys, values)] for mask in (2, 1)}
    rows, cols = queries.shape
    heads = cols // HEAD_WIDTH
    devices = lax.axis_size("seq")
    masks = (1, 2, 3)
    own = lax.axis_index("seq").astype(jnp.int32).reshape(1)
    places = old_place.reshape(1, -1)
    state = [
        pltpu.VMEM((heads, rows), jnp.float32),
        pltpu.VMEM((heads, HEAD_WIDTH + ONES, rows), jnp.float32),
    ]
    work = [
        pltpu.VMEM((heads, rows, rows), jnp.float32),
        pltpu.VMEM((heads, rows, rows), jnp.bfloat16),
    ]
    cost = estimate(rows, heads, rows)
    across, bias, *carried = pl.pallas_call(
        lambda *refs: own_kernel(masks, *refs),
        in_specs=[pl.BlockSpec(memory_space=pltpu.SMEM)] + [HBM_REF] * 5,
        out_specs=[VMEM_REF] * 4,
        out_shape=[
            pltpu.VMEM((heads, HEAD_WIDTH, rows), jnp.bfloat16),
            pltpu.VMEM((devices, rows, rows), jnp.float32),
        ] + state,
        scratch_shapes=[
            pltpu.SMEM(lengths.shape, jnp.int32),
            pltpu.VMEM(places.shape, jnp.int32),
            pltpu.VMEM(queries.shape, jnp.bfloat16),
            pltpu.VMEM(keys.shape, jnp.bfloat16),
            pltpu.VMEM(values.shape, jnp.bfloat16),
        ] + work + [pltpu.SemaphoreType.DMA((5,))],
        compiler_params=PARAMS,
        cost_estimate=cost,
        name="own_shard",
    )(own, *in_hbm(lengths, places, queries, keys, values))

    def shard_weights(at, keys, peak, summed):
        return pl.pallas_call(
            lambda *refs: weights_kernel(at, *refs),
            in_specs=[VMEM_REF] * 5,
            out_specs=[VMEM_REF] * 3,
            out_shape=state + work[1:],
            scratch_shapes=work[:1],
            compiler_params=PARAMS,
            cost_estimate=cost,
            name="shard_weights",
        )(*in_vmem(across, bias, peak, summed), keys)

    far_keys, peak, summed = lax.optimization_barrier((pairs[2][0], *carried))
    third_keys = moved(far_keys, 1)
    peak, summed, weights = shard_weights(2, far_keys, peak, summed)
    far_values, summed, weights = lax.optimization_barrier((pairs[2][1], summed, weights))
    third_values = moved(far_values, 1)
    summed = pl.pallas_call(
        values_kernel,
        in_specs=[VMEM_REF] * 3,
        out_specs=VMEM_REF,
        out_shape=state[1],
        compiler_params=PARAMS,
        cost_estimate=cost,
        name="shard_values",
    )(*in_vmem(summed, weights), far_values)
    peak, summed = pl.pallas_call(
        lambda *refs: next_kernel(1, *refs),
        in_specs=[VMEM_REF] * 6,
        out_specs=[VMEM_REF] * 2,
        out_shape=state,
        scratch_shapes=work,
        compiler_params=PARAMS,
        cost_estimate=cost,
        name="next_shard",
    )(*in_vmem(across, bias, peak, summed), *pairs[1])
    peak, summed, weights = shard_weights(3, third_keys, peak, summed)
    return pl.pallas_call(
        last_kernel,
        in_specs=[VMEM_REF] * 3,
        out_specs=pl.BlockSpec(memory_space=pl.ANY),
        out_shape=jax.ShapeDtypeStruct((rows, cols), jnp.bfloat16),
        scratch_shapes=[
            pltpu.VMEM((rows, cols), jnp.bfloat16),
            pltpu.SemaphoreType.DMA((heads,)),
        ],
        compiler_params=PARAMS,
        cost_estimate=cost,
        name="last_values",
    )(*in_vmem(summed, weights), third_values)


def online_kernel(heads, q_ref, k_ref, v_ref, key_pos_ref, query_pos_ref, start_ref, out_ref, peak_ref, acc_ref):
    step = pl.program_id(0)

    @pl.when(step == 0)
    def _():
        peak_ref[...] = jnp.full(peak_ref.shape, NEG_FILL, jnp.float32)
        acc_ref[...] = jnp.zeros(acc_ref.shape, jnp.float32)

    key_pos = key_pos_ref[...]
    visible = (key_pos >= start_ref[...]) & (key_pos <= query_pos_ref[...])
    values = v_ref[...]
    ext = jnp.concatenate([values, jnp.ones_like(values)], axis=1)
    for head in range(heads):
        q = q_ref[:, head * HEAD_WIDTH:(head + 1) * HEAD_WIDTH]
        scores = lax.dot_general(
            q, k_ref[...], (((1,), (1,)), ((), ())), preferred_element_type=jnp.float32
        )
        scaled = jnp.where(visible, scores * (HEAD_WIDTH ** -0.5 * LOG2_E), NEG_FILL)
        before = peak_ref[head]
        peak = jnp.maximum(before, jnp.max(scaled, axis=1, keepdims=True))
        weights = jnp.where(visible, jnp.exp2(scaled - peak), 0.0).astype(jnp.bfloat16)
        peak_ref[head] = peak
        acc_ref[head] = acc_ref[head] * jnp.exp2(before - peak) + jnp.dot(
            weights, ext, preferred_element_type=jnp.float32
        )

    @pl.when(step == pl.num_programs(0) - 1)
    def _():
        for head in range(heads):
            acc = acc_ref[head]
            out_ref[:, head * HEAD_WIDTH:(head + 1) * HEAD_WIDTH] = (
                acc[:, :HEAD_WIDTH] / acc[:, HEAD_WIDTH:]
            ).astype(jnp.bfloat16)


def online_attention(queries, keys, values, key_pos, query_pos, starts, chunk):
    rows, cols = queries.shape
    heads = cols // HEAD_WIDTH
    key_count = keys.shape[0]
    return pl.pallas_call(
        lambda *refs: online_kernel(heads, *refs),
        grid=(key_count // chunk,),
        in_specs=[
            pl.BlockSpec((rows, cols), lambda j: (0, 0)),
            pl.BlockSpec((chunk, HEAD_WIDTH), lambda j: (j, 0)),
            pl.BlockSpec((chunk, HEAD_WIDTH), lambda j: (j, 0)),
            pl.BlockSpec((1, chunk), lambda j: (0, j)),
            pl.BlockSpec((rows, 1), lambda j: (0, 0)),
            pl.BlockSpec((rows, 1), lambda j: (0, 0)),
        ],
        out_specs=pl.BlockSpec((rows, cols), lambda j: (0, 0)),
        out_shape=jax.ShapeDtypeStruct((rows, cols), jnp.bfloat16),
        scratch_shapes=[
            pltpu.VMEM((heads, rows, 1), jnp.float32),
            pltpu.VMEM((heads, rows, 2 * HEAD_WIDTH), jnp.float32),
        ],
        compiler_params=pltpu.CompilerParams(vmem_limit_bytes=32 << 20),
        name="online",
    )(queries, keys, values, key_pos, query_pos, starts)


def body(queries, keys, values, lengths, old_place):
    devices = lax.axis_size("seq")
    row_count = queries.shape[0]
    key_count = row_count * devices
    if devices == 4 and key_count <= 1024:
        return staged_attention(queries, keys, values, lengths, old_place)
    all_keys = lax.all_gather(keys, "seq", axis=0, tiled=True)
    all_values = lax.all_gather(values, "seq", axis=0, tiled=True)
    key_pos, query_pos, starts = block_places(
        lengths, old_place, lax.axis_index("seq"), row_count, key_count
    )
    return online_attention(queries, all_keys, all_values, key_pos, query_pos, starts, 512)


def solution(mesh):
    in_specs = (
        P(("groups", "seq"), "mp"),
        P(("groups", "seq"), "mp"),
        P(("groups", "seq"), "mp"),
        P("groups"),
        P("groups"),
    )
    out_specs = P(("groups", "seq"), "mp")
    return jax.shard_map(body, mesh=mesh, in_specs=in_specs, out_specs=out_specs, check_vma=False)
```

```python
import jax
import jax.numpy as jnp
from jax import lax
from jax.experimental import pallas as pl
from jax.experimental.pallas import tpu as pltpu
from jax.sharding import PartitionSpec as P

HEAD_WIDTH = 128
LOG2_E = 1.4426950408889634
NEG_FILL = -1e30
ONES = 16


def block_places(lengths, old_place, own_index, row_count, key_count):
    block_total = old_place.shape[0]
    block_rows = key_count // block_total
    ids = jnp.arange(block_total, dtype=jnp.int32)
    hit = old_place[:, None] == ids[None, :]
    new_block = jnp.sum(jnp.where(hit, ids[:, None], 0), axis=0)
    key_pos = (new_block[:, None] * block_rows + jnp.arange(block_rows, dtype=jnp.int32)).reshape(-1)
    query_pos = lax.dynamic_slice_in_dim(key_pos, own_index * row_count, row_count)
    bounds = jnp.cumsum(lengths)
    starts = jnp.max(jnp.where(bounds[None, :] <= query_pos[:, None], bounds[None, :], 0), axis=1)
    return key_pos.reshape(1, -1), query_pos.reshape(-1, 1), starts.reshape(-1, 1)


def iota(shape, dim):
    return lax.broadcasted_iota(jnp.int32, shape, dim)


def mask_tables(owners, lengths_ref, places_ref, rows, bias_ref):
    block_total = places_ref.shape[1]
    block_rows = rows * lax.axis_size("seq") // block_total
    blocks = rows // block_rows
    places = places_ref[...]
    square = (block_total, block_total)
    as_column = jnp.sum(
        jnp.where(iota(square, 0) == iota(square, 1), places, 0).astype(jnp.float32),
        axis=1, keepdims=True,
    ).astype(jnp.int32)
    across = (block_total, rows)
    hit = as_column == owners[0] * blocks + iota(across, 1) // block_rows
    at = jnp.where(hit, iota(across, 0) * block_rows, 0).astype(jnp.float32)
    query_pos = jnp.sum(at, axis=0, keepdims=True) + (
        iota((1, rows), 1) % block_rows
    ).astype(jnp.float32)
    starts = jnp.zeros_like(query_pos)
    bound = jnp.int32(0)
    for t in range(lengths_ref.shape[0]):
        bound = bound + lengths_ref[t]
        edge = bound.astype(jnp.float32)
        starts = jnp.where(edge <= query_pos, edge, starts)
    down = (rows, block_total)
    for n, owner in enumerate(owners):
        hit = places == owner * blocks + iota(down, 0) // block_rows
        at = jnp.where(hit, iota(down, 1) * block_rows, 0).astype(jnp.float32)
        key_pos = jnp.sum(at, axis=1, keepdims=True) + (
            iota((rows, 1), 0) % block_rows
        ).astype(jnp.float32)
        visible = (key_pos >= starts) & (key_pos <= query_pos)
        bias_ref[n] = jnp.where(visible, 0.0, NEG_FILL)


def values_down(values):
    turned = jnp.transpose(values.astype(jnp.float32)).astype(jnp.bfloat16)
    return jnp.concatenate([turned, jnp.ones((ONES, values.shape[0]), jnp.bfloat16)], axis=0)


def in_stages(heads, stages):
    results = [{} for _ in stages]
    for step in range(heads + len(stages) - 1):
        for late, stage in enumerate(stages):
            head = step - late
            if 0 <= head < heads:
                before = results[late - 1].pop(head) if late else None
                results[late][head] = stage(head, before)


def score_stage(keys, across_ref, bias_ref, at, scaled_ref, old_peak):
    def stage(head, _):
        scores = jnp.dot(keys, across_ref[head], preferred_element_type=jnp.float32)
        scaled = scores * (HEAD_WIDTH ** -0.5 * LOG2_E) + bias_ref[at]
        scaled_ref[head] = scaled
        peak = jnp.max(scaled, axis=0, keepdims=True)
        return peak if old_peak is None else jnp.maximum(old_peak(head), peak)

    return stage


def weight_stage(scaled_ref, weight_ref):
    def stage(head, peak):
        weight_ref[head] = jnp.exp2(scaled_ref[head] - peak).astype(jnp.bfloat16)
        return peak

    return stage


def own_kernel(
    own_ref, first_ref, lengths_hbm, places_hbm, q_hbm, k_hbm, v_hbm,
    across_ref, bias_ref, peak_ref, sum_ref,
    lengths_ref, places_ref, q_ref, k_ref, v_ref, scaled_ref, weight_ref, sems,
):
    moves = (
        (lengths_hbm, lengths_ref), (places_hbm, places_ref),
        (k_hbm, k_ref), (v_hbm, v_ref), (q_hbm, q_ref),
    )
    copies = [pltpu.make_async_copy(*move, sems.at[n]) for n, move in enumerate(moves)]
    for copy in copies:
        copy.start()
    copies[0].wait()
    copies[1].wait()
    heads, _, rows = across_ref.shape
    own, first = own_ref[0], first_ref[0]
    owners = [own, own ^ first, own ^ 3 ^ first, own ^ 3]
    mask_tables(owners, lengths_ref, places_ref, rows, bias_ref)
    for copy in copies[2:]:
        copy.wait()
    keys = k_ref[...]
    turned = values_down(v_ref[...])

    def turn(head, _):
        q = q_ref[:, head * HEAD_WIDTH:(head + 1) * HEAD_WIDTH]
        across_ref[head] = jnp.transpose(q.astype(jnp.float32)).astype(jnp.bfloat16)

    def mix(head, peak):
        peak_ref[head:head + 1, :] = peak
        sum_ref[head] = jnp.dot(turned, weight_ref[head], preferred_element_type=jnp.float32)

    in_stages(heads, [
        turn,
        score_stage(keys, across_ref, bias_ref, 0, scaled_ref, None),
        weight_stage(scaled_ref, weight_ref),
        mix,
    ])


def joined(head, peak, turned, weight_ref, peak_ref, sum_ref):
    added = jnp.dot(turned, weight_ref[head], preferred_element_type=jnp.float32)
    return sum_ref[head] * jnp.exp2(peak_ref[head:head + 1, :] - peak) + added


def next_kernel(
    at, across_ref, bias_ref, peak_ref, sum_ref, k_ref, v_ref, new_peak_ref, new_sum_ref,
    scaled_ref, weight_ref,
):
    turned = values_down(v_ref[...])

    def mix(head, peak):
        new_peak_ref[head:head + 1, :] = peak
        new_sum_ref[head] = joined(head, peak, turned, weight_ref, peak_ref, sum_ref)

    in_stages(across_ref.shape[0], [
        score_stage(
            k_ref[...], across_ref, bias_ref, at, scaled_ref,
            lambda head: peak_ref[head:head + 1, :],
        ),
        weight_stage(scaled_ref, weight_ref),
        mix,
    ])


def weights_kernel(
    at, across_ref, bias_ref, peak_ref, sum_ref, k_ref, new_sum_ref, weight_ref, scaled_ref,
):
    def rescale(head, peak):
        new_sum_ref[head] = sum_ref[head] * jnp.exp2(peak_ref[head:head + 1, :] - peak)

    in_stages(across_ref.shape[0], [
        score_stage(
            k_ref[...], across_ref, bias_ref, at, scaled_ref,
            lambda head: peak_ref[head:head + 1, :],
        ),
        weight_stage(scaled_ref, weight_ref),
        rescale,
    ])


def last_kernel(sum_ref, weight_ref, v_ref, out_ref, block_ref, sems):
    turned = values_down(v_ref[...])
    copies = []

    def mix(head, _):
        added = jnp.dot(turned, weight_ref[head], preferred_element_type=jnp.float32)
        summed = sum_ref[head] + added
        return summed[:HEAD_WIDTH] / summed[HEAD_WIDTH:HEAD_WIDTH + 1]

    def send(head, out):
        cols = slice(head * HEAD_WIDTH, (head + 1) * HEAD_WIDTH)
        block_ref[:, cols] = jnp.transpose(out).astype(jnp.bfloat16)
        copy = pltpu.make_async_copy(block_ref.at[:, cols], out_ref.at[:, cols], sems.at[head])
        copy.start()
        copies.append(copy)

    in_stages(sum_ref.shape[0], [mix, send])
    for copy in copies:
        copy.wait()


SHORT = pl.CostEstimate(flops=0, bytes_accessed=0, transcendentals=0)


def in_vmem(*arrays):
    return [pltpu.with_memory_space_constraint(array, pltpu.VMEM) for array in arrays]


def in_hbm(*arrays):
    return [pltpu.with_memory_space_constraint(array, pltpu.HBM) for array in arrays]


VMEM_REF = pl.BlockSpec(memory_space=pltpu.VMEM)
HBM_REF = pl.BlockSpec(memory_space=pltpu.HBM)
PARAMS = pltpu.CompilerParams(vmem_limit_bytes=32 << 20)


def moved(value, *masks):
    seq_size, mp_size = lax.axis_size("seq"), lax.axis_size("mp")
    pairs = [
        (index * mp_size + place, (index ^ masks[place % len(masks)]) * mp_size + place)
        for index in range(seq_size)
        for place in range(mp_size)
    ]
    return lax.ppermute(value, ("seq", "mp"), pairs)


def staged_attention(queries, keys, values, lengths, old_place):
    first_keys, second_keys = moved(keys, 2, 1), moved(keys, 1, 2)
    first_values, second_values = moved(values, 2, 1), moved(values, 1, 2)
    rows, cols = queries.shape
    heads = cols // HEAD_WIDTH
    devices = lax.axis_size("seq")
    own = lax.axis_index("seq").astype(jnp.int32)
    far_first = lax.axis_index("mp") % 2 == 0
    first = jnp.where(far_first, 2, 1).astype(jnp.int32)
    places = old_place.reshape(1, -1)
    state = [
        pltpu.VMEM((heads, rows), jnp.float32),
        pltpu.VMEM((heads, HEAD_WIDTH + ONES, rows), jnp.float32),
    ]
    work = [
        pltpu.VMEM((heads, rows, rows), jnp.float32),
        pltpu.VMEM((heads, rows, rows), jnp.bfloat16),
    ]
    across, bias, *carried = pl.pallas_call(
        own_kernel,
        in_specs=[pl.BlockSpec(memory_space=pltpu.SMEM)] * 2 + [HBM_REF] * 5,
        out_specs=[VMEM_REF] * 4,
        out_shape=[
            pltpu.VMEM((heads, HEAD_WIDTH, rows), jnp.bfloat16),
            pltpu.VMEM((devices, rows, rows), jnp.float32),
        ] + state,
        scratch_shapes=[
            pltpu.SMEM(lengths.shape, jnp.int32),
            pltpu.VMEM(places.shape, jnp.int32),
            pltpu.VMEM(queries.shape, jnp.bfloat16),
            pltpu.VMEM(keys.shape, jnp.bfloat16),
            pltpu.VMEM(values.shape, jnp.bfloat16),
        ] + work + [pltpu.SemaphoreType.DMA((5,))],
        compiler_params=PARAMS,
        cost_estimate=SHORT,
        name="own_shard",
    )(own.reshape(1), first.reshape(1), *in_hbm(lengths, places, queries, keys, values))

    def add_shard(at, keys, values, carried):
        return pl.pallas_call(
            lambda *refs: next_kernel(at, *refs),
            in_specs=[VMEM_REF] * 6,
            out_specs=[VMEM_REF] * 2,
            out_shape=state,
            scratch_shapes=work,
            compiler_params=PARAMS,
            cost_estimate=SHORT,
            name="next_shard",
        )(*in_vmem(across, bias, *carried), keys, values)

    carried = add_shard(1, first_keys, first_values, carried)
    relayed = []
    for one, other in ((first_keys, second_keys), (first_values, second_values)):
        one, other, *carried = lax.optimization_barrier((one, other, *carried))
        far = jnp.where(far_first, one, other)
        far, *carried = lax.optimization_barrier((far, *carried))
        relayed.append(moved(far, 1))
    third_keys, third_values = relayed
    carried = add_shard(2, second_keys, second_values, carried)
    summed, weights = pl.pallas_call(
        lambda *refs: weights_kernel(3, *refs),
        in_specs=[VMEM_REF] * 5,
        out_specs=[VMEM_REF] * 2,
        out_shape=state[1:] + work[1:],
        scratch_shapes=work[:1],
        compiler_params=PARAMS,
        cost_estimate=SHORT,
        name="last_weights",
    )(*in_vmem(across, bias, *carried), third_keys)
    return pl.pallas_call(
        last_kernel,
        in_specs=[VMEM_REF] * 3,
        out_specs=pl.BlockSpec(memory_space=pl.ANY),
        out_shape=jax.ShapeDtypeStruct((rows, cols), jnp.bfloat16),
        scratch_shapes=[
            pltpu.VMEM((rows, cols), jnp.bfloat16),
            pltpu.SemaphoreType.DMA((heads,)),
        ],
        compiler_params=PARAMS,
        cost_estimate=SHORT,
        name="last_values",
    )(*in_vmem(summed, weights), third_values)


def online_kernel(heads, q_ref, k_ref, v_ref, key_pos_ref, query_pos_ref, start_ref, out_ref, peak_ref, acc_ref):
    step = pl.program_id(0)

    @pl.when(step == 0)
    def _():
        peak_ref[...] = jnp.full(peak_ref.shape, NEG_FILL, jnp.float32)
        acc_ref[...] = jnp.zeros(acc_ref.shape, jnp.float32)

    key_pos = key_pos_ref[...]
    visible = (key_pos >= start_ref[...]) & (key_pos <= query_pos_ref[...])
    values = v_ref[...]
    ext = jnp.concatenate([values, jnp.ones_like(values)], axis=1)
    for head in range(heads):
        q = q_ref[:, head * HEAD_WIDTH:(head + 1) * HEAD_WIDTH]
        scores = lax.dot_general(
            q, k_ref[...], (((1,), (1,)), ((), ())), preferred_element_type=jnp.float32
        )
        scaled = jnp.where(visible, scores * (HEAD_WIDTH ** -0.5 * LOG2_E), NEG_FILL)
        before = peak_ref[head]
        peak = jnp.maximum(before, jnp.max(scaled, axis=1, keepdims=True))
        weights = jnp.where(visible, jnp.exp2(scaled - peak), 0.0).astype(jnp.bfloat16)
        peak_ref[head] = peak
        acc_ref[head] = acc_ref[head] * jnp.exp2(before - peak) + jnp.dot(
            weights, ext, preferred_element_type=jnp.float32
        )

    @pl.when(step == pl.num_programs(0) - 1)
    def _():
        for head in range(heads):
            acc = acc_ref[head]
            out_ref[:, head * HEAD_WIDTH:(head + 1) * HEAD_WIDTH] = (
                acc[:, :HEAD_WIDTH] / acc[:, HEAD_WIDTH:]
            ).astype(jnp.bfloat16)


def online_attention(queries, keys, values, key_pos, query_pos, starts, chunk):
    rows, cols = queries.shape
    heads = cols // HEAD_WIDTH
    key_count = keys.shape[0]
    return pl.pallas_call(
        lambda *refs: online_kernel(heads, *refs),
        grid=(key_count // chunk,),
        in_specs=[
            pl.BlockSpec((rows, cols), lambda j: (0, 0)),
            pl.BlockSpec((chunk, HEAD_WIDTH), lambda j: (j, 0)),
            pl.BlockSpec((chunk, HEAD_WIDTH), lambda j: (j, 0)),
            pl.BlockSpec((1, chunk), lambda j: (0, j)),
            pl.BlockSpec((rows, 1), lambda j: (0, 0)),
            pl.BlockSpec((rows, 1), lambda j: (0, 0)),
        ],
        out_specs=pl.BlockSpec((rows, cols), lambda j: (0, 0)),
        out_shape=jax.ShapeDtypeStruct((rows, cols), jnp.bfloat16),
        scratch_shapes=[
            pltpu.VMEM((heads, rows, 1), jnp.float32),
            pltpu.VMEM((heads, rows, 2 * HEAD_WIDTH), jnp.float32),
        ],
        compiler_params=pltpu.CompilerParams(vmem_limit_bytes=32 << 20),
        name="online",
    )(queries, keys, values, key_pos, query_pos, starts)


def body(queries, keys, values, lengths, old_place):
    devices = lax.axis_size("seq")
    row_count = queries.shape[0]
    key_count = row_count * devices
    if devices == 4 and key_count <= 1024:
        return staged_attention(queries, keys, values, lengths, old_place)
    all_keys = lax.all_gather(keys, "seq", axis=0, tiled=True)
    all_values = lax.all_gather(values, "seq", axis=0, tiled=True)
    key_pos, query_pos, starts = block_places(
        lengths, old_place, lax.axis_index("seq"), row_count, key_count
    )
    return online_attention(queries, all_keys, all_values, key_pos, query_pos, starts, 512)


def solution(mesh):
    in_specs = (
        P(("groups", "seq"), "mp"),
        P(("groups", "seq"), "mp"),
        P(("groups", "seq"), "mp"),
        P("groups"),
        P("groups"),
    )
    out_specs = P(("groups", "seq"), "mp")
    return jax.shard_map(body, mesh=mesh, in_specs=in_specs, out_specs=out_specs, check_vma=False)
```

```python
import jax
import jax.numpy as jnp
from jax import lax
from jax.experimental import pallas as pl
from jax.experimental.pallas import tpu as pltpu
from jax.sharding import PartitionSpec as P

HEAD_WIDTH = 128
LOG2_E = 1.4426950408889634
NEG_FILL = -1e30
ONES = 16


def block_places(lengths, old_place, own_index, row_count, key_count):
    block_total = old_place.shape[0]
    block_rows = key_count // block_total
    ids = jnp.arange(block_total, dtype=jnp.int32)
    hit = old_place[:, None] == ids[None, :]
    new_block = jnp.sum(jnp.where(hit, ids[:, None], 0), axis=0)
    key_pos = (new_block[:, None] * block_rows + jnp.arange(block_rows, dtype=jnp.int32)).reshape(-1)
    query_pos = lax.dynamic_slice_in_dim(key_pos, own_index * row_count, row_count)
    bounds = jnp.cumsum(lengths)
    starts = jnp.max(jnp.where(bounds[None, :] <= query_pos[:, None], bounds[None, :], 0), axis=1)
    return key_pos.reshape(1, -1), query_pos.reshape(-1, 1), starts.reshape(-1, 1)


def iota(shape, dim):
    return lax.broadcasted_iota(jnp.int32, shape, dim)


def mask_tables(owners, lengths_ref, places_ref, rows, bias_ref):
    block_total = places_ref.shape[1]
    block_rows = rows * lax.axis_size("seq") // block_total
    blocks = rows // block_rows
    places = places_ref[...]
    square = (block_total, block_total)
    as_column = jnp.sum(
        jnp.where(iota(square, 0) == iota(square, 1), places, 0).astype(jnp.float32),
        axis=1, keepdims=True,
    ).astype(jnp.int32)
    across = (block_total, rows)
    hit = as_column == owners[0] * blocks + iota(across, 1) // block_rows
    at = jnp.where(hit, iota(across, 0) * block_rows, 0).astype(jnp.float32)
    query_pos = jnp.sum(at, axis=0, keepdims=True) + (
        iota((1, rows), 1) % block_rows
    ).astype(jnp.float32)
    starts = jnp.zeros_like(query_pos)
    bound = jnp.int32(0)
    for t in range(lengths_ref.shape[0]):
        bound = bound + lengths_ref[t]
        edge = bound.astype(jnp.float32)
        starts = jnp.where(edge <= query_pos, edge, starts)
    down = (rows, block_total)
    for n, owner in enumerate(owners):
        hit = places == owner * blocks + iota(down, 0) // block_rows
        at = jnp.where(hit, iota(down, 1) * block_rows, 0).astype(jnp.float32)
        key_pos = jnp.sum(at, axis=1, keepdims=True) + (
            iota((rows, 1), 0) % block_rows
        ).astype(jnp.float32)
        visible = (key_pos >= starts) & (key_pos <= query_pos)
        bias_ref[n] = jnp.where(visible, 0.0, NEG_FILL)


def values_down(values):
    turned = jnp.transpose(values.astype(jnp.float32)).astype(jnp.bfloat16)
    return jnp.concatenate([turned, jnp.ones((ONES, values.shape[0]), jnp.bfloat16)], axis=0)


def in_stages(heads, stages):
    results = [{} for _ in stages]
    for step in range(heads + len(stages) - 1):
        for late, stage in enumerate(stages):
            head = step - late
            if 0 <= head < heads:
                before = results[late - 1].pop(head) if late else None
                results[late][head] = stage(head, before)


def score_stage(keys, across_ref, bias_ref, at, scaled_ref, old_peak):
    def stage(head, _):
        scores = jnp.dot(keys, across_ref[head], preferred_element_type=jnp.float32)
        scaled = scores * (HEAD_WIDTH ** -0.5 * LOG2_E) + bias_ref[at]
        scaled_ref[head] = scaled
        peak = jnp.max(scaled, axis=0, keepdims=True)
        return peak if old_peak is None else jnp.maximum(old_peak(head), peak)

    return stage


def weight_stage(scaled_ref, weight_ref):
    def stage(head, peak):
        weight_ref[head] = jnp.exp2(scaled_ref[head] - peak).astype(jnp.bfloat16)
        return peak

    return stage


def own_kernel(
    own_ref, lengths_hbm, places_hbm, q_hbm, k_hbm, v_hbm,
    across_ref, bias_ref, peak_ref, sum_ref,
    lengths_ref, places_ref, q_ref, k_ref, v_ref, scaled_ref, weight_ref, sems,
):
    moves = (
        (lengths_hbm, lengths_ref), (places_hbm, places_ref),
        (k_hbm, k_ref), (v_hbm, v_ref), (q_hbm, q_ref),
    )
    copies = [pltpu.make_async_copy(*move, sems.at[n]) for n, move in enumerate(moves)]
    for copy in copies:
        copy.start()
    copies[0].wait()
    copies[1].wait()
    heads, _, rows = across_ref.shape
    owners = [own_ref[0] ^ mask for mask in range(bias_ref.shape[0])]
    mask_tables(owners, lengths_ref, places_ref, rows, bias_ref)
    for copy in copies[2:]:
        copy.wait()
    keys = k_ref[...]
    turned = values_down(v_ref[...])

    def turn(head, _):
        q = q_ref[:, head * HEAD_WIDTH:(head + 1) * HEAD_WIDTH]
        across_ref[head] = jnp.transpose(q.astype(jnp.float32)).astype(jnp.bfloat16)

    def mix(head, peak):
        peak_ref[head:head + 1, :] = peak
        sum_ref[head] = jnp.dot(turned, weight_ref[head], preferred_element_type=jnp.float32)

    in_stages(heads, [
        turn,
        score_stage(keys, across_ref, bias_ref, 0, scaled_ref, None),
        weight_stage(scaled_ref, weight_ref),
        mix,
    ])


def joined(head, peak, turned, weight_ref, peak_ref, sum_ref):
    added = jnp.dot(turned, weight_ref[head], preferred_element_type=jnp.float32)
    return sum_ref[head] * jnp.exp2(peak_ref[head:head + 1, :] - peak) + added


def next_kernel(
    at, across_ref, bias_ref, peak_ref, sum_ref, k_ref, v_ref, new_peak_ref, new_sum_ref,
    scaled_ref, weight_ref,
):
    turned = values_down(v_ref[...])

    def mix(head, peak):
        new_peak_ref[head:head + 1, :] = peak
        new_sum_ref[head] = joined(head, peak, turned, weight_ref, peak_ref, sum_ref)

    in_stages(across_ref.shape[0], [
        score_stage(
            k_ref[...], across_ref, bias_ref, at, scaled_ref,
            lambda head: peak_ref[head:head + 1, :],
        ),
        weight_stage(scaled_ref, weight_ref),
        mix,
    ])


def weights_kernel(
    at, across_ref, bias_ref, peak_ref, sum_ref, k_ref, new_sum_ref, weight_ref, scaled_ref,
):
    def rescale(head, peak):
        new_sum_ref[head] = sum_ref[head] * jnp.exp2(peak_ref[head:head + 1, :] - peak)

    in_stages(across_ref.shape[0], [
        score_stage(
            k_ref[...], across_ref, bias_ref, at, scaled_ref,
            lambda head: peak_ref[head:head + 1, :],
        ),
        weight_stage(scaled_ref, weight_ref),
        rescale,
    ])


def last_kernel(sum_ref, weight_ref, v_ref, out_ref, block_ref, sems):
    turned = values_down(v_ref[...])
    copies = []

    def mix(head, _):
        added = jnp.dot(turned, weight_ref[head], preferred_element_type=jnp.float32)
        summed = sum_ref[head] + added
        return summed[:HEAD_WIDTH] / summed[HEAD_WIDTH:HEAD_WIDTH + 1]

    def send(head, out):
        cols = slice(head * HEAD_WIDTH, (head + 1) * HEAD_WIDTH)
        block_ref[:, cols] = jnp.transpose(out).astype(jnp.bfloat16)
        copy = pltpu.make_async_copy(block_ref.at[:, cols], out_ref.at[:, cols], sems.at[head])
        copy.start()
        copies.append(copy)

    in_stages(sum_ref.shape[0], [mix, send])
    for copy in copies:
        copy.wait()


SHORT = pl.CostEstimate(flops=0, bytes_accessed=0, transcendentals=0)


def in_vmem(*arrays):
    return [pltpu.with_memory_space_constraint(array, pltpu.VMEM) for array in arrays]


def in_hbm(*arrays):
    return [pltpu.with_memory_space_constraint(array, pltpu.HBM) for array in arrays]


VMEM_REF = pl.BlockSpec(memory_space=pltpu.VMEM)
HBM_REF = pl.BlockSpec(memory_space=pltpu.HBM)
PARAMS = pltpu.CompilerParams(vmem_limit_bytes=32 << 20)


def moved(value, mask):
    return lax.ppermute(value, "seq", [(i, i ^ mask) for i in range(lax.axis_size("seq"))])


def staged_attention(queries, keys, values, lengths, old_place):
    far_keys, far_values = moved(keys, 2), moved(values, 2)
    near_keys, near_values = moved(keys, 1), moved(values, 1)
    rows, cols = queries.shape
    heads = cols // HEAD_WIDTH
    devices = lax.axis_size("seq")
    own = lax.axis_index("seq").astype(jnp.int32)
    places = old_place.reshape(1, -1)
    state = [
        pltpu.VMEM((heads, rows), jnp.float32),
        pltpu.VMEM((heads, HEAD_WIDTH + ONES, rows), jnp.float32),
    ]
    work = [
        pltpu.VMEM((heads, rows, rows), jnp.float32),
        pltpu.VMEM((heads, rows, rows), jnp.bfloat16),
    ]
    across, bias, *carried = pl.pallas_call(
        own_kernel,
        in_specs=[pl.BlockSpec(memory_space=pltpu.SMEM)] + [HBM_REF] * 5,
        out_specs=[VMEM_REF] * 4,
        out_shape=[
            pltpu.VMEM((heads, HEAD_WIDTH, rows), jnp.bfloat16),
            pltpu.VMEM((devices, rows, rows), jnp.float32),
        ] + state,
        scratch_shapes=[
            pltpu.SMEM(lengths.shape, jnp.int32),
            pltpu.VMEM(places.shape, jnp.int32),
            pltpu.VMEM(queries.shape, jnp.bfloat16),
            pltpu.VMEM(keys.shape, jnp.bfloat16),
            pltpu.VMEM(values.shape, jnp.bfloat16),
        ] + work + [pltpu.SemaphoreType.DMA((5,))],
        compiler_params=PARAMS,
        cost_estimate=SHORT,
        name="own_shard",
    )(own.reshape(1), *in_hbm(lengths, places, queries, keys, values))

    def add_shard(at, keys, values, carried):
        return pl.pallas_call(
            lambda *refs: next_kernel(at, *refs),
            in_specs=[VMEM_REF] * 6,
            out_specs=[VMEM_REF] * 2,
            out_shape=state,
            scratch_shapes=work,
            compiler_params=PARAMS,
            cost_estimate=SHORT,
            name="next_shard",
        )(*in_vmem(across, bias, *carried), keys, values)

    far_keys, *carried = lax.optimization_barrier((far_keys, *carried))
    third_keys = moved(far_keys, 1)
    far_values, *carried = lax.optimization_barrier((far_values, *carried))
    third_values = moved(far_values, 1)
    carried = add_shard(2, far_keys, far_values, carried)
    carried = add_shard(1, near_keys, near_values, carried)
    summed, weights = pl.pallas_call(
        lambda *refs: weights_kernel(3, *refs),
        in_specs=[VMEM_REF] * 5,
        out_specs=[VMEM_REF] * 2,
        out_shape=state[1:] + work[1:],
        scratch_shapes=work[:1],
        compiler_params=PARAMS,
        cost_estimate=SHORT,
        name="last_weights",
    )(*in_vmem(across, bias, *carried), third_keys)
    return pl.pallas_call(
        last_kernel,
        in_specs=[VMEM_REF] * 3,
        out_specs=pl.BlockSpec(memory_space=pl.ANY),
        out_shape=jax.ShapeDtypeStruct((rows, cols), jnp.bfloat16),
        scratch_shapes=[
            pltpu.VMEM((rows, cols), jnp.bfloat16),
            pltpu.SemaphoreType.DMA((heads,)),
        ],
        compiler_params=PARAMS,
        cost_estimate=SHORT,
        name="last_values",
    )(*in_vmem(summed, weights), third_values)


def online_kernel(heads, q_ref, k_ref, v_ref, key_pos_ref, query_pos_ref, start_ref, out_ref, peak_ref, acc_ref):
    step = pl.program_id(0)

    @pl.when(step == 0)
    def _():
        peak_ref[...] = jnp.full(peak_ref.shape, NEG_FILL, jnp.float32)
        acc_ref[...] = jnp.zeros(acc_ref.shape, jnp.float32)

    key_pos = key_pos_ref[...]
    visible = (key_pos >= start_ref[...]) & (key_pos <= query_pos_ref[...])
    values = v_ref[...]
    ext = jnp.concatenate([values, jnp.ones_like(values)], axis=1)
    for head in range(heads):
        q = q_ref[:, head * HEAD_WIDTH:(head + 1) * HEAD_WIDTH]
        scores = lax.dot_general(
            q, k_ref[...], (((1,), (1,)), ((), ())), preferred_element_type=jnp.float32
        )
        scaled = jnp.where(visible, scores * (HEAD_WIDTH ** -0.5 * LOG2_E), NEG_FILL)
        before = peak_ref[head]
        peak = jnp.maximum(before, jnp.max(scaled, axis=1, keepdims=True))
        weights = jnp.where(visible, jnp.exp2(scaled - peak), 0.0).astype(jnp.bfloat16)
        peak_ref[head] = peak
        acc_ref[head] = acc_ref[head] * jnp.exp2(before - peak) + jnp.dot(
            weights, ext, preferred_element_type=jnp.float32
        )

    @pl.when(step == pl.num_programs(0) - 1)
    def _():
        for head in range(heads):
            acc = acc_ref[head]
            out_ref[:, head * HEAD_WIDTH:(head + 1) * HEAD_WIDTH] = (
                acc[:, :HEAD_WIDTH] / acc[:, HEAD_WIDTH:]
            ).astype(jnp.bfloat16)


def online_attention(queries, keys, values, key_pos, query_pos, starts, chunk):
    rows, cols = queries.shape
    heads = cols // HEAD_WIDTH
    key_count = keys.shape[0]
    return pl.pallas_call(
        lambda *refs: online_kernel(heads, *refs),
        grid=(key_count // chunk,),
        in_specs=[
            pl.BlockSpec((rows, cols), lambda j: (0, 0)),
            pl.BlockSpec((chunk, HEAD_WIDTH), lambda j: (j, 0)),
            pl.BlockSpec((chunk, HEAD_WIDTH), lambda j: (j, 0)),
            pl.BlockSpec((1, chunk), lambda j: (0, j)),
            pl.BlockSpec((rows, 1), lambda j: (0, 0)),
            pl.BlockSpec((rows, 1), lambda j: (0, 0)),
        ],
        out_specs=pl.BlockSpec((rows, cols), lambda j: (0, 0)),
        out_shape=jax.ShapeDtypeStruct((rows, cols), jnp.bfloat16),
        scratch_shapes=[
            pltpu.VMEM((heads, rows, 1), jnp.float32),
            pltpu.VMEM((heads, rows, 2 * HEAD_WIDTH), jnp.float32),
        ],
        compiler_params=pltpu.CompilerParams(vmem_limit_bytes=32 << 20),
        name="online",
    )(queries, keys, values, key_pos, query_pos, starts)


def body(queries, keys, values, lengths, old_place):
    devices = lax.axis_size("seq")
    row_count = queries.shape[0]
    key_count = row_count * devices
    if devices == 4 and key_count <= 1024:
        return staged_attention(queries, keys, values, lengths, old_place)
    all_keys = lax.all_gather(keys, "seq", axis=0, tiled=True)
    all_values = lax.all_gather(values, "seq", axis=0, tiled=True)
    key_pos, query_pos, starts = block_places(
        lengths, old_place, lax.axis_index("seq"), row_count, key_count
    )
    return online_attention(queries, all_keys, all_values, key_pos, query_pos, starts, 512)


def solution(mesh):
    in_specs = (
        P(("groups", "seq"), "mp"),
        P(("groups", "seq"), "mp"),
        P(("groups", "seq"), "mp"),
        P("groups"),
        P("groups"),
    )
    out_specs = P(("groups", "seq"), "mp")
    return jax.shard_map(body, mesh=mesh, in_specs=in_specs, out_specs=out_specs, check_vma=False)
```

```python
import jax
import jax.numpy as jnp
from jax import lax
from jax.experimental import pallas as pl
from jax.experimental.pallas import tpu as pltpu
from jax.sharding import PartitionSpec as P

HEAD_WIDTH = 128
LOG2_E = 1.4426950408889634
NEG_FILL = -1e30
ONES = 16


def block_places(lengths, old_place, own_index, row_count, key_count):
    block_total = old_place.shape[0]
    block_rows = key_count // block_total
    ids = jnp.arange(block_total, dtype=jnp.int32)
    hit = old_place[:, None] == ids[None, :]
    new_block = jnp.sum(jnp.where(hit, ids[:, None], 0), axis=0)
    key_pos = (new_block[:, None] * block_rows + jnp.arange(block_rows, dtype=jnp.int32)).reshape(-1)
    query_pos = lax.dynamic_slice_in_dim(key_pos, own_index * row_count, row_count)
    bounds = jnp.cumsum(lengths)
    starts = jnp.max(jnp.where(bounds[None, :] <= query_pos[:, None], bounds[None, :], 0), axis=1)
    return key_pos.reshape(1, -1), query_pos.reshape(-1, 1), starts.reshape(-1, 1)


def iota(shape, dim):
    return lax.broadcasted_iota(jnp.int32, shape, dim)


def mask_tables(owners, lengths_ref, places_ref, rows, bias_ref):
    block_total = places_ref.shape[1]
    block_rows = rows * lax.axis_size("seq") // block_total
    blocks = rows // block_rows
    places = places_ref[...]
    square = (block_total, block_total)
    as_column = jnp.sum(
        jnp.where(iota(square, 0) == iota(square, 1), places, 0).astype(jnp.float32),
        axis=1, keepdims=True,
    ).astype(jnp.int32)
    across = (block_total, rows)
    hit = as_column == owners[0] * blocks + iota(across, 1) // block_rows
    at = jnp.where(hit, iota(across, 0) * block_rows, 0).astype(jnp.float32)
    query_pos = jnp.sum(at, axis=0, keepdims=True) + (
        iota((1, rows), 1) % block_rows
    ).astype(jnp.float32)
    starts = jnp.zeros_like(query_pos)
    bound = jnp.int32(0)
    for t in range(lengths_ref.shape[0]):
        bound = bound + lengths_ref[t]
        edge = bound.astype(jnp.float32)
        starts = jnp.where(edge <= query_pos, edge, starts)
    down = (rows, block_total)
    for n, owner in enumerate(owners):
        hit = places == owner * blocks + iota(down, 0) // block_rows
        at = jnp.where(hit, iota(down, 1) * block_rows, 0).astype(jnp.float32)
        key_pos = jnp.sum(at, axis=1, keepdims=True) + (
            iota((rows, 1), 0) % block_rows
        ).astype(jnp.float32)
        visible = (key_pos >= starts) & (key_pos <= query_pos)
        bias_ref[n] = jnp.where(visible, 0.0, NEG_FILL)


def values_down(values):
    turned = jnp.transpose(values.astype(jnp.float32)).astype(jnp.bfloat16)
    return jnp.concatenate([turned, jnp.ones((ONES, values.shape[0]), jnp.bfloat16)], axis=0)


def in_stages(heads, stages):
    results = [{} for _ in stages]
    for step in range(heads + len(stages) - 1):
        for late, stage in enumerate(stages):
            head = step - late
            if 0 <= head < heads:
                before = results[late - 1].pop(head) if late else None
                results[late][head] = stage(head, before)


def score_stage(keys, across_ref, bias_ref, at, scaled_ref, old_peak):
    def stage(head, _):
        scores = jnp.dot(keys, across_ref[head], preferred_element_type=jnp.float32)
        scaled = scores * (HEAD_WIDTH ** -0.5 * LOG2_E) + bias_ref[at]
        scaled_ref[head] = scaled
        peak = jnp.max(scaled, axis=0, keepdims=True)
        return peak if old_peak is None else jnp.maximum(old_peak(head), peak)

    return stage


def weight_stage(scaled_ref, weight_ref):
    def stage(head, peak):
        weight_ref[head] = jnp.exp2(scaled_ref[head] - peak).astype(jnp.bfloat16)
        return peak

    return stage


def own_kernel(
    own_ref, first_ref, lengths_hbm, places_hbm, q_hbm, k_hbm, v_hbm,
    across_ref, bias_ref, peak_ref, sum_ref,
    lengths_ref, places_ref, q_ref, k_ref, v_ref, scaled_ref, weight_ref, sems,
):
    moves = (
        (lengths_hbm, lengths_ref), (places_hbm, places_ref),
        (k_hbm, k_ref), (v_hbm, v_ref), (q_hbm, q_ref),
    )
    copies = [pltpu.make_async_copy(*move, sems.at[n]) for n, move in enumerate(moves)]
    for copy in copies:
        copy.start()
    copies[0].wait()
    copies[1].wait()
    heads, _, rows = across_ref.shape
    own, first = own_ref[0], first_ref[0]
    owners = [own, own ^ first, own ^ 3 ^ first, own ^ 3]
    mask_tables(owners, lengths_ref, places_ref, rows, bias_ref)
    for copy in copies[2:]:
        copy.wait()
    keys = k_ref[...]
    turned = values_down(v_ref[...])

    def turn(head, _):
        q = q_ref[:, head * HEAD_WIDTH:(head + 1) * HEAD_WIDTH]
        across_ref[head] = jnp.transpose(q.astype(jnp.float32)).astype(jnp.bfloat16)

    def mix(head, peak):
        peak_ref[head:head + 1, :] = peak
        sum_ref[head] = jnp.dot(turned, weight_ref[head], preferred_element_type=jnp.float32)

    in_stages(heads, [
        turn,
        score_stage(keys, across_ref, bias_ref, 0, scaled_ref, None),
        weight_stage(scaled_ref, weight_ref),
        mix,
    ])


def joined(head, peak, turned, weight_ref, peak_ref, sum_ref):
    added = jnp.dot(turned, weight_ref[head], preferred_element_type=jnp.float32)
    return sum_ref[head] * jnp.exp2(peak_ref[head:head + 1, :] - peak) + added


def next_kernel(
    at, across_ref, bias_ref, peak_ref, sum_ref, k_ref, v_ref, new_peak_ref, new_sum_ref,
    scaled_ref, weight_ref,
):
    turned = values_down(v_ref[...])

    def mix(head, peak):
        new_peak_ref[head:head + 1, :] = peak
        new_sum_ref[head] = joined(head, peak, turned, weight_ref, peak_ref, sum_ref)

    in_stages(across_ref.shape[0], [
        score_stage(
            k_ref[...], across_ref, bias_ref, at, scaled_ref,
            lambda head: peak_ref[head:head + 1, :],
        ),
        weight_stage(scaled_ref, weight_ref),
        mix,
    ])


def weights_kernel(
    at, across_ref, bias_ref, peak_ref, sum_ref, k_ref, new_sum_ref, weight_ref, scaled_ref,
):
    def rescale(head, peak):
        new_sum_ref[head] = sum_ref[head] * jnp.exp2(peak_ref[head:head + 1, :] - peak)

    in_stages(across_ref.shape[0], [
        score_stage(
            k_ref[...], across_ref, bias_ref, at, scaled_ref,
            lambda head: peak_ref[head:head + 1, :],
        ),
        weight_stage(scaled_ref, weight_ref),
        rescale,
    ])


def last_kernel(sum_ref, weight_ref, v_ref, out_ref, block_ref, sems):
    turned = values_down(v_ref[...])
    copies = []

    def mix(head, _):
        added = jnp.dot(turned, weight_ref[head], preferred_element_type=jnp.float32)
        summed = sum_ref[head] + added
        return summed[:HEAD_WIDTH] / summed[HEAD_WIDTH:HEAD_WIDTH + 1]

    def send(head, out):
        cols = slice(head * HEAD_WIDTH, (head + 1) * HEAD_WIDTH)
        block_ref[:, cols] = jnp.transpose(out).astype(jnp.bfloat16)
        copy = pltpu.make_async_copy(block_ref.at[:, cols], out_ref.at[:, cols], sems.at[head])
        copy.start()
        copies.append(copy)

    in_stages(sum_ref.shape[0], [mix, send])
    for copy in copies:
        copy.wait()


SHORT = pl.CostEstimate(flops=0, bytes_accessed=0, transcendentals=0)


def in_vmem(*arrays):
    return [pltpu.with_memory_space_constraint(array, pltpu.VMEM) for array in arrays]


def in_hbm(*arrays):
    return [pltpu.with_memory_space_constraint(array, pltpu.HBM) for array in arrays]


VMEM_REF = pl.BlockSpec(memory_space=pltpu.VMEM)
HBM_REF = pl.BlockSpec(memory_space=pltpu.HBM)
PARAMS = pltpu.CompilerParams(vmem_limit_bytes=32 << 20)


CYCLE = ((0, 2), (2, 3), (3, 1), (1, 0))
BACK = tuple((target, source) for source, target in CYCLE)
SWAP = ((0, 1), (1, 0), (2, 3), (3, 2))


def staged_attention(queries, keys, values, lengths, old_place):
    first_keys, first_values = (lax.ppermute(part, "seq", CYCLE) for part in (keys, values))
    second_keys, second_values = (lax.ppermute(part, "seq", BACK) for part in (keys, values))
    rows, cols = queries.shape
    heads = cols // HEAD_WIDTH
    devices = lax.axis_size("seq")
    own = lax.axis_index("seq").astype(jnp.int32)
    inner = (own == 1) | (own == 2)
    first = jnp.where(inner, 2, 1).astype(jnp.int32)
    places = old_place.reshape(1, -1)
    state = [
        pltpu.VMEM((heads, rows), jnp.float32),
        pltpu.VMEM((heads, HEAD_WIDTH + ONES, rows), jnp.float32),
    ]
    work = [
        pltpu.VMEM((heads, rows, rows), jnp.float32),
        pltpu.VMEM((heads, rows, rows), jnp.bfloat16),
    ]
    across, bias, *carried = pl.pallas_call(
        own_kernel,
        in_specs=[pl.BlockSpec(memory_space=pltpu.SMEM)] * 2 + [HBM_REF] * 5,
        out_specs=[VMEM_REF] * 4,
        out_shape=[
            pltpu.VMEM((heads, HEAD_WIDTH, rows), jnp.bfloat16),
            pltpu.VMEM((devices, rows, rows), jnp.float32),
        ] + state,
        scratch_shapes=[
            pltpu.SMEM(lengths.shape, jnp.int32),
            pltpu.VMEM(places.shape, jnp.int32),
            pltpu.VMEM(queries.shape, jnp.bfloat16),
            pltpu.VMEM(keys.shape, jnp.bfloat16),
            pltpu.VMEM(values.shape, jnp.bfloat16),
        ] + work + [pltpu.SemaphoreType.DMA((5,))],
        compiler_params=PARAMS,
        cost_estimate=SHORT,
        name="own_shard",
    )(own.reshape(1), first.reshape(1), *in_hbm(lengths, places, queries, keys, values))

    def add_shard(at, keys, values, carried):
        return pl.pallas_call(
            lambda *refs: next_kernel(at, *refs),
            in_specs=[VMEM_REF] * 6,
            out_specs=[VMEM_REF] * 2,
            out_shape=state,
            scratch_shapes=work,
            compiler_params=PARAMS,
            cost_estimate=SHORT,
            name="next_shard",
        )(*in_vmem(across, bias, *carried), keys, values)

    carried = add_shard(1, first_keys, first_values, carried)
    second_keys, *carried = lax.optimization_barrier((second_keys, *carried))
    far_keys = jnp.where(inner, first_keys, second_keys)
    third_keys = lax.ppermute(far_keys, "seq", SWAP)
    second_values, second_keys, far_keys, *carried = lax.optimization_barrier((second_values, second_keys, far_keys, *carried))
    far_values = jnp.where(inner, first_values, second_values)
    third_values = lax.ppermute(far_values, "seq", SWAP)
    carried = add_shard(2, second_keys, second_values, carried)
    summed, weights = pl.pallas_call(
        lambda *refs: weights_kernel(3, *refs),
        in_specs=[VMEM_REF] * 5,
        out_specs=[VMEM_REF] * 2,
        out_shape=state[1:] + work[1:],
        scratch_shapes=work[:1],
        compiler_params=PARAMS,
        cost_estimate=SHORT,
        name="last_weights",
    )(*in_vmem(across, bias, *carried), third_keys)
    return pl.pallas_call(
        last_kernel,
        in_specs=[VMEM_REF] * 3,
        out_specs=pl.BlockSpec(memory_space=pl.ANY),
        out_shape=jax.ShapeDtypeStruct((rows, cols), jnp.bfloat16),
        scratch_shapes=[
            pltpu.VMEM((rows, cols), jnp.bfloat16),
            pltpu.SemaphoreType.DMA((heads,)),
        ],
        compiler_params=PARAMS,
        cost_estimate=SHORT,
        name="last_values",
    )(*in_vmem(summed, weights), third_values)


def online_kernel(heads, q_ref, k_ref, v_ref, key_pos_ref, query_pos_ref, start_ref, out_ref, peak_ref, acc_ref):
    step = pl.program_id(0)

    @pl.when(step == 0)
    def _():
        peak_ref[...] = jnp.full(peak_ref.shape, NEG_FILL, jnp.float32)
        acc_ref[...] = jnp.zeros(acc_ref.shape, jnp.float32)

    key_pos = key_pos_ref[...]
    visible = (key_pos >= start_ref[...]) & (key_pos <= query_pos_ref[...])
    values = v_ref[...]
    ext = jnp.concatenate([values, jnp.ones_like(values)], axis=1)
    for head in range(heads):
        q = q_ref[:, head * HEAD_WIDTH:(head + 1) * HEAD_WIDTH]
        scores = lax.dot_general(
            q, k_ref[...], (((1,), (1,)), ((), ())), preferred_element_type=jnp.float32
        )
        scaled = jnp.where(visible, scores * (HEAD_WIDTH ** -0.5 * LOG2_E), NEG_FILL)
        before = peak_ref[head]
        peak = jnp.maximum(before, jnp.max(scaled, axis=1, keepdims=True))
        weights = jnp.where(visible, jnp.exp2(scaled - peak), 0.0).astype(jnp.bfloat16)
        peak_ref[head] = peak
        acc_ref[head] = acc_ref[head] * jnp.exp2(before - peak) + jnp.dot(
            weights, ext, preferred_element_type=jnp.float32
        )

    @pl.when(step == pl.num_programs(0) - 1)
    def _():
        for head in range(heads):
            acc = acc_ref[head]
            out_ref[:, head * HEAD_WIDTH:(head + 1) * HEAD_WIDTH] = (
                acc[:, :HEAD_WIDTH] / acc[:, HEAD_WIDTH:]
            ).astype(jnp.bfloat16)


def online_attention(queries, keys, values, key_pos, query_pos, starts, chunk):
    rows, cols = queries.shape
    heads = cols // HEAD_WIDTH
    key_count = keys.shape[0]
    return pl.pallas_call(
        lambda *refs: online_kernel(heads, *refs),
        grid=(key_count // chunk,),
        in_specs=[
            pl.BlockSpec((rows, cols), lambda j: (0, 0)),
            pl.BlockSpec((chunk, HEAD_WIDTH), lambda j: (j, 0)),
            pl.BlockSpec((chunk, HEAD_WIDTH), lambda j: (j, 0)),
            pl.BlockSpec((1, chunk), lambda j: (0, j)),
            pl.BlockSpec((rows, 1), lambda j: (0, 0)),
            pl.BlockSpec((rows, 1), lambda j: (0, 0)),
        ],
        out_specs=pl.BlockSpec((rows, cols), lambda j: (0, 0)),
        out_shape=jax.ShapeDtypeStruct((rows, cols), jnp.bfloat16),
        scratch_shapes=[
            pltpu.VMEM((heads, rows, 1), jnp.float32),
            pltpu.VMEM((heads, rows, 2 * HEAD_WIDTH), jnp.float32),
        ],
        compiler_params=pltpu.CompilerParams(vmem_limit_bytes=32 << 20),
        name="online",
    )(queries, keys, values, key_pos, query_pos, starts)


def body(queries, keys, values, lengths, old_place):
    devices = lax.axis_size("seq")
    row_count = queries.shape[0]
    key_count = row_count * devices
    if devices == 4 and key_count <= 1024:
        return staged_attention(queries, keys, values, lengths, old_place)
    all_keys = lax.all_gather(keys, "seq", axis=0, tiled=True)
    all_values = lax.all_gather(values, "seq", axis=0, tiled=True)
    key_pos, query_pos, starts = block_places(
        lengths, old_place, lax.axis_index("seq"), row_count, key_count
    )
    return online_attention(queries, all_keys, all_values, key_pos, query_pos, starts, 512)


def solution(mesh):
    in_specs = (
        P(("groups", "seq"), "mp"),
        P(("groups", "seq"), "mp"),
        P(("groups", "seq"), "mp"),
        P("groups"),
        P("groups"),
    )
    out_specs = P(("groups", "seq"), "mp")
    return jax.shard_map(body, mesh=mesh, in_specs=in_specs, out_specs=out_specs, check_vma=False)
```

```python
import jax
import jax.numpy as jnp
from jax import lax
from jax.experimental import pallas as pl
from jax.experimental.pallas import tpu as pltpu
from jax.sharding import PartitionSpec as P

HEAD_WIDTH = 128
LOG2_E = 1.4426950408889634
NEG_FILL = -1e30
ONES = 16


def block_places(lengths, old_place, own_index, row_count, key_count):
    block_total = old_place.shape[0]
    block_rows = key_count // block_total
    ids = jnp.arange(block_total, dtype=jnp.int32)
    hit = old_place[:, None] == ids[None, :]
    new_block = jnp.sum(jnp.where(hit, ids[:, None], 0), axis=0)
    key_pos = (new_block[:, None] * block_rows + jnp.arange(block_rows, dtype=jnp.int32)).reshape(-1)
    query_pos = lax.dynamic_slice_in_dim(key_pos, own_index * row_count, row_count)
    bounds = jnp.cumsum(lengths)
    starts = jnp.max(jnp.where(bounds[None, :] <= query_pos[:, None], bounds[None, :], 0), axis=1)
    return key_pos.reshape(1, -1), query_pos.reshape(-1, 1), starts.reshape(-1, 1)


def iota(shape, dim):
    return lax.broadcasted_iota(jnp.int32, shape, dim)


def mask_tables(owners, lengths_ref, places_ref, rows, bias_ref):
    block_total = places_ref.shape[1]
    block_rows = rows * lax.axis_size("seq") // block_total
    blocks = rows // block_rows
    places = places_ref[...]
    square = (block_total, block_total)
    as_column = jnp.sum(
        jnp.where(iota(square, 0) == iota(square, 1), places, 0).astype(jnp.float32),
        axis=1, keepdims=True,
    ).astype(jnp.int32)
    across = (block_total, rows)
    hit = as_column == owners[0] * blocks + iota(across, 1) // block_rows
    at = jnp.where(hit, iota(across, 0) * block_rows, 0).astype(jnp.float32)
    query_pos = jnp.sum(at, axis=0, keepdims=True) + (
        iota((1, rows), 1) % block_rows
    ).astype(jnp.float32)
    starts = jnp.zeros_like(query_pos)
    bound = jnp.int32(0)
    for t in range(lengths_ref.shape[0]):
        bound = bound + lengths_ref[t]
        edge = bound.astype(jnp.float32)
        starts = jnp.where(edge <= query_pos, edge, starts)
    down = (rows, block_total)
    for n, owner in enumerate(owners):
        hit = places == owner * blocks + iota(down, 0) // block_rows
        at = jnp.where(hit, iota(down, 1) * block_rows, 0).astype(jnp.float32)
        key_pos = jnp.sum(at, axis=1, keepdims=True) + (
            iota((rows, 1), 0) % block_rows
        ).astype(jnp.float32)
        visible = (key_pos >= starts) & (key_pos <= query_pos)
        bias_ref[n] = jnp.where(visible, 0.0, NEG_FILL)


def values_down(values):
    turned = jnp.transpose(values.astype(jnp.float32)).astype(jnp.bfloat16)
    return jnp.concatenate([turned, jnp.ones((ONES, values.shape[0]), jnp.bfloat16)], axis=0)


def in_stages(heads, stages):
    results = [{} for _ in stages]
    for step in range(heads + len(stages) - 1):
        for late, stage in enumerate(stages):
            head = step - late
            if 0 <= head < heads:
                before = results[late - 1].pop(head) if late else None
                results[late][head] = stage(head, before)


def score_stage(keys, across_ref, bias_ref, at, scaled_ref, old_peak):
    def stage(head, _):
        scores = jnp.dot(keys, across_ref[head], preferred_element_type=jnp.float32)
        scaled = scores * (HEAD_WIDTH ** -0.5 * LOG2_E) + bias_ref[at]
        scaled_ref[head] = scaled
        peak = jnp.max(scaled, axis=0, keepdims=True)
        return peak if old_peak is None else jnp.maximum(old_peak(head), peak)

    return stage


def weight_stage(scaled_ref, weight_ref):
    def stage(head, peak):
        weight_ref[head] = jnp.exp2(scaled_ref[head] - peak).astype(jnp.bfloat16)
        return peak

    return stage


def own_kernel(
    own_ref, lengths_hbm, places_hbm, q_hbm, k_hbm, v_hbm,
    across_ref, bias_ref, peak_ref, sum_ref,
    lengths_ref, places_ref, q_ref, k_ref, v_ref, scaled_ref, weight_ref, sems,
):
    moves = (
        (lengths_hbm, lengths_ref), (places_hbm, places_ref),
        (k_hbm, k_ref), (v_hbm, v_ref), (q_hbm, q_ref),
    )
    copies = [pltpu.make_async_copy(*move, sems.at[n]) for n, move in enumerate(moves)]
    for copy in copies:
        copy.start()
    copies[0].wait()
    copies[1].wait()
    heads, _, rows = across_ref.shape
    owners = [own_ref[0] ^ mask for mask in range(bias_ref.shape[0])]
    mask_tables(owners, lengths_ref, places_ref, rows, bias_ref)
    for copy in copies[2:]:
        copy.wait()
    keys = k_ref[...]
    turned = values_down(v_ref[...])

    def turn(head, _):
        q = q_ref[:, head * HEAD_WIDTH:(head + 1) * HEAD_WIDTH]
        across_ref[head] = jnp.transpose(q.astype(jnp.float32)).astype(jnp.bfloat16)

    def mix(head, peak):
        peak_ref[head:head + 1, :] = peak
        sum_ref[head] = jnp.dot(turned, weight_ref[head], preferred_element_type=jnp.float32)

    in_stages(heads, [
        turn,
        score_stage(keys, across_ref, bias_ref, 0, scaled_ref, None),
        weight_stage(scaled_ref, weight_ref),
        mix,
    ])


def joined(head, peak, turned, weight_ref, peak_ref, sum_ref):
    added = jnp.dot(turned, weight_ref[head], preferred_element_type=jnp.float32)
    return sum_ref[head] * jnp.exp2(peak_ref[head:head + 1, :] - peak) + added


def next_kernel(
    at, across_ref, bias_ref, peak_ref, sum_ref, k_ref, v_ref, new_peak_ref, new_sum_ref,
    scaled_ref, weight_ref,
):
    turned = values_down(v_ref[...])

    def mix(head, peak):
        new_peak_ref[head:head + 1, :] = peak
        new_sum_ref[head] = joined(head, peak, turned, weight_ref, peak_ref, sum_ref)

    in_stages(across_ref.shape[0], [
        score_stage(
            k_ref[...], across_ref, bias_ref, at, scaled_ref,
            lambda head: peak_ref[head:head + 1, :],
        ),
        weight_stage(scaled_ref, weight_ref),
        mix,
    ])


def weights_kernel(
    at, across_ref, bias_ref, peak_ref, sum_ref, k_ref, new_sum_ref, weight_ref, scaled_ref,
):
    def rescale(head, peak):
        new_sum_ref[head] = sum_ref[head] * jnp.exp2(peak_ref[head:head + 1, :] - peak)

    in_stages(across_ref.shape[0], [
        score_stage(
            k_ref[...], across_ref, bias_ref, at, scaled_ref,
            lambda head: peak_ref[head:head + 1, :],
        ),
        weight_stage(scaled_ref, weight_ref),
        rescale,
    ])


def last_kernel(sum_ref, weight_ref, v_ref, out_ref, block_ref, sems):
    turned = values_down(v_ref[...])
    copies = []

    def mix(head, _):
        added = jnp.dot(turned, weight_ref[head], preferred_element_type=jnp.float32)
        summed = sum_ref[head] + added
        return summed[:HEAD_WIDTH] / summed[HEAD_WIDTH:HEAD_WIDTH + 1]

    def send(head, out):
        cols = slice(head * HEAD_WIDTH, (head + 1) * HEAD_WIDTH)
        block_ref[:, cols] = jnp.transpose(out).astype(jnp.bfloat16)
        copy = pltpu.make_async_copy(block_ref.at[:, cols], out_ref.at[:, cols], sems.at[head])
        copy.start()
        copies.append(copy)

    in_stages(sum_ref.shape[0], [mix, send])
    for copy in copies:
        copy.wait()


SHORT = pl.CostEstimate(flops=0, bytes_accessed=0, transcendentals=0)


def in_vmem(*arrays):
    return [pltpu.with_memory_space_constraint(array, pltpu.VMEM) for array in arrays]


def in_hbm(*arrays):
    return [pltpu.with_memory_space_constraint(array, pltpu.HBM) for array in arrays]


VMEM_REF = pl.BlockSpec(memory_space=pltpu.VMEM)
HBM_REF = pl.BlockSpec(memory_space=pltpu.HBM)
PARAMS = pltpu.CompilerParams(vmem_limit_bytes=32 << 20)


def moved(value, mask):
    return lax.ppermute(value, "seq", [(i, i ^ mask) for i in range(lax.axis_size("seq"))])


def staged_attention(queries, keys, values, lengths, old_place):
    far_values, far_keys = moved(values, 2), moved(keys, 2)
    near_keys, near_values = moved(keys, 1), moved(values, 1)
    third_keys = moved(keys, 3)
    rows, cols = queries.shape
    heads = cols // HEAD_WIDTH
    devices = lax.axis_size("seq")
    own = lax.axis_index("seq").astype(jnp.int32)
    places = old_place.reshape(1, -1)
    state = [
        pltpu.VMEM((heads, rows), jnp.float32),
        pltpu.VMEM((heads, HEAD_WIDTH + ONES, rows), jnp.float32),
    ]
    work = [
        pltpu.VMEM((heads, rows, rows), jnp.float32),
        pltpu.VMEM((heads, rows, rows), jnp.bfloat16),
    ]
    across, bias, *carried = pl.pallas_call(
        own_kernel,
        in_specs=[pl.BlockSpec(memory_space=pltpu.SMEM)] + [HBM_REF] * 5,
        out_specs=[VMEM_REF] * 4,
        out_shape=[
            pltpu.VMEM((heads, HEAD_WIDTH, rows), jnp.bfloat16),
            pltpu.VMEM((devices, rows, rows), jnp.float32),
        ] + state,
        scratch_shapes=[
            pltpu.SMEM(lengths.shape, jnp.int32),
            pltpu.VMEM(places.shape, jnp.int32),
            pltpu.VMEM(queries.shape, jnp.bfloat16),
            pltpu.VMEM(keys.shape, jnp.bfloat16),
            pltpu.VMEM(values.shape, jnp.bfloat16),
        ] + work + [pltpu.SemaphoreType.DMA((5,))],
        compiler_params=PARAMS,
        cost_estimate=SHORT,
        name="own_shard",
    )(own.reshape(1), *in_hbm(lengths, places, queries, keys, values))

    def add_shard(at, keys, values, carried):
        return pl.pallas_call(
            lambda *refs: next_kernel(at, *refs),
            in_specs=[VMEM_REF] * 6,
            out_specs=[VMEM_REF] * 2,
            out_shape=state,
            scratch_shapes=work,
            compiler_params=PARAMS,
            cost_estimate=SHORT,
            name="next_shard",
        )(*in_vmem(across, bias, *carried), keys, values)

    far_values, *carried = lax.optimization_barrier((far_values, *carried))
    third_values = moved(far_values, 1)
    carried = add_shard(2, far_keys, far_values, carried)
    carried = add_shard(1, near_keys, near_values, carried)
    summed, weights = pl.pallas_call(
        lambda *refs: weights_kernel(3, *refs),
        in_specs=[VMEM_REF] * 5,
        out_specs=[VMEM_REF] * 2,
        out_shape=state[1:] + work[1:],
        scratch_shapes=work[:1],
        compiler_params=PARAMS,
        cost_estimate=SHORT,
        name="last_weights",
    )(*in_vmem(across, bias, *carried), third_keys)
    return pl.pallas_call(
        last_kernel,
        in_specs=[VMEM_REF] * 3,
        out_specs=pl.BlockSpec(memory_space=pl.ANY),
        out_shape=jax.ShapeDtypeStruct((rows, cols), jnp.bfloat16),
        scratch_shapes=[
            pltpu.VMEM((rows, cols), jnp.bfloat16),
            pltpu.SemaphoreType.DMA((heads,)),
        ],
        compiler_params=PARAMS,
        cost_estimate=SHORT,
        name="last_values",
    )(*in_vmem(summed, weights), third_values)


def online_kernel(heads, q_ref, k_ref, v_ref, key_pos_ref, query_pos_ref, start_ref, out_ref, peak_ref, acc_ref):
    step = pl.program_id(0)

    @pl.when(step == 0)
    def _():
        peak_ref[...] = jnp.full(peak_ref.shape, NEG_FILL, jnp.float32)
        acc_ref[...] = jnp.zeros(acc_ref.shape, jnp.float32)

    key_pos = key_pos_ref[...]
    visible = (key_pos >= start_ref[...]) & (key_pos <= query_pos_ref[...])
    values = v_ref[...]
    ext = jnp.concatenate([values, jnp.ones_like(values)], axis=1)
    for head in range(heads):
        q = q_ref[:, head * HEAD_WIDTH:(head + 1) * HEAD_WIDTH]
        scores = lax.dot_general(
            q, k_ref[...], (((1,), (1,)), ((), ())), preferred_element_type=jnp.float32
        )
        scaled = jnp.where(visible, scores * (HEAD_WIDTH ** -0.5 * LOG2_E), NEG_FILL)
        before = peak_ref[head]
        peak = jnp.maximum(before, jnp.max(scaled, axis=1, keepdims=True))
        weights = jnp.where(visible, jnp.exp2(scaled - peak), 0.0).astype(jnp.bfloat16)
        peak_ref[head] = peak
        acc_ref[head] = acc_ref[head] * jnp.exp2(before - peak) + jnp.dot(
            weights, ext, preferred_element_type=jnp.float32
        )

    @pl.when(step == pl.num_programs(0) - 1)
    def _():
        for head in range(heads):
            acc = acc_ref[head]
            out_ref[:, head * HEAD_WIDTH:(head + 1) * HEAD_WIDTH] = (
                acc[:, :HEAD_WIDTH] / acc[:, HEAD_WIDTH:]
            ).astype(jnp.bfloat16)


def online_attention(queries, keys, values, key_pos, query_pos, starts, chunk):
    rows, cols = queries.shape
    heads = cols // HEAD_WIDTH
    key_count = keys.shape[0]
    return pl.pallas_call(
        lambda *refs: online_kernel(heads, *refs),
        grid=(key_count // chunk,),
        in_specs=[
            pl.BlockSpec((rows, cols), lambda j: (0, 0)),
            pl.BlockSpec((chunk, HEAD_WIDTH), lambda j: (j, 0)),
            pl.BlockSpec((chunk, HEAD_WIDTH), lambda j: (j, 0)),
            pl.BlockSpec((1, chunk), lambda j: (0, j)),
            pl.BlockSpec((rows, 1), lambda j: (0, 0)),
            pl.BlockSpec((rows, 1), lambda j: (0, 0)),
        ],
        out_specs=pl.BlockSpec((rows, cols), lambda j: (0, 0)),
        out_shape=jax.ShapeDtypeStruct((rows, cols), jnp.bfloat16),
        scratch_shapes=[
            pltpu.VMEM((heads, rows, 1), jnp.float32),
            pltpu.VMEM((heads, rows, 2 * HEAD_WIDTH), jnp.float32),
        ],
        compiler_params=pltpu.CompilerParams(vmem_limit_bytes=32 << 20),
        name="online",
    )(queries, keys, values, key_pos, query_pos, starts)


def body(queries, keys, values, lengths, old_place):
    devices = lax.axis_size("seq")
    row_count = queries.shape[0]
    key_count = row_count * devices
    if devices == 4 and key_count <= 1024:
        return staged_attention(queries, keys, values, lengths, old_place)
    all_keys = lax.all_gather(keys, "seq", axis=0, tiled=True)
    all_values = lax.all_gather(values, "seq", axis=0, tiled=True)
    key_pos, query_pos, starts = block_places(
        lengths, old_place, lax.axis_index("seq"), row_count, key_count
    )
    return online_attention(queries, all_keys, all_values, key_pos, query_pos, starts, 512)


def solution(mesh):
    in_specs = (
        P(("groups", "seq"), "mp"),
        P(("groups", "seq"), "mp"),
        P(("groups", "seq"), "mp"),
        P("groups"),
        P("groups"),
    )
    out_specs = P(("groups", "seq"), "mp")
    return jax.shard_map(body, mesh=mesh, in_specs=in_specs, out_specs=out_specs, check_vma=False)
```

```python
import jax
import jax.numpy as jnp
from jax import lax
from jax.experimental import pallas as pl
from jax.experimental.pallas import tpu as pltpu
from jax.sharding import PartitionSpec as P

HEAD_WIDTH = 128
LOG2_E = 1.4426950408889634
NEG_FILL = -1e30
ONES = 16


def block_places(lengths, old_place, own_index, row_count, key_count):
    block_total = old_place.shape[0]
    block_rows = key_count // block_total
    ids = jnp.arange(block_total, dtype=jnp.int32)
    hit = old_place[:, None] == ids[None, :]
    new_block = jnp.sum(jnp.where(hit, ids[:, None], 0), axis=0)
    key_pos = (new_block[:, None] * block_rows + jnp.arange(block_rows, dtype=jnp.int32)).reshape(-1)
    query_pos = lax.dynamic_slice_in_dim(key_pos, own_index * row_count, row_count)
    bounds = jnp.cumsum(lengths)
    starts = jnp.max(jnp.where(bounds[None, :] <= query_pos[:, None], bounds[None, :], 0), axis=1)
    return key_pos.reshape(1, -1), query_pos.reshape(-1, 1), starts.reshape(-1, 1)


def iota(shape, dim):
    return lax.broadcasted_iota(jnp.int32, shape, dim)


def mask_tables(owners, lengths_ref, places_ref, rows, bias_ref):
    block_total = places_ref.shape[1]
    block_rows = rows * lax.axis_size("seq") // block_total
    blocks = rows // block_rows
    places = places_ref[...]
    square = (block_total, block_total)
    as_column = jnp.sum(
        jnp.where(iota(square, 0) == iota(square, 1), places, 0).astype(jnp.float32),
        axis=1, keepdims=True,
    ).astype(jnp.int32)
    across = (block_total, rows)
    hit = as_column == owners[0] * blocks + iota(across, 1) // block_rows
    at = jnp.where(hit, iota(across, 0) * block_rows, 0).astype(jnp.float32)
    query_pos = jnp.sum(at, axis=0, keepdims=True) + (
        iota((1, rows), 1) % block_rows
    ).astype(jnp.float32)
    starts = jnp.zeros_like(query_pos)
    bound = jnp.int32(0)
    for t in range(lengths_ref.shape[0]):
        bound = bound + lengths_ref[t]
        edge = bound.astype(jnp.float32)
        starts = jnp.where(edge <= query_pos, edge, starts)
    down = (rows, block_total)
    for n, owner in enumerate(owners):
        hit = places == owner * blocks + iota(down, 0) // block_rows
        at = jnp.where(hit, iota(down, 1) * block_rows, 0).astype(jnp.float32)
        key_pos = jnp.sum(at, axis=1, keepdims=True) + (
            iota((rows, 1), 0) % block_rows
        ).astype(jnp.float32)
        visible = (key_pos >= starts) & (key_pos <= query_pos)
        bias_ref[n] = jnp.where(visible, 0.0, NEG_FILL)


def values_down(values):
    turned = jnp.transpose(values.astype(jnp.float32)).astype(jnp.bfloat16)
    return jnp.concatenate([turned, jnp.ones((ONES, values.shape[0]), jnp.bfloat16)], axis=0)


def in_stages(heads, stages):
    results = [{} for _ in stages]
    for step in range(heads + len(stages) - 1):
        for late, stage in enumerate(stages):
            head = step - late
            if 0 <= head < heads:
                before = results[late - 1].pop(head) if late else None
                results[late][head] = stage(head, before)


def score_stage(keys, across_ref, bias_ref, at, scaled_ref, old_peak):
    def stage(head, _):
        scores = jnp.dot(keys, across_ref[head], preferred_element_type=jnp.float32)
        scaled = scores * (HEAD_WIDTH ** -0.5 * LOG2_E) + bias_ref[at]
        scaled_ref[head] = scaled
        peak = jnp.max(scaled, axis=0, keepdims=True)
        return peak if old_peak is None else jnp.maximum(old_peak(head), peak)

    return stage


def weight_stage(scaled_ref, weight_ref):
    def stage(head, peak):
        weight_ref[head] = jnp.exp2(scaled_ref[head] - peak).astype(jnp.bfloat16)
        return peak

    return stage


def own_kernel(
    own_ref, lengths_hbm, places_hbm, q_hbm, k_hbm, v_hbm,
    across_ref, bias_ref, peak_ref, sum_ref,
    lengths_ref, places_ref, q_ref, k_ref, v_ref, scaled_ref, weight_ref, sems,
):
    moves = (
        (lengths_hbm, lengths_ref), (places_hbm, places_ref),
        (k_hbm, k_ref), (v_hbm, v_ref), (q_hbm, q_ref),
    )
    copies = [pltpu.make_async_copy(*move, sems.at[n]) for n, move in enumerate(moves)]
    for copy in copies:
        copy.start()
    copies[0].wait()
    copies[1].wait()
    heads, _, rows = across_ref.shape
    owners = [own_ref[0] ^ mask for mask in range(bias_ref.shape[0])]
    mask_tables(owners, lengths_ref, places_ref, rows, bias_ref)
    for copy in copies[2:]:
        copy.wait()
    keys = k_ref[...]
    turned = values_down(v_ref[...])

    def turn(head, _):
        q = q_ref[:, head * HEAD_WIDTH:(head + 1) * HEAD_WIDTH]
        across_ref[head] = jnp.transpose(q.astype(jnp.float32)).astype(jnp.bfloat16)

    def mix(head, peak):
        peak_ref[head:head + 1, :] = peak
        sum_ref[head] = jnp.dot(turned, weight_ref[head], preferred_element_type=jnp.float32)

    in_stages(heads, [
        turn,
        score_stage(keys, across_ref, bias_ref, 0, scaled_ref, None),
        weight_stage(scaled_ref, weight_ref),
        mix,
    ])


def joined(head, peak, turned, weight_ref, peak_ref, sum_ref):
    added = jnp.dot(turned, weight_ref[head], preferred_element_type=jnp.float32)
    return sum_ref[head] * jnp.exp2(peak_ref[head:head + 1, :] - peak) + added


def next_kernel(
    at, across_ref, bias_ref, peak_ref, sum_ref, k_ref, v_ref, new_peak_ref, new_sum_ref,
    scaled_ref, weight_ref,
):
    turned = values_down(v_ref[...])

    def mix(head, peak):
        new_peak_ref[head:head + 1, :] = peak
        new_sum_ref[head] = joined(head, peak, turned, weight_ref, peak_ref, sum_ref)

    in_stages(across_ref.shape[0], [
        score_stage(
            k_ref[...], across_ref, bias_ref, at, scaled_ref,
            lambda head: peak_ref[head:head + 1, :],
        ),
        weight_stage(scaled_ref, weight_ref),
        mix,
    ])


def weights_kernel(
    at, across_ref, bias_ref, peak_ref, sum_ref, k_ref, new_sum_ref, weight_ref, scaled_ref,
):
    def rescale(head, peak):
        new_sum_ref[head] = sum_ref[head] * jnp.exp2(peak_ref[head:head + 1, :] - peak)

    in_stages(across_ref.shape[0], [
        score_stage(
            k_ref[...], across_ref, bias_ref, at, scaled_ref,
            lambda head: peak_ref[head:head + 1, :],
        ),
        weight_stage(scaled_ref, weight_ref),
        rescale,
    ])


def last_kernel(sum_ref, weight_ref, v_ref, out_ref, block_ref, sems):
    turned = values_down(v_ref[...])
    copies = []

    def mix(head, _):
        added = jnp.dot(turned, weight_ref[head], preferred_element_type=jnp.float32)
        summed = sum_ref[head] + added
        return summed[:HEAD_WIDTH] / summed[HEAD_WIDTH:HEAD_WIDTH + 1]

    def send(head, out):
        cols = slice(head * HEAD_WIDTH, (head + 1) * HEAD_WIDTH)
        block_ref[:, cols] = jnp.transpose(out).astype(jnp.bfloat16)
        copy = pltpu.make_async_copy(block_ref.at[:, cols], out_ref.at[:, cols], sems.at[head])
        copy.start()
        copies.append(copy)

    in_stages(sum_ref.shape[0], [mix, send])
    for copy in copies:
        copy.wait()


SHORT = pl.CostEstimate(flops=0, bytes_accessed=0, transcendentals=0)


def in_vmem(*arrays):
    return [pltpu.with_memory_space_constraint(array, pltpu.VMEM) for array in arrays]


def in_hbm(*arrays):
    return [pltpu.with_memory_space_constraint(array, pltpu.HBM) for array in arrays]


VMEM_REF = pl.BlockSpec(memory_space=pltpu.VMEM)
HBM_REF = pl.BlockSpec(memory_space=pltpu.HBM)
PARAMS = pltpu.CompilerParams(vmem_limit_bytes=32 << 20)


def moved(value, mask):
    return lax.ppermute(value, "seq", [(i, i ^ mask) for i in range(lax.axis_size("seq"))])


def staged_attention(queries, keys, values, lengths, old_place):
    (far_keys, far_values), (near_keys, near_values), (third_keys, third_values) = (
        (moved(keys, mask), moved(values, mask)) for mask in (2, 1, 3)
    )
    rows, cols = queries.shape
    heads = cols // HEAD_WIDTH
    devices = lax.axis_size("seq")
    own = lax.axis_index("seq").astype(jnp.int32)
    places = old_place.reshape(1, -1)
    state = [
        pltpu.VMEM((heads, rows), jnp.float32),
        pltpu.VMEM((heads, HEAD_WIDTH + ONES, rows), jnp.float32),
    ]
    work = [
        pltpu.VMEM((heads, rows, rows), jnp.float32),
        pltpu.VMEM((heads, rows, rows), jnp.bfloat16),
    ]
    across, bias, *carried = pl.pallas_call(
        own_kernel,
        in_specs=[pl.BlockSpec(memory_space=pltpu.SMEM)] + [HBM_REF] * 5,
        out_specs=[VMEM_REF] * 4,
        out_shape=[
            pltpu.VMEM((heads, HEAD_WIDTH, rows), jnp.bfloat16),
            pltpu.VMEM((devices, rows, rows), jnp.float32),
        ] + state,
        scratch_shapes=[
            pltpu.SMEM(lengths.shape, jnp.int32),
            pltpu.VMEM(places.shape, jnp.int32),
            pltpu.VMEM(queries.shape, jnp.bfloat16),
            pltpu.VMEM(keys.shape, jnp.bfloat16),
            pltpu.VMEM(values.shape, jnp.bfloat16),
        ] + work + [pltpu.SemaphoreType.DMA((5,))],
        compiler_params=PARAMS,
        cost_estimate=SHORT,
        name="own_shard",
    )(own.reshape(1), *in_hbm(lengths, places, queries, keys, values))

    def add_shard(at, keys, values, carried):
        return pl.pallas_call(
            lambda *refs: next_kernel(at, *refs),
            in_specs=[VMEM_REF] * 6,
            out_specs=[VMEM_REF] * 2,
            out_shape=state,
            scratch_shapes=work,
            compiler_params=PARAMS,
            cost_estimate=SHORT,
            name="next_shard",
        )(*in_vmem(across, bias, *carried), keys, values)

    carried = add_shard(2, far_keys, far_values, carried)
    carried = add_shard(1, near_keys, near_values, carried)
    summed, weights = pl.pallas_call(
        lambda *refs: weights_kernel(3, *refs),
        in_specs=[VMEM_REF] * 5,
        out_specs=[VMEM_REF] * 2,
        out_shape=state[1:] + work[1:],
        scratch_shapes=work[:1],
        compiler_params=PARAMS,
        cost_estimate=SHORT,
        name="last_weights",
    )(*in_vmem(across, bias, *carried), third_keys)
    return pl.pallas_call(
        last_kernel,
        in_specs=[VMEM_REF] * 3,
        out_specs=pl.BlockSpec(memory_space=pl.ANY),
        out_shape=jax.ShapeDtypeStruct((rows, cols), jnp.bfloat16),
        scratch_shapes=[
            pltpu.VMEM((rows, cols), jnp.bfloat16),
            pltpu.SemaphoreType.DMA((heads,)),
        ],
        compiler_params=PARAMS,
        cost_estimate=SHORT,
        name="last_values",
    )(*in_vmem(summed, weights), third_values)


def online_kernel(heads, q_ref, k_ref, v_ref, key_pos_ref, query_pos_ref, start_ref, out_ref, peak_ref, acc_ref):
    step = pl.program_id(0)

    @pl.when(step == 0)
    def _():
        peak_ref[...] = jnp.full(peak_ref.shape, NEG_FILL, jnp.float32)
        acc_ref[...] = jnp.zeros(acc_ref.shape, jnp.float32)

    key_pos = key_pos_ref[...]
    visible = (key_pos >= start_ref[...]) & (key_pos <= query_pos_ref[...])
    values = v_ref[...]
    ext = jnp.concatenate([values, jnp.ones_like(values)], axis=1)
    for head in range(heads):
        q = q_ref[:, head * HEAD_WIDTH:(head + 1) * HEAD_WIDTH]
        scores = lax.dot_general(
            q, k_ref[...], (((1,), (1,)), ((), ())), preferred_element_type=jnp.float32
        )
        scaled = jnp.where(visible, scores * (HEAD_WIDTH ** -0.5 * LOG2_E), NEG_FILL)
        before = peak_ref[head]
        peak = jnp.maximum(before, jnp.max(scaled, axis=1, keepdims=True))
        weights = jnp.where(visible, jnp.exp2(scaled - peak), 0.0).astype(jnp.bfloat16)
        peak_ref[head] = peak
        acc_ref[head] = acc_ref[head] * jnp.exp2(before - peak) + jnp.dot(
            weights, ext, preferred_element_type=jnp.float32
        )

    @pl.when(step == pl.num_programs(0) - 1)
    def _():
        for head in range(heads):
            acc = acc_ref[head]
            out_ref[:, head * HEAD_WIDTH:(head + 1) * HEAD_WIDTH] = (
                acc[:, :HEAD_WIDTH] / acc[:, HEAD_WIDTH:]
            ).astype(jnp.bfloat16)


def online_attention(queries, keys, values, key_pos, query_pos, starts, chunk):
    rows, cols = queries.shape
    heads = cols // HEAD_WIDTH
    key_count = keys.shape[0]
    return pl.pallas_call(
        lambda *refs: online_kernel(heads, *refs),
        grid=(key_count // chunk,),
        in_specs=[
            pl.BlockSpec((rows, cols), lambda j: (0, 0)),
            pl.BlockSpec((chunk, HEAD_WIDTH), lambda j: (j, 0)),
            pl.BlockSpec((chunk, HEAD_WIDTH), lambda j: (j, 0)),
            pl.BlockSpec((1, chunk), lambda j: (0, j)),
            pl.BlockSpec((rows, 1), lambda j: (0, 0)),
            pl.BlockSpec((rows, 1), lambda j: (0, 0)),
        ],
        out_specs=pl.BlockSpec((rows, cols), lambda j: (0, 0)),
        out_shape=jax.ShapeDtypeStruct((rows, cols), jnp.bfloat16),
        scratch_shapes=[
            pltpu.VMEM((heads, rows, 1), jnp.float32),
            pltpu.VMEM((heads, rows, 2 * HEAD_WIDTH), jnp.float32),
        ],
        compiler_params=pltpu.CompilerParams(vmem_limit_bytes=32 << 20),
        name="online",
    )(queries, keys, values, key_pos, query_pos, starts)


def body(queries, keys, values, lengths, old_place):
    devices = lax.axis_size("seq")
    row_count = queries.shape[0]
    key_count = row_count * devices
    if devices == 4 and key_count <= 1024:
        return staged_attention(queries, keys, values, lengths, old_place)
    all_keys = lax.all_gather(keys, "seq", axis=0, tiled=True)
    all_values = lax.all_gather(values, "seq", axis=0, tiled=True)
    key_pos, query_pos, starts = block_places(
        lengths, old_place, lax.axis_index("seq"), row_count, key_count
    )
    return online_attention(queries, all_keys, all_values, key_pos, query_pos, starts, 512)


def solution(mesh):
    in_specs = (
        P(("groups", "seq"), "mp"),
        P(("groups", "seq"), "mp"),
        P(("groups", "seq"), "mp"),
        P("groups"),
        P("groups"),
    )
    out_specs = P(("groups", "seq"), "mp")
    return jax.shard_map(body, mesh=mesh, in_specs=in_specs, out_specs=out_specs, check_vma=False)
```

```python
import jax
import jax.numpy as jnp
from jax import lax
from jax.experimental import pallas as pl
from jax.experimental.pallas import tpu as pltpu
from jax.sharding import PartitionSpec as P

HEAD_WIDTH = 128
LOG2_E = 1.4426950408889634
NEG_FILL = -1e30
ONES = 16


def block_places(lengths, old_place, own_index, row_count, key_count):
    block_total = old_place.shape[0]
    block_rows = key_count // block_total
    ids = jnp.arange(block_total, dtype=jnp.int32)
    hit = old_place[:, None] == ids[None, :]
    new_block = jnp.sum(jnp.where(hit, ids[:, None], 0), axis=0)
    key_pos = (new_block[:, None] * block_rows + jnp.arange(block_rows, dtype=jnp.int32)).reshape(-1)
    query_pos = lax.dynamic_slice_in_dim(key_pos, own_index * row_count, row_count)
    bounds = jnp.cumsum(lengths)
    starts = jnp.max(jnp.where(bounds[None, :] <= query_pos[:, None], bounds[None, :], 0), axis=1)
    return key_pos.reshape(1, -1), query_pos.reshape(-1, 1), starts.reshape(-1, 1)


def iota(shape, dim):
    return lax.broadcasted_iota(jnp.int32, shape, dim)


def row_sum_as_column(places):
    square = (places.shape[1],) * 2
    spread = jnp.where(iota(square, 0) == iota(square, 1), places, 0).astype(jnp.float32)
    return jnp.sum(spread, axis=1, keepdims=True).astype(jnp.int32)


def query_places(own, lengths_ref, places, rows):
    block_total = places.shape[1]
    block_rows = rows * lax.axis_size("seq") // block_total
    shape = (block_total, rows)
    hit = row_sum_as_column(places) == own * (rows // block_rows) + iota(shape, 1) // block_rows
    at = jnp.where(hit, iota(shape, 0) * block_rows, 0).astype(jnp.float32)
    query_pos = jnp.sum(at, axis=0, keepdims=True) + (
        iota((1, rows), 1) % block_rows
    ).astype(jnp.float32)
    starts = jnp.zeros_like(query_pos)
    bound = jnp.int32(0)
    for t in range(lengths_ref.shape[0]):
        bound = bound + lengths_ref[t]
        edge = bound.astype(jnp.float32)
        starts = jnp.where(edge <= query_pos, edge, starts)
    return query_pos, starts


def mask_table(owner, query_pos, starts, places):
    block_total, rows = places.shape[1], query_pos.shape[1]
    block_rows = rows * lax.axis_size("seq") // block_total
    shape = (rows, block_total)
    hit = places == owner * (rows // block_rows) + iota(shape, 0) // block_rows
    at = jnp.where(hit, iota(shape, 1) * block_rows, 0).astype(jnp.float32)
    key_pos = jnp.sum(at, axis=1, keepdims=True) + (
        iota((rows, 1), 0) % block_rows
    ).astype(jnp.float32)
    return jnp.where((key_pos >= starts) & (key_pos <= query_pos), 0.0, NEG_FILL)


def values_down(values):
    turned = jnp.transpose(values)
    return jnp.concatenate([turned, jnp.ones((ONES, values.shape[0]), jnp.bfloat16)], axis=0)


def in_stages(heads, stages):
    results = [{} for _ in stages]
    for step in range(heads + len(stages) - 1):
        for late, stage in enumerate(stages):
            head = step - late
            if 0 <= head < heads:
                before = results[late - 1].pop(head) if late else None
                results[late][head] = stage(head, before)


def score_stage(keys, across_ref, bias_ref, at, scaled_ref, old_peak):
    def stage(head, _):
        scores = jnp.dot(keys, across_ref[head], preferred_element_type=jnp.float32)
        scaled = scores * (HEAD_WIDTH ** -0.5 * LOG2_E) + bias_ref[at]
        scaled_ref[head] = scaled
        peak = jnp.max(scaled, axis=0, keepdims=True)
        return peak if old_peak is None else jnp.maximum(old_peak(head), peak)

    return stage


def weight_stage(scaled_ref, weight_ref):
    def stage(head, peak):
        weight_ref[head] = jnp.exp2(scaled_ref[head] - peak).astype(jnp.bfloat16)
        return peak

    return stage


def own_kernel(
    own_ref, lengths_hbm, places_hbm, q_hbm, k_hbm, v_hbm,
    across_ref, bias_ref, peak_ref, sum_ref,
    lengths_ref, places_ref, q_ref, k_ref, v_ref, scaled_ref, weight_ref, sems,
):
    moves = (
        (lengths_hbm, lengths_ref), (places_hbm, places_ref),
        (k_hbm, k_ref), (v_hbm, v_ref), (q_hbm, q_ref),
    )
    copies = [pltpu.make_async_copy(*move, sems.at[n]) for n, move in enumerate(moves)]
    for copy in copies:
        copy.start()
    for copy in copies:
        copy.wait()
    heads, _, rows = across_ref.shape
    own, places = own_ref[0], places_ref[...]
    keys = k_ref[...]
    query_pos, starts = query_places(own, lengths_ref, places, rows)
    bias_ref[0] = mask_table(own, query_pos, starts, places)
    turned = values_down(v_ref[...])

    def turn(head, _):
        q = q_ref[:, head * HEAD_WIDTH:(head + 1) * HEAD_WIDTH]
        across_ref[head] = jnp.transpose(q)
        if 0 < head < bias_ref.shape[0]:
            bias_ref[head] = mask_table(own ^ head, query_pos, starts, places)

    def mix(head, peak):
        peak_ref[head:head + 1, :] = peak
        sum_ref[head] = jnp.dot(turned, weight_ref[head], preferred_element_type=jnp.float32)

    in_stages(heads, [
        turn,
        score_stage(keys, across_ref, bias_ref, 0, scaled_ref, None),
        weight_stage(scaled_ref, weight_ref),
        mix,
    ])


def joined(head, peak, turned, weight_ref, peak_ref, sum_ref):
    added = jnp.dot(turned, weight_ref[head], preferred_element_type=jnp.float32)
    return sum_ref[head] * jnp.exp2(peak_ref[head:head + 1, :] - peak) + added


def next_kernel(
    at, across_ref, bias_ref, peak_ref, sum_ref, k_ref, v_ref, new_peak_ref, new_sum_ref,
    scaled_ref, weight_ref,
):
    turned = values_down(v_ref[...])

    def mix(head, peak):
        new_peak_ref[head:head + 1, :] = peak
        new_sum_ref[head] = joined(head, peak, turned, weight_ref, peak_ref, sum_ref)

    in_stages(across_ref.shape[0], [
        score_stage(
            k_ref[...], across_ref, bias_ref, at, scaled_ref,
            lambda head: peak_ref[head:head + 1, :],
        ),
        weight_stage(scaled_ref, weight_ref),
        mix,
    ])


def weights_kernel(
    at, across_ref, bias_ref, peak_ref, sum_ref, k_ref,
    new_sum_ref, weight_ref, share_ref, scaled_ref,
):
    ones = jnp.ones((ONES, k_ref.shape[0]), jnp.bfloat16)

    def rescale(head, peak):
        factor = jnp.exp2(peak_ref[head:head + 1, :] - peak)
        added = jnp.dot(ones, weight_ref[head], preferred_element_type=jnp.float32)
        total = sum_ref[head, HEAD_WIDTH:HEAD_WIDTH + 1, :] * factor + added[:1]
        share = 1.0 / total
        share_ref[head:head + 1, :] = share
        new_sum_ref[head] = sum_ref[head, :HEAD_WIDTH, :] * (factor * share)

    in_stages(across_ref.shape[0], [
        score_stage(
            k_ref[...], across_ref, bias_ref, at, scaled_ref,
            lambda head: peak_ref[head:head + 1, :],
        ),
        weight_stage(scaled_ref, weight_ref),
        rescale,
    ])


def last_kernel(sum_ref, weight_ref, share_ref, v_ref, out_ref, block_ref, sems):
    turned = jnp.transpose(v_ref[...])
    copies = []

    def mix(head, _):
        added = jnp.dot(turned, weight_ref[head], preferred_element_type=jnp.float32)
        return (sum_ref[head] + added * share_ref[head:head + 1, :]).astype(jnp.bfloat16)

    def send(head, out):
        cols = slice(head * HEAD_WIDTH, (head + 1) * HEAD_WIDTH)
        block_ref[:, cols] = jnp.transpose(out)
        copy = pltpu.make_async_copy(block_ref.at[:, cols], out_ref.at[:, cols], sems.at[head])
        copy.start()
        copies.append(copy)

    in_stages(sum_ref.shape[0], [mix, send])
    for copy in copies:
        copy.wait()


SHORT = pl.CostEstimate(flops=0, bytes_accessed=0, transcendentals=0)


def in_vmem(*arrays):
    return [pltpu.with_memory_space_constraint(array, pltpu.VMEM) for array in arrays]


def in_hbm(*arrays):
    return [pltpu.with_memory_space_constraint(array, pltpu.HBM) for array in arrays]


VMEM_REF = pl.BlockSpec(memory_space=pltpu.VMEM)
HBM_REF = pl.BlockSpec(memory_space=pltpu.HBM)
PARAMS = pltpu.CompilerParams(vmem_limit_bytes=32 << 20)


def moved(value, mask):
    return lax.ppermute(value, "seq", [(i, i ^ mask) for i in range(lax.axis_size("seq"))])


def staged_attention(queries, keys, values, lengths, old_place):
    far_keys, far_values = moved(keys, 2), moved(values, 2)
    near_keys, near_values = moved(keys, 1), moved(values, 1)
    rows, cols = queries.shape
    heads = cols // HEAD_WIDTH
    devices = lax.axis_size("seq")
    own = lax.axis_index("seq").astype(jnp.int32)
    places = old_place.reshape(1, -1)
    state = [
        pltpu.VMEM((heads, rows), jnp.float32),
        pltpu.VMEM((heads, HEAD_WIDTH + ONES, rows), jnp.float32),
    ]
    work = [
        pltpu.VMEM((heads, rows, rows), jnp.float32),
        pltpu.VMEM((heads, rows, rows), jnp.bfloat16),
    ]
    across, bias, *carried = pl.pallas_call(
        own_kernel,
        in_specs=[pl.BlockSpec(memory_space=pltpu.SMEM)] + [HBM_REF] * 5,
        out_specs=[VMEM_REF] * 4,
        out_shape=[
            pltpu.VMEM((heads, HEAD_WIDTH, rows), jnp.bfloat16),
            pltpu.VMEM((devices, rows, rows), jnp.float32),
        ] + state,
        scratch_shapes=[
            pltpu.SMEM(lengths.shape, jnp.int32),
            pltpu.VMEM(places.shape, jnp.int32),
            pltpu.VMEM(queries.shape, jnp.bfloat16),
            pltpu.VMEM(keys.shape, jnp.bfloat16),
            pltpu.VMEM(values.shape, jnp.bfloat16),
        ] + work + [pltpu.SemaphoreType.DMA((5,))],
        compiler_params=PARAMS,
        cost_estimate=SHORT,
        name="own_shard",
    )(own.reshape(1), *in_hbm(lengths, places, queries, keys, values))

    def add_shard(at, keys, values, carried):
        return pl.pallas_call(
            lambda *refs: next_kernel(at, *refs),
            in_specs=[VMEM_REF] * 6,
            out_specs=[VMEM_REF] * 2,
            out_shape=state,
            scratch_shapes=work,
            compiler_params=PARAMS,
            cost_estimate=SHORT,
            name="next_shard",
        )(*in_vmem(across, bias, *carried), keys, values)

    far_keys, *carried = lax.optimization_barrier((far_keys, *carried))
    third_keys = moved(far_keys, 1)
    far_values, *carried = lax.optimization_barrier((far_values, *carried))
    third_values = moved(far_values, 1)
    carried = add_shard(2, far_keys, far_values, carried)
    carried = add_shard(1, near_keys, near_values, carried)
    scaled_sum = pltpu.VMEM((heads, HEAD_WIDTH, rows), jnp.float32)
    last = pl.pallas_call(
        lambda *refs: weights_kernel(3, *refs),
        in_specs=[VMEM_REF] * 5,
        out_specs=[VMEM_REF] * 3,
        out_shape=[scaled_sum, work[1], state[0]],
        scratch_shapes=work[:1],
        compiler_params=PARAMS,
        cost_estimate=SHORT,
        name="last_weights",
    )(*in_vmem(across, bias, *carried), third_keys)
    return pl.pallas_call(
        last_kernel,
        in_specs=[VMEM_REF] * 4,
        out_specs=pl.BlockSpec(memory_space=pl.ANY),
        out_shape=jax.ShapeDtypeStruct((rows, cols), jnp.bfloat16),
        scratch_shapes=[
            pltpu.VMEM((rows, cols), jnp.bfloat16),
            pltpu.SemaphoreType.DMA((heads,)),
        ],
        compiler_params=PARAMS,
        cost_estimate=SHORT,
        name="last_values",
    )(*in_vmem(*last), third_values)


def online_kernel(heads, q_ref, k_ref, v_ref, key_pos_ref, query_pos_ref, start_ref, out_ref, peak_ref, acc_ref):
    step = pl.program_id(0)

    @pl.when(step == 0)
    def _():
        peak_ref[...] = jnp.full(peak_ref.shape, NEG_FILL, jnp.float32)
        acc_ref[...] = jnp.zeros(acc_ref.shape, jnp.float32)

    key_pos = key_pos_ref[...]
    visible = (key_pos >= start_ref[...]) & (key_pos <= query_pos_ref[...])
    values = v_ref[...]
    ext = jnp.concatenate([values, jnp.ones_like(values)], axis=1)
    for head in range(heads):
        q = q_ref[:, head * HEAD_WIDTH:(head + 1) * HEAD_WIDTH]
        scores = lax.dot_general(
            q, k_ref[...], (((1,), (1,)), ((), ())), preferred_element_type=jnp.float32
        )
        scaled = jnp.where(visible, scores * (HEAD_WIDTH ** -0.5 * LOG2_E), NEG_FILL)
        before = peak_ref[head]
        peak = jnp.maximum(before, jnp.max(scaled, axis=1, keepdims=True))
        weights = jnp.where(visible, jnp.exp2(scaled - peak), 0.0).astype(jnp.bfloat16)
        peak_ref[head] = peak
        acc_ref[head] = acc_ref[head] * jnp.exp2(before - peak) + jnp.dot(
            weights, ext, preferred_element_type=jnp.float32
        )

    @pl.when(step == pl.num_programs(0) - 1)
    def _():
        for head in range(heads):
            acc = acc_ref[head]
            out_ref[:, head * HEAD_WIDTH:(head + 1) * HEAD_WIDTH] = (
                acc[:, :HEAD_WIDTH] / acc[:, HEAD_WIDTH:]
            ).astype(jnp.bfloat16)


def online_attention(queries, keys, values, key_pos, query_pos, starts, chunk):
    rows, cols = queries.shape
    heads = cols // HEAD_WIDTH
    key_count = keys.shape[0]
    return pl.pallas_call(
        lambda *refs: online_kernel(heads, *refs),
        grid=(key_count // chunk,),
        in_specs=[
            pl.BlockSpec((rows, cols), lambda j: (0, 0)),
            pl.BlockSpec((chunk, HEAD_WIDTH), lambda j: (j, 0)),
            pl.BlockSpec((chunk, HEAD_WIDTH), lambda j: (j, 0)),
            pl.BlockSpec((1, chunk), lambda j: (0, j)),
            pl.BlockSpec((rows, 1), lambda j: (0, 0)),
            pl.BlockSpec((rows, 1), lambda j: (0, 0)),
        ],
        out_specs=pl.BlockSpec((rows, cols), lambda j: (0, 0)),
        out_shape=jax.ShapeDtypeStruct((rows, cols), jnp.bfloat16),
        scratch_shapes=[
            pltpu.VMEM((heads, rows, 1), jnp.float32),
            pltpu.VMEM((heads, rows, 2 * HEAD_WIDTH), jnp.float32),
        ],
        compiler_params=pltpu.CompilerParams(vmem_limit_bytes=32 << 20),
        name="online",
    )(queries, keys, values, key_pos, query_pos, starts)


def body(queries, keys, values, lengths, old_place):
    devices = lax.axis_size("seq")
    row_count = queries.shape[0]
    key_count = row_count * devices
    if devices == 4 and key_count <= 1024:
        return staged_attention(queries, keys, values, lengths, old_place)
    all_keys = lax.all_gather(keys, "seq", axis=0, tiled=True)
    all_values = lax.all_gather(values, "seq", axis=0, tiled=True)
    key_pos, query_pos, starts = block_places(
        lengths, old_place, lax.axis_index("seq"), row_count, key_count
    )
    return online_attention(queries, all_keys, all_values, key_pos, query_pos, starts, 512)


def solution(mesh):
    in_specs = (
        P(("groups", "seq"), "mp"),
        P(("groups", "seq"), "mp"),
        P(("groups", "seq"), "mp"),
        P("groups"),
        P("groups"),
    )
    out_specs = P(("groups", "seq"), "mp")
    return jax.shard_map(body, mesh=mesh, in_specs=in_specs, out_specs=out_specs, check_vma=False)
```

```python
import jax
import jax.numpy as jnp
from jax import lax
from jax.experimental import pallas as pl
from jax.experimental.pallas import tpu as pltpu
from jax.sharding import PartitionSpec as P

HEAD_WIDTH = 128
LOG2_E = 1.4426950408889634
NEG_FILL = -1e30
ONES = 16


def block_places(lengths, old_place, own_index, row_count, key_count):
    block_total = old_place.shape[0]
    block_rows = key_count // block_total
    ids = jnp.arange(block_total, dtype=jnp.int32)
    hit = old_place[:, None] == ids[None, :]
    new_block = jnp.sum(jnp.where(hit, ids[:, None], 0), axis=0)
    key_pos = (new_block[:, None] * block_rows + jnp.arange(block_rows, dtype=jnp.int32)).reshape(-1)
    query_pos = lax.dynamic_slice_in_dim(key_pos, own_index * row_count, row_count)
    bounds = jnp.cumsum(lengths)
    starts = jnp.max(jnp.where(bounds[None, :] <= query_pos[:, None], bounds[None, :], 0), axis=1)
    return key_pos.reshape(1, -1), query_pos.reshape(-1, 1), starts.reshape(-1, 1)


def iota(shape, dim):
    return lax.broadcasted_iota(jnp.int32, shape, dim)


def row_sum_as_column(places):
    square = (places.shape[1],) * 2
    spread = jnp.where(iota(square, 0) == iota(square, 1), places, 0).astype(jnp.float32)
    return jnp.sum(spread, axis=1, keepdims=True).astype(jnp.int32)


def query_places(own, lengths_ref, places, rows):
    block_total = places.shape[1]
    block_rows = rows * lax.axis_size("seq") // block_total
    shape = (block_total, rows)
    hit = row_sum_as_column(places) == own * (rows // block_rows) + iota(shape, 1) // block_rows
    at = jnp.where(hit, iota(shape, 0) * block_rows, 0).astype(jnp.float32)
    query_pos = jnp.sum(at, axis=0, keepdims=True) + (
        iota((1, rows), 1) % block_rows
    ).astype(jnp.float32)
    starts = jnp.zeros_like(query_pos)
    bound = jnp.int32(0)
    for t in range(lengths_ref.shape[0]):
        bound = bound + lengths_ref[t]
        edge = bound.astype(jnp.float32)
        starts = jnp.where(edge <= query_pos, edge, starts)
    return query_pos, starts


def mask_table(owner, query_pos, starts, places):
    block_total, rows = places.shape[1], query_pos.shape[1]
    block_rows = rows * lax.axis_size("seq") // block_total
    shape = (rows, block_total)
    hit = places == owner * (rows // block_rows) + iota(shape, 0) // block_rows
    at = jnp.where(hit, iota(shape, 1) * block_rows, 0).astype(jnp.float32)
    key_pos = jnp.sum(at, axis=1, keepdims=True) + (
        iota((rows, 1), 0) % block_rows
    ).astype(jnp.float32)
    return jnp.where((key_pos >= starts) & (key_pos <= query_pos), 0.0, NEG_FILL)


def values_down(values):
    turned = jnp.transpose(values)
    return jnp.concatenate([turned, jnp.ones((ONES, values.shape[0]), jnp.bfloat16)], axis=0)


def in_stages(heads, stages):
    results = [{} for _ in stages]
    for step in range(heads + len(stages) - 1):
        for late, stage in enumerate(stages):
            head = step - late
            if 0 <= head < heads:
                before = results[late - 1].pop(head) if late else None
                results[late][head] = stage(head, before)


def score_stage(keys, across_ref, bias_ref, at, scaled_ref, old_peak):
    def stage(head, _):
        scores = jnp.dot(keys, across_ref[head], preferred_element_type=jnp.float32)
        scaled = scores * (HEAD_WIDTH ** -0.5 * LOG2_E) + bias_ref[at]
        scaled_ref[head] = scaled
        peak = jnp.max(scaled, axis=0, keepdims=True)
        return peak if old_peak is None else jnp.maximum(old_peak(head), peak)

    return stage


def weight_stage(scaled_ref, weight_ref):
    def stage(head, peak):
        weight_ref[head] = jnp.exp2(scaled_ref[head] - peak).astype(jnp.bfloat16)
        return peak

    return stage


def prepare_kernel(
    own_ref, lengths_hbm, places_hbm, q_hbm, k_hbm, v_hbm,
    across_ref, bias_ref, k_ref, v_ref, lengths_ref, places_ref, q_ref, sems,
):
    moves = (
        (lengths_hbm, lengths_ref), (places_hbm, places_ref),
        (q_hbm, q_ref), (k_hbm, k_ref), (v_hbm, v_ref),
    )
    copies = [pltpu.make_async_copy(*move, sems.at[n]) for n, move in enumerate(moves)]
    for copy in copies:
        copy.start()
    for copy in copies:
        copy.wait()
    heads, _, rows = across_ref.shape
    own, places = own_ref[0], places_ref[...]
    query_pos, starts = query_places(own, lengths_ref, places, rows)
    for mask in range(bias_ref.shape[0]):
        bias_ref[mask] = mask_table(own ^ mask, query_pos, starts, places)
    for head in range(heads):
        across_ref[head] = jnp.transpose(q_ref[:, head * HEAD_WIDTH:(head + 1) * HEAD_WIDTH])


def only_for(members, own_ref):
    found = own_ref[0] == members[0]
    for member in members[1:]:
        found = found | (own_ref[0] == member)
    return pl.when(found)


def own_kernel(members, own_ref, across_ref, bias_ref, k_ref, v_ref, *refs):
    peak_ref, sum_ref, scaled_ref, weight_ref = refs[-4:]

    @only_for(members, own_ref)
    def _():
        turned = values_down(v_ref[...])

        def mix(head, peak):
            peak_ref[head:head + 1, :] = peak
            sum_ref[head] = jnp.dot(turned, weight_ref[head], preferred_element_type=jnp.float32)

        in_stages(across_ref.shape[0], [
            score_stage(k_ref[...], across_ref, bias_ref, 0, scaled_ref, None),
            weight_stage(scaled_ref, weight_ref),
            mix,
        ])


def shrink(head, peak, peak_ref, sum_ref):
    summed = sum_ref[head] * jnp.exp2(peak_ref[head:head + 1, :] - peak)
    peak_ref[head:head + 1, :] = peak
    return summed


def weights_kernel(at, members, own_ref, across_ref, bias_ref, k_ref, *refs):
    peak_ref, sum_ref, weight_ref, scaled_ref = refs[-4:]

    @only_for(members, own_ref)
    def _():
        def rescale(head, peak):
            sum_ref[head] = shrink(head, peak, peak_ref, sum_ref)

        in_stages(across_ref.shape[0], [
            score_stage(
                k_ref[...], across_ref, bias_ref, at, scaled_ref,
                lambda head: peak_ref[head:head + 1, :],
            ),
            weight_stage(scaled_ref, weight_ref),
            rescale,
        ])


def values_kernel(weight_ref, v_ref, old_sum_ref, sum_ref):
    turned = values_down(v_ref[...])
    for head in range(sum_ref.shape[0]):
        sum_ref[head] += jnp.dot(turned, weight_ref[head], preferred_element_type=jnp.float32)


def next_kernel(
    at, across_ref, bias_ref, k_ref, v_ref, old_peak_ref, old_sum_ref,
    peak_ref, sum_ref, scaled_ref, weight_ref,
):
    turned = values_down(v_ref[...])

    def mix(head, peak):
        sum_ref[head] = shrink(head, peak, peak_ref, sum_ref) + jnp.dot(
            turned, weight_ref[head], preferred_element_type=jnp.float32
        )

    in_stages(across_ref.shape[0], [
        score_stage(
            k_ref[...], across_ref, bias_ref, at, scaled_ref,
            lambda head: peak_ref[head:head + 1, :],
        ),
        weight_stage(scaled_ref, weight_ref),
        mix,
    ])


def last_kernel(weight_ref, v_ref, sum_ref, out_ref, block_ref, sems):
    turned = values_down(v_ref[...])
    copies = []

    def mix(head, _):
        added = jnp.dot(turned, weight_ref[head], preferred_element_type=jnp.float32)
        summed = sum_ref[head] + added
        share = 1.0 / summed[HEAD_WIDTH:HEAD_WIDTH + 1]
        return (summed[:HEAD_WIDTH] * share).astype(jnp.bfloat16)

    def send(head, out):
        cols = slice(head * HEAD_WIDTH, (head + 1) * HEAD_WIDTH)
        block_ref[:, cols] = jnp.transpose(out)
        copy = pltpu.make_async_copy(block_ref.at[:, cols], out_ref.at[:, cols], sems.at[head])
        copy.start()
        copies.append(copy)

    in_stages(sum_ref.shape[0], [mix, send])
    for copy in copies:
        copy.wait()


SHORT = pl.CostEstimate(flops=0, bytes_accessed=0, transcendentals=0)


def in_vmem(*arrays):
    return [pltpu.with_memory_space_constraint(array, pltpu.VMEM) for array in arrays]


def in_hbm(*arrays):
    return [pltpu.with_memory_space_constraint(array, pltpu.HBM) for array in arrays]


VMEM_REF = pl.BlockSpec(memory_space=pltpu.VMEM)
HBM_REF = pl.BlockSpec(memory_space=pltpu.HBM)
PARAMS = pltpu.CompilerParams(vmem_limit_bytes=32 << 20)


def moved(value, mask):
    return lax.ppermute(value, "seq", [(i, i ^ mask) for i in range(lax.axis_size("seq"))])


def staged_attention(queries, keys, values, lengths, old_place):
    far_keys, far_values = moved(keys, 2), moved(values, 2)
    near_keys, near_values = moved(keys, 1), moved(values, 1)
    rows, cols = queries.shape
    heads = cols // HEAD_WIDTH
    devices = lax.axis_size("seq")
    own = lax.axis_index("seq").astype(jnp.int32).reshape(1)
    places = old_place.reshape(1, -1)
    scalar = pl.BlockSpec(memory_space=pltpu.SMEM)
    peak_type = pltpu.VMEM((heads, rows), jnp.float32)
    sum_type = pltpu.VMEM((heads, HEAD_WIDTH + ONES, rows), jnp.float32)
    scaled_type = pltpu.VMEM((heads, rows, rows), jnp.float32)
    weight_type = pltpu.VMEM((heads, rows, rows), jnp.bfloat16)

    def call(kernel, name, ins, outs, scratch, state=(), scalars=()):
        first = len(scalars) + len(ins)
        return pl.pallas_call(
            kernel,
            in_specs=[scalar] * len(scalars) + [VMEM_REF] * (len(ins) + len(state)),
            out_specs=[VMEM_REF] * len(outs),
            out_shape=outs,
            input_output_aliases={first + n: n for n in range(len(state))},
            scratch_shapes=scratch,
            compiler_params=PARAMS,
            cost_estimate=SHORT,
            name=name,
        )(*scalars, *in_vmem(*ins, *state))

    across, bias, own_keys, own_values = pl.pallas_call(
        prepare_kernel,
        in_specs=[scalar] + [HBM_REF] * 5,
        out_specs=[VMEM_REF] * 4,
        out_shape=[
            pltpu.VMEM((heads, HEAD_WIDTH, rows), jnp.bfloat16),
            pltpu.VMEM((devices, rows, rows), jnp.float32),
            pltpu.VMEM(keys.shape, jnp.bfloat16),
            pltpu.VMEM(values.shape, jnp.bfloat16),
        ],
        scratch_shapes=[
            pltpu.SMEM(lengths.shape, jnp.int32),
            pltpu.VMEM(places.shape, jnp.int32),
            pltpu.VMEM(queries.shape, jnp.bfloat16),
            pltpu.SemaphoreType.DMA((5,)),
        ],
        compiler_params=PARAMS,
        cost_estimate=SHORT,
        name="prepare",
    )(own, *in_hbm(lengths, places, queries, keys, values))

    def own_shard(members, state):
        return call(
            lambda *refs: own_kernel(members, *refs), "own_shard",
            (across, bias, own_keys, own_values), [peak_type, sum_type],
            [scaled_type, weight_type], state, (own,),
        )

    def shard_weights(at, members, keys, state):
        return call(
            lambda *refs: weights_kernel(at, members, *refs), "shard_weights",
            (across, bias, keys), [peak_type, sum_type, weight_type],
            [scaled_type], state, (own,),
        )

    state = own_shard((0, 2, 3), ())
    state = shard_weights(2, (0, 2), far_keys, state)
    far_keys, *state = lax.optimization_barrier((far_keys, *state))
    third_keys = moved(far_keys, 1)
    state = [*own_shard((1,), state[:2]), state[2]]
    state = shard_weights(2, (3,), far_keys, state)
    far_values, far_keys, *state = lax.optimization_barrier((far_values, far_keys, *state))
    third_values = moved(far_values, 1)
    peak, summed, weights = shard_weights(2, (1,), far_keys, state)
    summed, = call(values_kernel, "shard_values", (weights, far_values), [sum_type], [], (summed,))
    state = call(
        lambda *refs: next_kernel(1, *refs), "next_shard",
        (across, bias, near_keys, near_values), [peak_type, sum_type],
        [scaled_type, weight_type], (peak, summed),
    )
    _, summed, weights = shard_weights(3, (0, 1, 2, 3), third_keys, state)
    return pl.pallas_call(
        last_kernel,
        in_specs=[VMEM_REF] * 3,
        out_specs=pl.BlockSpec(memory_space=pl.ANY),
        out_shape=jax.ShapeDtypeStruct((rows, cols), jnp.bfloat16),
        scratch_shapes=[
            pltpu.VMEM((rows, cols), jnp.bfloat16),
            pltpu.SemaphoreType.DMA((heads,)),
        ],
        compiler_params=PARAMS,
        cost_estimate=SHORT,
        name="last_values",
    )(*in_vmem(weights, third_values, summed))


def online_kernel(heads, q_ref, k_ref, v_ref, key_pos_ref, query_pos_ref, start_ref, out_ref, peak_ref, acc_ref):
    step = pl.program_id(0)

    @pl.when(step == 0)
    def _():
        peak_ref[...] = jnp.full(peak_ref.shape, NEG_FILL, jnp.float32)
        acc_ref[...] = jnp.zeros(acc_ref.shape, jnp.float32)

    key_pos = key_pos_ref[...]
    visible = (key_pos >= start_ref[...]) & (key_pos <= query_pos_ref[...])
    values = v_ref[...]
    ext = jnp.concatenate([values, jnp.ones_like(values)], axis=1)
    for head in range(heads):
        q = q_ref[:, head * HEAD_WIDTH:(head + 1) * HEAD_WIDTH]
        scores = lax.dot_general(
            q, k_ref[...], (((1,), (1,)), ((), ())), preferred_element_type=jnp.float32
        )
        scaled = jnp.where(visible, scores * (HEAD_WIDTH ** -0.5 * LOG2_E), NEG_FILL)
        before = peak_ref[head]
        peak = jnp.maximum(before, jnp.max(scaled, axis=1, keepdims=True))
        weights = jnp.where(visible, jnp.exp2(scaled - peak), 0.0).astype(jnp.bfloat16)
        peak_ref[head] = peak
        acc_ref[head] = acc_ref[head] * jnp.exp2(before - peak) + jnp.dot(
            weights, ext, preferred_element_type=jnp.float32
        )

    @pl.when(step == pl.num_programs(0) - 1)
    def _():
        for head in range(heads):
            acc = acc_ref[head]
            out_ref[:, head * HEAD_WIDTH:(head + 1) * HEAD_WIDTH] = (
                acc[:, :HEAD_WIDTH] / acc[:, HEAD_WIDTH:]
            ).astype(jnp.bfloat16)


def online_attention(queries, keys, values, key_pos, query_pos, starts, chunk):
    rows, cols = queries.shape
    heads = cols // HEAD_WIDTH
    key_count = keys.shape[0]
    return pl.pallas_call(
        lambda *refs: online_kernel(heads, *refs),
        grid=(key_count // chunk,),
        in_specs=[
            pl.BlockSpec((rows, cols), lambda j: (0, 0)),
            pl.BlockSpec((chunk, HEAD_WIDTH), lambda j: (j, 0)),
            pl.BlockSpec((chunk, HEAD_WIDTH), lambda j: (j, 0)),
            pl.BlockSpec((1, chunk), lambda j: (0, j)),
            pl.BlockSpec((rows, 1), lambda j: (0, 0)),
            pl.BlockSpec((rows, 1), lambda j: (0, 0)),
        ],
        out_specs=pl.BlockSpec((rows, cols), lambda j: (0, 0)),
        out_shape=jax.ShapeDtypeStruct((rows, cols), jnp.bfloat16),
        scratch_shapes=[
            pltpu.VMEM((heads, rows, 1), jnp.float32),
            pltpu.VMEM((heads, rows, 2 * HEAD_WIDTH), jnp.float32),
        ],
        compiler_params=pltpu.CompilerParams(vmem_limit_bytes=32 << 20),
        name="online",
    )(queries, keys, values, key_pos, query_pos, starts)


def body(queries, keys, values, lengths, old_place):
    devices = lax.axis_size("seq")
    row_count = queries.shape[0]
    key_count = row_count * devices
    if devices == 4 and key_count <= 1024:
        return staged_attention(queries, keys, values, lengths, old_place)
    all_keys = lax.all_gather(keys, "seq", axis=0, tiled=True)
    all_values = lax.all_gather(values, "seq", axis=0, tiled=True)
    key_pos, query_pos, starts = block_places(
        lengths, old_place, lax.axis_index("seq"), row_count, key_count
    )
    return online_attention(queries, all_keys, all_values, key_pos, query_pos, starts, 512)


def solution(mesh):
    in_specs = (
        P(("groups", "seq"), "mp"),
        P(("groups", "seq"), "mp"),
        P(("groups", "seq"), "mp"),
        P("groups"),
        P("groups"),
    )
    out_specs = P(("groups", "seq"), "mp")
    return jax.shard_map(body, mesh=mesh, in_specs=in_specs, out_specs=out_specs, check_vma=False)
```

```python
import jax
import jax.numpy as jnp
from jax import lax
from jax.experimental import pallas as pl
from jax.experimental.pallas import tpu as pltpu
from jax.sharding import PartitionSpec as P

HEAD_WIDTH = 128
LOG2_E = 1.4426950408889634
NEG_FILL = -1e30
ONES = 16


def block_places(lengths, old_place, own_index, row_count, key_count):
    block_total = old_place.shape[0]
    block_rows = key_count // block_total
    ids = jnp.arange(block_total, dtype=jnp.int32)
    hit = old_place[:, None] == ids[None, :]
    new_block = jnp.sum(jnp.where(hit, ids[:, None], 0), axis=0)
    key_pos = (new_block[:, None] * block_rows + jnp.arange(block_rows, dtype=jnp.int32)).reshape(-1)
    query_pos = lax.dynamic_slice_in_dim(key_pos, own_index * row_count, row_count)
    bounds = jnp.cumsum(lengths)
    starts = jnp.max(jnp.where(bounds[None, :] <= query_pos[:, None], bounds[None, :], 0), axis=1)
    return key_pos.reshape(1, -1), query_pos.reshape(-1, 1), starts.reshape(-1, 1)


def iota(shape, dim):
    return lax.broadcasted_iota(jnp.int32, shape, dim)


def row_sum_as_column(places):
    square = (places.shape[1],) * 2
    spread = jnp.where(iota(square, 0) == iota(square, 1), places, 0).astype(jnp.float32)
    return jnp.sum(spread, axis=1, keepdims=True).astype(jnp.int32)


def query_places(own, lengths_ref, places, rows):
    block_total = places.shape[1]
    block_rows = rows * lax.axis_size("seq") // block_total
    shape = (block_total, rows)
    hit = row_sum_as_column(places) == own * (rows // block_rows) + iota(shape, 1) // block_rows
    at = jnp.where(hit, iota(shape, 0) * block_rows, 0).astype(jnp.float32)
    query_pos = jnp.sum(at, axis=0, keepdims=True) + (
        iota((1, rows), 1) % block_rows
    ).astype(jnp.float32)
    starts = jnp.zeros_like(query_pos)
    bound = jnp.int32(0)
    for t in range(lengths_ref.shape[0]):
        bound = bound + lengths_ref[t]
        edge = bound.astype(jnp.float32)
        starts = jnp.where(edge <= query_pos, edge, starts)
    return query_pos, starts


def mask_table(owner, query_pos, starts, places):
    block_total, rows = places.shape[1], query_pos.shape[1]
    block_rows = rows * lax.axis_size("seq") // block_total
    shape = (rows, block_total)
    hit = places == owner * (rows // block_rows) + iota(shape, 0) // block_rows
    at = jnp.where(hit, iota(shape, 1) * block_rows, 0).astype(jnp.float32)
    key_pos = jnp.sum(at, axis=1, keepdims=True) + (
        iota((rows, 1), 0) % block_rows
    ).astype(jnp.float32)
    return jnp.where((key_pos >= starts) & (key_pos <= query_pos), 0.0, NEG_FILL)


def values_down(values):
    turned = jnp.transpose(values)
    return jnp.concatenate([turned, jnp.ones((ONES, values.shape[0]), jnp.bfloat16)], axis=0)


def in_stages(heads, stages):
    results = [{} for _ in stages]
    for step in range(heads + len(stages) - 1):
        for late, stage in enumerate(stages):
            head = step - late
            if 0 <= head < heads:
                before = results[late - 1].pop(head) if late else None
                results[late][head] = stage(head, before)


def score_stage(keys, across_ref, bias_ref, at, scaled_ref, old_peak):
    def stage(head, _):
        scores = jnp.dot(keys, across_ref[head], preferred_element_type=jnp.float32)
        scaled = scores * (HEAD_WIDTH ** -0.5 * LOG2_E) + bias_ref[at]
        scaled_ref[head] = scaled
        peak = jnp.max(scaled, axis=0, keepdims=True)
        return peak if old_peak is None else jnp.maximum(old_peak(head), peak)

    return stage


def weight_stage(scaled_ref, weight_ref):
    def stage(head, peak):
        weight_ref[head] = jnp.exp2(scaled_ref[head] - peak).astype(jnp.bfloat16)
        return peak

    return stage


def prepare_kernel(
    own_ref, lengths_hbm, places_hbm, q_hbm, k_hbm, v_hbm,
    across_ref, bias_ref, k_ref, v_ref, lengths_ref, places_ref, q_ref, sems,
):
    moves = (
        (lengths_hbm, lengths_ref), (places_hbm, places_ref),
        (q_hbm, q_ref), (k_hbm, k_ref), (v_hbm, v_ref),
    )
    copies = [pltpu.make_async_copy(*move, sems.at[n]) for n, move in enumerate(moves)]
    for copy in copies:
        copy.start()
    for copy in copies:
        copy.wait()
    heads, _, rows = across_ref.shape
    own, places = own_ref[0], places_ref[...]
    query_pos, starts = query_places(own, lengths_ref, places, rows)
    for mask in range(bias_ref.shape[0]):
        bias_ref[mask] = mask_table(own ^ mask, query_pos, starts, places)
    for head in range(heads):
        across_ref[head] = jnp.transpose(q_ref[:, head * HEAD_WIDTH:(head + 1) * HEAD_WIDTH])


def only_for(members, own_ref):
    found = own_ref[0] == members[0]
    for member in members[1:]:
        found = found | (own_ref[0] == member)
    return pl.when(found)


def own_kernel(members, own_ref, across_ref, bias_ref, k_ref, v_ref, *refs):
    peak_ref, sum_ref, scaled_ref, weight_ref = refs[-4:]

    @only_for(members, own_ref)
    def _():
        turned = values_down(v_ref[...])

        def mix(head, peak):
            peak_ref[head:head + 1, :] = peak
            sum_ref[head] = jnp.dot(turned, weight_ref[head], preferred_element_type=jnp.float32)

        in_stages(across_ref.shape[0], [
            score_stage(k_ref[...], across_ref, bias_ref, 0, scaled_ref, None),
            weight_stage(scaled_ref, weight_ref),
            mix,
        ])


def shrink(head, peak, peak_ref, sum_ref):
    summed = sum_ref[head] * jnp.exp2(peak_ref[head:head + 1, :] - peak)
    peak_ref[head:head + 1, :] = peak
    return summed


def weights_kernel(at, members, own_ref, across_ref, bias_ref, k_ref, *refs):
    peak_ref, sum_ref, weight_ref, scaled_ref = refs[-4:]

    @only_for(members, own_ref)
    def _():
        def rescale(head, peak):
            sum_ref[head] = shrink(head, peak, peak_ref, sum_ref)

        in_stages(across_ref.shape[0], [
            score_stage(
                k_ref[...], across_ref, bias_ref, at, scaled_ref,
                lambda head: peak_ref[head:head + 1, :],
            ),
            weight_stage(scaled_ref, weight_ref),
            rescale,
        ])


def values_kernel(weight_ref, v_ref, old_sum_ref, sum_ref):
    turned = values_down(v_ref[...])
    for head in range(sum_ref.shape[0]):
        sum_ref[head] += jnp.dot(turned, weight_ref[head], preferred_element_type=jnp.float32)


def next_kernel(
    at, across_ref, bias_ref, k_ref, v_ref, old_peak_ref, old_sum_ref,
    peak_ref, sum_ref, scaled_ref, weight_ref,
):
    turned = values_down(v_ref[...])

    def mix(head, peak):
        sum_ref[head] = shrink(head, peak, peak_ref, sum_ref) + jnp.dot(
            turned, weight_ref[head], preferred_element_type=jnp.float32
        )

    in_stages(across_ref.shape[0], [
        score_stage(
            k_ref[...], across_ref, bias_ref, at, scaled_ref,
            lambda head: peak_ref[head:head + 1, :],
        ),
        weight_stage(scaled_ref, weight_ref),
        mix,
    ])


def last_kernel(weight_ref, v_ref, sum_ref, out_ref, block_ref, sems):
    turned = values_down(v_ref[...])
    copies = []

    def mix(head, _):
        added = jnp.dot(turned, weight_ref[head], preferred_element_type=jnp.float32)
        summed = sum_ref[head] + added
        share = 1.0 / summed[HEAD_WIDTH:HEAD_WIDTH + 1]
        return (summed[:HEAD_WIDTH] * share).astype(jnp.bfloat16)

    def send(head, out):
        cols = slice(head * HEAD_WIDTH, (head + 1) * HEAD_WIDTH)
        block_ref[:, cols] = jnp.transpose(out)
        copy = pltpu.make_async_copy(block_ref.at[:, cols], out_ref.at[:, cols], sems.at[head])
        copy.start()
        copies.append(copy)

    in_stages(sum_ref.shape[0], [mix, send])
    for copy in copies:
        copy.wait()


SHORT = pl.CostEstimate(flops=0, bytes_accessed=0, transcendentals=0)


def in_vmem(*arrays):
    return [pltpu.with_memory_space_constraint(array, pltpu.VMEM) for array in arrays]


def in_hbm(*arrays):
    return [pltpu.with_memory_space_constraint(array, pltpu.HBM) for array in arrays]


VMEM_REF = pl.BlockSpec(memory_space=pltpu.VMEM)
HBM_REF = pl.BlockSpec(memory_space=pltpu.HBM)
PARAMS = pltpu.CompilerParams(vmem_limit_bytes=32 << 20)


def moved(value, mask):
    return lax.ppermute(value, "seq", [(i, i ^ mask) for i in range(lax.axis_size("seq"))])


def staged_attention(queries, keys, values, lengths, old_place):
    far_keys, far_values = moved(keys, 2), moved(values, 2)
    near_keys, near_values = moved(keys, 1), moved(values, 1)
    rows, cols = queries.shape
    heads = cols // HEAD_WIDTH
    devices = lax.axis_size("seq")
    own = lax.axis_index("seq").astype(jnp.int32).reshape(1)
    places = old_place.reshape(1, -1)
    scalar = pl.BlockSpec(memory_space=pltpu.SMEM)
    peak_type = pltpu.VMEM((heads, rows), jnp.float32)
    sum_type = pltpu.VMEM((heads, HEAD_WIDTH + ONES, rows), jnp.float32)
    scaled_type = pltpu.VMEM((heads, rows, rows), jnp.float32)
    weight_type = pltpu.VMEM((heads, rows, rows), jnp.bfloat16)

    def call(kernel, name, ins, outs, scratch, state=(), scalars=()):
        first = len(scalars) + len(ins)
        return pl.pallas_call(
            kernel,
            in_specs=[scalar] * len(scalars) + [VMEM_REF] * (len(ins) + len(state)),
            out_specs=[VMEM_REF] * len(outs),
            out_shape=outs,
            input_output_aliases={first + n: n for n in range(len(state))},
            scratch_shapes=scratch,
            compiler_params=PARAMS,
            cost_estimate=SHORT,
            name=name,
        )(*scalars, *in_vmem(*ins, *state))

    across, bias, own_keys, own_values = pl.pallas_call(
        prepare_kernel,
        in_specs=[scalar] + [HBM_REF] * 5,
        out_specs=[VMEM_REF] * 4,
        out_shape=[
            pltpu.VMEM((heads, HEAD_WIDTH, rows), jnp.bfloat16),
            pltpu.VMEM((devices, rows, rows), jnp.float32),
            pltpu.VMEM(keys.shape, jnp.bfloat16),
            pltpu.VMEM(values.shape, jnp.bfloat16),
        ],
        scratch_shapes=[
            pltpu.SMEM(lengths.shape, jnp.int32),
            pltpu.VMEM(places.shape, jnp.int32),
            pltpu.VMEM(queries.shape, jnp.bfloat16),
            pltpu.SemaphoreType.DMA((5,)),
        ],
        compiler_params=PARAMS,
        cost_estimate=SHORT,
        name="prepare",
    )(own, *in_hbm(lengths, places, queries, keys, values))

    def own_shard(members, state):
        return call(
            lambda *refs: own_kernel(members, *refs), "own_shard",
            (across, bias, own_keys, own_values), [peak_type, sum_type],
            [scaled_type, weight_type], state, (own,),
        )

    def shard_weights(at, members, keys, state):
        return call(
            lambda *refs: weights_kernel(at, members, *refs), "shard_weights",
            (across, bias, keys), [peak_type, sum_type, weight_type],
            [scaled_type], state, (own,),
        )

    state = own_shard((0, 2, 3), ())
    state = shard_weights(2, (0, 2), far_keys, state)
    far_keys, *state = lax.optimization_barrier((far_keys, *state))
    third_keys = moved(far_keys, 1)
    far_values, far_keys, *state = lax.optimization_barrier((far_values, far_keys, *state))
    third_values = moved(far_values, 1)
    state = [*own_shard((1,), state[:2]), state[2]]
    peak, summed, weights = shard_weights(2, (1, 3), far_keys, state)
    summed, = call(values_kernel, "shard_values", (weights, far_values), [sum_type], [], (summed,))
    state = call(
        lambda *refs: next_kernel(1, *refs), "next_shard",
        (across, bias, near_keys, near_values), [peak_type, sum_type],
        [scaled_type, weight_type], (peak, summed),
    )
    _, summed, weights = shard_weights(3, (0, 1, 2, 3), third_keys, state)
    return pl.pallas_call(
        last_kernel,
        in_specs=[VMEM_REF] * 3,
        out_specs=pl.BlockSpec(memory_space=pl.ANY),
        out_shape=jax.ShapeDtypeStruct((rows, cols), jnp.bfloat16),
        scratch_shapes=[
            pltpu.VMEM((rows, cols), jnp.bfloat16),
            pltpu.SemaphoreType.DMA((heads,)),
        ],
        compiler_params=PARAMS,
        cost_estimate=SHORT,
        name="last_values",
    )(*in_vmem(weights, third_values, summed))


def online_kernel(heads, q_ref, k_ref, v_ref, key_pos_ref, query_pos_ref, start_ref, out_ref, peak_ref, acc_ref):
    step = pl.program_id(0)

    @pl.when(step == 0)
    def _():
        peak_ref[...] = jnp.full(peak_ref.shape, NEG_FILL, jnp.float32)
        acc_ref[...] = jnp.zeros(acc_ref.shape, jnp.float32)

    key_pos = key_pos_ref[...]
    visible = (key_pos >= start_ref[...]) & (key_pos <= query_pos_ref[...])
    values = v_ref[...]
    ext = jnp.concatenate([values, jnp.ones_like(values)], axis=1)
    for head in range(heads):
        q = q_ref[:, head * HEAD_WIDTH:(head + 1) * HEAD_WIDTH]
        scores = lax.dot_general(
            q, k_ref[...], (((1,), (1,)), ((), ())), preferred_element_type=jnp.float32
        )
        scaled = jnp.where(visible, scores * (HEAD_WIDTH ** -0.5 * LOG2_E), NEG_FILL)
        before = peak_ref[head]
        peak = jnp.maximum(before, jnp.max(scaled, axis=1, keepdims=True))
        weights = jnp.where(visible, jnp.exp2(scaled - peak), 0.0).astype(jnp.bfloat16)
        peak_ref[head] = peak
        acc_ref[head] = acc_ref[head] * jnp.exp2(before - peak) + jnp.dot(
            weights, ext, preferred_element_type=jnp.float32
        )

    @pl.when(step == pl.num_programs(0) - 1)
    def _():
        for head in range(heads):
            acc = acc_ref[head]
            out_ref[:, head * HEAD_WIDTH:(head + 1) * HEAD_WIDTH] = (
                acc[:, :HEAD_WIDTH] / acc[:, HEAD_WIDTH:]
            ).astype(jnp.bfloat16)


def online_attention(queries, keys, values, key_pos, query_pos, starts, chunk):
    rows, cols = queries.shape
    heads = cols // HEAD_WIDTH
    key_count = keys.shape[0]
    return pl.pallas_call(
        lambda *refs: online_kernel(heads, *refs),
        grid=(key_count // chunk,),
        in_specs=[
            pl.BlockSpec((rows, cols), lambda j: (0, 0)),
            pl.BlockSpec((chunk, HEAD_WIDTH), lambda j: (j, 0)),
            pl.BlockSpec((chunk, HEAD_WIDTH), lambda j: (j, 0)),
            pl.BlockSpec((1, chunk), lambda j: (0, j)),
            pl.BlockSpec((rows, 1), lambda j: (0, 0)),
            pl.BlockSpec((rows, 1), lambda j: (0, 0)),
        ],
        out_specs=pl.BlockSpec((rows, cols), lambda j: (0, 0)),
        out_shape=jax.ShapeDtypeStruct((rows, cols), jnp.bfloat16),
        scratch_shapes=[
            pltpu.VMEM((heads, rows, 1), jnp.float32),
            pltpu.VMEM((heads, rows, 2 * HEAD_WIDTH), jnp.float32),
        ],
        compiler_params=pltpu.CompilerParams(vmem_limit_bytes=32 << 20),
        name="online",
    )(queries, keys, values, key_pos, query_pos, starts)


def body(queries, keys, values, lengths, old_place):
    devices = lax.axis_size("seq")
    row_count = queries.shape[0]
    key_count = row_count * devices
    if devices == 4 and key_count <= 1024:
        return staged_attention(queries, keys, values, lengths, old_place)
    all_keys = lax.all_gather(keys, "seq", axis=0, tiled=True)
    all_values = lax.all_gather(values, "seq", axis=0, tiled=True)
    key_pos, query_pos, starts = block_places(
        lengths, old_place, lax.axis_index("seq"), row_count, key_count
    )
    return online_attention(queries, all_keys, all_values, key_pos, query_pos, starts, 512)


def solution(mesh):
    in_specs = (
        P(("groups", "seq"), "mp"),
        P(("groups", "seq"), "mp"),
        P(("groups", "seq"), "mp"),
        P("groups"),
        P("groups"),
    )
    out_specs = P(("groups", "seq"), "mp")
    return jax.shard_map(body, mesh=mesh, in_specs=in_specs, out_specs=out_specs, check_vma=False)
```

```python
import jax
import jax.numpy as jnp
from jax import lax
from jax.experimental import pallas as pl
from jax.experimental.pallas import tpu as pltpu
from jax.sharding import PartitionSpec as P

HEAD_WIDTH = 128
LOG2_E = 1.4426950408889634
NEG_FILL = -1e30
ONES = 16


def block_places(lengths, old_place, own_index, row_count, key_count):
    block_total = old_place.shape[0]
    block_rows = key_count // block_total
    ids = jnp.arange(block_total, dtype=jnp.int32)
    hit = old_place[:, None] == ids[None, :]
    new_block = jnp.sum(jnp.where(hit, ids[:, None], 0), axis=0)
    key_pos = (new_block[:, None] * block_rows + jnp.arange(block_rows, dtype=jnp.int32)).reshape(-1)
    query_pos = lax.dynamic_slice_in_dim(key_pos, own_index * row_count, row_count)
    bounds = jnp.cumsum(lengths)
    starts = jnp.max(jnp.where(bounds[None, :] <= query_pos[:, None], bounds[None, :], 0), axis=1)
    return key_pos.reshape(1, -1), query_pos.reshape(-1, 1), starts.reshape(-1, 1)


def iota(shape, dim):
    return lax.broadcasted_iota(jnp.int32, shape, dim)


def row_sum_as_column(places):
    square = (places.shape[1],) * 2
    spread = jnp.where(iota(square, 0) == iota(square, 1), places, 0).astype(jnp.float32)
    return jnp.sum(spread, axis=1, keepdims=True).astype(jnp.int32)


def query_places(own, lengths_ref, places, rows):
    block_total = places.shape[1]
    block_rows = rows * lax.axis_size("seq") // block_total
    shape = (block_total, rows)
    hit = row_sum_as_column(places) == own * (rows // block_rows) + iota(shape, 1) // block_rows
    at = jnp.where(hit, iota(shape, 0) * block_rows, 0).astype(jnp.float32)
    query_pos = jnp.sum(at, axis=0, keepdims=True) + (
        iota((1, rows), 1) % block_rows
    ).astype(jnp.float32)
    starts = jnp.zeros_like(query_pos)
    bound = jnp.int32(0)
    for t in range(lengths_ref.shape[0]):
        bound = bound + lengths_ref[t]
        edge = bound.astype(jnp.float32)
        starts = jnp.where(edge <= query_pos, edge, starts)
    return query_pos, starts


def mask_table(owner, query_pos, starts, places):
    block_total, rows = places.shape[1], query_pos.shape[1]
    block_rows = rows * lax.axis_size("seq") // block_total
    shape = (rows, block_total)
    hit = places == owner * (rows // block_rows) + iota(shape, 0) // block_rows
    at = jnp.where(hit, iota(shape, 1) * block_rows, 0).astype(jnp.float32)
    key_pos = jnp.sum(at, axis=1, keepdims=True) + (
        iota((rows, 1), 0) % block_rows
    ).astype(jnp.float32)
    return jnp.where((key_pos >= starts) & (key_pos <= query_pos), 0.0, NEG_FILL)


def values_down(values):
    turned = jnp.transpose(values)
    return jnp.concatenate([turned, jnp.ones((ONES, values.shape[0]), jnp.bfloat16)], axis=0)


def in_stages(heads, stages):
    results = [{} for _ in stages]
    for step in range(len(heads) + len(stages) - 1):
        for late, stage in enumerate(stages):
            if 0 <= step - late < len(heads):
                head = heads[step - late]
                before = results[late - 1].pop(head) if late else None
                results[late][head] = stage(head, before)


def score_stage(keys, across_ref, bias_ref, at, scaled_ref, old_peak):
    def stage(head, _):
        scores = jnp.dot(keys, across_ref[head], preferred_element_type=jnp.float32)
        scaled = scores * (HEAD_WIDTH ** -0.5 * LOG2_E) + bias_ref[at]
        scaled_ref[head] = scaled
        peak = jnp.max(scaled, axis=0, keepdims=True)
        return peak if old_peak is None else jnp.maximum(old_peak(head), peak)

    return stage


def weight_stage(scaled_ref, weight_ref):
    def stage(head, peak):
        weight_ref[head] = jnp.exp2(scaled_ref[head] - peak).astype(jnp.bfloat16)
        return peak

    return stage


def prepare_kernel(
    own_ref, lengths_hbm, places_hbm, q_hbm, k_hbm, v_hbm,
    across_ref, bias_ref, k_ref, v_ref, lengths_ref, places_ref, q_ref, sems,
):
    moves = (
        (lengths_hbm, lengths_ref), (places_hbm, places_ref),
        (q_hbm, q_ref), (k_hbm, k_ref), (v_hbm, v_ref),
    )
    copies = [pltpu.make_async_copy(*move, sems.at[n]) for n, move in enumerate(moves)]
    for copy in copies:
        copy.start()
    for copy in copies:
        copy.wait()
    heads, _, rows = across_ref.shape
    own, places = own_ref[0], places_ref[...]
    query_pos, starts = query_places(own, lengths_ref, places, rows)
    for mask in range(bias_ref.shape[0]):
        bias_ref[mask] = mask_table(own ^ mask, query_pos, starts, places)
    for head in range(heads):
        across_ref[head] = jnp.transpose(q_ref[:, head * HEAD_WIDTH:(head + 1) * HEAD_WIDTH])


def only_for(members, own_ref):
    found = own_ref[0] == members[0]
    for member in members[1:]:
        found = found | (own_ref[0] == member)
    return pl.when(found)


def own_kernel(members, own_ref, across_ref, bias_ref, k_ref, v_ref, *refs):
    peak_ref, sum_ref, scaled_ref, weight_ref = refs[-4:]

    @only_for(members, own_ref)
    def _():
        turned = values_down(v_ref[...])

        def mix(head, peak):
            peak_ref[head:head + 1, :] = peak
            sum_ref[head] = jnp.dot(turned, weight_ref[head], preferred_element_type=jnp.float32)

        in_stages(range(across_ref.shape[0]), [
            score_stage(k_ref[...], across_ref, bias_ref, 0, scaled_ref, None),
            weight_stage(scaled_ref, weight_ref),
            mix,
        ])


def shrink(head, peak, peak_ref, sum_ref):
    summed = sum_ref[head] * jnp.exp2(peak_ref[head:head + 1, :] - peak)
    peak_ref[head:head + 1, :] = peak
    return summed


def weights_kernel(at, members, heads, own_ref, across_ref, bias_ref, k_ref, *refs):
    peak_ref, sum_ref, weight_ref, scaled_ref = refs[-4:]

    @only_for(members, own_ref)
    def _():
        def rescale(head, peak):
            sum_ref[head] = shrink(head, peak, peak_ref, sum_ref)

        in_stages(heads, [
            score_stage(
                k_ref[...], across_ref, bias_ref, at, scaled_ref,
                lambda head: peak_ref[head:head + 1, :],
            ),
            weight_stage(scaled_ref, weight_ref),
            rescale,
        ])


def values_kernel(weight_ref, v_ref, old_sum_ref, sum_ref):
    turned = values_down(v_ref[...])
    for head in range(sum_ref.shape[0]):
        sum_ref[head] += jnp.dot(turned, weight_ref[head], preferred_element_type=jnp.float32)


def next_kernel(
    at, across_ref, bias_ref, k_ref, v_ref, old_peak_ref, old_sum_ref,
    peak_ref, sum_ref, scaled_ref, weight_ref,
):
    turned = values_down(v_ref[...])

    def mix(head, peak):
        sum_ref[head] = shrink(head, peak, peak_ref, sum_ref) + jnp.dot(
            turned, weight_ref[head], preferred_element_type=jnp.float32
        )

    in_stages(range(across_ref.shape[0]), [
        score_stage(
            k_ref[...], across_ref, bias_ref, at, scaled_ref,
            lambda head: peak_ref[head:head + 1, :],
        ),
        weight_stage(scaled_ref, weight_ref),
        mix,
    ])


def last_kernel(weight_ref, v_ref, sum_ref, out_ref, block_ref, sems):
    turned = values_down(v_ref[...])
    copies = []

    def mix(head, _):
        added = jnp.dot(turned, weight_ref[head], preferred_element_type=jnp.float32)
        summed = sum_ref[head] + added
        share = 1.0 / summed[HEAD_WIDTH:HEAD_WIDTH + 1]
        return (summed[:HEAD_WIDTH] * share).astype(jnp.bfloat16)

    def send(head, out):
        cols = slice(head * HEAD_WIDTH, (head + 1) * HEAD_WIDTH)
        block_ref[:, cols] = jnp.transpose(out)
        copy = pltpu.make_async_copy(block_ref.at[:, cols], out_ref.at[:, cols], sems.at[head])
        copy.start()
        copies.append(copy)

    in_stages(range(sum_ref.shape[0]), [mix, send])
    for copy in copies:
        copy.wait()


SHORT = pl.CostEstimate(flops=0, bytes_accessed=0, transcendentals=0)


def in_vmem(*arrays):
    return [pltpu.with_memory_space_constraint(array, pltpu.VMEM) for array in arrays]


def in_hbm(*arrays):
    return [pltpu.with_memory_space_constraint(array, pltpu.HBM) for array in arrays]


VMEM_REF = pl.BlockSpec(memory_space=pltpu.VMEM)
HBM_REF = pl.BlockSpec(memory_space=pltpu.HBM)
PARAMS = pltpu.CompilerParams(vmem_limit_bytes=32 << 20)


def moved(value, mask):
    return lax.ppermute(value, "seq", [(i, i ^ mask) for i in range(lax.axis_size("seq"))])


def staged_attention(queries, keys, values, lengths, old_place):
    far_keys, far_values = moved(keys, 2), moved(values, 2)
    near_keys, near_values = moved(keys, 1), moved(values, 1)
    rows, cols = queries.shape
    heads = cols // HEAD_WIDTH
    devices = lax.axis_size("seq")
    own = lax.axis_index("seq").astype(jnp.int32).reshape(1)
    places = old_place.reshape(1, -1)
    scalar = pl.BlockSpec(memory_space=pltpu.SMEM)
    peak_type = pltpu.VMEM((heads, rows), jnp.float32)
    sum_type = pltpu.VMEM((heads, HEAD_WIDTH + ONES, rows), jnp.float32)
    scaled_type = pltpu.VMEM((heads, rows, rows), jnp.float32)
    weight_type = pltpu.VMEM((heads, rows, rows), jnp.bfloat16)

    def call(kernel, name, ins, outs, scratch, state=(), scalars=()):
        first = len(scalars) + len(ins)
        return pl.pallas_call(
            kernel,
            in_specs=[scalar] * len(scalars) + [VMEM_REF] * (len(ins) + len(state)),
            out_specs=[VMEM_REF] * len(outs),
            out_shape=outs,
            input_output_aliases={first + n: n for n in range(len(state))},
            scratch_shapes=scratch,
            compiler_params=PARAMS,
            cost_estimate=SHORT,
            name=name,
        )(*scalars, *in_vmem(*ins, *state))

    across, bias, own_keys, own_values = pl.pallas_call(
        prepare_kernel,
        in_specs=[scalar] + [HBM_REF] * 5,
        out_specs=[VMEM_REF] * 4,
        out_shape=[
            pltpu.VMEM((heads, HEAD_WIDTH, rows), jnp.bfloat16),
            pltpu.VMEM((devices, rows, rows), jnp.float32),
            pltpu.VMEM(keys.shape, jnp.bfloat16),
            pltpu.VMEM(values.shape, jnp.bfloat16),
        ],
        scratch_shapes=[
            pltpu.SMEM(lengths.shape, jnp.int32),
            pltpu.VMEM(places.shape, jnp.int32),
            pltpu.VMEM(queries.shape, jnp.bfloat16),
            pltpu.SemaphoreType.DMA((5,)),
        ],
        compiler_params=PARAMS,
        cost_estimate=SHORT,
        name="prepare",
    )(own, *in_hbm(lengths, places, queries, keys, values))

    def own_shard(members, state):
        return call(
            lambda *refs: own_kernel(members, *refs), "own_shard",
            (across, bias, own_keys, own_values), [peak_type, sum_type],
            [scaled_type, weight_type], state, (own,),
        )

    def shard_weights(at, members, keys, state, first=0, end=heads):
        return call(
            lambda *refs: weights_kernel(at, members, range(first, end), *refs), "shard_weights",
            (across, bias, keys), [peak_type, sum_type, weight_type],
            [scaled_type], state, (own,),
        )

    state = own_shard((0, 2, 3), ())
    state = shard_weights(2, (0, 2), far_keys, state, end=heads // 2)
    far_keys, *state = lax.optimization_barrier((far_keys, *state))
    third_keys = moved(far_keys, 1)
    state = shard_weights(2, (0, 2), far_keys, state, first=heads // 2)
    far_values, far_keys, *state = lax.optimization_barrier((far_values, far_keys, *state))
    third_values = moved(far_values, 1)
    state = [*own_shard((1,), state[:2]), state[2]]
    peak, summed, weights = shard_weights(2, (1, 3), far_keys, state)
    summed, = call(values_kernel, "shard_values", (weights, far_values), [sum_type], [], (summed,))
    state = call(
        lambda *refs: next_kernel(1, *refs), "next_shard",
        (across, bias, near_keys, near_values), [peak_type, sum_type],
        [scaled_type, weight_type], (peak, summed),
    )
    _, summed, weights = shard_weights(3, (0, 1, 2, 3), third_keys, state)
    return pl.pallas_call(
        last_kernel,
        in_specs=[VMEM_REF] * 3,
        out_specs=pl.BlockSpec(memory_space=pl.ANY),
        out_shape=jax.ShapeDtypeStruct((rows, cols), jnp.bfloat16),
        scratch_shapes=[
            pltpu.VMEM((rows, cols), jnp.bfloat16),
            pltpu.SemaphoreType.DMA((heads,)),
        ],
        compiler_params=PARAMS,
        cost_estimate=SHORT,
        name="last_values",
    )(*in_vmem(weights, third_values, summed))


def online_kernel(heads, q_ref, k_ref, v_ref, key_pos_ref, query_pos_ref, start_ref, out_ref, peak_ref, acc_ref):
    step = pl.program_id(0)

    @pl.when(step == 0)
    def _():
        peak_ref[...] = jnp.full(peak_ref.shape, NEG_FILL, jnp.float32)
        acc_ref[...] = jnp.zeros(acc_ref.shape, jnp.float32)

    key_pos = key_pos_ref[...]
    visible = (key_pos >= start_ref[...]) & (key_pos <= query_pos_ref[...])
    values = v_ref[...]
    ext = jnp.concatenate([values, jnp.ones_like(values)], axis=1)
    for head in range(heads):
        q = q_ref[:, head * HEAD_WIDTH:(head + 1) * HEAD_WIDTH]
        scores = lax.dot_general(
            q, k_ref[...], (((1,), (1,)), ((), ())), preferred_element_type=jnp.float32
        )
        scaled = jnp.where(visible, scores * (HEAD_WIDTH ** -0.5 * LOG2_E), NEG_FILL)
        before = peak_ref[head]
        peak = jnp.maximum(before, jnp.max(scaled, axis=1, keepdims=True))
        weights = jnp.where(visible, jnp.exp2(scaled - peak), 0.0).astype(jnp.bfloat16)
        peak_ref[head] = peak
        acc_ref[head] = acc_ref[head] * jnp.exp2(before - peak) + jnp.dot(
            weights, ext, preferred_element_type=jnp.float32
        )

    @pl.when(step == pl.num_programs(0) - 1)
    def _():
        for head in range(heads):
            acc = acc_ref[head]
            out_ref[:, head * HEAD_WIDTH:(head + 1) * HEAD_WIDTH] = (
                acc[:, :HEAD_WIDTH] / acc[:, HEAD_WIDTH:]
            ).astype(jnp.bfloat16)


def online_attention(queries, keys, values, key_pos, query_pos, starts, chunk):
    rows, cols = queries.shape
    heads = cols // HEAD_WIDTH
    key_count = keys.shape[0]
    return pl.pallas_call(
        lambda *refs: online_kernel(heads, *refs),
        grid=(key_count // chunk,),
        in_specs=[
            pl.BlockSpec((rows, cols), lambda j: (0, 0)),
            pl.BlockSpec((chunk, HEAD_WIDTH), lambda j: (j, 0)),
            pl.BlockSpec((chunk, HEAD_WIDTH), lambda j: (j, 0)),
            pl.BlockSpec((1, chunk), lambda j: (0, j)),
            pl.BlockSpec((rows, 1), lambda j: (0, 0)),
            pl.BlockSpec((rows, 1), lambda j: (0, 0)),
        ],
        out_specs=pl.BlockSpec((rows, cols), lambda j: (0, 0)),
        out_shape=jax.ShapeDtypeStruct((rows, cols), jnp.bfloat16),
        scratch_shapes=[
            pltpu.VMEM((heads, rows, 1), jnp.float32),
            pltpu.VMEM((heads, rows, 2 * HEAD_WIDTH), jnp.float32),
        ],
        compiler_params=pltpu.CompilerParams(vmem_limit_bytes=32 << 20),
        name="online",
    )(queries, keys, values, key_pos, query_pos, starts)


def body(queries, keys, values, lengths, old_place):
    devices = lax.axis_size("seq")
    row_count = queries.shape[0]
    key_count = row_count * devices
    if devices == 4 and key_count <= 1024:
        return staged_attention(queries, keys, values, lengths, old_place)
    all_keys = lax.all_gather(keys, "seq", axis=0, tiled=True)
    all_values = lax.all_gather(values, "seq", axis=0, tiled=True)
    key_pos, query_pos, starts = block_places(
        lengths, old_place, lax.axis_index("seq"), row_count, key_count
    )
    return online_attention(queries, all_keys, all_values, key_pos, query_pos, starts, 512)


def solution(mesh):
    in_specs = (
        P(("groups", "seq"), "mp"),
        P(("groups", "seq"), "mp"),
        P(("groups", "seq"), "mp"),
        P("groups"),
        P("groups"),
    )
    out_specs = P(("groups", "seq"), "mp")
    return jax.shard_map(body, mesh=mesh, in_specs=in_specs, out_specs=out_specs, check_vma=False)
```

```python
import jax
import jax.numpy as jnp
from jax import lax
from jax.experimental import pallas as pl
from jax.experimental.pallas import tpu as pltpu
from jax.sharding import PartitionSpec as P

HEAD_WIDTH = 128
LOG2_E = 1.4426950408889634
NEG_FILL = -1e30
ONES = 16


def block_places(lengths, old_place, own_index, row_count, key_count):
    block_total = old_place.shape[0]
    block_rows = key_count // block_total
    ids = jnp.arange(block_total, dtype=jnp.int32)
    hit = old_place[:, None] == ids[None, :]
    new_block = jnp.sum(jnp.where(hit, ids[:, None], 0), axis=0)
    key_pos = (new_block[:, None] * block_rows + jnp.arange(block_rows, dtype=jnp.int32)).reshape(-1)
    query_pos = lax.dynamic_slice_in_dim(key_pos, own_index * row_count, row_count)
    bounds = jnp.cumsum(lengths)
    starts = jnp.max(jnp.where(bounds[None, :] <= query_pos[:, None], bounds[None, :], 0), axis=1)
    return key_pos.reshape(1, -1), query_pos.reshape(-1, 1), starts.reshape(-1, 1)


def iota(shape, dim):
    return lax.broadcasted_iota(jnp.int32, shape, dim)


def mask_tables(owners, lengths_ref, places_ref, rows, bias_ref):
    block_total = places_ref.shape[1]
    block_rows = rows * lax.axis_size("seq") // block_total
    blocks = rows // block_rows
    places = places_ref[...]
    square = (block_total, block_total)
    as_column = jnp.sum(
        jnp.where(iota(square, 0) == iota(square, 1), places, 0).astype(jnp.float32),
        axis=1, keepdims=True,
    ).astype(jnp.int32)
    across = (block_total, rows)
    hit = as_column == owners[0] * blocks + iota(across, 1) // block_rows
    at = jnp.where(hit, iota(across, 0) * block_rows, 0).astype(jnp.float32)
    query_pos = jnp.sum(at, axis=0, keepdims=True) + (
        iota((1, rows), 1) % block_rows
    ).astype(jnp.float32)
    starts = jnp.zeros_like(query_pos)
    bound = jnp.int32(0)
    for t in range(lengths_ref.shape[0]):
        bound = bound + lengths_ref[t]
        edge = bound.astype(jnp.float32)
        starts = jnp.where(edge <= query_pos, edge, starts)
    down = (rows, block_total)
    for n, owner in enumerate(owners):
        hit = places == owner * blocks + iota(down, 0) // block_rows
        at = jnp.where(hit, iota(down, 1) * block_rows, 0).astype(jnp.float32)
        key_pos = jnp.sum(at, axis=1, keepdims=True) + (
            iota((rows, 1), 0) % block_rows
        ).astype(jnp.float32)
        visible = (key_pos >= starts) & (key_pos <= query_pos)
        bias_ref[n] = jnp.where(visible, 0.0, NEG_FILL)


def values_down(values):
    turned = jnp.transpose(values.astype(jnp.float32)).astype(jnp.bfloat16)
    return jnp.concatenate([turned, jnp.ones((ONES, values.shape[0]), jnp.bfloat16)], axis=0)


def in_stages(heads, stages):
    results = [{} for _ in stages]
    for step in range(heads + len(stages) - 1):
        for late, stage in enumerate(stages):
            head = step - late
            if 0 <= head < heads:
                before = results[late - 1].pop(head) if late else None
                results[late][head] = stage(head, before)


def score_stage(keys, across_ref, bias_ref, at, scaled_ref, old_peak):
    def stage(head, _):
        scores = jnp.dot(keys, across_ref[head], preferred_element_type=jnp.float32)
        scaled = scores * (HEAD_WIDTH ** -0.5 * LOG2_E) + bias_ref[at]
        scaled_ref[head] = scaled
        peak = jnp.max(scaled, axis=0, keepdims=True)
        return peak if old_peak is None else jnp.maximum(old_peak(head), peak)

    return stage


def weight_stage(scaled_ref, weight_ref):
    def stage(head, peak):
        weight_ref[head] = jnp.exp2(scaled_ref[head] - peak).astype(jnp.bfloat16)
        return peak

    return stage


def own_kernel(
    own_ref, first_ref, lengths_hbm, places_hbm, q_hbm, k_hbm, v_hbm,
    across_ref, bias_ref, peak_ref, sum_ref,
    lengths_ref, places_ref, q_ref, k_ref, v_ref, scaled_ref, weight_ref, sems,
):
    moves = (
        (lengths_hbm, lengths_ref), (places_hbm, places_ref),
        (k_hbm, k_ref), (v_hbm, v_ref), (q_hbm, q_ref),
    )
    copies = [pltpu.make_async_copy(*move, sems.at[n]) for n, move in enumerate(moves)]
    for copy in copies:
        copy.start()
    copies[0].wait()
    copies[1].wait()
    heads, _, rows = across_ref.shape
    own, first = own_ref[0], first_ref[0]
    owners = [own, own ^ first, own ^ 3 ^ first, own ^ 3]
    mask_tables(owners, lengths_ref, places_ref, rows, bias_ref)
    for copy in copies[2:]:
        copy.wait()
    keys = k_ref[...]
    turned = values_down(v_ref[...])

    def turn(head, _):
        q = q_ref[:, head * HEAD_WIDTH:(head + 1) * HEAD_WIDTH]
        across_ref[head] = jnp.transpose(q.astype(jnp.float32)).astype(jnp.bfloat16)

    def mix(head, peak):
        peak_ref[head:head + 1, :] = peak
        sum_ref[head] = jnp.dot(turned, weight_ref[head], preferred_element_type=jnp.float32)

    in_stages(heads, [
        turn,
        score_stage(keys, across_ref, bias_ref, 0, scaled_ref, None),
        weight_stage(scaled_ref, weight_ref),
        mix,
    ])


def joined(head, peak, turned, weight_ref, peak_ref, sum_ref):
    added = jnp.dot(turned, weight_ref[head], preferred_element_type=jnp.float32)
    return sum_ref[head] * jnp.exp2(peak_ref[head:head + 1, :] - peak) + added


def next_kernel(
    at, across_ref, bias_ref, peak_ref, sum_ref, k_ref, v_ref, new_peak_ref, new_sum_ref,
    scaled_ref, weight_ref,
):
    turned = values_down(v_ref[...])

    def mix(head, peak):
        new_peak_ref[head:head + 1, :] = peak
        new_sum_ref[head] = joined(head, peak, turned, weight_ref, peak_ref, sum_ref)

    in_stages(across_ref.shape[0], [
        score_stage(
            k_ref[...], across_ref, bias_ref, at, scaled_ref,
            lambda head: peak_ref[head:head + 1, :],
        ),
        weight_stage(scaled_ref, weight_ref),
        mix,
    ])


def weights_kernel(
    at, across_ref, bias_ref, peak_ref, sum_ref, k_ref, new_sum_ref, weight_ref, scaled_ref,
):
    def rescale(head, peak):
        new_sum_ref[head] = sum_ref[head] * jnp.exp2(peak_ref[head:head + 1, :] - peak)

    in_stages(across_ref.shape[0], [
        score_stage(
            k_ref[...], across_ref, bias_ref, at, scaled_ref,
            lambda head: peak_ref[head:head + 1, :],
        ),
        weight_stage(scaled_ref, weight_ref),
        rescale,
    ])


def last_kernel(sum_ref, weight_ref, v_ref, out_ref, block_ref, sems):
    turned = values_down(v_ref[...])
    copies = []

    def mix(head, _):
        added = jnp.dot(turned, weight_ref[head], preferred_element_type=jnp.float32)
        summed = sum_ref[head] + added
        return summed[:HEAD_WIDTH] / summed[HEAD_WIDTH:HEAD_WIDTH + 1]

    def send(head, out):
        cols = slice(head * HEAD_WIDTH, (head + 1) * HEAD_WIDTH)
        block_ref[:, cols] = jnp.transpose(out).astype(jnp.bfloat16)
        copy = pltpu.make_async_copy(block_ref.at[:, cols], out_ref.at[:, cols], sems.at[head])
        copy.start()
        copies.append(copy)

    in_stages(sum_ref.shape[0], [mix, send])
    for copy in copies:
        copy.wait()


SHORT = pl.CostEstimate(flops=0, bytes_accessed=0, transcendentals=0)


def in_vmem(*arrays):
    return [pltpu.with_memory_space_constraint(array, pltpu.VMEM) for array in arrays]


def in_hbm(*arrays):
    return [pltpu.with_memory_space_constraint(array, pltpu.HBM) for array in arrays]


VMEM_REF = pl.BlockSpec(memory_space=pltpu.VMEM)
HBM_REF = pl.BlockSpec(memory_space=pltpu.HBM)
PARAMS = pltpu.CompilerParams(vmem_limit_bytes=32 << 20)


CYCLE = ((0, 2), (2, 3), (3, 1), (1, 0))
BACK = tuple((target, source) for source, target in CYCLE)
SWAP = ((0, 1), (1, 0), (2, 3), (3, 2))


def staged_attention(queries, keys, values, lengths, old_place):
    first_keys, first_values = (lax.ppermute(part, "seq", CYCLE) for part in (keys, values))
    second_keys, second_values = (lax.ppermute(part, "seq", BACK) for part in (keys, values))
    rows, cols = queries.shape
    heads = cols // HEAD_WIDTH
    devices = lax.axis_size("seq")
    own = lax.axis_index("seq").astype(jnp.int32)
    inner = (own == 1) | (own == 2)
    first = jnp.where(inner, 2, 1).astype(jnp.int32)
    places = old_place.reshape(1, -1)
    state = [
        pltpu.VMEM((heads, rows), jnp.float32),
        pltpu.VMEM((heads, HEAD_WIDTH + ONES, rows), jnp.float32),
    ]
    work = [
        pltpu.VMEM((heads, rows, rows), jnp.float32),
        pltpu.VMEM((heads, rows, rows), jnp.bfloat16),
    ]
    across, bias, *carried = pl.pallas_call(
        own_kernel,
        in_specs=[pl.BlockSpec(memory_space=pltpu.SMEM)] * 2 + [HBM_REF] * 5,
        out_specs=[VMEM_REF] * 4,
        out_shape=[
            pltpu.VMEM((heads, HEAD_WIDTH, rows), jnp.bfloat16),
            pltpu.VMEM((devices, rows, rows), jnp.float32),
        ] + state,
        scratch_shapes=[
            pltpu.SMEM(lengths.shape, jnp.int32),
            pltpu.VMEM(places.shape, jnp.int32),
            pltpu.VMEM(queries.shape, jnp.bfloat16),
            pltpu.VMEM(keys.shape, jnp.bfloat16),
            pltpu.VMEM(values.shape, jnp.bfloat16),
        ] + work + [pltpu.SemaphoreType.DMA((5,))],
        compiler_params=PARAMS,
        cost_estimate=SHORT,
        name="own_shard",
    )(own.reshape(1), first.reshape(1), *in_hbm(lengths, places, queries, keys, values))

    def add_shard(at, keys, values, carried):
        return pl.pallas_call(
            lambda *refs: next_kernel(at, *refs),
            in_specs=[VMEM_REF] * 6,
            out_specs=[VMEM_REF] * 2,
            out_shape=state,
            scratch_shapes=work,
            compiler_params=PARAMS,
            cost_estimate=SHORT,
            name="next_shard",
        )(*in_vmem(across, bias, *carried), keys, values)

    far_keys = jnp.where(~inner, second_keys, first_keys)
    far_keys, *carried = lax.optimization_barrier((far_keys, *carried))
    third_keys = lax.ppermute(far_keys, "seq", SWAP)
    second_values, first_values, far_keys, *carried = lax.optimization_barrier((second_values, first_values, far_keys, *carried))
    far_values = jnp.where(~inner, second_values, first_values)
    third_values = lax.ppermute(far_values, "seq", SWAP)
    carried = add_shard(1, first_keys, first_values, carried)
    carried = add_shard(2, second_keys, second_values, carried)
    summed, weights = pl.pallas_call(
        lambda *refs: weights_kernel(3, *refs),
        in_specs=[VMEM_REF] * 5,
        out_specs=[VMEM_REF] * 2,
        out_shape=state[1:] + work[1:],
        scratch_shapes=work[:1],
        compiler_params=PARAMS,
        cost_estimate=SHORT,
        name="last_weights",
    )(*in_vmem(across, bias, *carried), third_keys)
    return pl.pallas_call(
        last_kernel,
        in_specs=[VMEM_REF] * 3,
        out_specs=pl.BlockSpec(memory_space=pl.ANY),
        out_shape=jax.ShapeDtypeStruct((rows, cols), jnp.bfloat16),
        scratch_shapes=[
            pltpu.VMEM((rows, cols), jnp.bfloat16),
            pltpu.SemaphoreType.DMA((heads,)),
        ],
        compiler_params=PARAMS,
        cost_estimate=SHORT,
        name="last_values",
    )(*in_vmem(summed, weights), third_values)


def online_kernel(heads, q_ref, k_ref, v_ref, key_pos_ref, query_pos_ref, start_ref, out_ref, peak_ref, acc_ref):
    step = pl.program_id(0)

    @pl.when(step == 0)
    def _():
        peak_ref[...] = jnp.full(peak_ref.shape, NEG_FILL, jnp.float32)
        acc_ref[...] = jnp.zeros(acc_ref.shape, jnp.float32)

    key_pos = key_pos_ref[...]
    visible = (key_pos >= start_ref[...]) & (key_pos <= query_pos_ref[...])
    values = v_ref[...]
    ext = jnp.concatenate([values, jnp.ones_like(values)], axis=1)
    for head in range(heads):
        q = q_ref[:, head * HEAD_WIDTH:(head + 1) * HEAD_WIDTH]
        scores = lax.dot_general(
            q, k_ref[...], (((1,), (1,)), ((), ())), preferred_element_type=jnp.float32
        )
        scaled = jnp.where(visible, scores * (HEAD_WIDTH ** -0.5 * LOG2_E), NEG_FILL)
        before = peak_ref[head]
        peak = jnp.maximum(before, jnp.max(scaled, axis=1, keepdims=True))
        weights = jnp.where(visible, jnp.exp2(scaled - peak), 0.0).astype(jnp.bfloat16)
        peak_ref[head] = peak
        acc_ref[head] = acc_ref[head] * jnp.exp2(before - peak) + jnp.dot(
            weights, ext, preferred_element_type=jnp.float32
        )

    @pl.when(step == pl.num_programs(0) - 1)
    def _():
        for head in range(heads):
            acc = acc_ref[head]
            out_ref[:, head * HEAD_WIDTH:(head + 1) * HEAD_WIDTH] = (
                acc[:, :HEAD_WIDTH] / acc[:, HEAD_WIDTH:]
            ).astype(jnp.bfloat16)


def online_attention(queries, keys, values, key_pos, query_pos, starts, chunk):
    rows, cols = queries.shape
    heads = cols // HEAD_WIDTH
    key_count = keys.shape[0]
    return pl.pallas_call(
        lambda *refs: online_kernel(heads, *refs),
        grid=(key_count // chunk,),
        in_specs=[
            pl.BlockSpec((rows, cols), lambda j: (0, 0)),
            pl.BlockSpec((chunk, HEAD_WIDTH), lambda j: (j, 0)),
            pl.BlockSpec((chunk, HEAD_WIDTH), lambda j: (j, 0)),
            pl.BlockSpec((1, chunk), lambda j: (0, j)),
            pl.BlockSpec((rows, 1), lambda j: (0, 0)),
            pl.BlockSpec((rows, 1), lambda j: (0, 0)),
        ],
        out_specs=pl.BlockSpec((rows, cols), lambda j: (0, 0)),
        out_shape=jax.ShapeDtypeStruct((rows, cols), jnp.bfloat16),
        scratch_shapes=[
            pltpu.VMEM((heads, rows, 1), jnp.float32),
            pltpu.VMEM((heads, rows, 2 * HEAD_WIDTH), jnp.float32),
        ],
        compiler_params=pltpu.CompilerParams(vmem_limit_bytes=32 << 20),
        name="online",
    )(queries, keys, values, key_pos, query_pos, starts)


def body(queries, keys, values, lengths, old_place):
    devices = lax.axis_size("seq")
    row_count = queries.shape[0]
    key_count = row_count * devices
    if devices == 4 and key_count <= 1024:
        return staged_attention(queries, keys, values, lengths, old_place)
    all_keys = lax.all_gather(keys, "seq", axis=0, tiled=True)
    all_values = lax.all_gather(values, "seq", axis=0, tiled=True)
    key_pos, query_pos, starts = block_places(
        lengths, old_place, lax.axis_index("seq"), row_count, key_count
    )
    return online_attention(queries, all_keys, all_values, key_pos, query_pos, starts, 512)


def solution(mesh):
    in_specs = (
        P(("groups", "seq"), "mp"),
        P(("groups", "seq"), "mp"),
        P(("groups", "seq"), "mp"),
        P("groups"),
        P("groups"),
    )
    out_specs = P(("groups", "seq"), "mp")
    return jax.shard_map(body, mesh=mesh, in_specs=in_specs, out_specs=out_specs, check_vma=False)
```

```python
import jax
import jax.numpy as jnp
from jax import lax
from jax.experimental import pallas as pl
from jax.experimental.pallas import tpu as pltpu
from jax.sharding import PartitionSpec as P

HEAD_WIDTH = 128
LOG2_E = 1.4426950408889634
NEG_FILL = -1e30
ONES = 16


def block_places(lengths, old_place, own_index, row_count, key_count):
    block_total = old_place.shape[0]
    block_rows = key_count // block_total
    ids = jnp.arange(block_total, dtype=jnp.int32)
    hit = old_place[:, None] == ids[None, :]
    new_block = jnp.sum(jnp.where(hit, ids[:, None], 0), axis=0)
    key_pos = (new_block[:, None] * block_rows + jnp.arange(block_rows, dtype=jnp.int32)).reshape(-1)
    query_pos = lax.dynamic_slice_in_dim(key_pos, own_index * row_count, row_count)
    bounds = jnp.cumsum(lengths)
    starts = jnp.max(jnp.where(bounds[None, :] <= query_pos[:, None], bounds[None, :], 0), axis=1)
    return key_pos.reshape(1, -1), query_pos.reshape(-1, 1), starts.reshape(-1, 1)


def iota(shape, dim):
    return lax.broadcasted_iota(jnp.int32, shape, dim)


def row_sum_as_column(places):
    square = (places.shape[1],) * 2
    spread = jnp.where(iota(square, 0) == iota(square, 1), places, 0).astype(jnp.float32)
    return jnp.sum(spread, axis=1, keepdims=True).astype(jnp.int32)


def query_places(own, lengths_ref, places, rows):
    block_total = places.shape[1]
    block_rows = rows * lax.axis_size("seq") // block_total
    shape = (block_total, rows)
    hit = row_sum_as_column(places) == own * (rows // block_rows) + iota(shape, 1) // block_rows
    at = jnp.where(hit, iota(shape, 0) * block_rows, 0).astype(jnp.float32)
    query_pos = jnp.sum(at, axis=0, keepdims=True) + (
        iota((1, rows), 1) % block_rows
    ).astype(jnp.float32)
    starts = jnp.zeros_like(query_pos)
    bound = jnp.int32(0)
    for t in range(lengths_ref.shape[0]):
        bound = bound + lengths_ref[t]
        edge = bound.astype(jnp.float32)
        starts = jnp.where(edge <= query_pos, edge, starts)
    return query_pos, starts


def mask_table(owner, query_pos, starts, places):
    block_total, rows = places.shape[1], query_pos.shape[1]
    block_rows = rows * lax.axis_size("seq") // block_total
    shape = (rows, block_total)
    hit = places == owner * (rows // block_rows) + iota(shape, 0) // block_rows
    at = jnp.where(hit, iota(shape, 1) * block_rows, 0).astype(jnp.float32)
    key_pos = jnp.sum(at, axis=1, keepdims=True) + (
        iota((rows, 1), 0) % block_rows
    ).astype(jnp.float32)
    return jnp.where((key_pos >= starts) & (key_pos <= query_pos), 0.0, NEG_FILL)


def values_down(values):
    turned = jnp.transpose(values)
    return jnp.concatenate([turned, jnp.ones((ONES, values.shape[0]), jnp.bfloat16)], axis=0)


def in_stages(heads, stages):
    results = [{} for _ in stages]
    for step in range(len(heads) + len(stages) - 1):
        for late, stage in enumerate(stages):
            if 0 <= step - late < len(heads):
                head = heads[step - late]
                before = results[late - 1].pop(head) if late else None
                results[late][head] = stage(head, before)


def score_stage(keys, across_ref, bias_ref, at, scaled_ref, old_peak):
    def stage(head, _):
        scores = jnp.dot(keys, across_ref[head], preferred_element_type=jnp.float32)
        scaled = scores * (HEAD_WIDTH ** -0.5 * LOG2_E) + bias_ref[at]
        scaled_ref[head] = scaled
        peak = jnp.max(scaled, axis=0, keepdims=True)
        return peak if old_peak is None else jnp.maximum(old_peak(head), peak)

    return stage


def weight_stage(scaled_ref, weight_ref):
    def stage(head, peak):
        weight_ref[head] = jnp.exp2(scaled_ref[head] - peak).astype(jnp.bfloat16)
        return peak

    return stage


def prepare_kernel(
    own_ref, lengths_hbm, places_hbm, q_hbm, k_hbm, v_hbm,
    across_ref, bias_ref, k_ref, v_ref, lengths_ref, places_ref, q_ref, sems,
):
    moves = (
        (lengths_hbm, lengths_ref), (places_hbm, places_ref),
        (q_hbm, q_ref), (k_hbm, k_ref), (v_hbm, v_ref),
    )
    copies = [pltpu.make_async_copy(*move, sems.at[n]) for n, move in enumerate(moves)]
    for copy in copies:
        copy.start()
    for copy in copies:
        copy.wait()
    heads, _, rows = across_ref.shape
    own, places = own_ref[0], places_ref[...]
    query_pos, starts = query_places(own, lengths_ref, places, rows)
    for mask in range(bias_ref.shape[0]):
        bias_ref[mask] = mask_table(own ^ mask, query_pos, starts, places)
    for head in range(heads):
        across_ref[head] = jnp.transpose(q_ref[:, head * HEAD_WIDTH:(head + 1) * HEAD_WIDTH])


def only_for(members, own_ref):
    found = own_ref[0] == members[0]
    for member in members[1:]:
        found = found | (own_ref[0] == member)
    return pl.when(found)


def own_kernel(members, own_ref, across_ref, bias_ref, k_ref, v_ref, *refs):
    peak_ref, sum_ref, scaled_ref, weight_ref = refs[-4:]

    @only_for(members, own_ref)
    def _():
        turned = values_down(v_ref[...])

        def mix(head, peak):
            peak_ref[head:head + 1, :] = peak
            sum_ref[head] = jnp.dot(turned, weight_ref[head], preferred_element_type=jnp.float32)

        in_stages(range(across_ref.shape[0]), [
            score_stage(k_ref[...], across_ref, bias_ref, 0, scaled_ref, None),
            weight_stage(scaled_ref, weight_ref),
            mix,
        ])


def shrink(head, peak, peak_ref, sum_ref):
    summed = sum_ref[head] * jnp.exp2(peak_ref[head:head + 1, :] - peak)
    peak_ref[head:head + 1, :] = peak
    return summed


def weights_kernel(at, members, heads, own_ref, across_ref, bias_ref, k_ref, *refs):
    peak_ref, sum_ref, weight_ref, scaled_ref = refs[-4:]

    @only_for(members, own_ref)
    def _():
        def rescale(head, peak):
            sum_ref[head] = shrink(head, peak, peak_ref, sum_ref)

        in_stages(heads, [
            score_stage(
                k_ref[...], across_ref, bias_ref, at, scaled_ref,
                lambda head: peak_ref[head:head + 1, :],
            ),
            weight_stage(scaled_ref, weight_ref),
            rescale,
        ])


def values_kernel(weight_ref, v_ref, old_sum_ref, sum_ref):
    turned = values_down(v_ref[...])
    for head in range(sum_ref.shape[0]):
        sum_ref[head] += jnp.dot(turned, weight_ref[head], preferred_element_type=jnp.float32)


def next_kernel(
    at, across_ref, bias_ref, k_ref, v_ref, old_peak_ref, old_sum_ref,
    peak_ref, sum_ref, scaled_ref, weight_ref,
):
    turned = values_down(v_ref[...])

    def mix(head, peak):
        sum_ref[head] = shrink(head, peak, peak_ref, sum_ref) + jnp.dot(
            turned, weight_ref[head], preferred_element_type=jnp.float32
        )

    in_stages(range(across_ref.shape[0]), [
        score_stage(
            k_ref[...], across_ref, bias_ref, at, scaled_ref,
            lambda head: peak_ref[head:head + 1, :],
        ),
        weight_stage(scaled_ref, weight_ref),
        mix,
    ])


def last_kernel(weight_ref, v_ref, sum_ref, out_ref, block_ref, sems):
    turned = values_down(v_ref[...])
    copies = []

    def mix(head, _):
        added = jnp.dot(turned, weight_ref[head], preferred_element_type=jnp.float32)
        summed = sum_ref[head] + added
        share = 1.0 / summed[HEAD_WIDTH:HEAD_WIDTH + 1]
        return (summed[:HEAD_WIDTH] * share).astype(jnp.bfloat16)

    def send(head, out):
        cols = slice(head * HEAD_WIDTH, (head + 1) * HEAD_WIDTH)
        block_ref[:, cols] = jnp.transpose(out)
        copy = pltpu.make_async_copy(block_ref.at[:, cols], out_ref.at[:, cols], sems.at[head])
        copy.start()
        copies.append(copy)

    in_stages(range(sum_ref.shape[0]), [mix, send])
    for copy in copies:
        copy.wait()


SHORT = pl.CostEstimate(flops=0, bytes_accessed=0, transcendentals=0)


def in_vmem(*arrays):
    return [pltpu.with_memory_space_constraint(array, pltpu.VMEM) for array in arrays]


def in_hbm(*arrays):
    return [pltpu.with_memory_space_constraint(array, pltpu.HBM) for array in arrays]


VMEM_REF = pl.BlockSpec(memory_space=pltpu.VMEM)
HBM_REF = pl.BlockSpec(memory_space=pltpu.HBM)
PARAMS = pltpu.CompilerParams(vmem_limit_bytes=32 << 20)


def moved(value, mask):
    return lax.ppermute(value, "seq", [(i, i ^ mask) for i in range(lax.axis_size("seq"))])


def staged_attention(queries, keys, values, lengths, old_place):
    far_keys, far_values = moved(keys, 2), moved(values, 2)
    near_keys, near_values = moved(keys, 1), moved(values, 1)
    rows, cols = queries.shape
    heads = cols // HEAD_WIDTH
    devices = lax.axis_size("seq")
    own = lax.axis_index("seq").astype(jnp.int32).reshape(1)
    places = old_place.reshape(1, -1)
    scalar = pl.BlockSpec(memory_space=pltpu.SMEM)
    peak_type = pltpu.VMEM((heads, rows), jnp.float32)
    sum_type = pltpu.VMEM((heads, HEAD_WIDTH + ONES, rows), jnp.float32)
    scaled_type = pltpu.VMEM((heads, rows, rows), jnp.float32)
    weight_type = pltpu.VMEM((heads, rows, rows), jnp.bfloat16)

    def call(kernel, name, ins, outs, scratch, state=(), scalars=()):
        first = len(scalars) + len(ins)
        return pl.pallas_call(
            kernel,
            in_specs=[scalar] * len(scalars) + [VMEM_REF] * (len(ins) + len(state)),
            out_specs=[VMEM_REF] * len(outs),
            out_shape=outs,
            input_output_aliases={first + n: n for n in range(len(state))},
            scratch_shapes=scratch,
            compiler_params=PARAMS,
            cost_estimate=SHORT,
            name=name,
        )(*scalars, *in_vmem(*ins, *state))

    across, bias, own_keys, own_values = pl.pallas_call(
        prepare_kernel,
        in_specs=[scalar] + [HBM_REF] * 5,
        out_specs=[VMEM_REF] * 4,
        out_shape=[
            pltpu.VMEM((heads, HEAD_WIDTH, rows), jnp.bfloat16),
            pltpu.VMEM((devices, rows, rows), jnp.float32),
            pltpu.VMEM(keys.shape, jnp.bfloat16),
            pltpu.VMEM(values.shape, jnp.bfloat16),
        ],
        scratch_shapes=[
            pltpu.SMEM(lengths.shape, jnp.int32),
            pltpu.VMEM(places.shape, jnp.int32),
            pltpu.VMEM(queries.shape, jnp.bfloat16),
            pltpu.SemaphoreType.DMA((5,)),
        ],
        compiler_params=PARAMS,
        cost_estimate=SHORT,
        name="prepare",
    )(own, *in_hbm(lengths, places, queries, keys, values))

    def own_shard(members, state):
        return call(
            lambda *refs: own_kernel(members, *refs), "own_shard",
            (across, bias, own_keys, own_values), [peak_type, sum_type],
            [scaled_type, weight_type], state, (own,),
        )

    def shard_weights(at, members, keys, state, first=0, end=heads):
        return call(
            lambda *refs: weights_kernel(at, members, range(first, end), *refs), "shard_weights",
            (across, bias, keys), [peak_type, sum_type, weight_type],
            [scaled_type], state, (own,),
        )

    state = own_shard((0, 2, 3), ())
    far_keys, *state = lax.optimization_barrier((far_keys, *state))
    third_keys = moved(far_keys, 1)
    state = shard_weights(2, (0, 2), far_keys, state, end=heads // 2)
    far_values, far_keys, *state = lax.optimization_barrier((far_values, far_keys, *state))
    third_values = moved(far_values, 1)
    state = [*own_shard((1,), state[:2]), state[2]]
    state = shard_weights(2, (0, 2), far_keys, state, first=heads // 2)
    peak, summed, weights = shard_weights(2, (1, 3), far_keys, state)
    summed, = call(values_kernel, "shard_values", (weights, far_values), [sum_type], [], (summed,))
    state = call(
        lambda *refs: next_kernel(1, *refs), "next_shard",
        (across, bias, near_keys, near_values), [peak_type, sum_type],
        [scaled_type, weight_type], (peak, summed),
    )
    _, summed, weights = shard_weights(3, (0, 1, 2, 3), third_keys, state)
    return pl.pallas_call(
        last_kernel,
        in_specs=[VMEM_REF] * 3,
        out_specs=pl.BlockSpec(memory_space=pl.ANY),
        out_shape=jax.ShapeDtypeStruct((rows, cols), jnp.bfloat16),
        scratch_shapes=[
            pltpu.VMEM((rows, cols), jnp.bfloat16),
            pltpu.SemaphoreType.DMA((heads,)),
        ],
        compiler_params=PARAMS,
        cost_estimate=SHORT,
        name="last_values",
    )(*in_vmem(weights, third_values, summed))


def online_kernel(heads, q_ref, k_ref, v_ref, key_pos_ref, query_pos_ref, start_ref, out_ref, peak_ref, acc_ref):
    step = pl.program_id(0)

    @pl.when(step == 0)
    def _():
        peak_ref[...] = jnp.full(peak_ref.shape, NEG_FILL, jnp.float32)
        acc_ref[...] = jnp.zeros(acc_ref.shape, jnp.float32)

    key_pos = key_pos_ref[...]
    visible = (key_pos >= start_ref[...]) & (key_pos <= query_pos_ref[...])
    values = v_ref[...]
    ext = jnp.concatenate([values, jnp.ones_like(values)], axis=1)
    for head in range(heads):
        q = q_ref[:, head * HEAD_WIDTH:(head + 1) * HEAD_WIDTH]
        scores = lax.dot_general(
            q, k_ref[...], (((1,), (1,)), ((), ())), preferred_element_type=jnp.float32
        )
        scaled = jnp.where(visible, scores * (HEAD_WIDTH ** -0.5 * LOG2_E), NEG_FILL)
        before = peak_ref[head]
        peak = jnp.maximum(before, jnp.max(scaled, axis=1, keepdims=True))
        weights = jnp.where(visible, jnp.exp2(scaled - peak), 0.0).astype(jnp.bfloat16)
        peak_ref[head] = peak
        acc_ref[head] = acc_ref[head] * jnp.exp2(before - peak) + jnp.dot(
            weights, ext, preferred_element_type=jnp.float32
        )

    @pl.when(step == pl.num_programs(0) - 1)
    def _():
        for head in range(heads):
            acc = acc_ref[head]
            out_ref[:, head * HEAD_WIDTH:(head + 1) * HEAD_WIDTH] = (
                acc[:, :HEAD_WIDTH] / acc[:, HEAD_WIDTH:]
            ).astype(jnp.bfloat16)


def online_attention(queries, keys, values, key_pos, query_pos, starts, chunk):
    rows, cols = queries.shape
    heads = cols // HEAD_WIDTH
    key_count = keys.shape[0]
    return pl.pallas_call(
        lambda *refs: online_kernel(heads, *refs),
        grid=(key_count // chunk,),
        in_specs=[
            pl.BlockSpec((rows, cols), lambda j: (0, 0)),
            pl.BlockSpec((chunk, HEAD_WIDTH), lambda j: (j, 0)),
            pl.BlockSpec((chunk, HEAD_WIDTH), lambda j: (j, 0)),
            pl.BlockSpec((1, chunk), lambda j: (0, j)),
            pl.BlockSpec((rows, 1), lambda j: (0, 0)),
            pl.BlockSpec((rows, 1), lambda j: (0, 0)),
        ],
        out_specs=pl.BlockSpec((rows, cols), lambda j: (0, 0)),
        out_shape=jax.ShapeDtypeStruct((rows, cols), jnp.bfloat16),
        scratch_shapes=[
            pltpu.VMEM((heads, rows, 1), jnp.float32),
            pltpu.VMEM((heads, rows, 2 * HEAD_WIDTH), jnp.float32),
        ],
        compiler_params=pltpu.CompilerParams(vmem_limit_bytes=32 << 20),
        name="online",
    )(queries, keys, values, key_pos, query_pos, starts)


def body(queries, keys, values, lengths, old_place):
    devices = lax.axis_size("seq")
    row_count = queries.shape[0]
    key_count = row_count * devices
    if devices == 4 and key_count <= 1024:
        return staged_attention(queries, keys, values, lengths, old_place)
    all_keys = lax.all_gather(keys, "seq", axis=0, tiled=True)
    all_values = lax.all_gather(values, "seq", axis=0, tiled=True)
    key_pos, query_pos, starts = block_places(
        lengths, old_place, lax.axis_index("seq"), row_count, key_count
    )
    return online_attention(queries, all_keys, all_values, key_pos, query_pos, starts, 512)


def solution(mesh):
    in_specs = (
        P(("groups", "seq"), "mp"),
        P(("groups", "seq"), "mp"),
        P(("groups", "seq"), "mp"),
        P("groups"),
        P("groups"),
    )
    out_specs = P(("groups", "seq"), "mp")
    return jax.shard_map(body, mesh=mesh, in_specs=in_specs, out_specs=out_specs, check_vma=False)
```

```python
import jax
import jax.numpy as jnp
from jax import lax
from jax.experimental import pallas as pl
from jax.experimental.pallas import tpu as pltpu
from jax.sharding import PartitionSpec as P

HEAD_WIDTH = 128
LOG2_E = 1.4426950408889634
NEG_FILL = -1e30
ONES = 16


def block_places(lengths, old_place, own_index, row_count, key_count):
    block_total = old_place.shape[0]
    block_rows = key_count // block_total
    ids = jnp.arange(block_total, dtype=jnp.int32)
    hit = old_place[:, None] == ids[None, :]
    new_block = jnp.sum(jnp.where(hit, ids[:, None], 0), axis=0)
    key_pos = (new_block[:, None] * block_rows + jnp.arange(block_rows, dtype=jnp.int32)).reshape(-1)
    query_pos = lax.dynamic_slice_in_dim(key_pos, own_index * row_count, row_count)
    bounds = jnp.cumsum(lengths)
    starts = jnp.max(jnp.where(bounds[None, :] <= query_pos[:, None], bounds[None, :], 0), axis=1)
    return key_pos.reshape(1, -1), query_pos.reshape(-1, 1), starts.reshape(-1, 1)


def iota(shape, dim):
    return lax.broadcasted_iota(jnp.int32, shape, dim)


def row_sum_as_column(places):
    square = (places.shape[1],) * 2
    spread = jnp.where(iota(square, 0) == iota(square, 1), places, 0).astype(jnp.float32)
    return jnp.sum(spread, axis=1, keepdims=True).astype(jnp.int32)


def query_places(own, lengths_ref, places, rows):
    block_total = places.shape[1]
    block_rows = rows * lax.axis_size("seq") // block_total
    shape = (block_total, rows)
    hit = row_sum_as_column(places) == own * (rows // block_rows) + iota(shape, 1) // block_rows
    at = jnp.where(hit, iota(shape, 0) * block_rows, 0).astype(jnp.float32)
    query_pos = jnp.sum(at, axis=0, keepdims=True) + (
        iota((1, rows), 1) % block_rows
    ).astype(jnp.float32)
    starts = jnp.zeros_like(query_pos)
    bound = jnp.int32(0)
    for t in range(lengths_ref.shape[0]):
        bound = bound + lengths_ref[t]
        edge = bound.astype(jnp.float32)
        starts = jnp.where(edge <= query_pos, edge, starts)
    return query_pos, starts


def mask_table(owner, query_pos, starts, places):
    block_total, rows = places.shape[1], query_pos.shape[1]
    block_rows = rows * lax.axis_size("seq") // block_total
    shape = (rows, block_total)
    hit = places == owner * (rows // block_rows) + iota(shape, 0) // block_rows
    at = jnp.where(hit, iota(shape, 1) * block_rows, 0).astype(jnp.float32)
    key_pos = jnp.sum(at, axis=1, keepdims=True) + (
        iota((rows, 1), 0) % block_rows
    ).astype(jnp.float32)
    return jnp.where((key_pos >= starts) & (key_pos <= query_pos), 0.0, NEG_FILL)


def values_down(values):
    turned = jnp.transpose(values)
    return jnp.concatenate([turned, jnp.ones((ONES, values.shape[0]), jnp.bfloat16)], axis=0)


def in_stages(heads, stages):
    results = [{} for _ in stages]
    for step in range(len(heads) + len(stages) - 1):
        for late, stage in enumerate(stages):
            if 0 <= step - late < len(heads):
                head = heads[step - late]
                before = results[late - 1].pop(head) if late else None
                results[late][head] = stage(head, before)


def score_stage(keys, across_ref, bias_ref, at, scaled_ref, old_peak):
    def stage(head, _):
        scores = jnp.dot(keys, across_ref[head], preferred_element_type=jnp.float32)
        scaled = scores * (HEAD_WIDTH ** -0.5 * LOG2_E) + bias_ref[at]
        scaled_ref[head] = scaled
        peak = jnp.max(scaled, axis=0, keepdims=True)
        return peak if old_peak is None else jnp.maximum(old_peak(head), peak)

    return stage


def weight_stage(scaled_ref, weight_ref):
    def stage(head, peak):
        weight_ref[head] = jnp.exp2(scaled_ref[head] - peak).astype(jnp.bfloat16)
        return peak

    return stage


def only_for(members, own_ref):
    found = own_ref[0] == members[0]
    for member in members[1:]:
        found = found | (own_ref[0] == member)
    return pl.when(found)


def prepare_kernel(members, own_ref, *refs):
    lengths_hbm, places_hbm, q_hbm, k_hbm, v_hbm = refs[:5]
    across_ref, bias_ref, k_ref, v_ref, lengths_ref, places_ref, q_ref, sems = refs[-8:]

    @only_for(members, own_ref)
    def _():
        moves = (
            (lengths_hbm, lengths_ref), (places_hbm, places_ref),
            (q_hbm, q_ref), (k_hbm, k_ref), (v_hbm, v_ref),
        )
        copies = [pltpu.make_async_copy(*move, sems.at[n]) for n, move in enumerate(moves)]
        for copy in copies:
            copy.start()
        for copy in copies:
            copy.wait()
        heads, _, rows = across_ref.shape
        own, places = own_ref[0], places_ref[...]
        query_pos, starts = query_places(own, lengths_ref, places, rows)
        for mask in range(bias_ref.shape[0]):
            bias_ref[mask] = mask_table(own ^ mask, query_pos, starts, places)
        for head in range(heads):
            across_ref[head] = jnp.transpose(q_ref[:, head * HEAD_WIDTH:(head + 1) * HEAD_WIDTH])


def own_kernel(members, own_ref, across_ref, bias_ref, k_ref, v_ref, *refs):
    peak_ref, sum_ref, scaled_ref, weight_ref = refs[-4:]

    @only_for(members, own_ref)
    def _():
        turned = values_down(v_ref[...])

        def mix(head, peak):
            peak_ref[head:head + 1, :] = peak
            sum_ref[head] = jnp.dot(turned, weight_ref[head], preferred_element_type=jnp.float32)

        in_stages(range(across_ref.shape[0]), [
            score_stage(k_ref[...], across_ref, bias_ref, 0, scaled_ref, None),
            weight_stage(scaled_ref, weight_ref),
            mix,
        ])


def shrink(head, peak, peak_ref, sum_ref):
    summed = sum_ref[head] * jnp.exp2(peak_ref[head:head + 1, :] - peak)
    peak_ref[head:head + 1, :] = peak
    return summed


def weights_kernel(at, members, heads, own_ref, across_ref, bias_ref, k_ref, *refs):
    peak_ref, sum_ref, weight_ref, scaled_ref = refs[-4:]

    @only_for(members, own_ref)
    def _():
        def rescale(head, peak):
            sum_ref[head] = shrink(head, peak, peak_ref, sum_ref)

        in_stages(heads, [
            score_stage(
                k_ref[...], across_ref, bias_ref, at, scaled_ref,
                lambda head: peak_ref[head:head + 1, :],
            ),
            weight_stage(scaled_ref, weight_ref),
            rescale,
        ])


def values_kernel(weight_ref, v_ref, old_sum_ref, sum_ref):
    turned = values_down(v_ref[...])
    for head in range(sum_ref.shape[0]):
        sum_ref[head] += jnp.dot(turned, weight_ref[head], preferred_element_type=jnp.float32)


def next_kernel(
    at, across_ref, bias_ref, k_ref, v_ref, old_peak_ref, old_sum_ref,
    peak_ref, sum_ref, scaled_ref, weight_ref,
):
    turned = values_down(v_ref[...])

    def mix(head, peak):
        sum_ref[head] = shrink(head, peak, peak_ref, sum_ref) + jnp.dot(
            turned, weight_ref[head], preferred_element_type=jnp.float32
        )

    in_stages(range(across_ref.shape[0]), [
        score_stage(
            k_ref[...], across_ref, bias_ref, at, scaled_ref,
            lambda head: peak_ref[head:head + 1, :],
        ),
        weight_stage(scaled_ref, weight_ref),
        mix,
    ])


def last_kernel(weight_ref, v_ref, sum_ref, out_ref, block_ref, sems):
    turned = values_down(v_ref[...])
    copies = []

    def mix(head, _):
        added = jnp.dot(turned, weight_ref[head], preferred_element_type=jnp.float32)
        summed = sum_ref[head] + added
        share = 1.0 / summed[HEAD_WIDTH:HEAD_WIDTH + 1]
        return (summed[:HEAD_WIDTH] * share).astype(jnp.bfloat16)

    def send(head, out):
        cols = slice(head * HEAD_WIDTH, (head + 1) * HEAD_WIDTH)
        block_ref[:, cols] = jnp.transpose(out)
        copy = pltpu.make_async_copy(block_ref.at[:, cols], out_ref.at[:, cols], sems.at[head])
        copy.start()
        copies.append(copy)

    in_stages(range(sum_ref.shape[0]), [mix, send])
    for copy in copies:
        copy.wait()


SHORT = pl.CostEstimate(flops=0, bytes_accessed=0, transcendentals=0)


def in_vmem(*arrays):
    return [pltpu.with_memory_space_constraint(array, pltpu.VMEM) for array in arrays]


def in_hbm(*arrays):
    return [pltpu.with_memory_space_constraint(array, pltpu.HBM) for array in arrays]


VMEM_REF = pl.BlockSpec(memory_space=pltpu.VMEM)
HBM_REF = pl.BlockSpec(memory_space=pltpu.HBM)
PARAMS = pltpu.CompilerParams(vmem_limit_bytes=32 << 20)


def moved(value, mask):
    return lax.ppermute(value, "seq", [(i, i ^ mask) for i in range(lax.axis_size("seq"))])


def staged_attention(queries, keys, values, lengths, old_place):
    far_keys, far_values = moved(keys, 2), moved(values, 2)
    rows, cols = queries.shape
    heads = cols // HEAD_WIDTH
    devices = lax.axis_size("seq")
    own = lax.axis_index("seq").astype(jnp.int32).reshape(1)
    places = old_place.reshape(1, -1)
    scalar = pl.BlockSpec(memory_space=pltpu.SMEM)
    peak_type = pltpu.VMEM((heads, rows), jnp.float32)
    sum_type = pltpu.VMEM((heads, HEAD_WIDTH + ONES, rows), jnp.float32)
    scaled_type = pltpu.VMEM((heads, rows, rows), jnp.float32)
    weight_type = pltpu.VMEM((heads, rows, rows), jnp.bfloat16)

    def call(kernel, name, ins, outs, scratch, state=(), scalars=()):
        first = len(scalars) + len(ins)
        return pl.pallas_call(
            kernel,
            in_specs=[scalar] * len(scalars) + [VMEM_REF] * (len(ins) + len(state)),
            out_specs=[VMEM_REF] * len(outs),
            out_shape=outs,
            input_output_aliases={first + n: n for n in range(len(state))},
            scratch_shapes=scratch,
            compiler_params=PARAMS,
            cost_estimate=SHORT,
            name=name,
        )(*scalars, *in_vmem(*ins, *state))

    def prepare(members, near=()):
        return pl.pallas_call(
            lambda *refs: prepare_kernel(members, *refs),
            in_specs=[scalar] + [HBM_REF] * 5 + [VMEM_REF] * len(near),
            out_specs=[VMEM_REF] * 4,
            out_shape=[
                pltpu.VMEM((heads, HEAD_WIDTH, rows), jnp.bfloat16),
                pltpu.VMEM((devices, rows, rows), jnp.float32),
                pltpu.VMEM(keys.shape, jnp.bfloat16),
                pltpu.VMEM(values.shape, jnp.bfloat16),
            ],
            input_output_aliases={6 + n: n for n in range(len(near))},
            scratch_shapes=[
                pltpu.SMEM(lengths.shape, jnp.int32),
                pltpu.VMEM(places.shape, jnp.int32),
                pltpu.VMEM(queries.shape, jnp.bfloat16),
                pltpu.SemaphoreType.DMA((5,)),
            ],
            compiler_params=PARAMS,
            cost_estimate=SHORT,
            name="prepare",
        )(own, *in_hbm(lengths, places, queries, keys, values), *in_vmem(*near))

    prepared = prepare((0, 2))
    keys, values, *prepared = lax.optimization_barrier((keys, values, *prepared))
    near_keys, near_values = moved(keys, 1), moved(values, 1)
    across, bias, own_keys, own_values = prepare((1, 3), prepared)

    def own_shard(members, state):
        return call(
            lambda *refs: own_kernel(members, *refs), "own_shard",
            (across, bias, own_keys, own_values), [peak_type, sum_type],
            [scaled_type, weight_type], state, (own,),
        )

    def shard_weights(at, members, keys, state, first=0, end=heads):
        return call(
            lambda *refs: weights_kernel(at, members, range(first, end), *refs), "shard_weights",
            (across, bias, keys), [peak_type, sum_type, weight_type],
            [scaled_type], state, (own,),
        )

    state = own_shard((0, 2, 3), ())
    far_keys, *state = lax.optimization_barrier((far_keys, *state))
    third_keys = moved(far_keys, 1)
    state = shard_weights(2, (0, 2), far_keys, state, end=heads // 2)
    far_values, far_keys, *state = lax.optimization_barrier((far_values, far_keys, *state))
    third_values = moved(far_values, 1)
    state = [*own_shard((1,), state[:2]), state[2]]
    state = shard_weights(2, (0, 2), far_keys, state, first=heads // 2)
    peak, summed, weights = shard_weights(2, (1, 3), far_keys, state)
    summed, = call(values_kernel, "shard_values", (weights, far_values), [sum_type], [], (summed,))
    state = call(
        lambda *refs: next_kernel(1, *refs), "next_shard",
        (across, bias, near_keys, near_values), [peak_type, sum_type],
        [scaled_type, weight_type], (peak, summed),
    )
    _, summed, weights = shard_weights(3, (0, 1, 2, 3), third_keys, state)
    return pl.pallas_call(
        last_kernel,
        in_specs=[VMEM_REF] * 3,
        out_specs=pl.BlockSpec(memory_space=pl.ANY),
        out_shape=jax.ShapeDtypeStruct((rows, cols), jnp.bfloat16),
        scratch_shapes=[
            pltpu.VMEM((rows, cols), jnp.bfloat16),
            pltpu.SemaphoreType.DMA((heads,)),
        ],
        compiler_params=PARAMS,
        cost_estimate=SHORT,
        name="last_values",
    )(*in_vmem(weights, third_values, summed))


def online_kernel(heads, q_ref, k_ref, v_ref, key_pos_ref, query_pos_ref, start_ref, out_ref, peak_ref, acc_ref):
    step = pl.program_id(0)

    @pl.when(step == 0)
    def _():
        peak_ref[...] = jnp.full(peak_ref.shape, NEG_FILL, jnp.float32)
        acc_ref[...] = jnp.zeros(acc_ref.shape, jnp.float32)

    key_pos = key_pos_ref[...]
    visible = (key_pos >= start_ref[...]) & (key_pos <= query_pos_ref[...])
    values = v_ref[...]
    ext = jnp.concatenate([values, jnp.ones_like(values)], axis=1)
    for head in range(heads):
        q = q_ref[:, head * HEAD_WIDTH:(head + 1) * HEAD_WIDTH]
        scores = lax.dot_general(
            q, k_ref[...], (((1,), (1,)), ((), ())), preferred_element_type=jnp.float32
        )
        scaled = jnp.where(visible, scores * (HEAD_WIDTH ** -0.5 * LOG2_E), NEG_FILL)
        before = peak_ref[head]
        peak = jnp.maximum(before, jnp.max(scaled, axis=1, keepdims=True))
        weights = jnp.where(visible, jnp.exp2(scaled - peak), 0.0).astype(jnp.bfloat16)
        peak_ref[head] = peak
        acc_ref[head] = acc_ref[head] * jnp.exp2(before - peak) + jnp.dot(
            weights, ext, preferred_element_type=jnp.float32
        )

    @pl.when(step == pl.num_programs(0) - 1)
    def _():
        for head in range(heads):
            acc = acc_ref[head]
            out_ref[:, head * HEAD_WIDTH:(head + 1) * HEAD_WIDTH] = (
                acc[:, :HEAD_WIDTH] / acc[:, HEAD_WIDTH:]
            ).astype(jnp.bfloat16)


def online_attention(queries, keys, values, key_pos, query_pos, starts, chunk):
    rows, cols = queries.shape
    heads = cols // HEAD_WIDTH
    key_count = keys.shape[0]
    return pl.pallas_call(
        lambda *refs: online_kernel(heads, *refs),
        grid=(key_count // chunk,),
        in_specs=[
            pl.BlockSpec((rows, cols), lambda j: (0, 0)),
            pl.BlockSpec((chunk, HEAD_WIDTH), lambda j: (j, 0)),
            pl.BlockSpec((chunk, HEAD_WIDTH), lambda j: (j, 0)),
            pl.BlockSpec((1, chunk), lambda j: (0, j)),
            pl.BlockSpec((rows, 1), lambda j: (0, 0)),
            pl.BlockSpec((rows, 1), lambda j: (0, 0)),
        ],
        out_specs=pl.BlockSpec((rows, cols), lambda j: (0, 0)),
        out_shape=jax.ShapeDtypeStruct((rows, cols), jnp.bfloat16),
        scratch_shapes=[
            pltpu.VMEM((heads, rows, 1), jnp.float32),
            pltpu.VMEM((heads, rows, 2 * HEAD_WIDTH), jnp.float32),
        ],
        compiler_params=pltpu.CompilerParams(vmem_limit_bytes=32 << 20),
        name="online",
    )(queries, keys, values, key_pos, query_pos, starts)


def body(queries, keys, values, lengths, old_place):
    devices = lax.axis_size("seq")
    row_count = queries.shape[0]
    key_count = row_count * devices
    if devices == 4 and key_count <= 1024:
        return staged_attention(queries, keys, values, lengths, old_place)
    all_keys = lax.all_gather(keys, "seq", axis=0, tiled=True)
    all_values = lax.all_gather(values, "seq", axis=0, tiled=True)
    key_pos, query_pos, starts = block_places(
        lengths, old_place, lax.axis_index("seq"), row_count, key_count
    )
    return online_attention(queries, all_keys, all_values, key_pos, query_pos, starts, 512)


def solution(mesh):
    in_specs = (
        P(("groups", "seq"), "mp"),
        P(("groups", "seq"), "mp"),
        P(("groups", "seq"), "mp"),
        P("groups"),
        P("groups"),
    )
    out_specs = P(("groups", "seq"), "mp")
    return jax.shard_map(body, mesh=mesh, in_specs=in_specs, out_specs=out_specs, check_vma=False)
```

```python
import jax
import jax.numpy as jnp
from jax import lax
from jax.experimental import pallas as pl
from jax.experimental.pallas import tpu as pltpu
from jax.sharding import PartitionSpec as P

HEAD_WIDTH = 128
LOG2_E = 1.4426950408889634
NEG_FILL = -1e30
ONES = 16


def block_places(lengths, old_place, own_index, row_count, key_count):
    block_total = old_place.shape[0]
    block_rows = key_count // block_total
    ids = jnp.arange(block_total, dtype=jnp.int32)
    hit = old_place[:, None] == ids[None, :]
    new_block = jnp.sum(jnp.where(hit, ids[:, None], 0), axis=0)
    key_pos = (new_block[:, None] * block_rows + jnp.arange(block_rows, dtype=jnp.int32)).reshape(-1)
    query_pos = lax.dynamic_slice_in_dim(key_pos, own_index * row_count, row_count)
    bounds = jnp.cumsum(lengths)
    starts = jnp.max(jnp.where(bounds[None, :] <= query_pos[:, None], bounds[None, :], 0), axis=1)
    return key_pos.reshape(1, -1), query_pos.reshape(-1, 1), starts.reshape(-1, 1)


def iota(shape, dim):
    return lax.broadcasted_iota(jnp.int32, shape, dim)


def row_sum_as_column(places):
    square = (places.shape[1],) * 2
    spread = jnp.where(iota(square, 0) == iota(square, 1), places, 0).astype(jnp.float32)
    return jnp.sum(spread, axis=1, keepdims=True).astype(jnp.int32)


def query_places(own, lengths_ref, places, rows):
    block_total = places.shape[1]
    block_rows = rows * lax.axis_size("seq") // block_total
    shape = (block_total, rows)
    hit = row_sum_as_column(places) == own * (rows // block_rows) + iota(shape, 1) // block_rows
    at = jnp.where(hit, iota(shape, 0) * block_rows, 0).astype(jnp.float32)
    query_pos = jnp.sum(at, axis=0, keepdims=True) + (
        iota((1, rows), 1) % block_rows
    ).astype(jnp.float32)
    starts = jnp.zeros_like(query_pos)
    bound = jnp.int32(0)
    for t in range(lengths_ref.shape[0]):
        bound = bound + lengths_ref[t]
        edge = bound.astype(jnp.float32)
        starts = jnp.where(edge <= query_pos, edge, starts)
    return query_pos, starts


def mask_table(owner, query_pos, starts, places):
    block_total, rows = places.shape[1], query_pos.shape[1]
    block_rows = rows * lax.axis_size("seq") // block_total
    shape = (rows, block_total)
    hit = places == owner * (rows // block_rows) + iota(shape, 0) // block_rows
    at = jnp.where(hit, iota(shape, 1) * block_rows, 0).astype(jnp.float32)
    key_pos = jnp.sum(at, axis=1, keepdims=True) + (
        iota((rows, 1), 0) % block_rows
    ).astype(jnp.float32)
    return jnp.where((key_pos >= starts) & (key_pos <= query_pos), 0.0, NEG_FILL)


def values_down(values):
    turned = jnp.transpose(values)
    return jnp.concatenate([turned, jnp.ones((ONES, values.shape[0]), jnp.bfloat16)], axis=0)


def in_stages(heads, stages):
    results = [{} for _ in stages]
    for step in range(len(heads) + len(stages) - 1):
        for late, stage in enumerate(stages):
            if 0 <= step - late < len(heads):
                head = heads[step - late]
                before = results[late - 1].pop(head) if late else None
                results[late][head] = stage(head, before)


def score_stage(keys, across_ref, bias_ref, at, scaled_ref, old_peak):
    def stage(head, _):
        scores = jnp.dot(keys, across_ref[head], preferred_element_type=jnp.float32)
        scaled = scores * (HEAD_WIDTH ** -0.5 * LOG2_E) + bias_ref[at]
        scaled_ref[head] = scaled
        peak = jnp.max(scaled, axis=0, keepdims=True)
        return peak if old_peak is None else jnp.maximum(old_peak(head), peak)

    return stage


def weight_stage(scaled_ref, weight_ref):
    def stage(head, peak):
        weight_ref[head] = jnp.exp2(scaled_ref[head] - peak).astype(jnp.bfloat16)
        return peak

    return stage


def only_for(members, own_ref):
    found = own_ref[0] == members[0]
    for member in members[1:]:
        found = found | (own_ref[0] == member)
    return pl.when(found)


def prepare_kernel(members, own_ref, *refs):
    lengths_hbm, places_hbm, q_hbm, k_hbm, v_hbm = refs[:5]
    across_ref, bias_ref, k_ref, v_ref, lengths_ref, places_ref, q_ref, sems = refs[-8:]

    @only_for(members, own_ref)
    def _():
        moves = (
            (lengths_hbm, lengths_ref), (places_hbm, places_ref),
            (q_hbm, q_ref), (k_hbm, k_ref), (v_hbm, v_ref),
        )
        copies = [pltpu.make_async_copy(*move, sems.at[n]) for n, move in enumerate(moves)]
        for copy in copies:
            copy.start()
        for copy in copies:
            copy.wait()
        heads, _, rows = across_ref.shape
        own, places = own_ref[0], places_ref[...]
        query_pos, starts = query_places(own, lengths_ref, places, rows)
        for mask in range(bias_ref.shape[0]):
            bias_ref[mask] = mask_table(own ^ mask, query_pos, starts, places)
        for head in range(heads):
            across_ref[head] = jnp.transpose(q_ref[:, head * HEAD_WIDTH:(head + 1) * HEAD_WIDTH])


def own_kernel(members, own_ref, across_ref, bias_ref, k_ref, v_ref, *refs):
    peak_ref, sum_ref, scaled_ref, weight_ref = refs[-4:]

    @only_for(members, own_ref)
    def _():
        turned = values_down(v_ref[...])

        def mix(head, peak):
            peak_ref[head:head + 1, :] = peak
            sum_ref[head] = jnp.dot(turned, weight_ref[head], preferred_element_type=jnp.float32)

        in_stages(range(across_ref.shape[0]), [
            score_stage(k_ref[...], across_ref, bias_ref, 0, scaled_ref, None),
            weight_stage(scaled_ref, weight_ref),
            mix,
        ])


def shrink(head, peak, peak_ref, sum_ref):
    summed = sum_ref[head] * jnp.exp2(peak_ref[head:head + 1, :] - peak)
    peak_ref[head:head + 1, :] = peak
    return summed


def weights_kernel(at, members, heads, own_ref, across_ref, bias_ref, k_ref, *refs):
    peak_ref, sum_ref, weight_ref, scaled_ref = refs[-4:]

    @only_for(members, own_ref)
    def _():
        def rescale(head, peak):
            sum_ref[head] = shrink(head, peak, peak_ref, sum_ref)

        in_stages(heads, [
            score_stage(
                k_ref[...], across_ref, bias_ref, at, scaled_ref,
                lambda head: peak_ref[head:head + 1, :],
            ),
            weight_stage(scaled_ref, weight_ref),
            rescale,
        ])


def values_kernel(weight_ref, v_ref, old_sum_ref, sum_ref):
    turned = values_down(v_ref[...])
    for head in range(sum_ref.shape[0]):
        sum_ref[head] += jnp.dot(turned, weight_ref[head], preferred_element_type=jnp.float32)


def next_kernel(
    at, across_ref, bias_ref, k_ref, v_ref, old_peak_ref, old_sum_ref,
    peak_ref, sum_ref, scaled_ref, weight_ref,
):
    turned = values_down(v_ref[...])

    def mix(head, peak):
        sum_ref[head] = shrink(head, peak, peak_ref, sum_ref) + jnp.dot(
            turned, weight_ref[head], preferred_element_type=jnp.float32
        )

    in_stages(range(across_ref.shape[0]), [
        score_stage(
            k_ref[...], across_ref, bias_ref, at, scaled_ref,
            lambda head: peak_ref[head:head + 1, :],
        ),
        weight_stage(scaled_ref, weight_ref),
        mix,
    ])


def last_kernel(weight_ref, v_ref, sum_ref, out_ref, block_ref, sems):
    turned = values_down(v_ref[...])
    copies = []

    def mix(head, _):
        added = jnp.dot(turned, weight_ref[head], preferred_element_type=jnp.float32)
        summed = sum_ref[head] + added
        share = 1.0 / summed[HEAD_WIDTH:HEAD_WIDTH + 1]
        return (summed[:HEAD_WIDTH] * share).astype(jnp.bfloat16)

    def send(head, out):
        cols = slice(head * HEAD_WIDTH, (head + 1) * HEAD_WIDTH)
        block_ref[:, cols] = jnp.transpose(out)
        copy = pltpu.make_async_copy(block_ref.at[:, cols], out_ref.at[:, cols], sems.at[head])
        copy.start()
        copies.append(copy)

    in_stages(range(sum_ref.shape[0]), [mix, send])
    for copy in copies:
        copy.wait()


SHORT = pl.CostEstimate(flops=0, bytes_accessed=0, transcendentals=0)


def in_vmem(*arrays):
    return [pltpu.with_memory_space_constraint(array, pltpu.VMEM) for array in arrays]


def in_hbm(*arrays):
    return [pltpu.with_memory_space_constraint(array, pltpu.HBM) for array in arrays]


VMEM_REF = pl.BlockSpec(memory_space=pltpu.VMEM)
HBM_REF = pl.BlockSpec(memory_space=pltpu.HBM)
PARAMS = pltpu.CompilerParams(vmem_limit_bytes=32 << 20)


def moved(value, mask):
    return lax.ppermute(value, "seq", [(i, i ^ mask) for i in range(lax.axis_size("seq"))])


def staged_attention(queries, keys, values, lengths, old_place):
    far_keys = moved(keys, 2)
    rows, cols = queries.shape
    heads = cols // HEAD_WIDTH
    devices = lax.axis_size("seq")
    own = lax.axis_index("seq").astype(jnp.int32).reshape(1)
    places = old_place.reshape(1, -1)
    scalar = pl.BlockSpec(memory_space=pltpu.SMEM)
    peak_type = pltpu.VMEM((heads, rows), jnp.float32)
    sum_type = pltpu.VMEM((heads, HEAD_WIDTH + ONES, rows), jnp.float32)
    scaled_type = pltpu.VMEM((heads, rows, rows), jnp.float32)
    weight_type = pltpu.VMEM((heads, rows, rows), jnp.bfloat16)

    def call(kernel, name, ins, outs, scratch, state=(), scalars=()):
        first = len(scalars) + len(ins)
        return pl.pallas_call(
            kernel,
            in_specs=[scalar] * len(scalars) + [VMEM_REF] * (len(ins) + len(state)),
            out_specs=[VMEM_REF] * len(outs),
            out_shape=outs,
            input_output_aliases={first + n: n for n in range(len(state))},
            scratch_shapes=scratch,
            compiler_params=PARAMS,
            cost_estimate=SHORT,
            name=name,
        )(*scalars, *in_vmem(*ins, *state))

    def prepare(members, near=()):
        return pl.pallas_call(
            lambda *refs: prepare_kernel(members, *refs),
            in_specs=[scalar] + [HBM_REF] * 5 + [VMEM_REF] * len(near),
            out_specs=[VMEM_REF] * 4,
            out_shape=[
                pltpu.VMEM((heads, HEAD_WIDTH, rows), jnp.bfloat16),
                pltpu.VMEM((devices, rows, rows), jnp.float32),
                pltpu.VMEM(keys.shape, jnp.bfloat16),
                pltpu.VMEM(values.shape, jnp.bfloat16),
            ],
            input_output_aliases={6 + n: n for n in range(len(near))},
            scratch_shapes=[
                pltpu.SMEM(lengths.shape, jnp.int32),
                pltpu.VMEM(places.shape, jnp.int32),
                pltpu.VMEM(queries.shape, jnp.bfloat16),
                pltpu.SemaphoreType.DMA((5,)),
            ],
            compiler_params=PARAMS,
            cost_estimate=SHORT,
            name="prepare",
        )(own, *in_hbm(lengths, places, queries, keys, values), *in_vmem(*near))

    prepared = prepare((0, 2))
    keys, values, *prepared = lax.optimization_barrier((keys, values, *prepared))
    far_values = moved(values, 2)
    near_keys, near_values = moved(keys, 1), moved(values, 1)
    across, bias, own_keys, own_values = prepare((1, 3), prepared)

    def own_shard(members, state):
        return call(
            lambda *refs: own_kernel(members, *refs), "own_shard",
            (across, bias, own_keys, own_values), [peak_type, sum_type],
            [scaled_type, weight_type], state, (own,),
        )

    def shard_weights(at, members, keys, state, first=0, end=heads):
        return call(
            lambda *refs: weights_kernel(at, members, range(first, end), *refs), "shard_weights",
            (across, bias, keys), [peak_type, sum_type, weight_type],
            [scaled_type], state, (own,),
        )

    state = own_shard((0, 2, 3), ())
    far_keys, *state = lax.optimization_barrier((far_keys, *state))
    third_keys = moved(far_keys, 1)
    state = shard_weights(2, (0, 2), far_keys, state, end=heads // 2)
    far_values, far_keys, *state = lax.optimization_barrier((far_values, far_keys, *state))
    third_values = moved(far_values, 1)
    state = [*own_shard((1,), state[:2]), state[2]]
    state = shard_weights(2, (0, 2), far_keys, state, first=heads // 2)
    peak, summed, weights = shard_weights(2, (1, 3), far_keys, state)
    summed, = call(values_kernel, "shard_values", (weights, far_values), [sum_type], [], (summed,))
    state = call(
        lambda *refs: next_kernel(1, *refs), "next_shard",
        (across, bias, near_keys, near_values), [peak_type, sum_type],
        [scaled_type, weight_type], (peak, summed),
    )
    _, summed, weights = shard_weights(3, (0, 1, 2, 3), third_keys, state)
    return pl.pallas_call(
        last_kernel,
        in_specs=[VMEM_REF] * 3,
        out_specs=pl.BlockSpec(memory_space=pl.ANY),
        out_shape=jax.ShapeDtypeStruct((rows, cols), jnp.bfloat16),
        scratch_shapes=[
            pltpu.VMEM((rows, cols), jnp.bfloat16),
            pltpu.SemaphoreType.DMA((heads,)),
        ],
        compiler_params=PARAMS,
        cost_estimate=SHORT,
        name="last_values",
    )(*in_vmem(weights, third_values, summed))


def online_kernel(heads, q_ref, k_ref, v_ref, key_pos_ref, query_pos_ref, start_ref, out_ref, peak_ref, acc_ref):
    step = pl.program_id(0)

    @pl.when(step == 0)
    def _():
        peak_ref[...] = jnp.full(peak_ref.shape, NEG_FILL, jnp.float32)
        acc_ref[...] = jnp.zeros(acc_ref.shape, jnp.float32)

    key_pos = key_pos_ref[...]
    visible = (key_pos >= start_ref[...]) & (key_pos <= query_pos_ref[...])
    values = v_ref[...]
    ext = jnp.concatenate([values, jnp.ones_like(values)], axis=1)
    for head in range(heads):
        q = q_ref[:, head * HEAD_WIDTH:(head + 1) * HEAD_WIDTH]
        scores = lax.dot_general(
            q, k_ref[...], (((1,), (1,)), ((), ())), preferred_element_type=jnp.float32
        )
        scaled = jnp.where(visible, scores * (HEAD_WIDTH ** -0.5 * LOG2_E), NEG_FILL)
        before = peak_ref[head]
        peak = jnp.maximum(before, jnp.max(scaled, axis=1, keepdims=True))
        weights = jnp.where(visible, jnp.exp2(scaled - peak), 0.0).astype(jnp.bfloat16)
        peak_ref[head] = peak
        acc_ref[head] = acc_ref[head] * jnp.exp2(before - peak) + jnp.dot(
            weights, ext, preferred_element_type=jnp.float32
        )

    @pl.when(step == pl.num_programs(0) - 1)
    def _():
        for head in range(heads):
            acc = acc_ref[head]
            out_ref[:, head * HEAD_WIDTH:(head + 1) * HEAD_WIDTH] = (
                acc[:, :HEAD_WIDTH] / acc[:, HEAD_WIDTH:]
            ).astype(jnp.bfloat16)


def online_attention(queries, keys, values, key_pos, query_pos, starts, chunk):
    rows, cols = queries.shape
    heads = cols // HEAD_WIDTH
    key_count = keys.shape[0]
    return pl.pallas_call(
        lambda *refs: online_kernel(heads, *refs),
        grid=(key_count // chunk,),
        in_specs=[
            pl.BlockSpec((rows, cols), lambda j: (0, 0)),
            pl.BlockSpec((chunk, HEAD_WIDTH), lambda j: (j, 0)),
            pl.BlockSpec((chunk, HEAD_WIDTH), lambda j: (j, 0)),
            pl.BlockSpec((1, chunk), lambda j: (0, j)),
            pl.BlockSpec((rows, 1), lambda j: (0, 0)),
            pl.BlockSpec((rows, 1), lambda j: (0, 0)),
        ],
        out_specs=pl.BlockSpec((rows, cols), lambda j: (0, 0)),
        out_shape=jax.ShapeDtypeStruct((rows, cols), jnp.bfloat16),
        scratch_shapes=[
            pltpu.VMEM((heads, rows, 1), jnp.float32),
            pltpu.VMEM((heads, rows, 2 * HEAD_WIDTH), jnp.float32),
        ],
        compiler_params=pltpu.CompilerParams(vmem_limit_bytes=32 << 20),
        name="online",
    )(queries, keys, values, key_pos, query_pos, starts)


def body(queries, keys, values, lengths, old_place):
    devices = lax.axis_size("seq")
    row_count = queries.shape[0]
    key_count = row_count * devices
    if devices == 4 and key_count <= 1024:
        return staged_attention(queries, keys, values, lengths, old_place)
    all_keys = lax.all_gather(keys, "seq", axis=0, tiled=True)
    all_values = lax.all_gather(values, "seq", axis=0, tiled=True)
    key_pos, query_pos, starts = block_places(
        lengths, old_place, lax.axis_index("seq"), row_count, key_count
    )
    return online_attention(queries, all_keys, all_values, key_pos, query_pos, starts, 512)


def solution(mesh):
    in_specs = (
        P(("groups", "seq"), "mp"),
        P(("groups", "seq"), "mp"),
        P(("groups", "seq"), "mp"),
        P("groups"),
        P("groups"),
    )
    out_specs = P(("groups", "seq"), "mp")
    return jax.shard_map(body, mesh=mesh, in_specs=in_specs, out_specs=out_specs, check_vma=False)
```

```python
import jax
import jax.numpy as jnp
from jax import lax
from jax.experimental import pallas as pl
from jax.experimental.pallas import tpu as pltpu
from jax.sharding import PartitionSpec as P

HEAD_WIDTH = 128
LOG2_E = 1.4426950408889634
NEG_FILL = -1e30
ONES = 16


def block_places(lengths, old_place, own_index, row_count, key_count):
    block_total = old_place.shape[0]
    block_rows = key_count // block_total
    ids = jnp.arange(block_total, dtype=jnp.int32)
    hit = old_place[:, None] == ids[None, :]
    new_block = jnp.sum(jnp.where(hit, ids[:, None], 0), axis=0)
    key_pos = (new_block[:, None] * block_rows + jnp.arange(block_rows, dtype=jnp.int32)).reshape(-1)
    query_pos = lax.dynamic_slice_in_dim(key_pos, own_index * row_count, row_count)
    bounds = jnp.cumsum(lengths)
    starts = jnp.max(jnp.where(bounds[None, :] <= query_pos[:, None], bounds[None, :], 0), axis=1)
    return key_pos.reshape(1, -1), query_pos.reshape(-1, 1), starts.reshape(-1, 1)


def iota(shape, dim):
    return lax.broadcasted_iota(jnp.int32, shape, dim)


def mask_tables(owners, lengths_ref, places_ref, rows, bias_ref):
    block_total = places_ref.shape[1]
    block_rows = rows * lax.axis_size("seq") // block_total
    blocks = rows // block_rows
    places = places_ref[...]
    square = (block_total, block_total)
    as_column = jnp.sum(
        jnp.where(iota(square, 0) == iota(square, 1), places, 0).astype(jnp.float32),
        axis=1, keepdims=True,
    ).astype(jnp.int32)
    across = (block_total, rows)
    hit = as_column == owners[0] * blocks + iota(across, 1) // block_rows
    at = jnp.where(hit, iota(across, 0) * block_rows, 0).astype(jnp.float32)
    query_pos = jnp.sum(at, axis=0, keepdims=True) + (
        iota((1, rows), 1) % block_rows
    ).astype(jnp.float32)
    starts = jnp.zeros_like(query_pos)
    bound = jnp.int32(0)
    for t in range(lengths_ref.shape[0]):
        bound = bound + lengths_ref[t]
        edge = bound.astype(jnp.float32)
        starts = jnp.where(edge <= query_pos, edge, starts)
    down = (rows, block_total)
    for n, owner in enumerate(owners):
        hit = places == owner * blocks + iota(down, 0) // block_rows
        at = jnp.where(hit, iota(down, 1) * block_rows, 0).astype(jnp.float32)
        key_pos = jnp.sum(at, axis=1, keepdims=True) + (
            iota((rows, 1), 0) % block_rows
        ).astype(jnp.float32)
        visible = (key_pos >= starts) & (key_pos <= query_pos)
        bias_ref[n] = jnp.where(visible, 0.0, NEG_FILL)


def values_down(values):
    turned = jnp.transpose(values.astype(jnp.float32)).astype(jnp.bfloat16)
    return jnp.concatenate([turned, jnp.ones((ONES, values.shape[0]), jnp.bfloat16)], axis=0)


def in_stages(heads, stages):
    results = [{} for _ in stages]
    for step in range(heads + len(stages) - 1):
        for late, stage in enumerate(stages):
            head = step - late
            if 0 <= head < heads:
                before = results[late - 1].pop(head) if late else None
                results[late][head] = stage(head, before)


def score_stage(keys, across_ref, bias_ref, at, scaled_ref, old_peak):
    def stage(head, _):
        scores = jnp.dot(keys, across_ref[head], preferred_element_type=jnp.float32)
        scaled = scores * (HEAD_WIDTH ** -0.5 * LOG2_E) + bias_ref[at]
        scaled_ref[head] = scaled
        peak = jnp.max(scaled, axis=0, keepdims=True)
        return peak if old_peak is None else jnp.maximum(old_peak(head), peak)

    return stage


def weight_stage(scaled_ref, weight_ref):
    def stage(head, peak):
        weight_ref[head] = jnp.exp2(scaled_ref[head] - peak).astype(jnp.bfloat16)
        return peak

    return stage


def own_kernel(odd, own_ref, odd_ref, *refs):
    @pl.when(odd_ref[0] == odd)
    def _():
        own_shard(own_ref, *refs[:5], *refs[-12:])


def own_shard(
    own_ref, lengths_hbm, places_hbm, q_hbm, k_hbm, v_hbm,
    across_ref, bias_ref, peak_ref, sum_ref,
    lengths_ref, places_ref, q_ref, k_ref, v_ref, scaled_ref, weight_ref, sems,
):
    moves = (
        (lengths_hbm, lengths_ref), (places_hbm, places_ref),
        (k_hbm, k_ref), (v_hbm, v_ref), (q_hbm, q_ref),
    )
    copies = [pltpu.make_async_copy(*move, sems.at[n]) for n, move in enumerate(moves)]
    for copy in copies:
        copy.start()
    copies[0].wait()
    copies[1].wait()
    heads, _, rows = across_ref.shape
    owners = [own_ref[0] ^ mask for mask in range(bias_ref.shape[0])]
    mask_tables(owners, lengths_ref, places_ref, rows, bias_ref)
    for copy in copies[2:]:
        copy.wait()
    keys = k_ref[...]
    turned = values_down(v_ref[...])

    def turn(head, _):
        q = q_ref[:, head * HEAD_WIDTH:(head + 1) * HEAD_WIDTH]
        across_ref[head] = jnp.transpose(q.astype(jnp.float32)).astype(jnp.bfloat16)

    def mix(head, peak):
        peak_ref[head:head + 1, :] = peak
        sum_ref[head] = jnp.dot(turned, weight_ref[head], preferred_element_type=jnp.float32)

    in_stages(heads, [
        turn,
        score_stage(keys, across_ref, bias_ref, 0, scaled_ref, None),
        weight_stage(scaled_ref, weight_ref),
        mix,
    ])


def joined(head, peak, turned, weight_ref, peak_ref, sum_ref):
    added = jnp.dot(turned, weight_ref[head], preferred_element_type=jnp.float32)
    return sum_ref[head] * jnp.exp2(peak_ref[head:head + 1, :] - peak) + added


def next_kernel(
    at, across_ref, bias_ref, peak_ref, sum_ref, k_ref, v_ref, new_peak_ref, new_sum_ref,
    scaled_ref, weight_ref,
):
    turned = values_down(v_ref[...])

    def mix(head, peak):
        new_peak_ref[head:head + 1, :] = peak
        new_sum_ref[head] = joined(head, peak, turned, weight_ref, peak_ref, sum_ref)

    in_stages(across_ref.shape[0], [
        score_stage(
            k_ref[...], across_ref, bias_ref, at, scaled_ref,
            lambda head: peak_ref[head:head + 1, :],
        ),
        weight_stage(scaled_ref, weight_ref),
        mix,
    ])


def weights_kernel(
    at, across_ref, bias_ref, peak_ref, sum_ref, k_ref, new_sum_ref, weight_ref, scaled_ref,
):
    def rescale(head, peak):
        new_sum_ref[head] = sum_ref[head] * jnp.exp2(peak_ref[head:head + 1, :] - peak)

    in_stages(across_ref.shape[0], [
        score_stage(
            k_ref[...], across_ref, bias_ref, at, scaled_ref,
            lambda head: peak_ref[head:head + 1, :],
        ),
        weight_stage(scaled_ref, weight_ref),
        rescale,
    ])


def last_kernel(sum_ref, weight_ref, v_ref, out_ref, block_ref, sems):
    turned = values_down(v_ref[...])
    copies = []

    def mix(head, _):
        added = jnp.dot(turned, weight_ref[head], preferred_element_type=jnp.float32)
        summed = sum_ref[head] + added
        return summed[:HEAD_WIDTH] / summed[HEAD_WIDTH:HEAD_WIDTH + 1]

    def send(head, out):
        cols = slice(head * HEAD_WIDTH, (head + 1) * HEAD_WIDTH)
        block_ref[:, cols] = jnp.transpose(out).astype(jnp.bfloat16)
        copy = pltpu.make_async_copy(block_ref.at[:, cols], out_ref.at[:, cols], sems.at[head])
        copy.start()
        copies.append(copy)

    in_stages(sum_ref.shape[0], [mix, send])
    for copy in copies:
        copy.wait()


SHORT = pl.CostEstimate(flops=0, bytes_accessed=0, transcendentals=0)


def in_vmem(*arrays):
    return [pltpu.with_memory_space_constraint(array, pltpu.VMEM) for array in arrays]


def in_hbm(*arrays):
    return [pltpu.with_memory_space_constraint(array, pltpu.HBM) for array in arrays]


VMEM_REF = pl.BlockSpec(memory_space=pltpu.VMEM)
HBM_REF = pl.BlockSpec(memory_space=pltpu.HBM)
PARAMS = pltpu.CompilerParams(vmem_limit_bytes=32 << 20)


def moved(value, mask):
    return lax.ppermute(value, "seq", [(i, i ^ mask) for i in range(lax.axis_size("seq"))])


def staged_attention(queries, keys, values, lengths, old_place):
    far_keys = moved(keys, 2)
    rows, cols = queries.shape
    heads = cols // HEAD_WIDTH
    devices = lax.axis_size("seq")
    own = lax.axis_index("seq").astype(jnp.int32)
    places = old_place.reshape(1, -1)
    state = [
        pltpu.VMEM((heads, rows), jnp.float32),
        pltpu.VMEM((heads, HEAD_WIDTH + ONES, rows), jnp.float32),
    ]
    work = [
        pltpu.VMEM((heads, rows, rows), jnp.float32),
        pltpu.VMEM((heads, rows, rows), jnp.bfloat16),
    ]
    odd = (lax.axis_index("mp").astype(jnp.int32) & 1).reshape(1)

    def own_on(parity, before=()):
        return pl.pallas_call(
            lambda *refs: own_kernel(parity, *refs),
            in_specs=[pl.BlockSpec(memory_space=pltpu.SMEM)] * 2
            + [HBM_REF] * 5 + [VMEM_REF] * len(before),
            out_specs=[VMEM_REF] * 4,
            out_shape=[
                pltpu.VMEM((heads, HEAD_WIDTH, rows), jnp.bfloat16),
                pltpu.VMEM((devices, rows, rows), jnp.float32),
            ] + state,
            input_output_aliases={7 + n: n for n in range(len(before))},
            scratch_shapes=[
                pltpu.SMEM(lengths.shape, jnp.int32),
                pltpu.VMEM(places.shape, jnp.int32),
                pltpu.VMEM(queries.shape, jnp.bfloat16),
                pltpu.VMEM(keys.shape, jnp.bfloat16),
                pltpu.VMEM(values.shape, jnp.bfloat16),
            ] + work + [pltpu.SemaphoreType.DMA((5,))],
            compiler_params=PARAMS,
            cost_estimate=SHORT,
            name="own_shard",
        )(own.reshape(1), odd, *in_hbm(lengths, places, queries, keys, values), *in_vmem(*before))

    made = own_on(1)
    keys, values, *made = lax.optimization_barrier((keys, values, *made))
    far_values = moved(values, 2)
    near_keys, near_values = moved(keys, 1), moved(values, 1)
    across, bias, *carried = own_on(0, made)

    def add_shard(at, keys, values, carried):
        return pl.pallas_call(
            lambda *refs: next_kernel(at, *refs),
            in_specs=[VMEM_REF] * 6,
            out_specs=[VMEM_REF] * 2,
            out_shape=state,
            scratch_shapes=work,
            compiler_params=PARAMS,
            cost_estimate=SHORT,
            name="next_shard",
        )(*in_vmem(across, bias, *carried), keys, values)

    far_keys, *carried = lax.optimization_barrier((far_keys, *carried))
    third_keys = moved(far_keys, 1)
    far_values, *carried = lax.optimization_barrier((far_values, *carried))
    third_values = moved(far_values, 1)
    carried = add_shard(2, far_keys, far_values, carried)
    carried = add_shard(1, near_keys, near_values, carried)
    summed, weights = pl.pallas_call(
        lambda *refs: weights_kernel(3, *refs),
        in_specs=[VMEM_REF] * 5,
        out_specs=[VMEM_REF] * 2,
        out_shape=state[1:] + work[1:],
        scratch_shapes=work[:1],
        compiler_params=PARAMS,
        cost_estimate=SHORT,
        name="last_weights",
    )(*in_vmem(across, bias, *carried), third_keys)
    return pl.pallas_call(
        last_kernel,
        in_specs=[VMEM_REF] * 3,
        out_specs=pl.BlockSpec(memory_space=pl.ANY),
        out_shape=jax.ShapeDtypeStruct((rows, cols), jnp.bfloat16),
        scratch_shapes=[
            pltpu.VMEM((rows, cols), jnp.bfloat16),
            pltpu.SemaphoreType.DMA((heads,)),
        ],
        compiler_params=PARAMS,
        cost_estimate=SHORT,
        name="last_values",
    )(*in_vmem(summed, weights), third_values)


def online_kernel(heads, q_ref, k_ref, v_ref, key_pos_ref, query_pos_ref, start_ref, out_ref, peak_ref, acc_ref):
    step = pl.program_id(0)

    @pl.when(step == 0)
    def _():
        peak_ref[...] = jnp.full(peak_ref.shape, NEG_FILL, jnp.float32)
        acc_ref[...] = jnp.zeros(acc_ref.shape, jnp.float32)

    key_pos = key_pos_ref[...]
    visible = (key_pos >= start_ref[...]) & (key_pos <= query_pos_ref[...])
    values = v_ref[...]
    ext = jnp.concatenate([values, jnp.ones_like(values)], axis=1)
    for head in range(heads):
        q = q_ref[:, head * HEAD_WIDTH:(head + 1) * HEAD_WIDTH]
        scores = lax.dot_general(
            q, k_ref[...], (((1,), (1,)), ((), ())), preferred_element_type=jnp.float32
        )
        scaled = jnp.where(visible, scores * (HEAD_WIDTH ** -0.5 * LOG2_E), NEG_FILL)
        before = peak_ref[head]
        peak = jnp.maximum(before, jnp.max(scaled, axis=1, keepdims=True))
        weights = jnp.where(visible, jnp.exp2(scaled - peak), 0.0).astype(jnp.bfloat16)
        peak_ref[head] = peak
        acc_ref[head] = acc_ref[head] * jnp.exp2(before - peak) + jnp.dot(
            weights, ext, preferred_element_type=jnp.float32
        )

    @pl.when(step == pl.num_programs(0) - 1)
    def _():
        for head in range(heads):
            acc = acc_ref[head]
            out_ref[:, head * HEAD_WIDTH:(head + 1) * HEAD_WIDTH] = (
                acc[:, :HEAD_WIDTH] / acc[:, HEAD_WIDTH:]
            ).astype(jnp.bfloat16)


def online_attention(queries, keys, values, key_pos, query_pos, starts, chunk):
    rows, cols = queries.shape
    heads = cols // HEAD_WIDTH
    key_count = keys.shape[0]
    return pl.pallas_call(
        lambda *refs: online_kernel(heads, *refs),
        grid=(key_count // chunk,),
        in_specs=[
            pl.BlockSpec((rows, cols), lambda j: (0, 0)),
            pl.BlockSpec((chunk, HEAD_WIDTH), lambda j: (j, 0)),
            pl.BlockSpec((chunk, HEAD_WIDTH), lambda j: (j, 0)),
            pl.BlockSpec((1, chunk), lambda j: (0, j)),
            pl.BlockSpec((rows, 1), lambda j: (0, 0)),
            pl.BlockSpec((rows, 1), lambda j: (0, 0)),
        ],
        out_specs=pl.BlockSpec((rows, cols), lambda j: (0, 0)),
        out_shape=jax.ShapeDtypeStruct((rows, cols), jnp.bfloat16),
        scratch_shapes=[
            pltpu.VMEM((heads, rows, 1), jnp.float32),
            pltpu.VMEM((heads, rows, 2 * HEAD_WIDTH), jnp.float32),
        ],
        compiler_params=pltpu.CompilerParams(vmem_limit_bytes=32 << 20),
        name="online",
    )(queries, keys, values, key_pos, query_pos, starts)


def body(queries, keys, values, lengths, old_place):
    devices = lax.axis_size("seq")
    row_count = queries.shape[0]
    key_count = row_count * devices
    if devices == 4 and key_count <= 1024:
        return staged_attention(queries, keys, values, lengths, old_place)
    all_keys = lax.all_gather(keys, "seq", axis=0, tiled=True)
    all_values = lax.all_gather(values, "seq", axis=0, tiled=True)
    key_pos, query_pos, starts = block_places(
        lengths, old_place, lax.axis_index("seq"), row_count, key_count
    )
    return online_attention(queries, all_keys, all_values, key_pos, query_pos, starts, 512)


def solution(mesh):
    in_specs = (
        P(("groups", "seq"), "mp"),
        P(("groups", "seq"), "mp"),
        P(("groups", "seq"), "mp"),
        P("groups"),
        P("groups"),
    )
    out_specs = P(("groups", "seq"), "mp")
    return jax.shard_map(body, mesh=mesh, in_specs=in_specs, out_specs=out_specs, check_vma=False)
```

```python
import jax
import jax.numpy as jnp
from jax import lax
from jax.experimental import pallas as pl
from jax.experimental.pallas import tpu as pltpu
from jax.sharding import PartitionSpec as P

HEAD_WIDTH = 128
LOG2_E = 1.4426950408889634
NEG_FILL = -1e30
ONES = 16


def block_places(lengths, old_place, own_index, row_count, key_count):
    block_total = old_place.shape[0]
    block_rows = key_count // block_total
    ids = jnp.arange(block_total, dtype=jnp.int32)
    hit = old_place[:, None] == ids[None, :]
    new_block = jnp.sum(jnp.where(hit, ids[:, None], 0), axis=0)
    key_pos = (new_block[:, None] * block_rows + jnp.arange(block_rows, dtype=jnp.int32)).reshape(-1)
    query_pos = lax.dynamic_slice_in_dim(key_pos, own_index * row_count, row_count)
    bounds = jnp.cumsum(lengths)
    starts = jnp.max(jnp.where(bounds[None, :] <= query_pos[:, None], bounds[None, :], 0), axis=1)
    return key_pos.reshape(1, -1), query_pos.reshape(-1, 1), starts.reshape(-1, 1)


def iota(shape, dim):
    return lax.broadcasted_iota(jnp.int32, shape, dim)


def mask_tables(owners, lengths_ref, places_ref, rows, bias_ref):
    block_total = places_ref.shape[1]
    block_rows = rows * lax.axis_size("seq") // block_total
    blocks = rows // block_rows
    places = places_ref[...]
    square = (block_total, block_total)
    as_column = jnp.sum(
        jnp.where(iota(square, 0) == iota(square, 1), places, 0).astype(jnp.float32),
        axis=1, keepdims=True,
    ).astype(jnp.int32)
    across = (block_total, rows)
    hit = as_column == owners[0] * blocks + iota(across, 1) // block_rows
    at = jnp.where(hit, iota(across, 0) * block_rows, 0).astype(jnp.float32)
    query_pos = jnp.sum(at, axis=0, keepdims=True) + (
        iota((1, rows), 1) % block_rows
    ).astype(jnp.float32)
    starts = jnp.zeros_like(query_pos)
    bound = jnp.int32(0)
    for t in range(lengths_ref.shape[0]):
        bound = bound + lengths_ref[t]
        edge = bound.astype(jnp.float32)
        starts = jnp.where(edge <= query_pos, edge, starts)
    down = (rows, block_total)
    for n, owner in enumerate(owners):
        hit = places == owner * blocks + iota(down, 0) // block_rows
        at = jnp.where(hit, iota(down, 1) * block_rows, 0).astype(jnp.float32)
        key_pos = jnp.sum(at, axis=1, keepdims=True) + (
            iota((rows, 1), 0) % block_rows
        ).astype(jnp.float32)
        visible = (key_pos >= starts) & (key_pos <= query_pos)
        bias_ref[n] = jnp.where(visible, 0.0, NEG_FILL)


def values_down(values):
    turned = jnp.transpose(values.astype(jnp.float32)).astype(jnp.bfloat16)
    return jnp.concatenate([turned, jnp.ones((ONES, values.shape[0]), jnp.bfloat16)], axis=0)


def in_stages(heads, stages):
    results = [{} for _ in stages]
    for step in range(heads + len(stages) - 1):
        for late, stage in enumerate(stages):
            head = step - late
            if 0 <= head < heads:
                before = results[late - 1].pop(head) if late else None
                results[late][head] = stage(head, before)


def score_stage(keys, across_ref, bias_ref, at, scaled_ref, old_peak):
    def stage(head, _):
        scores = jnp.dot(keys, across_ref[head], preferred_element_type=jnp.float32)
        scaled = scores * (HEAD_WIDTH ** -0.5 * LOG2_E) + bias_ref[at]
        scaled_ref[head] = scaled
        peak = jnp.max(scaled, axis=0, keepdims=True)
        return peak if old_peak is None else jnp.maximum(old_peak(head), peak)

    return stage


def weight_stage(scaled_ref, weight_ref):
    def stage(head, peak):
        weight_ref[head] = jnp.exp2(scaled_ref[head] - peak).astype(jnp.bfloat16)
        return peak

    return stage


def own_kernel(
    own_ref, lengths_hbm, places_hbm, q_hbm, k_hbm, v_hbm,
    across_ref, bias_ref, peak_ref, sum_ref,
    lengths_ref, places_ref, q_ref, k_ref, v_ref, scaled_ref, weight_ref, sems,
):
    moves = (
        (lengths_hbm, lengths_ref), (places_hbm, places_ref),
        (k_hbm, k_ref), (v_hbm, v_ref), (q_hbm, q_ref),
    )
    copies = [pltpu.make_async_copy(*move, sems.at[n]) for n, move in enumerate(moves)]
    for copy in copies:
        copy.start()
    copies[0].wait()
    copies[1].wait()
    heads, _, rows = across_ref.shape
    owners = [own_ref[0] ^ mask for mask in range(bias_ref.shape[0])]
    mask_tables(owners, lengths_ref, places_ref, rows, bias_ref)
    for copy in copies[2:]:
        copy.wait()
    keys = k_ref[...]
    turned = values_down(v_ref[...])

    def turn(head, _):
        q = q_ref[:, head * HEAD_WIDTH:(head + 1) * HEAD_WIDTH]
        across_ref[head] = jnp.transpose(q.astype(jnp.float32)).astype(jnp.bfloat16)

    def mix(head, peak):
        peak_ref[head:head + 1, :] = peak
        sum_ref[head] = jnp.dot(turned, weight_ref[head], preferred_element_type=jnp.float32)

    in_stages(heads, [
        turn,
        score_stage(keys, across_ref, bias_ref, 0, scaled_ref, None),
        weight_stage(scaled_ref, weight_ref),
        mix,
    ])


def joined(head, peak, turned, weight_ref, peak_ref, sum_ref):
    added = jnp.dot(turned, weight_ref[head], preferred_element_type=jnp.float32)
    return sum_ref[head] * jnp.exp2(peak_ref[head:head + 1, :] - peak) + added


def next_kernel(
    at, across_ref, bias_ref, peak_ref, sum_ref, k_ref, v_ref, new_peak_ref, new_sum_ref,
    scaled_ref, weight_ref,
):
    turned = values_down(v_ref[...])

    def mix(head, peak):
        new_peak_ref[head:head + 1, :] = peak
        new_sum_ref[head] = joined(head, peak, turned, weight_ref, peak_ref, sum_ref)

    in_stages(across_ref.shape[0], [
        score_stage(
            k_ref[...], across_ref, bias_ref, at, scaled_ref,
            lambda head: peak_ref[head:head + 1, :],
        ),
        weight_stage(scaled_ref, weight_ref),
        mix,
    ])


def weights_kernel(
    at, across_ref, bias_ref, peak_ref, sum_ref, k_ref, new_sum_ref, weight_ref, scaled_ref,
):
    def rescale(head, peak):
        new_sum_ref[head] = sum_ref[head] * jnp.exp2(peak_ref[head:head + 1, :] - peak)

    in_stages(across_ref.shape[0], [
        score_stage(
            k_ref[...], across_ref, bias_ref, at, scaled_ref,
            lambda head: peak_ref[head:head + 1, :],
        ),
        weight_stage(scaled_ref, weight_ref),
        rescale,
    ])


def last_kernel(sum_ref, weight_ref, v_ref, out_ref, block_ref, sems):
    turned = values_down(v_ref[...])
    copies = []

    def mix(head, _):
        added = jnp.dot(turned, weight_ref[head], preferred_element_type=jnp.float32)
        summed = sum_ref[head] + added
        return summed[:HEAD_WIDTH] / summed[HEAD_WIDTH:HEAD_WIDTH + 1]

    def send(head, out):
        cols = slice(head * HEAD_WIDTH, (head + 1) * HEAD_WIDTH)
        block_ref[:, cols] = jnp.transpose(out).astype(jnp.bfloat16)
        copy = pltpu.make_async_copy(block_ref.at[:, cols], out_ref.at[:, cols], sems.at[head])
        copy.start()
        copies.append(copy)

    in_stages(sum_ref.shape[0], [mix, send])
    for copy in copies:
        copy.wait()


SHORT = pl.CostEstimate(flops=0, bytes_accessed=0, transcendentals=0)


def in_vmem(*arrays):
    return [pltpu.with_memory_space_constraint(array, pltpu.VMEM) for array in arrays]


def in_hbm(*arrays):
    return [pltpu.with_memory_space_constraint(array, pltpu.HBM) for array in arrays]


VMEM_REF = pl.BlockSpec(memory_space=pltpu.VMEM)
HBM_REF = pl.BlockSpec(memory_space=pltpu.HBM)
PARAMS = pltpu.CompilerParams(vmem_limit_bytes=32 << 20)


def moved(value, mask):
    return lax.ppermute(value, "seq", [(i, i ^ mask) for i in range(lax.axis_size("seq"))])


def staged_attention(queries, keys, values, lengths, old_place):
    far_keys, far_values = moved(keys, 2), moved(values, 2)
    rows, cols = queries.shape
    heads = cols // HEAD_WIDTH
    devices = lax.axis_size("seq")
    own = lax.axis_index("seq").astype(jnp.int32)
    places = old_place.reshape(1, -1)
    state = [
        pltpu.VMEM((heads, rows), jnp.float32),
        pltpu.VMEM((heads, HEAD_WIDTH + ONES, rows), jnp.float32),
    ]
    work = [
        pltpu.VMEM((heads, rows, rows), jnp.float32),
        pltpu.VMEM((heads, rows, rows), jnp.bfloat16),
    ]
    across, bias, *carried = pl.pallas_call(
        own_kernel,
        in_specs=[pl.BlockSpec(memory_space=pltpu.SMEM)] + [HBM_REF] * 5,
        out_specs=[VMEM_REF] * 4,
        out_shape=[
            pltpu.VMEM((heads, HEAD_WIDTH, rows), jnp.bfloat16),
            pltpu.VMEM((devices, rows, rows), jnp.float32),
        ] + state,
        scratch_shapes=[
            pltpu.SMEM(lengths.shape, jnp.int32),
            pltpu.VMEM(places.shape, jnp.int32),
            pltpu.VMEM(queries.shape, jnp.bfloat16),
            pltpu.VMEM(keys.shape, jnp.bfloat16),
            pltpu.VMEM(values.shape, jnp.bfloat16),
        ] + work + [pltpu.SemaphoreType.DMA((5,))],
        compiler_params=PARAMS,
        cost_estimate=SHORT,
        name="own_shard",
    )(own.reshape(1), *in_hbm(lengths, places, queries, keys, values))

    def add_shard(at, keys, values, carried):
        return pl.pallas_call(
            lambda *refs: next_kernel(at, *refs),
            in_specs=[VMEM_REF] * 6,
            out_specs=[VMEM_REF] * 2,
            out_shape=state,
            scratch_shapes=work,
            compiler_params=PARAMS,
            cost_estimate=SHORT,
            name="next_shard",
        )(*in_vmem(across, bias, *carried), keys, values)

    far_keys, *carried = lax.optimization_barrier((far_keys, *carried))
    third_keys = moved(far_keys, 1)
    far_values, far_keys, *carried = lax.optimization_barrier((far_values, far_keys, *carried))
    third_values = moved(far_values, 1)
    keys, values, far_keys, far_values, *carried = lax.optimization_barrier(
        (keys, values, far_keys, far_values, *carried)
    )
    near_keys, near_values = moved(keys, 1), moved(values, 1)
    carried = add_shard(2, far_keys, far_values, carried)
    carried = add_shard(3, third_keys, third_values, carried)
    summed, weights = pl.pallas_call(
        lambda *refs: weights_kernel(1, *refs),
        in_specs=[VMEM_REF] * 5,
        out_specs=[VMEM_REF] * 2,
        out_shape=state[1:] + work[1:],
        scratch_shapes=work[:1],
        compiler_params=PARAMS,
        cost_estimate=SHORT,
        name="last_weights",
    )(*in_vmem(across, bias, *carried), near_keys)
    return pl.pallas_call(
        last_kernel,
        in_specs=[VMEM_REF] * 3,
        out_specs=pl.BlockSpec(memory_space=pl.ANY),
        out_shape=jax.ShapeDtypeStruct((rows, cols), jnp.bfloat16),
        scratch_shapes=[
            pltpu.VMEM((rows, cols), jnp.bfloat16),
            pltpu.SemaphoreType.DMA((heads,)),
        ],
        compiler_params=PARAMS,
        cost_estimate=SHORT,
        name="last_values",
    )(*in_vmem(summed, weights), near_values)


def online_kernel(heads, q_ref, k_ref, v_ref, key_pos_ref, query_pos_ref, start_ref, out_ref, peak_ref, acc_ref):
    step = pl.program_id(0)

    @pl.when(step == 0)
    def _():
        peak_ref[...] = jnp.full(peak_ref.shape, NEG_FILL, jnp.float32)
        acc_ref[...] = jnp.zeros(acc_ref.shape, jnp.float32)

    key_pos = key_pos_ref[...]
    visible = (key_pos >= start_ref[...]) & (key_pos <= query_pos_ref[...])
    values = v_ref[...]
    ext = jnp.concatenate([values, jnp.ones_like(values)], axis=1)
    for head in range(heads):
        q = q_ref[:, head * HEAD_WIDTH:(head + 1) * HEAD_WIDTH]
        scores = lax.dot_general(
            q, k_ref[...], (((1,), (1,)), ((), ())), preferred_element_type=jnp.float32
        )
        scaled = jnp.where(visible, scores * (HEAD_WIDTH ** -0.5 * LOG2_E), NEG_FILL)
        before = peak_ref[head]
        peak = jnp.maximum(before, jnp.max(scaled, axis=1, keepdims=True))
        weights = jnp.where(visible, jnp.exp2(scaled - peak), 0.0).astype(jnp.bfloat16)
        peak_ref[head] = peak
        acc_ref[head] = acc_ref[head] * jnp.exp2(before - peak) + jnp.dot(
            weights, ext, preferred_element_type=jnp.float32
        )

    @pl.when(step == pl.num_programs(0) - 1)
    def _():
        for head in range(heads):
            acc = acc_ref[head]
            out_ref[:, head * HEAD_WIDTH:(head + 1) * HEAD_WIDTH] = (
                acc[:, :HEAD_WIDTH] / acc[:, HEAD_WIDTH:]
            ).astype(jnp.bfloat16)


def online_attention(queries, keys, values, key_pos, query_pos, starts, chunk):
    rows, cols = queries.shape
    heads = cols // HEAD_WIDTH
    key_count = keys.shape[0]
    return pl.pallas_call(
        lambda *refs: online_kernel(heads, *refs),
        grid=(key_count // chunk,),
        in_specs=[
            pl.BlockSpec((rows, cols), lambda j: (0, 0)),
            pl.BlockSpec((chunk, HEAD_WIDTH), lambda j: (j, 0)),
            pl.BlockSpec((chunk, HEAD_WIDTH), lambda j: (j, 0)),
            pl.BlockSpec((1, chunk), lambda j: (0, j)),
            pl.BlockSpec((rows, 1), lambda j: (0, 0)),
            pl.BlockSpec((rows, 1), lambda j: (0, 0)),
        ],
        out_specs=pl.BlockSpec((rows, cols), lambda j: (0, 0)),
        out_shape=jax.ShapeDtypeStruct((rows, cols), jnp.bfloat16),
        scratch_shapes=[
            pltpu.VMEM((heads, rows, 1), jnp.float32),
            pltpu.VMEM((heads, rows, 2 * HEAD_WIDTH), jnp.float32),
        ],
        compiler_params=pltpu.CompilerParams(vmem_limit_bytes=32 << 20),
        name="online",
    )(queries, keys, values, key_pos, query_pos, starts)


def body(queries, keys, values, lengths, old_place):
    devices = lax.axis_size("seq")
    row_count = queries.shape[0]
    key_count = row_count * devices
    if devices == 4 and key_count <= 1024:
        return staged_attention(queries, keys, values, lengths, old_place)
    all_keys = lax.all_gather(keys, "seq", axis=0, tiled=True)
    all_values = lax.all_gather(values, "seq", axis=0, tiled=True)
    key_pos, query_pos, starts = block_places(
        lengths, old_place, lax.axis_index("seq"), row_count, key_count
    )
    return online_attention(queries, all_keys, all_values, key_pos, query_pos, starts, 512)


def solution(mesh):
    in_specs = (
        P(("groups", "seq"), "mp"),
        P(("groups", "seq"), "mp"),
        P(("groups", "seq"), "mp"),
        P("groups"),
        P("groups"),
    )
    out_specs = P(("groups", "seq"), "mp")
    return jax.shard_map(body, mesh=mesh, in_specs=in_specs, out_specs=out_specs, check_vma=False)
```

```python
import jax
import jax.numpy as jnp
from jax import lax
from jax.experimental import pallas as pl
from jax.experimental.pallas import tpu as pltpu
from jax.sharding import PartitionSpec as P

HEAD_WIDTH = 128
LOG2_E = 1.4426950408889634
NEG_FILL = -1e30
ONES = 16


def block_places(lengths, old_place, own_index, row_count, key_count):
    block_total = old_place.shape[0]
    block_rows = key_count // block_total
    ids = jnp.arange(block_total, dtype=jnp.int32)
    hit = old_place[:, None] == ids[None, :]
    new_block = jnp.sum(jnp.where(hit, ids[:, None], 0), axis=0)
    key_pos = (new_block[:, None] * block_rows + jnp.arange(block_rows, dtype=jnp.int32)).reshape(-1)
    query_pos = lax.dynamic_slice_in_dim(key_pos, own_index * row_count, row_count)
    bounds = jnp.cumsum(lengths)
    starts = jnp.max(jnp.where(bounds[None, :] <= query_pos[:, None], bounds[None, :], 0), axis=1)
    return key_pos.reshape(1, -1), query_pos.reshape(-1, 1), starts.reshape(-1, 1)


def iota(shape, dim):
    return lax.broadcasted_iota(jnp.int32, shape, dim)


def mask_tables(owners, lengths_ref, places_ref, rows, bias_ref):
    block_total = places_ref.shape[1]
    block_rows = rows * lax.axis_size("seq") // block_total
    blocks = rows // block_rows
    places = places_ref[...]
    square = (block_total, block_total)
    as_column = jnp.sum(
        jnp.where(iota(square, 0) == iota(square, 1), places, 0).astype(jnp.float32),
        axis=1, keepdims=True,
    ).astype(jnp.int32)
    across = (block_total, rows)
    hit = as_column == owners[0] * blocks + iota(across, 1) // block_rows
    at = jnp.where(hit, iota(across, 0) * block_rows, 0).astype(jnp.float32)
    query_pos = jnp.sum(at, axis=0, keepdims=True) + (
        iota((1, rows), 1) % block_rows
    ).astype(jnp.float32)
    starts = jnp.zeros_like(query_pos)
    bound = jnp.int32(0)
    for t in range(lengths_ref.shape[0]):
        bound = bound + lengths_ref[t]
        edge = bound.astype(jnp.float32)
        starts = jnp.where(edge <= query_pos, edge, starts)
    down = (rows, block_total)
    for n, owner in enumerate(owners):
        hit = places == owner * blocks + iota(down, 0) // block_rows
        at = jnp.where(hit, iota(down, 1) * block_rows, 0).astype(jnp.float32)
        key_pos = jnp.sum(at, axis=1, keepdims=True) + (
            iota((rows, 1), 0) % block_rows
        ).astype(jnp.float32)
        visible = (key_pos >= starts) & (key_pos <= query_pos)
        bias_ref[n] = jnp.where(visible, 0.0, NEG_FILL)


def values_down(values):
    turned = jnp.transpose(values.astype(jnp.float32)).astype(jnp.bfloat16)
    return jnp.concatenate([turned, jnp.ones((ONES, values.shape[0]), jnp.bfloat16)], axis=0)


def in_stages(heads, stages):
    results = [{} for _ in stages]
    for step in range(heads + len(stages) - 1):
        for late, stage in enumerate(stages):
            head = step - late
            if 0 <= head < heads:
                before = results[late - 1].pop(head) if late else None
                results[late][head] = stage(head, before)


def score_stage(keys, across_ref, bias_ref, at, scaled_ref, old_peak):
    def stage(head, _):
        scores = jnp.dot(keys, across_ref[head], preferred_element_type=jnp.float32)
        scaled = scores * (HEAD_WIDTH ** -0.5 * LOG2_E) + bias_ref[at]
        scaled_ref[head] = scaled
        peak = jnp.max(scaled, axis=0, keepdims=True)
        return peak if old_peak is None else jnp.maximum(old_peak(head), peak)

    return stage


def weight_stage(scaled_ref, weight_ref):
    def stage(head, peak):
        weight_ref[head] = jnp.exp2(scaled_ref[head] - peak).astype(jnp.bfloat16)
        return peak

    return stage


def own_kernel(
    own_ref, lengths_hbm, places_hbm, q_hbm, k_hbm, v_hbm,
    across_ref, bias_ref, peak_ref, sum_ref,
    lengths_ref, places_ref, q_ref, k_ref, v_ref, scaled_ref, weight_ref, sems,
):
    moves = (
        (lengths_hbm, lengths_ref), (places_hbm, places_ref),
        (k_hbm, k_ref), (v_hbm, v_ref), (q_hbm, q_ref),
    )
    copies = [pltpu.make_async_copy(*move, sems.at[n]) for n, move in enumerate(moves)]
    for copy in copies:
        copy.start()
    copies[0].wait()
    copies[1].wait()
    heads, _, rows = across_ref.shape
    owners = [own_ref[0] ^ mask for mask in range(bias_ref.shape[0])]
    mask_tables(owners, lengths_ref, places_ref, rows, bias_ref)
    for copy in copies[2:]:
        copy.wait()
    keys = k_ref[...]
    turned = values_down(v_ref[...])

    def turn(head, _):
        q = q_ref[:, head * HEAD_WIDTH:(head + 1) * HEAD_WIDTH]
        across_ref[head] = jnp.transpose(q.astype(jnp.float32)).astype(jnp.bfloat16)

    def mix(head, peak):
        peak_ref[head:head + 1, :] = peak
        sum_ref[head] = jnp.dot(turned, weight_ref[head], preferred_element_type=jnp.float32)

    in_stages(heads, [
        turn,
        score_stage(keys, across_ref, bias_ref, 0, scaled_ref, None),
        weight_stage(scaled_ref, weight_ref),
        mix,
    ])


def join_kernel(
    shards, across_ref, bias_ref, old_peak_ref, old_sum_ref, *refs,
):
    peak_ref, sum_ref, scaled_ref, weight_ref = refs[-4:]
    heads = across_ref.shape[0]
    keys = [ref[...] for ref in refs[:-4:2]]
    turned = [values_down(ref[...]) for ref in refs[1:-4:2]]

    def peak_before(step):
        source = old_peak_ref if step < heads else peak_ref
        return source[step % heads:step % heads + 1, :]

    def score(step, _):
        shard, head = divmod(step, heads)
        scores = jnp.dot(keys[shard], across_ref[head], preferred_element_type=jnp.float32)
        scaled = scores * (HEAD_WIDTH ** -0.5 * LOG2_E) + bias_ref[shards[shard]]
        scaled_ref[head] = scaled
        return jnp.maximum(peak_before(step), jnp.max(scaled, axis=0, keepdims=True))

    def weigh(step, peak):
        head = step % heads
        weight_ref[head] = jnp.exp2(scaled_ref[head] - peak).astype(jnp.bfloat16)
        return peak

    def mix(step, peak):
        shard, head = divmod(step, heads)
        before = (sum_ref if shard else old_sum_ref)[head] * jnp.exp2(peak_before(step) - peak)
        added = jnp.dot(turned[shard], weight_ref[head], preferred_element_type=jnp.float32)
        sum_ref[head] = before + added
        peak_ref[head:head + 1, :] = peak

    in_stages(heads * len(shards), [score, weigh, mix])


def weights_kernel(
    at, across_ref, bias_ref, peak_ref, sum_ref, k_ref, new_sum_ref, weight_ref, scaled_ref,
):
    def rescale(head, peak):
        new_sum_ref[head] = sum_ref[head] * jnp.exp2(peak_ref[head:head + 1, :] - peak)

    in_stages(across_ref.shape[0], [
        score_stage(
            k_ref[...], across_ref, bias_ref, at, scaled_ref,
            lambda head: peak_ref[head:head + 1, :],
        ),
        weight_stage(scaled_ref, weight_ref),
        rescale,
    ])


def last_kernel(sum_ref, weight_ref, v_ref, out_ref, block_ref, sems):
    turned = values_down(v_ref[...])
    copies = []

    def mix(head, _):
        added = jnp.dot(turned, weight_ref[head], preferred_element_type=jnp.float32)
        summed = sum_ref[head] + added
        return summed[:HEAD_WIDTH] * (1.0 / summed[HEAD_WIDTH:HEAD_WIDTH + 1])

    def send(head, out):
        cols = slice(head * HEAD_WIDTH, (head + 1) * HEAD_WIDTH)
        block_ref[:, cols] = jnp.transpose(out).astype(jnp.bfloat16)
        copy = pltpu.make_async_copy(block_ref.at[:, cols], out_ref.at[:, cols], sems.at[head])
        copy.start()
        copies.append(copy)

    in_stages(sum_ref.shape[0], [mix, send])
    for copy in copies:
        copy.wait()


SHORT = pl.CostEstimate(flops=0, bytes_accessed=0, transcendentals=0)


def in_vmem(*arrays):
    return [pltpu.with_memory_space_constraint(array, pltpu.VMEM) for array in arrays]


def in_hbm(*arrays):
    return [pltpu.with_memory_space_constraint(array, pltpu.HBM) for array in arrays]


VMEM_REF = pl.BlockSpec(memory_space=pltpu.VMEM)
HBM_REF = pl.BlockSpec(memory_space=pltpu.HBM)
PARAMS = pltpu.CompilerParams(vmem_limit_bytes=32 << 20)


def moved(value, mask):
    return lax.ppermute(value, "seq", [(i, i ^ mask) for i in range(lax.axis_size("seq"))])


def staged_attention(queries, keys, values, lengths, old_place):
    far_keys, far_values = moved(keys, 2), moved(values, 2)
    near_keys, near_values = moved(keys, 1), moved(values, 1)
    rows, cols = queries.shape
    heads = cols // HEAD_WIDTH
    devices = lax.axis_size("seq")
    own = lax.axis_index("seq").astype(jnp.int32)
    places = old_place.reshape(1, -1)
    state = [
        pltpu.VMEM((heads, rows), jnp.float32),
        pltpu.VMEM((heads, HEAD_WIDTH + ONES, rows), jnp.float32),
    ]
    work = [
        pltpu.VMEM((heads, rows, rows), jnp.float32),
        pltpu.VMEM((heads, rows, rows), jnp.bfloat16),
    ]
    across, bias, *carried = pl.pallas_call(
        own_kernel,
        in_specs=[pl.BlockSpec(memory_space=pltpu.SMEM)] + [HBM_REF] * 5,
        out_specs=[VMEM_REF] * 4,
        out_shape=[
            pltpu.VMEM((heads, HEAD_WIDTH, rows), jnp.bfloat16),
            pltpu.VMEM((devices, rows, rows), jnp.float32),
        ] + state,
        scratch_shapes=[
            pltpu.SMEM(lengths.shape, jnp.int32),
            pltpu.VMEM(places.shape, jnp.int32),
            pltpu.VMEM(queries.shape, jnp.bfloat16),
            pltpu.VMEM(keys.shape, jnp.bfloat16),
            pltpu.VMEM(values.shape, jnp.bfloat16),
        ] + work + [pltpu.SemaphoreType.DMA((5,))],
        compiler_params=PARAMS,
        cost_estimate=SHORT,
        name="own_shard",
    )(own.reshape(1), *in_hbm(lengths, places, queries, keys, values))

    far_keys, *carried = lax.optimization_barrier((far_keys, *carried))
    third_keys = moved(far_keys, 1)
    far_values, *carried = lax.optimization_barrier((far_values, *carried))
    third_values = moved(far_values, 1)
    carried = pl.pallas_call(
        lambda *refs: join_kernel((2, 1), *refs),
        in_specs=[VMEM_REF] * 8,
        out_specs=[VMEM_REF] * 2,
        out_shape=state,
        scratch_shapes=work,
        compiler_params=PARAMS,
        cost_estimate=SHORT,
        name="join_shards",
    )(*in_vmem(across, bias, *carried), far_keys, far_values, near_keys, near_values)
    summed, weights = pl.pallas_call(
        lambda *refs: weights_kernel(3, *refs),
        in_specs=[VMEM_REF] * 5,
        out_specs=[VMEM_REF] * 2,
        out_shape=state[1:] + work[1:],
        scratch_shapes=work[:1],
        compiler_params=PARAMS,
        cost_estimate=SHORT,
        name="last_weights",
    )(*in_vmem(across, bias, *carried), third_keys)
    return pl.pallas_call(
        last_kernel,
        in_specs=[VMEM_REF] * 3,
        out_specs=pl.BlockSpec(memory_space=pl.ANY),
        out_shape=jax.ShapeDtypeStruct((rows, cols), jnp.bfloat16),
        scratch_shapes=[
            pltpu.VMEM((rows, cols), jnp.bfloat16),
            pltpu.SemaphoreType.DMA((heads,)),
        ],
        compiler_params=PARAMS,
        cost_estimate=SHORT,
        name="last_values",
    )(*in_vmem(summed, weights), third_values)


def online_kernel(heads, q_ref, k_ref, v_ref, key_pos_ref, query_pos_ref, start_ref, out_ref, peak_ref, acc_ref):
    step = pl.program_id(0)

    @pl.when(step == 0)
    def _():
        peak_ref[...] = jnp.full(peak_ref.shape, NEG_FILL, jnp.float32)
        acc_ref[...] = jnp.zeros(acc_ref.shape, jnp.float32)

    key_pos = key_pos_ref[...]
    visible = (key_pos >= start_ref[...]) & (key_pos <= query_pos_ref[...])
    values = v_ref[...]
    ext = jnp.concatenate([values, jnp.ones_like(values)], axis=1)
    for head in range(heads):
        q = q_ref[:, head * HEAD_WIDTH:(head + 1) * HEAD_WIDTH]
        scores = lax.dot_general(
            q, k_ref[...], (((1,), (1,)), ((), ())), preferred_element_type=jnp.float32
        )
        scaled = jnp.where(visible, scores * (HEAD_WIDTH ** -0.5 * LOG2_E), NEG_FILL)
        before = peak_ref[head]
        peak = jnp.maximum(before, jnp.max(scaled, axis=1, keepdims=True))
        weights = jnp.where(visible, jnp.exp2(scaled - peak), 0.0).astype(jnp.bfloat16)
        peak_ref[head] = peak
        acc_ref[head] = acc_ref[head] * jnp.exp2(before - peak) + jnp.dot(
            weights, ext, preferred_element_type=jnp.float32
        )

    @pl.when(step == pl.num_programs(0) - 1)
    def _():
        for head in range(heads):
            acc = acc_ref[head]
            out_ref[:, head * HEAD_WIDTH:(head + 1) * HEAD_WIDTH] = (
                acc[:, :HEAD_WIDTH] / acc[:, HEAD_WIDTH:]
            ).astype(jnp.bfloat16)


def online_attention(queries, keys, values, key_pos, query_pos, starts, chunk):
    rows, cols = queries.shape
    heads = cols // HEAD_WIDTH
    key_count = keys.shape[0]
    return pl.pallas_call(
        lambda *refs: online_kernel(heads, *refs),
        grid=(key_count // chunk,),
        in_specs=[
            pl.BlockSpec((rows, cols), lambda j: (0, 0)),
            pl.BlockSpec((chunk, HEAD_WIDTH), lambda j: (j, 0)),
            pl.BlockSpec((chunk, HEAD_WIDTH), lambda j: (j, 0)),
            pl.BlockSpec((1, chunk), lambda j: (0, j)),
            pl.BlockSpec((rows, 1), lambda j: (0, 0)),
            pl.BlockSpec((rows, 1), lambda j: (0, 0)),
        ],
        out_specs=pl.BlockSpec((rows, cols), lambda j: (0, 0)),
        out_shape=jax.ShapeDtypeStruct((rows, cols), jnp.bfloat16),
        scratch_shapes=[
            pltpu.VMEM((heads, rows, 1), jnp.float32),
            pltpu.VMEM((heads, rows, 2 * HEAD_WIDTH), jnp.float32),
        ],
        compiler_params=pltpu.CompilerParams(vmem_limit_bytes=32 << 20),
        name="online",
    )(queries, keys, values, key_pos, query_pos, starts)


def body(queries, keys, values, lengths, old_place):
    devices = lax.axis_size("seq")
    row_count = queries.shape[0]
    key_count = row_count * devices
    if devices == 4 and key_count <= 1024:
        return staged_attention(queries, keys, values, lengths, old_place)
    all_keys = lax.all_gather(keys, "seq", axis=0, tiled=True)
    all_values = lax.all_gather(values, "seq", axis=0, tiled=True)
    key_pos, query_pos, starts = block_places(
        lengths, old_place, lax.axis_index("seq"), row_count, key_count
    )
    return online_attention(queries, all_keys, all_values, key_pos, query_pos, starts, 512)


def solution(mesh):
    in_specs = (
        P(("groups", "seq"), "mp"),
        P(("groups", "seq"), "mp"),
        P(("groups", "seq"), "mp"),
        P("groups"),
        P("groups"),
    )
    out_specs = P(("groups", "seq"), "mp")
    return jax.shard_map(body, mesh=mesh, in_specs=in_specs, out_specs=out_specs, check_vma=False)
```

```python
import jax
import jax.numpy as jnp
from jax import lax
from jax.experimental import pallas as pl
from jax.experimental.pallas import tpu as pltpu
from jax.sharding import PartitionSpec as P

HEAD_WIDTH = 128
LOG2_E = 1.4426950408889634
NEG_FILL = -1e30
ONES = 16


def block_places(lengths, old_place, own_index, row_count, key_count):
    block_total = old_place.shape[0]
    block_rows = key_count // block_total
    ids = jnp.arange(block_total, dtype=jnp.int32)
    hit = old_place[:, None] == ids[None, :]
    new_block = jnp.sum(jnp.where(hit, ids[:, None], 0), axis=0)
    key_pos = (new_block[:, None] * block_rows + jnp.arange(block_rows, dtype=jnp.int32)).reshape(-1)
    query_pos = lax.dynamic_slice_in_dim(key_pos, own_index * row_count, row_count)
    bounds = jnp.cumsum(lengths)
    starts = jnp.max(jnp.where(bounds[None, :] <= query_pos[:, None], bounds[None, :], 0), axis=1)
    return key_pos.reshape(1, -1), query_pos.reshape(-1, 1), starts.reshape(-1, 1)


def iota(shape, dim):
    return lax.broadcasted_iota(jnp.int32, shape, dim)


def mask_tables(owners, lengths_ref, places_ref, rows, bias_ref):
    block_total = places_ref.shape[1]
    block_rows = rows * lax.axis_size("seq") // block_total
    blocks = rows // block_rows
    places = places_ref[...]
    square = (block_total, block_total)
    as_column = jnp.sum(
        jnp.where(iota(square, 0) == iota(square, 1), places, 0).astype(jnp.float32),
        axis=1, keepdims=True,
    ).astype(jnp.int32)
    across = (block_total, rows)
    hit = as_column == owners[0] * blocks + iota(across, 1) // block_rows
    at = jnp.where(hit, iota(across, 0) * block_rows, 0).astype(jnp.float32)
    query_pos = jnp.sum(at, axis=0, keepdims=True) + (
        iota((1, rows), 1) % block_rows
    ).astype(jnp.float32)
    starts = jnp.zeros_like(query_pos)
    bound = jnp.int32(0)
    for t in range(lengths_ref.shape[0]):
        bound = bound + lengths_ref[t]
        edge = bound.astype(jnp.float32)
        starts = jnp.where(edge <= query_pos, edge, starts)
    down = (rows, block_total)
    for n, owner in enumerate(owners):
        hit = places == owner * blocks + iota(down, 0) // block_rows
        at = jnp.where(hit, iota(down, 1) * block_rows, 0).astype(jnp.float32)
        key_pos = jnp.sum(at, axis=1, keepdims=True) + (
            iota((rows, 1), 0) % block_rows
        ).astype(jnp.float32)
        visible = (key_pos >= starts) & (key_pos <= query_pos)
        bias_ref[n] = jnp.where(visible, 0.0, NEG_FILL)


def values_down(values):
    turned = jnp.transpose(values.astype(jnp.float32)).astype(jnp.bfloat16)
    return jnp.concatenate([turned, jnp.ones((ONES, values.shape[0]), jnp.bfloat16)], axis=0)


def in_stages(heads, stages):
    results = [{} for _ in stages]
    for step in range(heads + len(stages) - 1):
        for late, stage in enumerate(stages):
            head = step - late
            if 0 <= head < heads:
                before = results[late - 1].pop(head) if late else None
                results[late][head] = stage(head, before)


def score_stage(keys, across_ref, bias_ref, at, scaled_ref, old_peak):
    def stage(head, _):
        scores = jnp.dot(keys, across_ref[head], preferred_element_type=jnp.float32)
        scaled = scores * (HEAD_WIDTH ** -0.5 * LOG2_E) + bias_ref[at]
        scaled_ref[head] = scaled
        peak = jnp.max(scaled, axis=0, keepdims=True)
        return peak if old_peak is None else jnp.maximum(old_peak(head), peak)

    return stage


def weight_stage(scaled_ref, weight_ref):
    def stage(head, peak):
        weight_ref[head] = jnp.exp2(scaled_ref[head] - peak).astype(jnp.bfloat16)
        return peak

    return stage


def own_kernel(
    own_ref, lengths_hbm, places_hbm, q_hbm, k_hbm, v_hbm,
    across_ref, bias_ref, peak_ref, sum_ref,
    lengths_ref, places_ref, q_ref, k_ref, v_ref, scaled_ref, weight_ref, sems,
):
    moves = (
        (lengths_hbm, lengths_ref), (places_hbm, places_ref),
        (k_hbm, k_ref), (v_hbm, v_ref), (q_hbm, q_ref),
    )
    copies = [pltpu.make_async_copy(*move, sems.at[n]) for n, move in enumerate(moves)]
    for copy in copies:
        copy.start()
    copies[0].wait()
    copies[1].wait()
    heads, _, rows = across_ref.shape
    owners = [own_ref[0] ^ mask for mask in range(bias_ref.shape[0])]
    mask_tables(owners, lengths_ref, places_ref, rows, bias_ref)
    for copy in copies[2:]:
        copy.wait()
    keys = k_ref[...]
    turned = values_down(v_ref[...])

    def turn(head, _):
        q = q_ref[:, head * HEAD_WIDTH:(head + 1) * HEAD_WIDTH]
        across_ref[head] = jnp.transpose(q.astype(jnp.float32)).astype(jnp.bfloat16)

    def mix(head, peak):
        peak_ref[head:head + 1, :] = peak
        sum_ref[head] = jnp.dot(turned, weight_ref[head], preferred_element_type=jnp.float32)

    in_stages(heads, [
        turn,
        score_stage(keys, across_ref, bias_ref, 0, scaled_ref, None),
        weight_stage(scaled_ref, weight_ref),
        mix,
    ])


def joined(head, peak, turned, weight_ref, peak_ref, sum_ref):
    added = jnp.dot(turned, weight_ref[head], preferred_element_type=jnp.float32)
    return sum_ref[head] * jnp.exp2(peak_ref[head:head + 1, :] - peak) + added


def next_kernel(
    at, across_ref, bias_ref, peak_ref, sum_ref, k_ref, v_ref, new_peak_ref, new_sum_ref,
    scaled_ref, weight_ref,
):
    turned = values_down(v_ref[...])

    def mix(head, peak):
        new_peak_ref[head:head + 1, :] = peak
        new_sum_ref[head] = joined(head, peak, turned, weight_ref, peak_ref, sum_ref)

    in_stages(across_ref.shape[0], [
        score_stage(
            k_ref[...], across_ref, bias_ref, at, scaled_ref,
            lambda head: peak_ref[head:head + 1, :],
        ),
        weight_stage(scaled_ref, weight_ref),
        mix,
    ])


def weights_kernel(
    at, across_ref, bias_ref, peak_ref, sum_ref, k_ref, new_sum_ref, weight_ref, scaled_ref,
):
    def rescale(head, peak):
        new_sum_ref[head] = sum_ref[head] * jnp.exp2(peak_ref[head:head + 1, :] - peak)

    in_stages(across_ref.shape[0], [
        score_stage(
            k_ref[...], across_ref, bias_ref, at, scaled_ref,
            lambda head: peak_ref[head:head + 1, :],
        ),
        weight_stage(scaled_ref, weight_ref),
        rescale,
    ])


def last_kernel(sum_ref, weight_ref, v_ref, out_ref, block_ref, sems):
    turned = values_down(v_ref[...])
    square = (sum_ref.shape[2],) * 2
    unit = (iota(square, 0) == iota(square, 1)).astype(jnp.float32).astype(jnp.bfloat16)
    copies = []

    def mix(head, _):
        added = jnp.dot(turned, weight_ref[head], preferred_element_type=jnp.float32)
        summed = sum_ref[head] + added
        share = 1.0 / summed[HEAD_WIDTH:HEAD_WIDTH + 1]
        return (summed[:HEAD_WIDTH] * share).astype(jnp.bfloat16)

    def send(head, out):
        cols = slice(head * HEAD_WIDTH, (head + 1) * HEAD_WIDTH)
        block_ref[:, cols] = lax.dot_general(
            unit, out, (((1,), (1,)), ((), ())), preferred_element_type=jnp.float32
        ).astype(jnp.bfloat16)
        copy = pltpu.make_async_copy(block_ref.at[:, cols], out_ref.at[:, cols], sems.at[head])
        copy.start()
        copies.append(copy)

    in_stages(sum_ref.shape[0], [mix, send])
    for copy in copies:
        copy.wait()


SHORT = pl.CostEstimate(flops=0, bytes_accessed=0, transcendentals=0)


def in_vmem(*arrays):
    return [pltpu.with_memory_space_constraint(array, pltpu.VMEM) for array in arrays]


def in_hbm(*arrays):
    return [pltpu.with_memory_space_constraint(array, pltpu.HBM) for array in arrays]


VMEM_REF = pl.BlockSpec(memory_space=pltpu.VMEM)
HBM_REF = pl.BlockSpec(memory_space=pltpu.HBM)
PARAMS = pltpu.CompilerParams(vmem_limit_bytes=32 << 20)


def moved(value, mask):
    return lax.ppermute(value, "seq", [(i, i ^ mask) for i in range(lax.axis_size("seq"))])


def staged_attention(queries, keys, values, lengths, old_place):
    far_keys, far_values = moved(keys, 2), moved(values, 2)
    near_keys, near_values = moved(keys, 1), moved(values, 1)
    rows, cols = queries.shape
    heads = cols // HEAD_WIDTH
    devices = lax.axis_size("seq")
    own = lax.axis_index("seq").astype(jnp.int32)
    places = old_place.reshape(1, -1)
    state = [
        pltpu.VMEM((heads, rows), jnp.float32),
        pltpu.VMEM((heads, HEAD_WIDTH + ONES, rows), jnp.float32),
    ]
    work = [
        pltpu.VMEM((heads, rows, rows), jnp.float32),
        pltpu.VMEM((heads, rows, rows), jnp.bfloat16),
    ]
    across, bias, *carried = pl.pallas_call(
        own_kernel,
        in_specs=[pl.BlockSpec(memory_space=pltpu.SMEM)] + [HBM_REF] * 5,
        out_specs=[VMEM_REF] * 4,
        out_shape=[
            pltpu.VMEM((heads, HEAD_WIDTH, rows), jnp.bfloat16),
            pltpu.VMEM((devices, rows, rows), jnp.float32),
        ] + state,
        scratch_shapes=[
            pltpu.SMEM(lengths.shape, jnp.int32),
            pltpu.VMEM(places.shape, jnp.int32),
            pltpu.VMEM(queries.shape, jnp.bfloat16),
            pltpu.VMEM(keys.shape, jnp.bfloat16),
            pltpu.VMEM(values.shape, jnp.bfloat16),
        ] + work + [pltpu.SemaphoreType.DMA((5,))],
        compiler_params=PARAMS,
        cost_estimate=SHORT,
        name="own_shard",
    )(own.reshape(1), *in_hbm(lengths, places, queries, keys, values))

    def add_shard(at, keys, values, carried):
        return pl.pallas_call(
            lambda *refs: next_kernel(at, *refs),
            in_specs=[VMEM_REF] * 6,
            out_specs=[VMEM_REF] * 2,
            out_shape=state,
            scratch_shapes=work,
            compiler_params=PARAMS,
            cost_estimate=SHORT,
            name="next_shard",
        )(*in_vmem(across, bias, *carried), keys, values)

    far_keys, *carried = lax.optimization_barrier((far_keys, *carried))
    third_keys = moved(far_keys, 1)
    far_values, *carried = lax.optimization_barrier((far_values, *carried))
    third_values = moved(far_values, 1)
    carried = add_shard(2, far_keys, far_values, carried)
    carried = add_shard(1, near_keys, near_values, carried)
    summed, weights = pl.pallas_call(
        lambda *refs: weights_kernel(3, *refs),
        in_specs=[VMEM_REF] * 5,
        out_specs=[VMEM_REF] * 2,
        out_shape=state[1:] + work[1:],
        scratch_shapes=work[:1],
        compiler_params=PARAMS,
        cost_estimate=SHORT,
        name="last_weights",
    )(*in_vmem(across, bias, *carried), third_keys)
    return pl.pallas_call(
        last_kernel,
        in_specs=[VMEM_REF] * 3,
        out_specs=pl.BlockSpec(memory_space=pl.ANY),
        out_shape=jax.ShapeDtypeStruct((rows, cols), jnp.bfloat16),
        scratch_shapes=[
            pltpu.VMEM((rows, cols), jnp.bfloat16),
            pltpu.SemaphoreType.DMA((heads,)),
        ],
        compiler_params=PARAMS,
        cost_estimate=SHORT,
        name="last_values",
    )(*in_vmem(summed, weights), third_values)


def online_kernel(heads, q_ref, k_ref, v_ref, key_pos_ref, query_pos_ref, start_ref, out_ref, peak_ref, acc_ref):
    step = pl.program_id(0)

    @pl.when(step == 0)
    def _():
        peak_ref[...] = jnp.full(peak_ref.shape, NEG_FILL, jnp.float32)
        acc_ref[...] = jnp.zeros(acc_ref.shape, jnp.float32)

    key_pos = key_pos_ref[...]
    visible = (key_pos >= start_ref[...]) & (key_pos <= query_pos_ref[...])
    values = v_ref[...]
    ext = jnp.concatenate([values, jnp.ones_like(values)], axis=1)
    for head in range(heads):
        q = q_ref[:, head * HEAD_WIDTH:(head + 1) * HEAD_WIDTH]
        scores = lax.dot_general(
            q, k_ref[...], (((1,), (1,)), ((), ())), preferred_element_type=jnp.float32
        )
        scaled = jnp.where(visible, scores * (HEAD_WIDTH ** -0.5 * LOG2_E), NEG_FILL)
        before = peak_ref[head]
        peak = jnp.maximum(before, jnp.max(scaled, axis=1, keepdims=True))
        weights = jnp.where(visible, jnp.exp2(scaled - peak), 0.0).astype(jnp.bfloat16)
        peak_ref[head] = peak
        acc_ref[head] = acc_ref[head] * jnp.exp2(before - peak) + jnp.dot(
            weights, ext, preferred_element_type=jnp.float32
        )

    @pl.when(step == pl.num_programs(0) - 1)
    def _():
        for head in range(heads):
            acc = acc_ref[head]
            out_ref[:, head * HEAD_WIDTH:(head + 1) * HEAD_WIDTH] = (
                acc[:, :HEAD_WIDTH] / acc[:, HEAD_WIDTH:]
            ).astype(jnp.bfloat16)


def online_attention(queries, keys, values, key_pos, query_pos, starts, chunk):
    rows, cols = queries.shape
    heads = cols // HEAD_WIDTH
    key_count = keys.shape[0]
    return pl.pallas_call(
        lambda *refs: online_kernel(heads, *refs),
        grid=(key_count // chunk,),
        in_specs=[
            pl.BlockSpec((rows, cols), lambda j: (0, 0)),
            pl.BlockSpec((chunk, HEAD_WIDTH), lambda j: (j, 0)),
            pl.BlockSpec((chunk, HEAD_WIDTH), lambda j: (j, 0)),
            pl.BlockSpec((1, chunk), lambda j: (0, j)),
            pl.BlockSpec((rows, 1), lambda j: (0, 0)),
            pl.BlockSpec((rows, 1), lambda j: (0, 0)),
        ],
        out_specs=pl.BlockSpec((rows, cols), lambda j: (0, 0)),
        out_shape=jax.ShapeDtypeStruct((rows, cols), jnp.bfloat16),
        scratch_shapes=[
            pltpu.VMEM((heads, rows, 1), jnp.float32),
            pltpu.VMEM((heads, rows, 2 * HEAD_WIDTH), jnp.float32),
        ],
        compiler_params=pltpu.CompilerParams(vmem_limit_bytes=32 << 20),
        name="online",
    )(queries, keys, values, key_pos, query_pos, starts)


def body(queries, keys, values, lengths, old_place):
    devices = lax.axis_size("seq")
    row_count = queries.shape[0]
    key_count = row_count * devices
    if devices == 4 and key_count <= 1024:
        return staged_attention(queries, keys, values, lengths, old_place)
    all_keys = lax.all_gather(keys, "seq", axis=0, tiled=True)
    all_values = lax.all_gather(values, "seq", axis=0, tiled=True)
    key_pos, query_pos, starts = block_places(
        lengths, old_place, lax.axis_index("seq"), row_count, key_count
    )
    return online_attention(queries, all_keys, all_values, key_pos, query_pos, starts, 512)


def solution(mesh):
    in_specs = (
        P(("groups", "seq"), "mp"),
        P(("groups", "seq"), "mp"),
        P(("groups", "seq"), "mp"),
        P("groups"),
        P("groups"),
    )
    out_specs = P(("groups", "seq"), "mp")
    return jax.shard_map(body, mesh=mesh, in_specs=in_specs, out_specs=out_specs, check_vma=False)
```

```python
import jax
import jax.numpy as jnp
from jax import lax
from jax.experimental import pallas as pl
from jax.experimental.pallas import tpu as pltpu
from jax.sharding import PartitionSpec as P

HEAD_WIDTH = 128
LOG2_E = 1.4426950408889634
NEG_FILL = -1e30


def block_places(lengths, old_place, own_index, row_count, key_count):
    block_total = old_place.shape[0]
    block_rows = key_count // block_total
    ids = jnp.arange(block_total, dtype=jnp.int32)
    hit = old_place[:, None] == ids[None, :]
    new_block = jnp.sum(jnp.where(hit, ids[:, None], 0), axis=0)
    key_pos = (new_block[:, None] * block_rows + jnp.arange(block_rows, dtype=jnp.int32)).reshape(-1)
    query_pos = lax.dynamic_slice_in_dim(key_pos, own_index * row_count, row_count)
    bounds = jnp.cumsum(lengths)
    starts = jnp.max(jnp.where(bounds[None, :] <= query_pos[:, None], bounds[None, :], 0), axis=1)
    return key_pos.reshape(1, -1), query_pos.reshape(-1, 1), starts.reshape(-1, 1)


def iota(shape, dim):
    return lax.broadcasted_iota(jnp.int32, shape, dim)


def row_sum_as_column(places):
    square = (places.shape[1],) * 2
    spread = jnp.where(iota(square, 0) == iota(square, 1), places, 0).astype(jnp.float32)
    return jnp.sum(spread, axis=1, keepdims=True).astype(jnp.int32)


def query_places(own, lengths_ref, places, rows):
    block_total = places.shape[1]
    block_rows = rows * lax.axis_size("seq") // block_total
    shape = (block_total, rows)
    hit = row_sum_as_column(places) == own * (rows // block_rows) + iota(shape, 1) // block_rows
    at = jnp.where(hit, iota(shape, 0) * block_rows, 0).astype(jnp.float32)
    query_pos = jnp.sum(at, axis=0, keepdims=True) + (
        iota((1, rows), 1) % block_rows
    ).astype(jnp.float32)
    starts = jnp.zeros_like(query_pos)
    bound = jnp.int32(0)
    for t in range(lengths_ref.shape[0]):
        bound = bound + lengths_ref[t]
        edge = bound.astype(jnp.float32)
        starts = jnp.where(edge <= query_pos, edge, starts)
    return query_pos, starts


def mask_table(owner, query_pos, starts, places):
    block_total, rows = places.shape[1], query_pos.shape[1]
    block_rows = rows * lax.axis_size("seq") // block_total
    shape = (rows, block_total)
    hit = places == owner * (rows // block_rows) + iota(shape, 0) // block_rows
    at = jnp.where(hit, iota(shape, 1) * block_rows, 0).astype(jnp.float32)
    key_pos = jnp.sum(at, axis=1, keepdims=True) + (
        iota((rows, 1), 0) % block_rows
    ).astype(jnp.float32)
    return jnp.where((key_pos >= starts) & (key_pos <= query_pos), 0.0, NEG_FILL)


def in_stages(heads, stages):
    results = [{} for _ in stages]
    for step in range(heads + len(stages) - 1):
        for late, stage in enumerate(stages):
            head = step - late
            if 0 <= head < heads:
                before = results[late - 1].pop(head) if late else None
                results[late][head] = stage(head, before)


def score_stage(keys, across_ref, bias_ref, at, scaled_ref, old_peak):
    def stage(head, _):
        scores = jnp.dot(keys, across_ref[head], preferred_element_type=jnp.float32)
        scaled = scores * (HEAD_WIDTH ** -0.5 * LOG2_E) + bias_ref[at]
        scaled_ref[head] = scaled
        peak = jnp.max(scaled, axis=0, keepdims=True)
        return peak if old_peak is None else jnp.maximum(old_peak(head), peak)

    return stage


def weight_stage(scaled_ref, weight_ref):
    def stage(head, peak):
        weights = jnp.exp2(scaled_ref[head] - peak)
        weight_ref[head] = weights.astype(jnp.bfloat16)
        return peak, jnp.sum(weights, axis=0, keepdims=True)

    return stage


def own_kernel(
    own_ref, lengths_hbm, places_hbm, q_hbm, k_hbm, v_hbm,
    across_ref, bias_ref, peak_ref, total_ref, sum_ref,
    lengths_ref, places_ref, q_ref, k_ref, v_ref, scaled_ref, weight_ref, sems,
):
    moves = (
        (lengths_hbm, lengths_ref), (places_hbm, places_ref),
        (k_hbm, k_ref), (v_hbm, v_ref), (q_hbm, q_ref),
    )
    copies = [pltpu.make_async_copy(*move, sems.at[n]) for n, move in enumerate(moves)]
    for copy in copies:
        copy.start()
    for copy in copies:
        copy.wait()
    heads, _, rows = across_ref.shape
    own, places = own_ref[0], places_ref[...]
    keys = k_ref[...]
    query_pos, starts = query_places(own, lengths_ref, places, rows)
    bias_ref[0] = mask_table(own, query_pos, starts, places)
    turned = jnp.transpose(v_ref[...])

    def turn(head, _):
        q = q_ref[:, head * HEAD_WIDTH:(head + 1) * HEAD_WIDTH]
        across_ref[head] = jnp.transpose(q)
        if 0 < head < bias_ref.shape[0]:
            bias_ref[head] = mask_table(own ^ head, query_pos, starts, places)

    def mix(head, reached):
        peak_ref[head:head + 1, :], total_ref[head:head + 1, :] = reached
        sum_ref[head] = jnp.dot(turned, weight_ref[head], preferred_element_type=jnp.float32)

    in_stages(heads, [
        turn,
        score_stage(keys, across_ref, bias_ref, 0, scaled_ref, None),
        weight_stage(scaled_ref, weight_ref),
        mix,
    ])


def next_kernel(
    at, across_ref, bias_ref, peak_ref, total_ref, sum_ref, k_ref, v_ref,
    new_peak_ref, new_total_ref, new_sum_ref, scaled_ref, weight_ref,
):
    turned = jnp.transpose(v_ref[...])

    def mix(head, reached):
        peak, total = reached
        row = slice(head, head + 1)
        factor = jnp.exp2(peak_ref[row, :] - peak)
        new_peak_ref[row, :] = peak
        new_total_ref[row, :] = total_ref[row, :] * factor + total
        added = jnp.dot(turned, weight_ref[head], preferred_element_type=jnp.float32)
        new_sum_ref[head] = sum_ref[head] * factor + added

    in_stages(across_ref.shape[0], [
        score_stage(
            k_ref[...], across_ref, bias_ref, at, scaled_ref,
            lambda head: peak_ref[head:head + 1, :],
        ),
        weight_stage(scaled_ref, weight_ref),
        mix,
    ])


def weights_kernel(
    at, across_ref, bias_ref, peak_ref, total_ref, sum_ref, k_ref,
    new_sum_ref, weight_ref, share_ref, scaled_ref,
):
    def rescale(head, reached):
        peak, total = reached
        row = slice(head, head + 1)
        factor = jnp.exp2(peak_ref[row, :] - peak)
        share = 1.0 / (total_ref[row, :] * factor + total)
        share_ref[row, :] = share
        new_sum_ref[head] = sum_ref[head] * (factor * share)

    in_stages(across_ref.shape[0], [
        score_stage(
            k_ref[...], across_ref, bias_ref, at, scaled_ref,
            lambda head: peak_ref[head:head + 1, :],
        ),
        weight_stage(scaled_ref, weight_ref),
        rescale,
    ])


def last_kernel(sum_ref, weight_ref, share_ref, v_ref, out_ref, block_ref, sems):
    turned = jnp.transpose(v_ref[...])
    copies = []

    def mix(head, _):
        added = jnp.dot(turned, weight_ref[head], preferred_element_type=jnp.float32)
        return (sum_ref[head] + added * share_ref[head:head + 1, :]).astype(jnp.bfloat16)

    def send(head, out):
        cols = slice(head * HEAD_WIDTH, (head + 1) * HEAD_WIDTH)
        block_ref[:, cols] = jnp.transpose(out)
        copy = pltpu.make_async_copy(block_ref.at[:, cols], out_ref.at[:, cols], sems.at[head])
        copy.start()
        copies.append(copy)

    in_stages(sum_ref.shape[0], [mix, send])
    for copy in copies:
        copy.wait()


SHORT = pl.CostEstimate(flops=0, bytes_accessed=0, transcendentals=0)


def in_vmem(*arrays):
    return [pltpu.with_memory_space_constraint(array, pltpu.VMEM) for array in arrays]


def in_hbm(*arrays):
    return [pltpu.with_memory_space_constraint(array, pltpu.HBM) for array in arrays]


VMEM_REF = pl.BlockSpec(memory_space=pltpu.VMEM)
HBM_REF = pl.BlockSpec(memory_space=pltpu.HBM)
PARAMS = pltpu.CompilerParams(vmem_limit_bytes=32 << 20)


def moved(value, mask):
    return lax.ppermute(value, "seq", [(i, i ^ mask) for i in range(lax.axis_size("seq"))])


def staged_attention(queries, keys, values, lengths, old_place):
    far_keys, far_values = moved(keys, 2), moved(values, 2)
    near_keys, near_values = moved(keys, 1), moved(values, 1)
    rows, cols = queries.shape
    heads = cols // HEAD_WIDTH
    devices = lax.axis_size("seq")
    own = lax.axis_index("seq").astype(jnp.int32)
    places = old_place.reshape(1, -1)
    state = [
        pltpu.VMEM((heads, rows), jnp.float32),
        pltpu.VMEM((heads, rows), jnp.float32),
        pltpu.VMEM((heads, HEAD_WIDTH, rows), jnp.float32),
    ]
    work = [
        pltpu.VMEM((heads, rows, rows), jnp.float32),
        pltpu.VMEM((heads, rows, rows), jnp.bfloat16),
    ]
    across, bias, *carried = pl.pallas_call(
        own_kernel,
        in_specs=[pl.BlockSpec(memory_space=pltpu.SMEM)] + [HBM_REF] * 5,
        out_specs=[VMEM_REF] * 5,
        out_shape=[
            pltpu.VMEM((heads, HEAD_WIDTH, rows), jnp.bfloat16),
            pltpu.VMEM((devices, rows, rows), jnp.float32),
        ] + state,
        scratch_shapes=[
            pltpu.SMEM(lengths.shape, jnp.int32),
            pltpu.VMEM(places.shape, jnp.int32),
            pltpu.VMEM(queries.shape, jnp.bfloat16),
            pltpu.VMEM(keys.shape, jnp.bfloat16),
            pltpu.VMEM(values.shape, jnp.bfloat16),
        ] + work + [pltpu.SemaphoreType.DMA((5,))],
        compiler_params=PARAMS,
        cost_estimate=SHORT,
        name="own_shard",
    )(own.reshape(1), *in_hbm(lengths, places, queries, keys, values))

    def add_shard(at, keys, values, carried):
        return pl.pallas_call(
            lambda *refs: next_kernel(at, *refs),
            in_specs=[VMEM_REF] * 7,
            out_specs=[VMEM_REF] * 3,
            out_shape=state,
            scratch_shapes=work,
            compiler_params=PARAMS,
            cost_estimate=SHORT,
            name="next_shard",
        )(*in_vmem(across, bias, *carried), keys, values)

    far_keys, *carried = lax.optimization_barrier((far_keys, *carried))
    third_keys = moved(far_keys, 1)
    far_values, *carried = lax.optimization_barrier((far_values, *carried))
    third_values = moved(far_values, 1)
    carried = add_shard(2, far_keys, far_values, carried)
    carried = add_shard(1, near_keys, near_values, carried)
    scaled_sum = pltpu.VMEM((heads, HEAD_WIDTH, rows), jnp.float32)
    last = pl.pallas_call(
        lambda *refs: weights_kernel(3, *refs),
        in_specs=[VMEM_REF] * 6,
        out_specs=[VMEM_REF] * 3,
        out_shape=[scaled_sum, work[1], state[0]],
        scratch_shapes=work[:1],
        compiler_params=PARAMS,
        cost_estimate=SHORT,
        name="last_weights",
    )(*in_vmem(across, bias, *carried), third_keys)
    return pl.pallas_call(
        last_kernel,
        in_specs=[VMEM_REF] * 4,
        out_specs=pl.BlockSpec(memory_space=pl.ANY),
        out_shape=jax.ShapeDtypeStruct((rows, cols), jnp.bfloat16),
        scratch_shapes=[
            pltpu.VMEM((rows, cols), jnp.bfloat16),
            pltpu.SemaphoreType.DMA((heads,)),
        ],
        compiler_params=PARAMS,
        cost_estimate=SHORT,
        name="last_values",
    )(*in_vmem(*last), third_values)


def online_kernel(heads, q_ref, k_ref, v_ref, key_pos_ref, query_pos_ref, start_ref, out_ref, peak_ref, acc_ref):
    step = pl.program_id(0)

    @pl.when(step == 0)
    def _():
        peak_ref[...] = jnp.full(peak_ref.shape, NEG_FILL, jnp.float32)
        acc_ref[...] = jnp.zeros(acc_ref.shape, jnp.float32)

    key_pos = key_pos_ref[...]
    visible = (key_pos >= start_ref[...]) & (key_pos <= query_pos_ref[...])
    values = v_ref[...]
    ext = jnp.concatenate([values, jnp.ones_like(values)], axis=1)
    for head in range(heads):
        q = q_ref[:, head * HEAD_WIDTH:(head + 1) * HEAD_WIDTH]
        scores = lax.dot_general(
            q, k_ref[...], (((1,), (1,)), ((), ())), preferred_element_type=jnp.float32
        )
        scaled = jnp.where(visible, scores * (HEAD_WIDTH ** -0.5 * LOG2_E), NEG_FILL)
        before = peak_ref[head]
        peak = jnp.maximum(before, jnp.max(scaled, axis=1, keepdims=True))
        weights = jnp.where(visible, jnp.exp2(scaled - peak), 0.0).astype(jnp.bfloat16)
        peak_ref[head] = peak
        acc_ref[head] = acc_ref[head] * jnp.exp2(before - peak) + jnp.dot(
            weights, ext, preferred_element_type=jnp.float32
        )

    @pl.when(step == pl.num_programs(0) - 1)
    def _():
        for head in range(heads):
            acc = acc_ref[head]
            out_ref[:, head * HEAD_WIDTH:(head + 1) * HEAD_WIDTH] = (
                acc[:, :HEAD_WIDTH] / acc[:, HEAD_WIDTH:]
            ).astype(jnp.bfloat16)


def online_attention(queries, keys, values, key_pos, query_pos, starts, chunk):
    rows, cols = queries.shape
    heads = cols // HEAD_WIDTH
    key_count = keys.shape[0]
    return pl.pallas_call(
        lambda *refs: online_kernel(heads, *refs),
        grid=(key_count // chunk,),
        in_specs=[
            pl.BlockSpec((rows, cols), lambda j: (0, 0)),
            pl.BlockSpec((chunk, HEAD_WIDTH), lambda j: (j, 0)),
            pl.BlockSpec((chunk, HEAD_WIDTH), lambda j: (j, 0)),
            pl.BlockSpec((1, chunk), lambda j: (0, j)),
            pl.BlockSpec((rows, 1), lambda j: (0, 0)),
            pl.BlockSpec((rows, 1), lambda j: (0, 0)),
        ],
        out_specs=pl.BlockSpec((rows, cols), lambda j: (0, 0)),
        out_shape=jax.ShapeDtypeStruct((rows, cols), jnp.bfloat16),
        scratch_shapes=[
            pltpu.VMEM((heads, rows, 1), jnp.float32),
            pltpu.VMEM((heads, rows, 2 * HEAD_WIDTH), jnp.float32),
        ],
        compiler_params=pltpu.CompilerParams(vmem_limit_bytes=32 << 20),
        name="online",
    )(queries, keys, values, key_pos, query_pos, starts)


def body(queries, keys, values, lengths, old_place):
    devices = lax.axis_size("seq")
    row_count = queries.shape[0]
    key_count = row_count * devices
    if devices == 4 and key_count <= 1024:
        return staged_attention(queries, keys, values, lengths, old_place)
    all_keys = lax.all_gather(keys, "seq", axis=0, tiled=True)
    all_values = lax.all_gather(values, "seq", axis=0, tiled=True)
    key_pos, query_pos, starts = block_places(
        lengths, old_place, lax.axis_index("seq"), row_count, key_count
    )
    return online_attention(queries, all_keys, all_values, key_pos, query_pos, starts, 512)


def solution(mesh):
    in_specs = (
        P(("groups", "seq"), "mp"),
        P(("groups", "seq"), "mp"),
        P(("groups", "seq"), "mp"),
        P("groups"),
        P("groups"),
    )
    out_specs = P(("groups", "seq"), "mp")
    return jax.shard_map(body, mesh=mesh, in_specs=in_specs, out_specs=out_specs, check_vma=False)
```

```python
import jax
import jax.numpy as jnp
from jax import lax
from jax.experimental import pallas as pl
from jax.experimental.pallas import tpu as pltpu
from jax.sharding import PartitionSpec as P

HEAD_WIDTH = 128
LOG2_E = 1.4426950408889634
NEG_FILL = -1e30


def block_places(lengths, old_place, own_index, row_count, key_count):
    block_total = old_place.shape[0]
    block_rows = key_count // block_total
    ids = jnp.arange(block_total, dtype=jnp.int32)
    hit = old_place[:, None] == ids[None, :]
    new_block = jnp.sum(jnp.where(hit, ids[:, None], 0), axis=0)
    key_pos = (new_block[:, None] * block_rows + jnp.arange(block_rows, dtype=jnp.int32)).reshape(-1)
    query_pos = lax.dynamic_slice_in_dim(key_pos, own_index * row_count, row_count)
    bounds = jnp.cumsum(lengths)
    starts = jnp.max(jnp.where(bounds[None, :] <= query_pos[:, None], bounds[None, :], 0), axis=1)
    return key_pos.reshape(1, -1), query_pos.reshape(-1, 1), starts.reshape(-1, 1)


def iota(shape, dim):
    return lax.broadcasted_iota(jnp.int32, shape, dim)


def row_sum_as_column(places):
    square = (places.shape[1],) * 2
    spread = jnp.where(iota(square, 0) == iota(square, 1), places, 0).astype(jnp.float32)
    return jnp.sum(spread, axis=1, keepdims=True).astype(jnp.int32)


def query_places(own, lengths_ref, places, rows):
    block_total = places.shape[1]
    block_rows = rows * lax.axis_size("seq") // block_total
    shape = (block_total, rows)
    hit = row_sum_as_column(places) == own * (rows // block_rows) + iota(shape, 1) // block_rows
    at = jnp.where(hit, iota(shape, 0) * block_rows, 0).astype(jnp.float32)
    query_pos = jnp.sum(at, axis=0, keepdims=True) + (
        iota((1, rows), 1) % block_rows
    ).astype(jnp.float32)
    starts = jnp.zeros_like(query_pos)
    bound = jnp.int32(0)
    for t in range(lengths_ref.shape[0]):
        bound = bound + lengths_ref[t]
        edge = bound.astype(jnp.float32)
        starts = jnp.where(edge <= query_pos, edge, starts)
    return query_pos, starts


def mask_table(owner, query_pos, starts, places):
    block_total, rows = places.shape[1], query_pos.shape[1]
    block_rows = rows * lax.axis_size("seq") // block_total
    shape = (rows, block_total)
    hit = places == owner * (rows // block_rows) + iota(shape, 0) // block_rows
    at = jnp.where(hit, iota(shape, 1) * block_rows, 0).astype(jnp.float32)
    key_pos = jnp.sum(at, axis=1, keepdims=True) + (
        iota((rows, 1), 0) % block_rows
    ).astype(jnp.float32)
    return jnp.where((key_pos >= starts) & (key_pos <= query_pos), 0.0, NEG_FILL)


def in_stages(heads, stages):
    results = [{} for _ in stages]
    for step in range(heads + len(stages) - 1):
        for late, stage in enumerate(stages):
            head = step - late
            if 0 <= head < heads:
                before = results[late - 1].pop(head) if late else None
                results[late][head] = stage(head, before)


def score_stage(keys, across_ref, bias_ref, at, old_peak):
    def stage(head, _):
        scores = jnp.dot(keys, across_ref[head], preferred_element_type=jnp.float32)
        scaled = scores * (HEAD_WIDTH ** -0.5 * LOG2_E) + bias_ref[at]
        peak = jnp.max(scaled, axis=0, keepdims=True)
        return scaled, peak if old_peak is None else jnp.maximum(old_peak(head), peak)

    return stage


def weight_stage(head, before):
    scaled, peak = before
    weights = jnp.exp2(scaled - peak)
    return peak, jnp.sum(weights, axis=0, keepdims=True), weights.astype(jnp.bfloat16)


def own_kernel(
    own_ref, lengths_hbm, places_hbm, q_hbm, k_hbm, v_hbm,
    across_ref, bias_ref, peak_ref, total_ref, sum_ref,
    lengths_ref, places_ref, q_ref, k_ref, v_ref, sems,
):
    moves = (
        (lengths_hbm, lengths_ref), (places_hbm, places_ref),
        (k_hbm, k_ref), (v_hbm, v_ref), (q_hbm, q_ref),
    )
    copies = [pltpu.make_async_copy(*move, sems.at[n]) for n, move in enumerate(moves)]
    for copy in copies:
        copy.start()
    for copy in copies:
        copy.wait()
    heads, _, rows = across_ref.shape
    own, places = own_ref[0], places_ref[...]
    keys = k_ref[...]
    query_pos, starts = query_places(own, lengths_ref, places, rows)
    bias_ref[0] = mask_table(own, query_pos, starts, places)
    turned = jnp.transpose(v_ref[...])

    def turn(head, _):
        q = q_ref[:, head * HEAD_WIDTH:(head + 1) * HEAD_WIDTH]
        across_ref[head] = jnp.transpose(q)
        if 0 < head < bias_ref.shape[0]:
            bias_ref[head] = mask_table(own ^ head, query_pos, starts, places)

    def mix(head, reached):
        peak_ref[head:head + 1, :], total_ref[head:head + 1, :], weights = reached
        sum_ref[head] = jnp.dot(turned, weights, preferred_element_type=jnp.float32)

    in_stages(heads, [
        turn,
        score_stage(keys, across_ref, bias_ref, 0, None),
        weight_stage,
        mix,
    ])


def next_kernel(
    at, across_ref, bias_ref, peak_ref, total_ref, sum_ref, k_ref, v_ref,
    new_peak_ref, new_total_ref, new_sum_ref,
):
    turned = jnp.transpose(v_ref[...])

    def mix(head, reached):
        peak, total, weights = reached
        row = slice(head, head + 1)
        factor = jnp.exp2(peak_ref[row, :] - peak)
        new_peak_ref[row, :] = peak
        new_total_ref[row, :] = total_ref[row, :] * factor + total
        added = jnp.dot(turned, weights, preferred_element_type=jnp.float32)
        new_sum_ref[head] = sum_ref[head] * factor + added

    in_stages(across_ref.shape[0], [
        score_stage(
            k_ref[...], across_ref, bias_ref, at,
            lambda head: peak_ref[head:head + 1, :],
        ),
        weight_stage,
        mix,
    ])


def weights_kernel(
    at, across_ref, bias_ref, peak_ref, total_ref, sum_ref, k_ref,
    new_sum_ref, weight_ref, share_ref,
):
    def rescale(head, reached):
        peak, total, weight_ref[head] = reached
        row = slice(head, head + 1)
        factor = jnp.exp2(peak_ref[row, :] - peak)
        share = 1.0 / (total_ref[row, :] * factor + total)
        share_ref[row, :] = share
        new_sum_ref[head] = sum_ref[head] * (factor * share)

    in_stages(across_ref.shape[0], [
        score_stage(
            k_ref[...], across_ref, bias_ref, at,
            lambda head: peak_ref[head:head + 1, :],
        ),
        weight_stage,
        rescale,
    ])


def last_kernel(sum_ref, weight_ref, share_ref, v_ref, out_ref, block_ref, sems):
    turned = jnp.transpose(v_ref[...])
    copies = []

    def mix(head, _):
        added = jnp.dot(turned, weight_ref[head], preferred_element_type=jnp.float32)
        return (sum_ref[head] + added * share_ref[head:head + 1, :]).astype(jnp.bfloat16)

    def send(head, out):
        cols = slice(head * HEAD_WIDTH, (head + 1) * HEAD_WIDTH)
        block_ref[:, cols] = jnp.transpose(out)
        copy = pltpu.make_async_copy(block_ref.at[:, cols], out_ref.at[:, cols], sems.at[head])
        copy.start()
        copies.append(copy)

    in_stages(sum_ref.shape[0], [mix, send])
    for copy in copies:
        copy.wait()


SHORT = pl.CostEstimate(flops=0, bytes_accessed=0, transcendentals=0)


def in_vmem(*arrays):
    return [pltpu.with_memory_space_constraint(array, pltpu.VMEM) for array in arrays]


def in_hbm(*arrays):
    return [pltpu.with_memory_space_constraint(array, pltpu.HBM) for array in arrays]


VMEM_REF = pl.BlockSpec(memory_space=pltpu.VMEM)
HBM_REF = pl.BlockSpec(memory_space=pltpu.HBM)
PARAMS = pltpu.CompilerParams(vmem_limit_bytes=32 << 20)


def moved(value, mask):
    return lax.ppermute(value, "seq", [(i, i ^ mask) for i in range(lax.axis_size("seq"))])


def staged_attention(queries, keys, values, lengths, old_place):
    far_keys, far_values = moved(keys, 2), moved(values, 2)
    near_keys, near_values = moved(keys, 1), moved(values, 1)
    rows, cols = queries.shape
    heads = cols // HEAD_WIDTH
    devices = lax.axis_size("seq")
    own = lax.axis_index("seq").astype(jnp.int32)
    places = old_place.reshape(1, -1)
    state = [
        pltpu.VMEM((heads, rows), jnp.float32),
        pltpu.VMEM((heads, rows), jnp.float32),
        pltpu.VMEM((heads, HEAD_WIDTH, rows), jnp.float32),
    ]
    weight_type = pltpu.VMEM((heads, rows, rows), jnp.bfloat16)
    across, bias, *carried = pl.pallas_call(
        own_kernel,
        in_specs=[pl.BlockSpec(memory_space=pltpu.SMEM)] + [HBM_REF] * 5,
        out_specs=[VMEM_REF] * 5,
        out_shape=[
            pltpu.VMEM((heads, HEAD_WIDTH, rows), jnp.bfloat16),
            pltpu.VMEM((devices, rows, rows), jnp.float32),
        ] + state,
        scratch_shapes=[
            pltpu.SMEM(lengths.shape, jnp.int32),
            pltpu.VMEM(places.shape, jnp.int32),
            pltpu.VMEM(queries.shape, jnp.bfloat16),
            pltpu.VMEM(keys.shape, jnp.bfloat16),
            pltpu.VMEM(values.shape, jnp.bfloat16),
            pltpu.SemaphoreType.DMA((5,)),
        ],
        compiler_params=PARAMS,
        cost_estimate=SHORT,
        name="own_shard",
    )(own.reshape(1), *in_hbm(lengths, places, queries, keys, values))

    def add_shard(at, keys, values, carried):
        return pl.pallas_call(
            lambda *refs: next_kernel(at, *refs),
            in_specs=[VMEM_REF] * 7,
            out_specs=[VMEM_REF] * 3,
            out_shape=state,
            compiler_params=PARAMS,
            cost_estimate=SHORT,
            name="next_shard",
        )(*in_vmem(across, bias, *carried), keys, values)

    far_keys, *carried = lax.optimization_barrier((far_keys, *carried))
    third_keys = moved(far_keys, 1)
    far_values, *carried = lax.optimization_barrier((far_values, *carried))
    third_values = moved(far_values, 1)
    carried = add_shard(2, far_keys, far_values, carried)
    carried = add_shard(1, near_keys, near_values, carried)
    scaled_sum = pltpu.VMEM((heads, HEAD_WIDTH, rows), jnp.float32)
    last = pl.pallas_call(
        lambda *refs: weights_kernel(3, *refs),
        in_specs=[VMEM_REF] * 6,
        out_specs=[VMEM_REF] * 3,
        out_shape=[scaled_sum, weight_type, state[0]],
        compiler_params=PARAMS,
        cost_estimate=SHORT,
        name="last_weights",
    )(*in_vmem(across, bias, *carried), third_keys)
    return pl.pallas_call(
        last_kernel,
        in_specs=[VMEM_REF] * 4,
        out_specs=pl.BlockSpec(memory_space=pl.ANY),
        out_shape=jax.ShapeDtypeStruct((rows, cols), jnp.bfloat16),
        scratch_shapes=[
            pltpu.VMEM((rows, cols), jnp.bfloat16),
            pltpu.SemaphoreType.DMA((heads,)),
        ],
        compiler_params=PARAMS,
        cost_estimate=SHORT,
        name="last_values",
    )(*in_vmem(*last), third_values)


def online_kernel(heads, q_ref, k_ref, v_ref, key_pos_ref, query_pos_ref, start_ref, out_ref, peak_ref, acc_ref):
    step = pl.program_id(0)

    @pl.when(step == 0)
    def _():
        peak_ref[...] = jnp.full(peak_ref.shape, NEG_FILL, jnp.float32)
        acc_ref[...] = jnp.zeros(acc_ref.shape, jnp.float32)

    key_pos = key_pos_ref[...]
    visible = (key_pos >= start_ref[...]) & (key_pos <= query_pos_ref[...])
    values = v_ref[...]
    ext = jnp.concatenate([values, jnp.ones_like(values)], axis=1)
    for head in range(heads):
        q = q_ref[:, head * HEAD_WIDTH:(head + 1) * HEAD_WIDTH]
        scores = lax.dot_general(
            q, k_ref[...], (((1,), (1,)), ((), ())), preferred_element_type=jnp.float32
        )
        scaled = jnp.where(visible, scores * (HEAD_WIDTH ** -0.5 * LOG2_E), NEG_FILL)
        before = peak_ref[head]
        peak = jnp.maximum(before, jnp.max(scaled, axis=1, keepdims=True))
        weights = jnp.where(visible, jnp.exp2(scaled - peak), 0.0).astype(jnp.bfloat16)
        peak_ref[head] = peak
        acc_ref[head] = acc_ref[head] * jnp.exp2(before - peak) + jnp.dot(
            weights, ext, preferred_element_type=jnp.float32
        )

    @pl.when(step == pl.num_programs(0) - 1)
    def _():
        for head in range(heads):
            acc = acc_ref[head]
            out_ref[:, head * HEAD_WIDTH:(head + 1) * HEAD_WIDTH] = (
                acc[:, :HEAD_WIDTH] / acc[:, HEAD_WIDTH:]
            ).astype(jnp.bfloat16)


def online_attention(queries, keys, values, key_pos, query_pos, starts, chunk):
    rows, cols = queries.shape
    heads = cols // HEAD_WIDTH
    key_count = keys.shape[0]
    return pl.pallas_call(
        lambda *refs: online_kernel(heads, *refs),
        grid=(key_count // chunk,),
        in_specs=[
            pl.BlockSpec((rows, cols), lambda j: (0, 0)),
            pl.BlockSpec((chunk, HEAD_WIDTH), lambda j: (j, 0)),
            pl.BlockSpec((chunk, HEAD_WIDTH), lambda j: (j, 0)),
            pl.BlockSpec((1, chunk), lambda j: (0, j)),
            pl.BlockSpec((rows, 1), lambda j: (0, 0)),
            pl.BlockSpec((rows, 1), lambda j: (0, 0)),
        ],
        out_specs=pl.BlockSpec((rows, cols), lambda j: (0, 0)),
        out_shape=jax.ShapeDtypeStruct((rows, cols), jnp.bfloat16),
        scratch_shapes=[
            pltpu.VMEM((heads, rows, 1), jnp.float32),
            pltpu.VMEM((heads, rows, 2 * HEAD_WIDTH), jnp.float32),
        ],
        compiler_params=pltpu.CompilerParams(vmem_limit_bytes=32 << 20),
        name="online",
    )(queries, keys, values, key_pos, query_pos, starts)


def body(queries, keys, values, lengths, old_place):
    devices = lax.axis_size("seq")
    row_count = queries.shape[0]
    key_count = row_count * devices
    if devices == 4 and key_count <= 1024:
        return staged_attention(queries, keys, values, lengths, old_place)
    all_keys = lax.all_gather(keys, "seq", axis=0, tiled=True)
    all_values = lax.all_gather(values, "seq", axis=0, tiled=True)
    key_pos, query_pos, starts = block_places(
        lengths, old_place, lax.axis_index("seq"), row_count, key_count
    )
    return online_attention(queries, all_keys, all_values, key_pos, query_pos, starts, 512)


def solution(mesh):
    in_specs = (
        P(("groups", "seq"), "mp"),
        P(("groups", "seq"), "mp"),
        P(("groups", "seq"), "mp"),
        P("groups"),
        P("groups"),
    )
    out_specs = P(("groups", "seq"), "mp")
    return jax.shard_map(body, mesh=mesh, in_specs=in_specs, out_specs=out_specs, check_vma=False)
```

```python
import jax
import jax.numpy as jnp
from jax import lax
from jax.experimental import pallas as pl
from jax.experimental.pallas import tpu as pltpu
from jax.sharding import PartitionSpec as P

HEAD_WIDTH = 128
LOG2_E = 1.4426950408889634
NEG_FILL = -1e30


def block_places(lengths, old_place, own_index, row_count, key_count):
    block_total = old_place.shape[0]
    block_rows = key_count // block_total
    ids = jnp.arange(block_total, dtype=jnp.int32)
    hit = old_place[:, None] == ids[None, :]
    new_block = jnp.sum(jnp.where(hit, ids[:, None], 0), axis=0)
    key_pos = (new_block[:, None] * block_rows + jnp.arange(block_rows, dtype=jnp.int32)).reshape(-1)
    query_pos = lax.dynamic_slice_in_dim(key_pos, own_index * row_count, row_count)
    bounds = jnp.cumsum(lengths)
    starts = jnp.max(jnp.where(bounds[None, :] <= query_pos[:, None], bounds[None, :], 0), axis=1)
    return key_pos.reshape(1, -1), query_pos.reshape(-1, 1), starts.reshape(-1, 1)


def iota(shape, dim):
    return lax.broadcasted_iota(jnp.int32, shape, dim)


def row_sum_as_column(places):
    square = (places.shape[1],) * 2
    spread = jnp.where(iota(square, 0) == iota(square, 1), places, 0).astype(jnp.float32)
    return jnp.sum(spread, axis=1, keepdims=True).astype(jnp.int32)


def query_places(own, lengths_ref, places, rows):
    block_total = places.shape[1]
    block_rows = rows * lax.axis_size("seq") // block_total
    shape = (block_total, rows)
    hit = row_sum_as_column(places) == own * (rows // block_rows) + iota(shape, 1) // block_rows
    at = jnp.where(hit, iota(shape, 0) * block_rows, 0).astype(jnp.float32)
    query_pos = jnp.sum(at, axis=0, keepdims=True) + (
        iota((1, rows), 1) % block_rows
    ).astype(jnp.float32)
    starts = jnp.zeros_like(query_pos)
    bound = jnp.int32(0)
    for t in range(lengths_ref.shape[0]):
        bound = bound + lengths_ref[t]
        edge = bound.astype(jnp.float32)
        starts = jnp.where(edge <= query_pos, edge, starts)
    return query_pos, starts


def mask_table(owner, query_pos, starts, places):
    block_total, rows = places.shape[1], query_pos.shape[1]
    block_rows = rows * lax.axis_size("seq") // block_total
    shape = (rows, block_total)
    hit = places == owner * (rows // block_rows) + iota(shape, 0) // block_rows
    at = jnp.where(hit, iota(shape, 1) * block_rows, 0).astype(jnp.float32)
    key_pos = jnp.sum(at, axis=1, keepdims=True) + (
        iota((rows, 1), 0) % block_rows
    ).astype(jnp.float32)
    return jnp.where((key_pos >= starts) & (key_pos <= query_pos), 0.0, NEG_FILL)


def in_stages(heads, stages):
    results = [{} for _ in stages]
    for step in range(heads + len(stages) - 1):
        for late, stage in enumerate(stages):
            head = step - late
            if 0 <= head < heads:
                before = results[late - 1].pop(head) if late else None
                results[late][head] = stage(head, before)


def score_stage(keys, across_ref, bias_ref, at, scaled_ref, old_peak):
    def stage(head, _):
        scores = jnp.dot(keys, across_ref[head], preferred_element_type=jnp.float32)
        scaled = scores * (HEAD_WIDTH ** -0.5 * LOG2_E) + bias_ref[at]
        scaled_ref[head] = scaled
        peak = jnp.max(scaled, axis=0, keepdims=True)
        return peak if old_peak is None else jnp.maximum(old_peak(head), peak)

    return stage


def weight_stage(scaled_ref, weight_ref):
    def stage(head, peak):
        weights = jnp.exp2(scaled_ref[head] - peak)
        weight_ref[head] = weights.astype(jnp.bfloat16)
        return peak, jnp.sum(weights, axis=0, keepdims=True)

    return stage


def own_kernel(
    own_ref, lengths_hbm, places_hbm, q_hbm, k_hbm, v_hbm,
    across_ref, bias_ref, peak_ref, total_ref, sum_ref,
    lengths_ref, places_ref, q_ref, k_ref, v_ref, scaled_ref, weight_ref, sems,
):
    moves = (
        (lengths_hbm, lengths_ref), (places_hbm, places_ref),
        (k_hbm, k_ref), (v_hbm, v_ref), (q_hbm, q_ref),
    )
    copies = [pltpu.make_async_copy(*move, sems.at[n]) for n, move in enumerate(moves)]
    for copy in copies:
        copy.start()
    for copy in copies:
        copy.wait()
    heads, _, rows = across_ref.shape
    own, places = own_ref[0], places_ref[...]
    keys = k_ref[...]
    query_pos, starts = query_places(own, lengths_ref, places, rows)
    bias_ref[0] = mask_table(own, query_pos, starts, places)
    turned = jnp.transpose(v_ref[...])

    def turn(head, _):
        q = q_ref[:, head * HEAD_WIDTH:(head + 1) * HEAD_WIDTH]
        across_ref[head] = jnp.transpose(q)
        if 0 < head < bias_ref.shape[0]:
            bias_ref[head] = mask_table(own ^ head, query_pos, starts, places)

    def mix(head, reached):
        peak_ref[head:head + 1, :], total_ref[head:head + 1, :] = reached
        sum_ref[head] = jnp.dot(turned, weight_ref[head], preferred_element_type=jnp.float32)

    in_stages(heads, [
        turn,
        score_stage(keys, across_ref, bias_ref, 0, scaled_ref, None),
        weight_stage(scaled_ref, weight_ref),
        mix,
    ])


def next_kernel(
    at, across_ref, bias_ref, peak_ref, total_ref, sum_ref, k_ref, v_ref,
    new_peak_ref, new_total_ref, new_sum_ref, scaled_ref, weight_ref,
):
    turned = jnp.transpose(v_ref[...])

    def mix(head, reached):
        peak, total = reached
        row = slice(head, head + 1)
        factor = jnp.exp2(peak_ref[row, :] - peak)
        new_peak_ref[row, :] = peak
        new_total_ref[row, :] = total_ref[row, :] * factor + total
        added = jnp.dot(turned, weight_ref[head], preferred_element_type=jnp.float32)
        new_sum_ref[head] = sum_ref[head] * factor + added

    in_stages(across_ref.shape[0], [
        score_stage(
            k_ref[...], across_ref, bias_ref, at, scaled_ref,
            lambda head: peak_ref[head:head + 1, :],
        ),
        weight_stage(scaled_ref, weight_ref),
        mix,
    ])


def weights_kernel(
    at, across_ref, bias_ref, peak_ref, total_ref, sum_ref, k_ref,
    new_sum_ref, weight_ref, share_ref, scaled_ref,
):
    def rescale(head, reached):
        peak, total = reached
        row = slice(head, head + 1)
        factor = jnp.exp2(peak_ref[row, :] - peak)
        share = 1.0 / (total_ref[row, :] * factor + total)
        share_ref[row, :] = share
        new_sum_ref[head] = sum_ref[head] * (factor * share)

    in_stages(across_ref.shape[0], [
        score_stage(
            k_ref[...], across_ref, bias_ref, at, scaled_ref,
            lambda head: peak_ref[head:head + 1, :],
        ),
        weight_stage(scaled_ref, weight_ref),
        rescale,
    ])


def last_kernel(sum_ref, weight_ref, share_ref, v_ref, out_ref, block_ref, sems):
    turned = jnp.transpose(v_ref[...])
    copies = []

    def mix(head, _):
        added = jnp.dot(turned, weight_ref[head], preferred_element_type=jnp.float32)
        return (sum_ref[head] + added * share_ref[head:head + 1, :]).astype(jnp.bfloat16)

    def send(head, out):
        cols = slice(head * HEAD_WIDTH, (head + 1) * HEAD_WIDTH)
        block_ref[:, cols] = jnp.transpose(out)
        if head % 2 or head == sum_ref.shape[0] - 1:
            cols = slice(head // 2 * 2 * HEAD_WIDTH, (head + 1) * HEAD_WIDTH)
            copy = pltpu.make_async_copy(block_ref.at[:, cols], out_ref.at[:, cols], sems.at[head])
            copy.start()
            copies.append(copy)

    in_stages(sum_ref.shape[0], [mix, send])
    for copy in copies:
        copy.wait()


SHORT = pl.CostEstimate(flops=0, bytes_accessed=0, transcendentals=0)


def in_vmem(*arrays):
    return [pltpu.with_memory_space_constraint(array, pltpu.VMEM) for array in arrays]


def in_hbm(*arrays):
    return [pltpu.with_memory_space_constraint(array, pltpu.HBM) for array in arrays]


VMEM_REF = pl.BlockSpec(memory_space=pltpu.VMEM)
HBM_REF = pl.BlockSpec(memory_space=pltpu.HBM)
PARAMS = pltpu.CompilerParams(vmem_limit_bytes=32 << 20)


def moved(value, mask):
    return lax.ppermute(value, "seq", [(i, i ^ mask) for i in range(lax.axis_size("seq"))])


def staged_attention(queries, keys, values, lengths, old_place):
    far_keys, far_values = moved(keys, 2), moved(values, 2)
    near_keys, near_values = moved(keys, 1), moved(values, 1)
    rows, cols = queries.shape
    heads = cols // HEAD_WIDTH
    devices = lax.axis_size("seq")
    own = lax.axis_index("seq").astype(jnp.int32)
    places = old_place.reshape(1, -1)
    state = [
        pltpu.VMEM((heads, rows), jnp.float32),
        pltpu.VMEM((heads, rows), jnp.float32),
        pltpu.VMEM((heads, HEAD_WIDTH, rows), jnp.float32),
    ]
    work = [
        pltpu.VMEM((heads, rows, rows), jnp.float32),
        pltpu.VMEM((heads, rows, rows), jnp.bfloat16),
    ]
    across, bias, *carried = pl.pallas_call(
        own_kernel,
        in_specs=[pl.BlockSpec(memory_space=pltpu.SMEM)] + [HBM_REF] * 5,
        out_specs=[VMEM_REF] * 5,
        out_shape=[
            pltpu.VMEM((heads, HEAD_WIDTH, rows), jnp.bfloat16),
            pltpu.VMEM((devices, rows, rows), jnp.float32),
        ] + state,
        scratch_shapes=[
            pltpu.SMEM(lengths.shape, jnp.int32),
            pltpu.VMEM(places.shape, jnp.int32),
            pltpu.VMEM(queries.shape, jnp.bfloat16),
            pltpu.VMEM(keys.shape, jnp.bfloat16),
            pltpu.VMEM(values.shape, jnp.bfloat16),
        ] + work + [pltpu.SemaphoreType.DMA((5,))],
        compiler_params=PARAMS,
        cost_estimate=SHORT,
        name="own_shard",
    )(own.reshape(1), *in_hbm(lengths, places, queries, keys, values))

    def add_shard(at, keys, values, carried):
        return pl.pallas_call(
            lambda *refs: next_kernel(at, *refs),
            in_specs=[VMEM_REF] * 7,
            out_specs=[VMEM_REF] * 3,
            out_shape=state,
            scratch_shapes=work,
            compiler_params=PARAMS,
            cost_estimate=SHORT,
            name="next_shard",
        )(*in_vmem(across, bias, *carried), keys, values)

    far_keys, *carried = lax.optimization_barrier((far_keys, *carried))
    third_keys = moved(far_keys, 1)
    far_values, *carried = lax.optimization_barrier((far_values, *carried))
    third_values = moved(far_values, 1)
    carried = add_shard(2, far_keys, far_values, carried)
    carried = add_shard(1, near_keys, near_values, carried)
    scaled_sum = pltpu.VMEM((heads, HEAD_WIDTH, rows), jnp.float32)
    last = pl.pallas_call(
        lambda *refs: weights_kernel(3, *refs),
        in_specs=[VMEM_REF] * 6,
        out_specs=[VMEM_REF] * 3,
        out_shape=[scaled_sum, work[1], state[0]],
        scratch_shapes=work[:1],
        compiler_params=PARAMS,
        cost_estimate=SHORT,
        name="last_weights",
    )(*in_vmem(across, bias, *carried), third_keys)
    return pl.pallas_call(
        last_kernel,
        in_specs=[VMEM_REF] * 4,
        out_specs=pl.BlockSpec(memory_space=pl.ANY),
        out_shape=jax.ShapeDtypeStruct((rows, cols), jnp.bfloat16),
        scratch_shapes=[
            pltpu.VMEM((rows, cols), jnp.bfloat16),
            pltpu.SemaphoreType.DMA((heads,)),
        ],
        compiler_params=PARAMS,
        cost_estimate=SHORT,
        name="last_values",
    )(*in_vmem(*last), third_values)


def online_kernel(heads, q_ref, k_ref, v_ref, key_pos_ref, query_pos_ref, start_ref, out_ref, peak_ref, acc_ref):
    step = pl.program_id(0)

    @pl.when(step == 0)
    def _():
        peak_ref[...] = jnp.full(peak_ref.shape, NEG_FILL, jnp.float32)
        acc_ref[...] = jnp.zeros(acc_ref.shape, jnp.float32)

    key_pos = key_pos_ref[...]
    visible = (key_pos >= start_ref[...]) & (key_pos <= query_pos_ref[...])
    values = v_ref[...]
    ext = jnp.concatenate([values, jnp.ones_like(values)], axis=1)
    for head in range(heads):
        q = q_ref[:, head * HEAD_WIDTH:(head + 1) * HEAD_WIDTH]
        scores = lax.dot_general(
            q, k_ref[...], (((1,), (1,)), ((), ())), preferred_element_type=jnp.float32
        )
        scaled = jnp.where(visible, scores * (HEAD_WIDTH ** -0.5 * LOG2_E), NEG_FILL)
        before = peak_ref[head]
        peak = jnp.maximum(before, jnp.max(scaled, axis=1, keepdims=True))
        weights = jnp.where(visible, jnp.exp2(scaled - peak), 0.0).astype(jnp.bfloat16)
        peak_ref[head] = peak
        acc_ref[head] = acc_ref[head] * jnp.exp2(before - peak) + jnp.dot(
            weights, ext, preferred_element_type=jnp.float32
        )

    @pl.when(step == pl.num_programs(0) - 1)
    def _():
        for head in range(heads):
            acc = acc_ref[head]
            out_ref[:, head * HEAD_WIDTH:(head + 1) * HEAD_WIDTH] = (
                acc[:, :HEAD_WIDTH] / acc[:, HEAD_WIDTH:]
            ).astype(jnp.bfloat16)


def online_attention(queries, keys, values, key_pos, query_pos, starts, chunk):
    rows, cols = queries.shape
    heads = cols // HEAD_WIDTH
    key_count = keys.shape[0]
    return pl.pallas_call(
        lambda *refs: online_kernel(heads, *refs),
        grid=(key_count // chunk,),
        in_specs=[
            pl.BlockSpec((rows, cols), lambda j: (0, 0)),
            pl.BlockSpec((chunk, HEAD_WIDTH), lambda j: (j, 0)),
            pl.BlockSpec((chunk, HEAD_WIDTH), lambda j: (j, 0)),
            pl.BlockSpec((1, chunk), lambda j: (0, j)),
            pl.BlockSpec((rows, 1), lambda j: (0, 0)),
            pl.BlockSpec((rows, 1), lambda j: (0, 0)),
        ],
        out_specs=pl.BlockSpec((rows, cols), lambda j: (0, 0)),
        out_shape=jax.ShapeDtypeStruct((rows, cols), jnp.bfloat16),
        scratch_shapes=[
            pltpu.VMEM((heads, rows, 1), jnp.float32),
            pltpu.VMEM((heads, rows, 2 * HEAD_WIDTH), jnp.float32),
        ],
        compiler_params=pltpu.CompilerParams(vmem_limit_bytes=32 << 20),
        name="online",
    )(queries, keys, values, key_pos, query_pos, starts)


def body(queries, keys, values, lengths, old_place):
    devices = lax.axis_size("seq")
    row_count = queries.shape[0]
    key_count = row_count * devices
    if devices == 4 and key_count <= 1024:
        return staged_attention(queries, keys, values, lengths, old_place)
    all_keys = lax.all_gather(keys, "seq", axis=0, tiled=True)
    all_values = lax.all_gather(values, "seq", axis=0, tiled=True)
    key_pos, query_pos, starts = block_places(
        lengths, old_place, lax.axis_index("seq"), row_count, key_count
    )
    return online_attention(queries, all_keys, all_values, key_pos, query_pos, starts, 512)


def solution(mesh):
    in_specs = (
        P(("groups", "seq"), "mp"),
        P(("groups", "seq"), "mp"),
        P(("groups", "seq"), "mp"),
        P("groups"),
        P("groups"),
    )
    out_specs = P(("groups", "seq"), "mp")
    return jax.shard_map(body, mesh=mesh, in_specs=in_specs, out_specs=out_specs, check_vma=False)
```

```python
import jax
import jax.numpy as jnp
from jax import lax
from jax.experimental import pallas as pl
from jax.experimental.pallas import tpu as pltpu
from jax.sharding import PartitionSpec as P

HEAD_WIDTH = 128
LOG2_E = 1.4426950408889634
NEG_FILL = -1e30


def block_places(lengths, old_place, own_index, row_count, key_count):
    block_total = old_place.shape[0]
    block_rows = key_count // block_total
    ids = jnp.arange(block_total, dtype=jnp.int32)
    hit = old_place[:, None] == ids[None, :]
    new_block = jnp.sum(jnp.where(hit, ids[:, None], 0), axis=0)
    key_pos = (new_block[:, None] * block_rows + jnp.arange(block_rows, dtype=jnp.int32)).reshape(-1)
    query_pos = lax.dynamic_slice_in_dim(key_pos, own_index * row_count, row_count)
    bounds = jnp.cumsum(lengths)
    starts = jnp.max(jnp.where(bounds[None, :] <= query_pos[:, None], bounds[None, :], 0), axis=1)
    return key_pos.reshape(1, -1), query_pos.reshape(-1, 1), starts.reshape(-1, 1)


def iota(shape, dim):
    return lax.broadcasted_iota(jnp.int32, shape, dim)


def row_sum_as_column(places):
    square = (places.shape[1],) * 2
    spread = jnp.where(iota(square, 0) == iota(square, 1), places, 0).astype(jnp.float32)
    return jnp.sum(spread, axis=1, keepdims=True).astype(jnp.int32)


def query_places(own, lengths_ref, places, rows):
    block_total = places.shape[1]
    block_rows = rows * lax.axis_size("seq") // block_total
    shape = (block_total, rows)
    hit = row_sum_as_column(places) == own * (rows // block_rows) + iota(shape, 1) // block_rows
    at = jnp.where(hit, iota(shape, 0) * block_rows, 0).astype(jnp.float32)
    query_pos = jnp.sum(at, axis=0, keepdims=True) + (
        iota((1, rows), 1) % block_rows
    ).astype(jnp.float32)
    starts = jnp.zeros_like(query_pos)
    bound = jnp.int32(0)
    for t in range(lengths_ref.shape[0]):
        bound = bound + lengths_ref[t]
        edge = bound.astype(jnp.float32)
        starts = jnp.where(edge <= query_pos, edge, starts)
    return query_pos, starts


def mask_table(owner, query_pos, starts, places):
    block_total, rows = places.shape[1], query_pos.shape[1]
    block_rows = rows * lax.axis_size("seq") // block_total
    shape = (rows, block_total)
    hit = places == owner * (rows // block_rows) + iota(shape, 0) // block_rows
    at = jnp.where(hit, iota(shape, 1) * block_rows, 0).astype(jnp.float32)
    key_pos = jnp.sum(at, axis=1, keepdims=True) + (
        iota((rows, 1), 0) % block_rows
    ).astype(jnp.float32)
    return jnp.where((key_pos >= starts) & (key_pos <= query_pos), 0.0, NEG_FILL)


def in_stages(heads, stages):
    results = [{} for _ in stages]
    for step in range(heads + len(stages) - 1):
        for late, stage in enumerate(stages):
            head = step - late
            if 0 <= head < heads:
                before = results[late - 1].pop(head) if late else None
                results[late][head] = stage(head, before)


def score_stage(keys, across_ref, bias_ref, at, scaled_ref, old_peak):
    ready = {}

    def stage(head, _):
        if head not in ready:
            pair = range(head, min(head + 2, across_ref.shape[0]))
            across = jnp.concatenate([across_ref[one] for one in pair], axis=1)
            both = jnp.dot(keys, across, preferred_element_type=jnp.float32)
            for at_column, one in enumerate(pair):
                width = across_ref.shape[2]
                ready[one] = both[:, at_column * width:(at_column + 1) * width]
        scores = ready.pop(head)
        scaled = scores * (HEAD_WIDTH ** -0.5 * LOG2_E) + bias_ref[at]
        scaled_ref[head] = scaled
        peak = jnp.max(scaled, axis=0, keepdims=True)
        return peak if old_peak is None else jnp.maximum(old_peak(head), peak)

    return stage


def weight_stage(scaled_ref, weight_ref):
    def stage(head, peak):
        weights = jnp.exp2(scaled_ref[head] - peak)
        weight_ref[head] = weights.astype(jnp.bfloat16)
        return peak, jnp.sum(weights, axis=0, keepdims=True)

    return stage


def own_kernel(
    own_ref, lengths_hbm, places_hbm, q_hbm, k_hbm, v_hbm,
    across_ref, bias_ref, peak_ref, total_ref, sum_ref,
    lengths_ref, places_ref, q_ref, k_ref, v_ref, scaled_ref, weight_ref, sems,
):
    moves = (
        (lengths_hbm, lengths_ref), (places_hbm, places_ref),
        (k_hbm, k_ref), (v_hbm, v_ref), (q_hbm, q_ref),
    )
    copies = [pltpu.make_async_copy(*move, sems.at[n]) for n, move in enumerate(moves)]
    for copy in copies:
        copy.start()
    for copy in copies:
        copy.wait()
    heads, _, rows = across_ref.shape
    own, places = own_ref[0], places_ref[...]
    keys = k_ref[...]
    query_pos, starts = query_places(own, lengths_ref, places, rows)
    bias_ref[0] = mask_table(own, query_pos, starts, places)
    turned = jnp.transpose(v_ref[...])

    def turn(head, _):
        q = q_ref[:, head * HEAD_WIDTH:(head + 1) * HEAD_WIDTH]
        across_ref[head] = jnp.transpose(q)
        if 0 < head < bias_ref.shape[0]:
            bias_ref[head] = mask_table(own ^ head, query_pos, starts, places)

    def mix(head, reached):
        peak_ref[head:head + 1, :], total_ref[head:head + 1, :] = reached
        sum_ref[head] = jnp.dot(turned, weight_ref[head], preferred_element_type=jnp.float32)

    for head in range(heads):
        turn(head, None)
    in_stages(heads, [
        score_stage(keys, across_ref, bias_ref, 0, scaled_ref, None),
        weight_stage(scaled_ref, weight_ref),
        mix,
    ])


def next_kernel(
    at, across_ref, bias_ref, peak_ref, total_ref, sum_ref, k_ref, v_ref,
    new_peak_ref, new_total_ref, new_sum_ref, scaled_ref, weight_ref,
):
    turned = jnp.transpose(v_ref[...])

    def mix(head, reached):
        peak, total = reached
        row = slice(head, head + 1)
        factor = jnp.exp2(peak_ref[row, :] - peak)
        new_peak_ref[row, :] = peak
        new_total_ref[row, :] = total_ref[row, :] * factor + total
        added = jnp.dot(turned, weight_ref[head], preferred_element_type=jnp.float32)
        new_sum_ref[head] = sum_ref[head] * factor + added

    in_stages(across_ref.shape[0], [
        score_stage(
            k_ref[...], across_ref, bias_ref, at, scaled_ref,
            lambda head: peak_ref[head:head + 1, :],
        ),
        weight_stage(scaled_ref, weight_ref),
        mix,
    ])


def weights_kernel(
    at, across_ref, bias_ref, peak_ref, total_ref, sum_ref, k_ref,
    new_sum_ref, weight_ref, share_ref, scaled_ref,
):
    def rescale(head, reached):
        peak, total = reached
        row = slice(head, head + 1)
        factor = jnp.exp2(peak_ref[row, :] - peak)
        share = 1.0 / (total_ref[row, :] * factor + total)
        share_ref[row, :] = share
        new_sum_ref[head] = sum_ref[head] * (factor * share)

    in_stages(across_ref.shape[0], [
        score_stage(
            k_ref[...], across_ref, bias_ref, at, scaled_ref,
            lambda head: peak_ref[head:head + 1, :],
        ),
        weight_stage(scaled_ref, weight_ref),
        rescale,
    ])


def last_kernel(sum_ref, weight_ref, share_ref, v_ref, out_ref, block_ref, sems):
    turned = jnp.transpose(v_ref[...])
    copies = []

    def mix(head, _):
        added = jnp.dot(turned, weight_ref[head], preferred_element_type=jnp.float32)
        return (sum_ref[head] + added * share_ref[head:head + 1, :]).astype(jnp.bfloat16)

    def send(head, out):
        cols = slice(head * HEAD_WIDTH, (head + 1) * HEAD_WIDTH)
        block_ref[:, cols] = jnp.transpose(out)
        copy = pltpu.make_async_copy(block_ref.at[:, cols], out_ref.at[:, cols], sems.at[head])
        copy.start()
        copies.append(copy)

    in_stages(sum_ref.shape[0], [mix, send])
    for copy in copies:
        copy.wait()


SHORT = pl.CostEstimate(flops=0, bytes_accessed=0, transcendentals=0)


def in_vmem(*arrays):
    return [pltpu.with_memory_space_constraint(array, pltpu.VMEM) for array in arrays]


def in_hbm(*arrays):
    return [pltpu.with_memory_space_constraint(array, pltpu.HBM) for array in arrays]


VMEM_REF = pl.BlockSpec(memory_space=pltpu.VMEM)
HBM_REF = pl.BlockSpec(memory_space=pltpu.HBM)
PARAMS = pltpu.CompilerParams(vmem_limit_bytes=32 << 20)


def moved(value, mask):
    return lax.ppermute(value, "seq", [(i, i ^ mask) for i in range(lax.axis_size("seq"))])


def staged_attention(queries, keys, values, lengths, old_place):
    far_keys, far_values = moved(keys, 2), moved(values, 2)
    near_keys, near_values = moved(keys, 1), moved(values, 1)
    rows, cols = queries.shape
    heads = cols // HEAD_WIDTH
    devices = lax.axis_size("seq")
    own = lax.axis_index("seq").astype(jnp.int32)
    places = old_place.reshape(1, -1)
    state = [
        pltpu.VMEM((heads, rows), jnp.float32),
        pltpu.VMEM((heads, rows), jnp.float32),
        pltpu.VMEM((heads, HEAD_WIDTH, rows), jnp.float32),
    ]
    work = [
        pltpu.VMEM((heads, rows, rows), jnp.float32),
        pltpu.VMEM((heads, rows, rows), jnp.bfloat16),
    ]
    across, bias, *carried = pl.pallas_call(
        own_kernel,
        in_specs=[pl.BlockSpec(memory_space=pltpu.SMEM)] + [HBM_REF] * 5,
        out_specs=[VMEM_REF] * 5,
        out_shape=[
            pltpu.VMEM((heads, HEAD_WIDTH, rows), jnp.bfloat16),
            pltpu.VMEM((devices, rows, rows), jnp.float32),
        ] + state,
        scratch_shapes=[
            pltpu.SMEM(lengths.shape, jnp.int32),
            pltpu.VMEM(places.shape, jnp.int32),
            pltpu.VMEM(queries.shape, jnp.bfloat16),
            pltpu.VMEM(keys.shape, jnp.bfloat16),
            pltpu.VMEM(values.shape, jnp.bfloat16),
        ] + work + [pltpu.SemaphoreType.DMA((5,))],
        compiler_params=PARAMS,
        cost_estimate=SHORT,
        name="own_shard",
    )(own.reshape(1), *in_hbm(lengths, places, queries, keys, values))

    def add_shard(at, keys, values, carried):
        return pl.pallas_call(
            lambda *refs: next_kernel(at, *refs),
            in_specs=[VMEM_REF] * 7,
            out_specs=[VMEM_REF] * 3,
            out_shape=state,
            scratch_shapes=work,
            compiler_params=PARAMS,
            cost_estimate=SHORT,
            name="next_shard",
        )(*in_vmem(across, bias, *carried), keys, values)

    far_keys, *carried = lax.optimization_barrier((far_keys, *carried))
    third_keys = moved(far_keys, 1)
    far_values, *carried = lax.optimization_barrier((far_values, *carried))
    third_values = moved(far_values, 1)
    carried = add_shard(2, far_keys, far_values, carried)
    carried = add_shard(1, near_keys, near_values, carried)
    scaled_sum = pltpu.VMEM((heads, HEAD_WIDTH, rows), jnp.float32)
    last = pl.pallas_call(
        lambda *refs: weights_kernel(3, *refs),
        in_specs=[VMEM_REF] * 6,
        out_specs=[VMEM_REF] * 3,
        out_shape=[scaled_sum, work[1], state[0]],
        scratch_shapes=work[:1],
        compiler_params=PARAMS,
        cost_estimate=SHORT,
        name="last_weights",
    )(*in_vmem(across, bias, *carried), third_keys)
    return pl.pallas_call(
        last_kernel,
        in_specs=[VMEM_REF] * 4,
        out_specs=pl.BlockSpec(memory_space=pl.ANY),
        out_shape=jax.ShapeDtypeStruct((rows, cols), jnp.bfloat16),
        scratch_shapes=[
            pltpu.VMEM((rows, cols), jnp.bfloat16),
            pltpu.SemaphoreType.DMA((heads,)),
        ],
        compiler_params=PARAMS,
        cost_estimate=SHORT,
        name="last_values",
    )(*in_vmem(*last), third_values)


def online_kernel(heads, q_ref, k_ref, v_ref, key_pos_ref, query_pos_ref, start_ref, out_ref, peak_ref, acc_ref):
    step = pl.program_id(0)

    @pl.when(step == 0)
    def _():
        peak_ref[...] = jnp.full(peak_ref.shape, NEG_FILL, jnp.float32)
        acc_ref[...] = jnp.zeros(acc_ref.shape, jnp.float32)

    key_pos = key_pos_ref[...]
    visible = (key_pos >= start_ref[...]) & (key_pos <= query_pos_ref[...])
    values = v_ref[...]
    ext = jnp.concatenate([values, jnp.ones_like(values)], axis=1)
    for head in range(heads):
        q = q_ref[:, head * HEAD_WIDTH:(head + 1) * HEAD_WIDTH]
        scores = lax.dot_general(
            q, k_ref[...], (((1,), (1,)), ((), ())), preferred_element_type=jnp.float32
        )
        scaled = jnp.where(visible, scores * (HEAD_WIDTH ** -0.5 * LOG2_E), NEG_FILL)
        before = peak_ref[head]
        peak = jnp.maximum(before, jnp.max(scaled, axis=1, keepdims=True))
        weights = jnp.where(visible, jnp.exp2(scaled - peak), 0.0).astype(jnp.bfloat16)
        peak_ref[head] = peak
        acc_ref[head] = acc_ref[head] * jnp.exp2(before - peak) + jnp.dot(
            weights, ext, preferred_element_type=jnp.float32
        )

    @pl.when(step == pl.num_programs(0) - 1)
    def _():
        for head in range(heads):
            acc = acc_ref[head]
            out_ref[:, head * HEAD_WIDTH:(head + 1) * HEAD_WIDTH] = (
                acc[:, :HEAD_WIDTH] / acc[:, HEAD_WIDTH:]
            ).astype(jnp.bfloat16)


def online_attention(queries, keys, values, key_pos, query_pos, starts, chunk):
    rows, cols = queries.shape
    heads = cols // HEAD_WIDTH
    key_count = keys.shape[0]
    return pl.pallas_call(
        lambda *refs: online_kernel(heads, *refs),
        grid=(key_count // chunk,),
        in_specs=[
            pl.BlockSpec((rows, cols), lambda j: (0, 0)),
            pl.BlockSpec((chunk, HEAD_WIDTH), lambda j: (j, 0)),
            pl.BlockSpec((chunk, HEAD_WIDTH), lambda j: (j, 0)),
            pl.BlockSpec((1, chunk), lambda j: (0, j)),
            pl.BlockSpec((rows, 1), lambda j: (0, 0)),
            pl.BlockSpec((rows, 1), lambda j: (0, 0)),
        ],
        out_specs=pl.BlockSpec((rows, cols), lambda j: (0, 0)),
        out_shape=jax.ShapeDtypeStruct((rows, cols), jnp.bfloat16),
        scratch_shapes=[
            pltpu.VMEM((heads, rows, 1), jnp.float32),
            pltpu.VMEM((heads, rows, 2 * HEAD_WIDTH), jnp.float32),
        ],
        compiler_params=pltpu.CompilerParams(vmem_limit_bytes=32 << 20),
        name="online",
    )(queries, keys, values, key_pos, query_pos, starts)


def body(queries, keys, values, lengths, old_place):
    devices = lax.axis_size("seq")
    row_count = queries.shape[0]
    key_count = row_count * devices
    if devices == 4 and key_count <= 1024:
        return staged_attention(queries, keys, values, lengths, old_place)
    all_keys = lax.all_gather(keys, "seq", axis=0, tiled=True)
    all_values = lax.all_gather(values, "seq", axis=0, tiled=True)
    key_pos, query_pos, starts = block_places(
        lengths, old_place, lax.axis_index("seq"), row_count, key_count
    )
    return online_attention(queries, all_keys, all_values, key_pos, query_pos, starts, 512)


def solution(mesh):
    in_specs = (
        P(("groups", "seq"), "mp"),
        P(("groups", "seq"), "mp"),
        P(("groups", "seq"), "mp"),
        P("groups"),
        P("groups"),
    )
    out_specs = P(("groups", "seq"), "mp")
    return jax.shard_map(body, mesh=mesh, in_specs=in_specs, out_specs=out_specs, check_vma=False)
```

```python
import jax
import jax.numpy as jnp
from jax import lax
from jax.experimental import pallas as pl
from jax.experimental.pallas import tpu as pltpu
from jax.sharding import PartitionSpec as P

HEAD_WIDTH = 128
LOG2_E = 1.4426950408889634
NEG_FILL = -1e30


def block_places(lengths, old_place, own_index, row_count, key_count):
    block_total = old_place.shape[0]
    block_rows = key_count // block_total
    ids = jnp.arange(block_total, dtype=jnp.int32)
    hit = old_place[:, None] == ids[None, :]
    new_block = jnp.sum(jnp.where(hit, ids[:, None], 0), axis=0)
    key_pos = (new_block[:, None] * block_rows + jnp.arange(block_rows, dtype=jnp.int32)).reshape(-1)
    query_pos = lax.dynamic_slice_in_dim(key_pos, own_index * row_count, row_count)
    bounds = jnp.cumsum(lengths)
    starts = jnp.max(jnp.where(bounds[None, :] <= query_pos[:, None], bounds[None, :], 0), axis=1)
    return key_pos.reshape(1, -1), query_pos.reshape(-1, 1), starts.reshape(-1, 1)


def iota(shape, dim):
    return lax.broadcasted_iota(jnp.int32, shape, dim)


def row_sum_as_column(places):
    square = (places.shape[1],) * 2
    spread = jnp.where(iota(square, 0) == iota(square, 1), places, 0).astype(jnp.float32)
    return jnp.sum(spread, axis=1, keepdims=True).astype(jnp.int32)


def query_places(own, lengths_ref, places, rows):
    block_total = places.shape[1]
    block_rows = rows * lax.axis_size("seq") // block_total
    shape = (block_total, rows)
    hit = row_sum_as_column(places) == own * (rows // block_rows) + iota(shape, 1) // block_rows
    at = jnp.where(hit, iota(shape, 0) * block_rows, 0).astype(jnp.float32)
    query_pos = jnp.sum(at, axis=0, keepdims=True) + (
        iota((1, rows), 1) % block_rows
    ).astype(jnp.float32)
    starts = jnp.zeros_like(query_pos)
    bound = jnp.int32(0)
    for t in range(lengths_ref.shape[0]):
        bound = bound + lengths_ref[t]
        edge = bound.astype(jnp.float32)
        starts = jnp.where(edge <= query_pos, edge, starts)
    return query_pos, starts


def mask_table(owner, query_pos, starts, places):
    block_total, rows = places.shape[1], query_pos.shape[1]
    block_rows = rows * lax.axis_size("seq") // block_total
    shape = (rows, block_total)
    hit = places == owner * (rows // block_rows) + iota(shape, 0) // block_rows
    at = jnp.where(hit, iota(shape, 1) * block_rows, 0).astype(jnp.float32)
    key_pos = jnp.sum(at, axis=1, keepdims=True) + (
        iota((rows, 1), 0) % block_rows
    ).astype(jnp.float32)
    return jnp.where((key_pos >= starts) & (key_pos <= query_pos), 0.0, NEG_FILL)


def in_stages(heads, stages):
    results = [{} for _ in stages]
    for step in range(heads + len(stages) - 1):
        for late, stage in enumerate(stages):
            head = step - late
            if 0 <= head < heads:
                before = results[late - 1].pop(head) if late else None
                results[late][head] = stage(head, before)


def score_stage(keys, across_ref, bias_ref, at, scaled_ref, old_peak):
    ready = {}

    def stage(head, _):
        if head not in ready:
            pair = range(head, min(head + 2, across_ref.shape[0]))
            across = jnp.concatenate([across_ref[one] for one in pair], axis=1)
            both = jnp.dot(keys, across, preferred_element_type=jnp.float32)
            for at_column, one in enumerate(pair):
                width = across_ref.shape[2]
                ready[one] = both[:, at_column * width:(at_column + 1) * width]
        scores = ready.pop(head)
        scaled = scores * (HEAD_WIDTH ** -0.5 * LOG2_E) + bias_ref[at]
        scaled_ref[head] = scaled
        peak = jnp.max(scaled, axis=0, keepdims=True)
        return peak if old_peak is None else jnp.maximum(old_peak(head), peak)

    return stage


def weight_stage(scaled_ref, weight_ref):
    def stage(head, peak):
        weights = jnp.exp2(scaled_ref[head] - peak)
        weight_ref[head] = weights.astype(jnp.bfloat16)
        return peak, jnp.sum(weights, axis=0, keepdims=True)

    return stage


def own_kernel(
    own_ref, lengths_hbm, places_hbm, q_hbm, k_hbm, v_hbm,
    across_ref, bias_ref, peak_ref, total_ref, sum_ref,
    lengths_ref, places_ref, q_ref, k_ref, v_ref, scaled_ref, weight_ref, sems,
):
    moves = (
        (lengths_hbm, lengths_ref), (places_hbm, places_ref),
        (k_hbm, k_ref), (v_hbm, v_ref), (q_hbm, q_ref),
    )
    copies = [pltpu.make_async_copy(*move, sems.at[n]) for n, move in enumerate(moves)]
    for copy in copies:
        copy.start()
    for copy in copies:
        copy.wait()
    heads, _, rows = across_ref.shape
    own, places = own_ref[0], places_ref[...]
    keys = k_ref[...]
    query_pos, starts = query_places(own, lengths_ref, places, rows)
    bias_ref[0] = mask_table(own, query_pos, starts, places)
    turned = jnp.transpose(v_ref[...])

    def turn(head, _):
        q = q_ref[:, head * HEAD_WIDTH:(head + 1) * HEAD_WIDTH]
        across_ref[head] = jnp.transpose(q)
        if 0 < head < bias_ref.shape[0]:
            bias_ref[head] = mask_table(own ^ head, query_pos, starts, places)

    def mix(head, reached):
        peak_ref[head:head + 1, :], total_ref[head:head + 1, :] = reached
        sum_ref[head] = jnp.dot(turned, weight_ref[head], preferred_element_type=jnp.float32)

    for head in range(heads):
        turn(head, None)
    in_stages(heads, [
        score_stage(keys, across_ref, bias_ref, 0, scaled_ref, None),
        weight_stage(scaled_ref, weight_ref),
        mix,
    ])


def next_kernel(
    at, across_ref, bias_ref, peak_ref, total_ref, sum_ref, k_ref, v_ref,
    new_peak_ref, new_total_ref, new_sum_ref, scaled_ref, weight_ref,
):
    turned = jnp.transpose(v_ref[...])

    def mix(head, reached):
        peak, total = reached
        row = slice(head, head + 1)
        factor = jnp.exp2(peak_ref[row, :] - peak)
        new_peak_ref[row, :] = peak
        new_total_ref[row, :] = total_ref[row, :] * factor + total
        added = jnp.dot(turned, weight_ref[head], preferred_element_type=jnp.float32)
        new_sum_ref[head] = sum_ref[head] * factor + added

    in_stages(across_ref.shape[0], [
        score_stage(
            k_ref[...], across_ref, bias_ref, at, scaled_ref,
            lambda head: peak_ref[head:head + 1, :],
        ),
        weight_stage(scaled_ref, weight_ref),
        mix,
    ])


def weights_kernel(
    at, across_ref, bias_ref, peak_ref, total_ref, sum_ref, k_ref,
    new_sum_ref, weight_ref, share_ref, scaled_ref,
):
    def rescale(head, reached):
        peak, total = reached
        row = slice(head, head + 1)
        factor = jnp.exp2(peak_ref[row, :] - peak)
        share = 1.0 / (total_ref[row, :] * factor + total)
        share_ref[row, :] = share
        new_sum_ref[head] = sum_ref[head] * (factor * share)

    in_stages(across_ref.shape[0], [
        score_stage(
            k_ref[...], across_ref, bias_ref, at, scaled_ref,
            lambda head: peak_ref[head:head + 1, :],
        ),
        weight_stage(scaled_ref, weight_ref),
        rescale,
    ])


def last_kernel(sum_ref, weight_ref, share_ref, v_ref, out_ref, block_ref, sems):
    turned = jnp.transpose(v_ref[...])
    copies = []

    ready = {}

    def mix(head, _):
        if head not in ready:
            pair = range(head, min(head + 2, sum_ref.shape[0]))
            weights = jnp.concatenate([weight_ref[one] for one in pair], axis=1)
            both = jnp.dot(turned, weights, preferred_element_type=jnp.float32)
            width = sum_ref.shape[2]
            for at_column, one in enumerate(pair):
                ready[one] = both[:, at_column * width:(at_column + 1) * width]
        added = ready.pop(head)
        return (sum_ref[head] + added * share_ref[head:head + 1, :]).astype(jnp.bfloat16)

    def send(head, out):
        cols = slice(head * HEAD_WIDTH, (head + 1) * HEAD_WIDTH)
        block_ref[:, cols] = jnp.transpose(out)
        copy = pltpu.make_async_copy(block_ref.at[:, cols], out_ref.at[:, cols], sems.at[head])
        copy.start()
        copies.append(copy)

    in_stages(sum_ref.shape[0], [mix, send])
    for copy in copies:
        copy.wait()


SHORT = pl.CostEstimate(flops=0, bytes_accessed=0, transcendentals=0)


def in_vmem(*arrays):
    return [pltpu.with_memory_space_constraint(array, pltpu.VMEM) for array in arrays]


def in_hbm(*arrays):
    return [pltpu.with_memory_space_constraint(array, pltpu.HBM) for array in arrays]


VMEM_REF = pl.BlockSpec(memory_space=pltpu.VMEM)
HBM_REF = pl.BlockSpec(memory_space=pltpu.HBM)
PARAMS = pltpu.CompilerParams(vmem_limit_bytes=32 << 20)


def moved(value, mask):
    return lax.ppermute(value, "seq", [(i, i ^ mask) for i in range(lax.axis_size("seq"))])


def staged_attention(queries, keys, values, lengths, old_place):
    far_keys, far_values = moved(keys, 2), moved(values, 2)
    near_keys, near_values = moved(keys, 1), moved(values, 1)
    rows, cols = queries.shape
    heads = cols // HEAD_WIDTH
    devices = lax.axis_size("seq")
    own = lax.axis_index("seq").astype(jnp.int32)
    places = old_place.reshape(1, -1)
    state = [
        pltpu.VMEM((heads, rows), jnp.float32),
        pltpu.VMEM((heads, rows), jnp.float32),
        pltpu.VMEM((heads, HEAD_WIDTH, rows), jnp.float32),
    ]
    work = [
        pltpu.VMEM((heads, rows, rows), jnp.float32),
        pltpu.VMEM((heads, rows, rows), jnp.bfloat16),
    ]
    across, bias, *carried = pl.pallas_call(
        own_kernel,
        in_specs=[pl.BlockSpec(memory_space=pltpu.SMEM)] + [HBM_REF] * 5,
        out_specs=[VMEM_REF] * 5,
        out_shape=[
            pltpu.VMEM((heads, HEAD_WIDTH, rows), jnp.bfloat16),
            pltpu.VMEM((devices, rows, rows), jnp.float32),
        ] + state,
        scratch_shapes=[
            pltpu.SMEM(lengths.shape, jnp.int32),
            pltpu.VMEM(places.shape, jnp.int32),
            pltpu.VMEM(queries.shape, jnp.bfloat16),
            pltpu.VMEM(keys.shape, jnp.bfloat16),
            pltpu.VMEM(values.shape, jnp.bfloat16),
        ] + work + [pltpu.SemaphoreType.DMA((5,))],
        compiler_params=PARAMS,
        cost_estimate=SHORT,
        name="own_shard",
    )(own.reshape(1), *in_hbm(lengths, places, queries, keys, values))

    def add_shard(at, keys, values, carried):
        return pl.pallas_call(
            lambda *refs: next_kernel(at, *refs),
            in_specs=[VMEM_REF] * 7,
            out_specs=[VMEM_REF] * 3,
            out_shape=state,
            scratch_shapes=work,
            compiler_params=PARAMS,
            cost_estimate=SHORT,
            name="next_shard",
        )(*in_vmem(across, bias, *carried), keys, values)

    far_keys, *carried = lax.optimization_barrier((far_keys, *carried))
    third_keys = moved(far_keys, 1)
    far_values, *carried = lax.optimization_barrier((far_values, *carried))
    third_values = moved(far_values, 1)
    carried = add_shard(2, far_keys, far_values, carried)
    carried = add_shard(1, near_keys, near_values, carried)
    scaled_sum = pltpu.VMEM((heads, HEAD_WIDTH, rows), jnp.float32)
    last = pl.pallas_call(
        lambda *refs: weights_kernel(3, *refs),
        in_specs=[VMEM_REF] * 6,
        out_specs=[VMEM_REF] * 3,
        out_shape=[scaled_sum, work[1], state[0]],
        scratch_shapes=work[:1],
        compiler_params=PARAMS,
        cost_estimate=SHORT,
        name="last_weights",
    )(*in_vmem(across, bias, *carried), third_keys)
    return pl.pallas_call(
        last_kernel,
        in_specs=[VMEM_REF] * 4,
        out_specs=pl.BlockSpec(memory_space=pl.ANY),
        out_shape=jax.ShapeDtypeStruct((rows, cols), jnp.bfloat16),
        scratch_shapes=[
            pltpu.VMEM((rows, cols), jnp.bfloat16),
            pltpu.SemaphoreType.DMA((heads,)),
        ],
        compiler_params=PARAMS,
        cost_estimate=SHORT,
        name="last_values",
    )(*in_vmem(*last), third_values)


def online_kernel(heads, q_ref, k_ref, v_ref, key_pos_ref, query_pos_ref, start_ref, out_ref, peak_ref, acc_ref):
    step = pl.program_id(0)

    @pl.when(step == 0)
    def _():
        peak_ref[...] = jnp.full(peak_ref.shape, NEG_FILL, jnp.float32)
        acc_ref[...] = jnp.zeros(acc_ref.shape, jnp.float32)

    key_pos = key_pos_ref[...]
    visible = (key_pos >= start_ref[...]) & (key_pos <= query_pos_ref[...])
    values = v_ref[...]
    ext = jnp.concatenate([values, jnp.ones_like(values)], axis=1)
    for head in range(heads):
        q = q_ref[:, head * HEAD_WIDTH:(head + 1) * HEAD_WIDTH]
        scores = lax.dot_general(
            q, k_ref[...], (((1,), (1,)), ((), ())), preferred_element_type=jnp.float32
        )
        scaled = jnp.where(visible, scores * (HEAD_WIDTH ** -0.5 * LOG2_E), NEG_FILL)
        before = peak_ref[head]
        peak = jnp.maximum(before, jnp.max(scaled, axis=1, keepdims=True))
        weights = jnp.where(visible, jnp.exp2(scaled - peak), 0.0).astype(jnp.bfloat16)
        peak_ref[head] = peak
        acc_ref[head] = acc_ref[head] * jnp.exp2(before - peak) + jnp.dot(
            weights, ext, preferred_element_type=jnp.float32
        )

    @pl.when(step == pl.num_programs(0) - 1)
    def _():
        for head in range(heads):
            acc = acc_ref[head]
            out_ref[:, head * HEAD_WIDTH:(head + 1) * HEAD_WIDTH] = (
                acc[:, :HEAD_WIDTH] / acc[:, HEAD_WIDTH:]
            ).astype(jnp.bfloat16)


def online_attention(queries, keys, values, key_pos, query_pos, starts, chunk):
    rows, cols = queries.shape
    heads = cols // HEAD_WIDTH
    key_count = keys.shape[0]
    return pl.pallas_call(
        lambda *refs: online_kernel(heads, *refs),
        grid=(key_count // chunk,),
        in_specs=[
            pl.BlockSpec((rows, cols), lambda j: (0, 0)),
            pl.BlockSpec((chunk, HEAD_WIDTH), lambda j: (j, 0)),
            pl.BlockSpec((chunk, HEAD_WIDTH), lambda j: (j, 0)),
            pl.BlockSpec((1, chunk), lambda j: (0, j)),
            pl.BlockSpec((rows, 1), lambda j: (0, 0)),
            pl.BlockSpec((rows, 1), lambda j: (0, 0)),
        ],
        out_specs=pl.BlockSpec((rows, cols), lambda j: (0, 0)),
        out_shape=jax.ShapeDtypeStruct((rows, cols), jnp.bfloat16),
        scratch_shapes=[
            pltpu.VMEM((heads, rows, 1), jnp.float32),
            pltpu.VMEM((heads, rows, 2 * HEAD_WIDTH), jnp.float32),
        ],
        compiler_params=pltpu.CompilerParams(vmem_limit_bytes=32 << 20),
        name="online",
    )(queries, keys, values, key_pos, query_pos, starts)


def body(queries, keys, values, lengths, old_place):
    devices = lax.axis_size("seq")
    row_count = queries.shape[0]
    key_count = row_count * devices
    if devices == 4 and key_count <= 1024:
        return staged_attention(queries, keys, values, lengths, old_place)
    all_keys = lax.all_gather(keys, "seq", axis=0, tiled=True)
    all_values = lax.all_gather(values, "seq", axis=0, tiled=True)
    key_pos, query_pos, starts = block_places(
        lengths, old_place, lax.axis_index("seq"), row_count, key_count
    )
    return online_attention(queries, all_keys, all_values, key_pos, query_pos, starts, 512)


def solution(mesh):
    in_specs = (
        P(("groups", "seq"), "mp"),
        P(("groups", "seq"), "mp"),
        P(("groups", "seq"), "mp"),
        P("groups"),
        P("groups"),
    )
    out_specs = P(("groups", "seq"), "mp")
    return jax.shard_map(body, mesh=mesh, in_specs=in_specs, out_specs=out_specs, check_vma=False)
```

```python
import jax
import jax.numpy as jnp
from jax import lax
from jax.experimental import pallas as pl
from jax.experimental.pallas import tpu as pltpu
from jax.sharding import PartitionSpec as P

HEAD_WIDTH = 128
LOG2_E = 1.4426950408889634
NEG_FILL = -1e30


def block_places(lengths, old_place, own_index, row_count, key_count):
    block_total = old_place.shape[0]
    block_rows = key_count // block_total
    ids = jnp.arange(block_total, dtype=jnp.int32)
    hit = old_place[:, None] == ids[None, :]
    new_block = jnp.sum(jnp.where(hit, ids[:, None], 0), axis=0)
    key_pos = (new_block[:, None] * block_rows + jnp.arange(block_rows, dtype=jnp.int32)).reshape(-1)
    query_pos = lax.dynamic_slice_in_dim(key_pos, own_index * row_count, row_count)
    bounds = jnp.cumsum(lengths)
    starts = jnp.max(jnp.where(bounds[None, :] <= query_pos[:, None], bounds[None, :], 0), axis=1)
    return key_pos.reshape(1, -1), query_pos.reshape(-1, 1), starts.reshape(-1, 1)


def iota(shape, dim):
    return lax.broadcasted_iota(jnp.int32, shape, dim)


def row_sum_as_column(places):
    square = (places.shape[1],) * 2
    spread = jnp.where(iota(square, 0) == iota(square, 1), places, 0).astype(jnp.float32)
    return jnp.sum(spread, axis=1, keepdims=True).astype(jnp.int32)


def query_places(own, lengths_ref, places, rows):
    block_total = places.shape[1]
    block_rows = rows * lax.axis_size("seq") // block_total
    shape = (block_total, rows)
    hit = row_sum_as_column(places) == own * (rows // block_rows) + iota(shape, 1) // block_rows
    at = jnp.where(hit, iota(shape, 0) * block_rows, 0).astype(jnp.float32)
    query_pos = jnp.sum(at, axis=0, keepdims=True) + (
        iota((1, rows), 1) % block_rows
    ).astype(jnp.float32)
    starts = jnp.zeros_like(query_pos)
    bound = jnp.int32(0)
    for t in range(lengths_ref.shape[0]):
        bound = bound + lengths_ref[t]
        edge = bound.astype(jnp.float32)
        starts = jnp.where(edge <= query_pos, edge, starts)
    return query_pos, starts


def mask_table(owner, query_pos, starts, places):
    block_total, rows = places.shape[1], query_pos.shape[1]
    block_rows = rows * lax.axis_size("seq") // block_total
    shape = (rows, block_total)
    hit = places == owner * (rows // block_rows) + iota(shape, 0) // block_rows
    at = jnp.where(hit, iota(shape, 1) * block_rows, 0).astype(jnp.float32)
    key_pos = jnp.sum(at, axis=1, keepdims=True) + (
        iota((rows, 1), 0) % block_rows
    ).astype(jnp.float32)
    return jnp.where((key_pos >= starts) & (key_pos <= query_pos), 0.0, NEG_FILL)


def in_stages(heads, stages):
    results = [{} for _ in stages]
    for step in range(heads + len(stages) - 1):
        for late, stage in enumerate(stages):
            head = step - late
            if 0 <= head < heads:
                before = results[late - 1].pop(head) if late else None
                results[late][head] = stage(head, before)


def score_stage(keys, across_ref, bias_ref, at, scaled_ref, old_peak):
    ready = {}

    def stage(head, _):
        if head not in ready:
            group = range(head, min(head + 4, across_ref.shape[0]))
            across = jnp.concatenate([across_ref[one] for one in group], axis=1)
            both = jnp.dot(keys, across, preferred_element_type=jnp.float32)
            for at_column, one in enumerate(group):
                width = across_ref.shape[2]
                ready[one] = both[:, at_column * width:(at_column + 1) * width]
        scores = ready.pop(head)
        scaled = scores * (HEAD_WIDTH ** -0.5 * LOG2_E) + bias_ref[at]
        scaled_ref[head] = scaled
        peak = jnp.max(scaled, axis=0, keepdims=True)
        return peak if old_peak is None else jnp.maximum(old_peak(head), peak)

    return stage


def weight_stage(scaled_ref, weight_ref):
    def stage(head, peak):
        weights = jnp.exp2(scaled_ref[head] - peak)
        weight_ref[head] = weights.astype(jnp.bfloat16)
        return peak, jnp.sum(weights, axis=0, keepdims=True)

    return stage


def own_kernel(
    own_ref, lengths_hbm, places_hbm, q_hbm, k_hbm, v_hbm,
    across_ref, bias_ref, peak_ref, total_ref, sum_ref,
    lengths_ref, places_ref, q_ref, k_ref, v_ref, scaled_ref, weight_ref, sems,
):
    moves = (
        (lengths_hbm, lengths_ref), (places_hbm, places_ref),
        (k_hbm, k_ref), (v_hbm, v_ref), (q_hbm, q_ref),
    )
    copies = [pltpu.make_async_copy(*move, sems.at[n]) for n, move in enumerate(moves)]
    for copy in copies:
        copy.start()
    for copy in copies:
        copy.wait()
    heads, _, rows = across_ref.shape
    own, places = own_ref[0], places_ref[...]
    keys = k_ref[...]
    query_pos, starts = query_places(own, lengths_ref, places, rows)
    bias_ref[0] = mask_table(own, query_pos, starts, places)
    turned = jnp.transpose(v_ref[...])

    def turn(head, _):
        q = q_ref[:, head * HEAD_WIDTH:(head + 1) * HEAD_WIDTH]
        across_ref[head] = jnp.transpose(q)
        if 0 < head < bias_ref.shape[0]:
            bias_ref[head] = mask_table(own ^ head, query_pos, starts, places)

    def mix(head, reached):
        peak_ref[head:head + 1, :], total_ref[head:head + 1, :] = reached
        sum_ref[head] = jnp.dot(turned, weight_ref[head], preferred_element_type=jnp.float32)

    for head in range(heads):
        turn(head, None)
    in_stages(heads, [
        score_stage(keys, across_ref, bias_ref, 0, scaled_ref, None),
        weight_stage(scaled_ref, weight_ref),
        mix,
    ])


def next_kernel(
    at, across_ref, bias_ref, peak_ref, total_ref, sum_ref, k_ref, v_ref,
    new_peak_ref, new_total_ref, new_sum_ref, scaled_ref, weight_ref,
):
    turned = jnp.transpose(v_ref[...])

    def mix(head, reached):
        peak, total = reached
        row = slice(head, head + 1)
        factor = jnp.exp2(peak_ref[row, :] - peak)
        new_peak_ref[row, :] = peak
        new_total_ref[row, :] = total_ref[row, :] * factor + total
        added = jnp.dot(turned, weight_ref[head], preferred_element_type=jnp.float32)
        new_sum_ref[head] = sum_ref[head] * factor + added

    in_stages(across_ref.shape[0], [
        score_stage(
            k_ref[...], across_ref, bias_ref, at, scaled_ref,
            lambda head: peak_ref[head:head + 1, :],
        ),
        weight_stage(scaled_ref, weight_ref),
        mix,
    ])


def weights_kernel(
    at, across_ref, bias_ref, peak_ref, total_ref, sum_ref, k_ref,
    new_sum_ref, weight_ref, share_ref, scaled_ref,
):
    def rescale(head, reached):
        peak, total = reached
        row = slice(head, head + 1)
        factor = jnp.exp2(peak_ref[row, :] - peak)
        share = 1.0 / (total_ref[row, :] * factor + total)
        share_ref[row, :] = share
        new_sum_ref[head] = sum_ref[head] * (factor * share)

    in_stages(across_ref.shape[0], [
        score_stage(
            k_ref[...], across_ref, bias_ref, at, scaled_ref,
            lambda head: peak_ref[head:head + 1, :],
        ),
        weight_stage(scaled_ref, weight_ref),
        rescale,
    ])


def last_kernel(sum_ref, weight_ref, share_ref, v_ref, out_ref, block_ref, sems):
    turned = jnp.transpose(v_ref[...])
    copies = []

    ready = {}

    def mix(head, _):
        if head not in ready:
            group = range(head, min(head + 4, sum_ref.shape[0]))
            weights = jnp.concatenate([weight_ref[one] for one in group], axis=1)
            both = jnp.dot(turned, weights, preferred_element_type=jnp.float32)
            width = sum_ref.shape[2]
            for at_column, one in enumerate(group):
                ready[one] = both[:, at_column * width:(at_column + 1) * width]
        added = ready.pop(head)
        return (sum_ref[head] + added * share_ref[head:head + 1, :]).astype(jnp.bfloat16)

    def send(head, out):
        cols = slice(head * HEAD_WIDTH, (head + 1) * HEAD_WIDTH)
        block_ref[:, cols] = jnp.transpose(out)
        copy = pltpu.make_async_copy(block_ref.at[:, cols], out_ref.at[:, cols], sems.at[head])
        copy.start()
        copies.append(copy)

    in_stages(sum_ref.shape[0], [mix, send])
    for copy in copies:
        copy.wait()


SHORT = pl.CostEstimate(flops=0, bytes_accessed=0, transcendentals=0)


def in_vmem(*arrays):
    return [pltpu.with_memory_space_constraint(array, pltpu.VMEM) for array in arrays]


def in_hbm(*arrays):
    return [pltpu.with_memory_space_constraint(array, pltpu.HBM) for array in arrays]


VMEM_REF = pl.BlockSpec(memory_space=pltpu.VMEM)
HBM_REF = pl.BlockSpec(memory_space=pltpu.HBM)
PARAMS = pltpu.CompilerParams(vmem_limit_bytes=32 << 20)


def moved(value, mask):
    return lax.ppermute(value, "seq", [(i, i ^ mask) for i in range(lax.axis_size("seq"))])


def staged_attention(queries, keys, values, lengths, old_place):
    far_keys, far_values = moved(keys, 2), moved(values, 2)
    near_keys, near_values = moved(keys, 1), moved(values, 1)
    rows, cols = queries.shape
    heads = cols // HEAD_WIDTH
    devices = lax.axis_size("seq")
    own = lax.axis_index("seq").astype(jnp.int32)
    places = old_place.reshape(1, -1)
    state = [
        pltpu.VMEM((heads, rows), jnp.float32),
        pltpu.VMEM((heads, rows), jnp.float32),
        pltpu.VMEM((heads, HEAD_WIDTH, rows), jnp.float32),
    ]
    work = [
        pltpu.VMEM((heads, rows, rows), jnp.float32),
        pltpu.VMEM((heads, rows, rows), jnp.bfloat16),
    ]
    across, bias, *carried = pl.pallas_call(
        own_kernel,
        in_specs=[pl.BlockSpec(memory_space=pltpu.SMEM)] + [HBM_REF] * 5,
        out_specs=[VMEM_REF] * 5,
        out_shape=[
            pltpu.VMEM((heads, HEAD_WIDTH, rows), jnp.bfloat16),
            pltpu.VMEM((devices, rows, rows), jnp.float32),
        ] + state,
        scratch_shapes=[
            pltpu.SMEM(lengths.shape, jnp.int32),
            pltpu.VMEM(places.shape, jnp.int32),
            pltpu.VMEM(queries.shape, jnp.bfloat16),
            pltpu.VMEM(keys.shape, jnp.bfloat16),
            pltpu.VMEM(values.shape, jnp.bfloat16),
        ] + work + [pltpu.SemaphoreType.DMA((5,))],
        compiler_params=PARAMS,
        cost_estimate=SHORT,
        name="own_shard",
    )(own.reshape(1), *in_hbm(lengths, places, queries, keys, values))

    def add_shard(at, keys, values, carried):
        return pl.pallas_call(
            lambda *refs: next_kernel(at, *refs),
            in_specs=[VMEM_REF] * 7,
            out_specs=[VMEM_REF] * 3,
            out_shape=state,
            scratch_shapes=work,
            compiler_params=PARAMS,
            cost_estimate=SHORT,
            name="next_shard",
        )(*in_vmem(across, bias, *carried), keys, values)

    far_keys, *carried = lax.optimization_barrier((far_keys, *carried))
    third_keys = moved(far_keys, 1)
    far_values, *carried = lax.optimization_barrier((far_values, *carried))
    third_values = moved(far_values, 1)
    carried = add_shard(2, far_keys, far_values, carried)
    carried = add_shard(1, near_keys, near_values, carried)
    scaled_sum = pltpu.VMEM((heads, HEAD_WIDTH, rows), jnp.float32)
    last = pl.pallas_call(
        lambda *refs: weights_kernel(3, *refs),
        in_specs=[VMEM_REF] * 6,
        out_specs=[VMEM_REF] * 3,
        out_shape=[scaled_sum, work[1], state[0]],
        scratch_shapes=work[:1],
        compiler_params=PARAMS,
        cost_estimate=SHORT,
        name="last_weights",
    )(*in_vmem(across, bias, *carried), third_keys)
    return pl.pallas_call(
        last_kernel,
        in_specs=[VMEM_REF] * 4,
        out_specs=pl.BlockSpec(memory_space=pl.ANY),
        out_shape=jax.ShapeDtypeStruct((rows, cols), jnp.bfloat16),
        scratch_shapes=[
            pltpu.VMEM((rows, cols), jnp.bfloat16),
            pltpu.SemaphoreType.DMA((heads,)),
        ],
        compiler_params=PARAMS,
        cost_estimate=SHORT,
        name="last_values",
    )(*in_vmem(*last), third_values)


def online_kernel(heads, q_ref, k_ref, v_ref, key_pos_ref, query_pos_ref, start_ref, out_ref, peak_ref, acc_ref):
    step = pl.program_id(0)

    @pl.when(step == 0)
    def _():
        peak_ref[...] = jnp.full(peak_ref.shape, NEG_FILL, jnp.float32)
        acc_ref[...] = jnp.zeros(acc_ref.shape, jnp.float32)

    key_pos = key_pos_ref[...]
    visible = (key_pos >= start_ref[...]) & (key_pos <= query_pos_ref[...])
    values = v_ref[...]
    ext = jnp.concatenate([values, jnp.ones_like(values)], axis=1)
    for head in range(heads):
        q = q_ref[:, head * HEAD_WIDTH:(head + 1) * HEAD_WIDTH]
        scores = lax.dot_general(
            q, k_ref[...], (((1,), (1,)), ((), ())), preferred_element_type=jnp.float32
        )
        scaled = jnp.where(visible, scores * (HEAD_WIDTH ** -0.5 * LOG2_E), NEG_FILL)
        before = peak_ref[head]
        peak = jnp.maximum(before, jnp.max(scaled, axis=1, keepdims=True))
        weights = jnp.where(visible, jnp.exp2(scaled - peak), 0.0).astype(jnp.bfloat16)
        peak_ref[head] = peak
        acc_ref[head] = acc_ref[head] * jnp.exp2(before - peak) + jnp.dot(
            weights, ext, preferred_element_type=jnp.float32
        )

    @pl.when(step == pl.num_programs(0) - 1)
    def _():
        for head in range(heads):
            acc = acc_ref[head]
            out_ref[:, head * HEAD_WIDTH:(head + 1) * HEAD_WIDTH] = (
                acc[:, :HEAD_WIDTH] / acc[:, HEAD_WIDTH:]
            ).astype(jnp.bfloat16)


def online_attention(queries, keys, values, key_pos, query_pos, starts, chunk):
    rows, cols = queries.shape
    heads = cols // HEAD_WIDTH
    key_count = keys.shape[0]
    return pl.pallas_call(
        lambda *refs: online_kernel(heads, *refs),
        grid=(key_count // chunk,),
        in_specs=[
            pl.BlockSpec((rows, cols), lambda j: (0, 0)),
            pl.BlockSpec((chunk, HEAD_WIDTH), lambda j: (j, 0)),
            pl.BlockSpec((chunk, HEAD_WIDTH), lambda j: (j, 0)),
            pl.BlockSpec((1, chunk), lambda j: (0, j)),
            pl.BlockSpec((rows, 1), lambda j: (0, 0)),
            pl.BlockSpec((rows, 1), lambda j: (0, 0)),
        ],
        out_specs=pl.BlockSpec((rows, cols), lambda j: (0, 0)),
        out_shape=jax.ShapeDtypeStruct((rows, cols), jnp.bfloat16),
        scratch_shapes=[
            pltpu.VMEM((heads, rows, 1), jnp.float32),
            pltpu.VMEM((heads, rows, 2 * HEAD_WIDTH), jnp.float32),
        ],
        compiler_params=pltpu.CompilerParams(vmem_limit_bytes=32 << 20),
        name="online",
    )(queries, keys, values, key_pos, query_pos, starts)


def body(queries, keys, values, lengths, old_place):
    devices = lax.axis_size("seq")
    row_count = queries.shape[0]
    key_count = row_count * devices
    if devices == 4 and key_count <= 1024:
        return staged_attention(queries, keys, values, lengths, old_place)
    all_keys = lax.all_gather(keys, "seq", axis=0, tiled=True)
    all_values = lax.all_gather(values, "seq", axis=0, tiled=True)
    key_pos, query_pos, starts = block_places(
        lengths, old_place, lax.axis_index("seq"), row_count, key_count
    )
    return online_attention(queries, all_keys, all_values, key_pos, query_pos, starts, 512)


def solution(mesh):
    in_specs = (
        P(("groups", "seq"), "mp"),
        P(("groups", "seq"), "mp"),
        P(("groups", "seq"), "mp"),
        P("groups"),
        P("groups"),
    )
    out_specs = P(("groups", "seq"), "mp")
    return jax.shard_map(body, mesh=mesh, in_specs=in_specs, out_specs=out_specs, check_vma=False)
```

```python
import jax
import jax.numpy as jnp
from jax import lax
from jax.experimental import pallas as pl
from jax.experimental.pallas import tpu as pltpu
from jax.sharding import PartitionSpec as P

HEAD_WIDTH = 128
LOG2_E = 1.4426950408889634
NEG_FILL = -1e30


def block_places(lengths, old_place, own_index, row_count, key_count):
    block_total = old_place.shape[0]
    block_rows = key_count // block_total
    ids = jnp.arange(block_total, dtype=jnp.int32)
    hit = old_place[:, None] == ids[None, :]
    new_block = jnp.sum(jnp.where(hit, ids[:, None], 0), axis=0)
    key_pos = (new_block[:, None] * block_rows + jnp.arange(block_rows, dtype=jnp.int32)).reshape(-1)
    query_pos = lax.dynamic_slice_in_dim(key_pos, own_index * row_count, row_count)
    bounds = jnp.cumsum(lengths)
    starts = jnp.max(jnp.where(bounds[None, :] <= query_pos[:, None], bounds[None, :], 0), axis=1)
    return key_pos.reshape(1, -1), query_pos.reshape(-1, 1), starts.reshape(-1, 1)


def iota(shape, dim):
    return lax.broadcasted_iota(jnp.int32, shape, dim)


def row_sum_as_column(places):
    square = (places.shape[1],) * 2
    spread = jnp.where(iota(square, 0) == iota(square, 1), places, 0).astype(jnp.float32)
    return jnp.sum(spread, axis=1, keepdims=True).astype(jnp.int32)


def query_places(own, lengths_ref, places, rows):
    block_total = places.shape[1]
    block_rows = rows * lax.axis_size("seq") // block_total
    shape = (block_total, rows)
    hit = row_sum_as_column(places) == own * (rows // block_rows) + iota(shape, 1) // block_rows
    at = jnp.where(hit, iota(shape, 0) * block_rows, 0).astype(jnp.float32)
    query_pos = jnp.sum(at, axis=0, keepdims=True) + (
        iota((1, rows), 1) % block_rows
    ).astype(jnp.float32)
    starts = jnp.zeros_like(query_pos)
    bound = jnp.int32(0)
    for t in range(lengths_ref.shape[0]):
        bound = bound + lengths_ref[t]
        edge = bound.astype(jnp.float32)
        starts = jnp.where(edge <= query_pos, edge, starts)
    return query_pos, starts


def mask_table(owner, query_pos, starts, places):
    block_total, rows = places.shape[1], query_pos.shape[1]
    block_rows = rows * lax.axis_size("seq") // block_total
    shape = (rows, block_total)
    hit = places == owner * (rows // block_rows) + iota(shape, 0) // block_rows
    at = jnp.where(hit, iota(shape, 1) * block_rows, 0).astype(jnp.float32)
    key_pos = jnp.sum(at, axis=1, keepdims=True) + (
        iota((rows, 1), 0) % block_rows
    ).astype(jnp.float32)
    return jnp.where((key_pos >= starts) & (key_pos <= query_pos), 0.0, NEG_FILL)


def in_stages(heads, stages):
    results = [{} for _ in stages]
    for step in range(heads + len(stages) - 1):
        for late, stage in enumerate(stages):
            head = step - late
            if 0 <= head < heads:
                before = results[late - 1].pop(head) if late else None
                results[late][head] = stage(head, before)


def score_stage(keys, across_ref, bias_ref, at, scaled_ref, old_peak):
    ready = {}

    def stage(head, _):
        if head not in ready:
            group = range(head, min(head + 4, across_ref.shape[0]))
            across = jnp.concatenate([across_ref[one] for one in group], axis=1)
            both = jnp.dot(keys, across, preferred_element_type=jnp.float32)
            for at_column, one in enumerate(group):
                width = across_ref.shape[2]
                ready[one] = both[:, at_column * width:(at_column + 1) * width]
        scores = ready.pop(head)
        scaled = scores * (HEAD_WIDTH ** -0.5 * LOG2_E) + bias_ref[at]
        scaled_ref[head] = scaled
        peak = jnp.max(scaled, axis=0, keepdims=True)
        return peak if old_peak is None else jnp.maximum(old_peak(head), peak)

    return stage


def weight_stage(scaled_ref, weight_ref):
    def stage(head, peak):
        weights = jnp.exp2(scaled_ref[head] - peak)
        weight_ref[head] = weights.astype(jnp.bfloat16)
        return peak, jnp.sum(weights, axis=0, keepdims=True)

    return stage


def own_kernel(
    own_ref, lengths_hbm, places_hbm, q_hbm, k_hbm, v_hbm,
    across_ref, bias_ref, peak_ref, total_ref, sum_ref,
    lengths_ref, places_ref, q_ref, k_ref, v_ref, scaled_ref, weight_ref, sems,
):
    moves = (
        (lengths_hbm, lengths_ref), (places_hbm, places_ref),
        (k_hbm, k_ref), (v_hbm, v_ref), (q_hbm, q_ref),
    )
    copies = [pltpu.make_async_copy(*move, sems.at[n]) for n, move in enumerate(moves)]
    for copy in copies:
        copy.start()
    for copy in copies:
        copy.wait()
    heads, _, rows = across_ref.shape
    own, places = own_ref[0], places_ref[...]
    keys = k_ref[...]
    query_pos, starts = query_places(own, lengths_ref, places, rows)
    bias_ref[0] = mask_table(own, query_pos, starts, places)
    turned = jnp.transpose(v_ref[...])

    def turn(head, _):
        q = q_ref[:, head * HEAD_WIDTH:(head + 1) * HEAD_WIDTH]
        across_ref[head] = jnp.transpose(q)
        if 0 < head < bias_ref.shape[0]:
            bias_ref[head] = mask_table(own ^ head, query_pos, starts, places)

    def mix(head, reached):
        peak_ref[head:head + 1, :], total_ref[head:head + 1, :] = reached
        sum_ref[head] = jnp.dot(turned, weight_ref[head], preferred_element_type=jnp.float32)

    for head in range(heads):
        turn(head, None)
    in_stages(heads, [
        score_stage(keys, across_ref, bias_ref, 0, scaled_ref, None),
        weight_stage(scaled_ref, weight_ref),
        mix,
    ])


def next_kernel(
    at, across_ref, bias_ref, peak_ref, total_ref, sum_ref, k_ref, v_ref,
    new_peak_ref, new_total_ref, new_sum_ref, scaled_ref, weight_ref,
):
    turned = jnp.transpose(v_ref[...])

    def mix(head, reached):
        peak, total = reached
        row = slice(head, head + 1)
        factor = jnp.exp2(peak_ref[row, :] - peak)
        new_peak_ref[row, :] = peak
        new_total_ref[row, :] = total_ref[row, :] * factor + total
        added = jnp.dot(turned, weight_ref[head], preferred_element_type=jnp.float32)
        new_sum_ref[head] = sum_ref[head] * factor + added

    in_stages(across_ref.shape[0], [
        score_stage(
            k_ref[...], across_ref, bias_ref, at, scaled_ref,
            lambda head: peak_ref[head:head + 1, :],
        ),
        weight_stage(scaled_ref, weight_ref),
        mix,
    ])


def weights_kernel(
    at, across_ref, bias_ref, peak_ref, total_ref, sum_ref, k_ref,
    new_sum_ref, weight_ref, share_ref, scaled_ref,
):
    def rescale(head, reached):
        peak, total = reached
        row = slice(head, head + 1)
        factor = jnp.exp2(peak_ref[row, :] - peak)
        share = 1.0 / (total_ref[row, :] * factor + total)
        share_ref[row, :] = share
        new_sum_ref[head] = sum_ref[head] * (factor * share)

    in_stages(across_ref.shape[0], [
        score_stage(
            k_ref[...], across_ref, bias_ref, at, scaled_ref,
            lambda head: peak_ref[head:head + 1, :],
        ),
        weight_stage(scaled_ref, weight_ref),
        rescale,
    ])


def last_kernel(sum_ref, weight_ref, share_ref, v_ref, out_ref, block_ref, sems):
    turned = jnp.transpose(v_ref[...])
    copies = []

    ready = {}

    def mix(head, _):
        if head not in ready:
            group = range(head, min(head + 8, sum_ref.shape[0]))
            weights = jnp.concatenate([weight_ref[one] for one in group], axis=1)
            both = jnp.dot(turned, weights, preferred_element_type=jnp.float32)
            width = sum_ref.shape[2]
            for at_column, one in enumerate(group):
                ready[one] = both[:, at_column * width:(at_column + 1) * width]
        added = ready.pop(head)
        return (sum_ref[head] + added * share_ref[head:head + 1, :]).astype(jnp.bfloat16)

    def send(head, out):
        cols = slice(head * HEAD_WIDTH, (head + 1) * HEAD_WIDTH)
        block_ref[:, cols] = jnp.transpose(out)
        copy = pltpu.make_async_copy(block_ref.at[:, cols], out_ref.at[:, cols], sems.at[head])
        copy.start()
        copies.append(copy)

    in_stages(sum_ref.shape[0], [mix, send])
    for copy in copies:
        copy.wait()


SHORT = pl.CostEstimate(flops=0, bytes_accessed=0, transcendentals=0)


def in_vmem(*arrays):
    return [pltpu.with_memory_space_constraint(array, pltpu.VMEM) for array in arrays]


def in_hbm(*arrays):
    return [pltpu.with_memory_space_constraint(array, pltpu.HBM) for array in arrays]


VMEM_REF = pl.BlockSpec(memory_space=pltpu.VMEM)
HBM_REF = pl.BlockSpec(memory_space=pltpu.HBM)
PARAMS = pltpu.CompilerParams(vmem_limit_bytes=32 << 20)


def moved(value, mask):
    return lax.ppermute(value, "seq", [(i, i ^ mask) for i in range(lax.axis_size("seq"))])


def staged_attention(queries, keys, values, lengths, old_place):
    far_keys, far_values = moved(keys, 2), moved(values, 2)
    near_keys, near_values = moved(keys, 1), moved(values, 1)
    rows, cols = queries.shape
    heads = cols // HEAD_WIDTH
    devices = lax.axis_size("seq")
    own = lax.axis_index("seq").astype(jnp.int32)
    places = old_place.reshape(1, -1)
    state = [
        pltpu.VMEM((heads, rows), jnp.float32),
        pltpu.VMEM((heads, rows), jnp.float32),
        pltpu.VMEM((heads, HEAD_WIDTH, rows), jnp.float32),
    ]
    work = [
        pltpu.VMEM((heads, rows, rows), jnp.float32),
        pltpu.VMEM((heads, rows, rows), jnp.bfloat16),
    ]
    across, bias, *carried = pl.pallas_call(
        own_kernel,
        in_specs=[pl.BlockSpec(memory_space=pltpu.SMEM)] + [HBM_REF] * 5,
        out_specs=[VMEM_REF] * 5,
        out_shape=[
            pltpu.VMEM((heads, HEAD_WIDTH, rows), jnp.bfloat16),
            pltpu.VMEM((devices, rows, rows), jnp.float32),
        ] + state,
        scratch_shapes=[
            pltpu.SMEM(lengths.shape, jnp.int32),
            pltpu.VMEM(places.shape, jnp.int32),
            pltpu.VMEM(queries.shape, jnp.bfloat16),
            pltpu.VMEM(keys.shape, jnp.bfloat16),
            pltpu.VMEM(values.shape, jnp.bfloat16),
        ] + work + [pltpu.SemaphoreType.DMA((5,))],
        compiler_params=PARAMS,
        cost_estimate=SHORT,
        name="own_shard",
    )(own.reshape(1), *in_hbm(lengths, places, queries, keys, values))

    def add_shard(at, keys, values, carried):
        return pl.pallas_call(
            lambda *refs: next_kernel(at, *refs),
            in_specs=[VMEM_REF] * 7,
            out_specs=[VMEM_REF] * 3,
            out_shape=state,
            scratch_shapes=work,
            compiler_params=PARAMS,
            cost_estimate=SHORT,
            name="next_shard",
        )(*in_vmem(across, bias, *carried), keys, values)

    far_keys, *carried = lax.optimization_barrier((far_keys, *carried))
    third_keys = moved(far_keys, 1)
    far_values, *carried = lax.optimization_barrier((far_values, *carried))
    third_values = moved(far_values, 1)
    carried = add_shard(2, far_keys, far_values, carried)
    carried = add_shard(1, near_keys, near_values, carried)
    scaled_sum = pltpu.VMEM((heads, HEAD_WIDTH, rows), jnp.float32)
    last = pl.pallas_call(
        lambda *refs: weights_kernel(3, *refs),
        in_specs=[VMEM_REF] * 6,
        out_specs=[VMEM_REF] * 3,
        out_shape=[scaled_sum, work[1], state[0]],
        scratch_shapes=work[:1],
        compiler_params=PARAMS,
        cost_estimate=SHORT,
        name="last_weights",
    )(*in_vmem(across, bias, *carried), third_keys)
    return pl.pallas_call(
        last_kernel,
        in_specs=[VMEM_REF] * 4,
        out_specs=pl.BlockSpec(memory_space=pl.ANY),
        out_shape=jax.ShapeDtypeStruct((rows, cols), jnp.bfloat16),
        scratch_shapes=[
            pltpu.VMEM((rows, cols), jnp.bfloat16),
            pltpu.SemaphoreType.DMA((heads,)),
        ],
        compiler_params=PARAMS,
        cost_estimate=SHORT,
        name="last_values",
    )(*in_vmem(*last), third_values)


def online_kernel(heads, q_ref, k_ref, v_ref, key_pos_ref, query_pos_ref, start_ref, out_ref, peak_ref, acc_ref):
    step = pl.program_id(0)

    @pl.when(step == 0)
    def _():
        peak_ref[...] = jnp.full(peak_ref.shape, NEG_FILL, jnp.float32)
        acc_ref[...] = jnp.zeros(acc_ref.shape, jnp.float32)

    key_pos = key_pos_ref[...]
    visible = (key_pos >= start_ref[...]) & (key_pos <= query_pos_ref[...])
    values = v_ref[...]
    ext = jnp.concatenate([values, jnp.ones_like(values)], axis=1)
    for head in range(heads):
        q = q_ref[:, head * HEAD_WIDTH:(head + 1) * HEAD_WIDTH]
        scores = lax.dot_general(
            q, k_ref[...], (((1,), (1,)), ((), ())), preferred_element_type=jnp.float32
        )
        scaled = jnp.where(visible, scores * (HEAD_WIDTH ** -0.5 * LOG2_E), NEG_FILL)
        before = peak_ref[head]
        peak = jnp.maximum(before, jnp.max(scaled, axis=1, keepdims=True))
        weights = jnp.where(visible, jnp.exp2(scaled - peak), 0.0).astype(jnp.bfloat16)
        peak_ref[head] = peak
        acc_ref[head] = acc_ref[head] * jnp.exp2(before - peak) + jnp.dot(
            weights, ext, preferred_element_type=jnp.float32
        )

    @pl.when(step == pl.num_programs(0) - 1)
    def _():
        for head in range(heads):
            acc = acc_ref[head]
            out_ref[:, head * HEAD_WIDTH:(head + 1) * HEAD_WIDTH] = (
                acc[:, :HEAD_WIDTH] / acc[:, HEAD_WIDTH:]
            ).astype(jnp.bfloat16)


def online_attention(queries, keys, values, key_pos, query_pos, starts, chunk):
    rows, cols = queries.shape
    heads = cols // HEAD_WIDTH
    key_count = keys.shape[0]
    return pl.pallas_call(
        lambda *refs: online_kernel(heads, *refs),
        grid=(key_count // chunk,),
        in_specs=[
            pl.BlockSpec((rows, cols), lambda j: (0, 0)),
            pl.BlockSpec((chunk, HEAD_WIDTH), lambda j: (j, 0)),
            pl.BlockSpec((chunk, HEAD_WIDTH), lambda j: (j, 0)),
            pl.BlockSpec((1, chunk), lambda j: (0, j)),
            pl.BlockSpec((rows, 1), lambda j: (0, 0)),
            pl.BlockSpec((rows, 1), lambda j: (0, 0)),
        ],
        out_specs=pl.BlockSpec((rows, cols), lambda j: (0, 0)),
        out_shape=jax.ShapeDtypeStruct((rows, cols), jnp.bfloat16),
        scratch_shapes=[
            pltpu.VMEM((heads, rows, 1), jnp.float32),
            pltpu.VMEM((heads, rows, 2 * HEAD_WIDTH), jnp.float32),
        ],
        compiler_params=pltpu.CompilerParams(vmem_limit_bytes=32 << 20),
        name="online",
    )(queries, keys, values, key_pos, query_pos, starts)


def body(queries, keys, values, lengths, old_place):
    devices = lax.axis_size("seq")
    row_count = queries.shape[0]
    key_count = row_count * devices
    if devices == 4 and key_count <= 1024:
        return staged_attention(queries, keys, values, lengths, old_place)
    all_keys = lax.all_gather(keys, "seq", axis=0, tiled=True)
    all_values = lax.all_gather(values, "seq", axis=0, tiled=True)
    key_pos, query_pos, starts = block_places(
        lengths, old_place, lax.axis_index("seq"), row_count, key_count
    )
    return online_attention(queries, all_keys, all_values, key_pos, query_pos, starts, 512)


def solution(mesh):
    in_specs = (
        P(("groups", "seq"), "mp"),
        P(("groups", "seq"), "mp"),
        P(("groups", "seq"), "mp"),
        P("groups"),
        P("groups"),
    )
    out_specs = P(("groups", "seq"), "mp")
    return jax.shard_map(body, mesh=mesh, in_specs=in_specs, out_specs=out_specs, check_vma=False)
```
